32 devices in a mesh: tm: 8 (over y, x, core), head: 4 (over z).
Axes of the slice: x: 2, y: 2, z: 4, core: 2. Of those that a mesh axis runs over, the one named last changes fastest.
Arguments:
- query_rows: bfloat16 [2048, 4096], P('tm', 'head'), may hold values from -6 to 6
- key_rows: bfloat16 [2048, 4096], P('tm', 'head'), may hold values from -6 to 6
- value_rows: bfloat16 [2048, 4096], P('tm', 'head'), may hold values from -12 to 12
- frame_counts: int32 [8], replicated, may hold values from 1 to 4, 24 in all
- history: bfloat16 [16, 4096], P('tm', 'head'), may hold values from -3 to 3
- offsets: int32 [8, 8], P('tm'), may hold values from 0 to 7, each once within a row
- cotangent: bfloat16 [2176, 2048], P('tm'), may hold values from -0.1875 to 0.1875
Outputs:
- attended: bfloat16 [2048, 4096], P('tm', 'head')
- disc_grad: float32 [2048, 4096], P('tm', 'head')
The draws below stay inside these ranges and needn't reach their ends.
Inputs may be any that keep to these rules, and one draw needn't show every extreme that they name: Each row of offsets names every number below 8 once.
All inputs are finite; a program needn't handle non-finite values.
Results may differ from the reference program's by a relative error of at most 0.0049.
Values may be sent and summed in bfloat16 or wider, within the bound.
No kernel may reach another device: no remote copies, remote signals or barrier semaphores. Data moves between devices by JAX's collectives and lax.ppermute only.
A program may use at most 64 MiB of HBM per device.

```python
import math
import jax
import jax.numpy as jnp
import numpy as np
from jax import lax

H = 32
HD = 128
D = 4096
FRAMES = 4
TPF = 64
TOK_DEV = 256
WINB = 4
TILE = 2
CLIP = 8
CLIP_TOK = 16
DH = 2048
TOKENS = 2048
HIST = 16
ROWS_ALL = 2176
N_TM = 8


def draw_query_rows(key, part):
    sub_key = jax.random.fold_in(key, 11)
    values_raw = jnp.clip(jax.random.normal(sub_key, (TOKENS, H * HD), jnp.float32), -6.0, 6.0)
    return values_raw.astype(jnp.bfloat16)


def draw_key_rows(key, part):
    sub_key = jax.random.fold_in(key, 12)
    values_raw = jnp.clip(jax.random.normal(sub_key, (TOKENS, H * HD), jnp.float32), -6.0, 6.0)
    return values_raw.astype(jnp.bfloat16)


def spiked(entries, key, source, target, parts, factor):
    owner, partner = [(jnp.arange(entries.shape[dim]) // (entries.shape[dim] // parts)).reshape([-1 if axis == dim else 1 for axis in range(entries.ndim)]) for dim in (source, target)]
    chosen = jax.random.permutation(key, parts)[partner]
    strong = (owner == chosen) | (owner == (partner + parts // 2) % parts)
    return jnp.where(strong, factor * entries, entries)


def block_levels(stream_key, shape, pieces, least, top_value):
    def one(position, parts):
        heights = jax.random.uniform(jax.random.fold_in(jax.random.fold_in(stream_key, 6), position), (parts,), jnp.float32, least / len(pieces), top_value / len(pieces))
        return jnp.repeat(jnp.exp(heights), shape[position] // parts).reshape((-1,) + (1,) * (len(shape) - position - 1))

    factor_of = one(*pieces[0])
    for cut in pieces[1:]:
        factor_of = factor_of * one(*cut)
    return factor_of


def split_up(amount, total, reach, skew):
    weights = [(1 << 20) // math.isqrt(rank ** skew) + 1 for rank in range(2, amount + 1)]
    spare, counts = total - reach - (amount - 1), [1] * (amount - 1)
    while spare > 0:
        candidates = [i for i in range(amount - 1) if counts[i] < reach]
        whole, budget = sum([weights[i] for i in candidates]), spare
        for i in candidates:
            extra = min(reach - counts[i], max(1, budget * weights[i] // whole), spare)
            counts[i] = counts[i] + extra
            spare = spare - extra
    return np.array([reach] + counts)


def ragged(stream_key, number_of, total, limit, skew):
    if number_of == 2:
        one = jax.random.randint(stream_key, (), max(1, total - limit), min(limit, total - 1) + 1)
        return jnp.stack([one, total - one])
    tallies = jnp.asarray(split_up(number_of, total, limit, skew), jnp.int32)
    pairs = (number_of - 1) // 2
    donor, sink = tallies[1:1 + 2 * pairs:2], tallies[2:2 + 2 * pairs:2]
    slack = jnp.minimum(donor - 1, limit - sink)
    passed = jax.random.randint(jax.random.fold_in(stream_key, 1), (pairs,), 0, 1 << 20) % (slack + 1)
    tallies = tallies.at[1:1 + 2 * pairs:2].set(donor - passed).at[2:2 + 2 * pairs:2].set(sink + passed)
    return tallies[jax.random.permutation(jax.random.fold_in(stream_key, 2), number_of)]


def centred(rng, shape, scale, bound, split=(), kind=jnp.bfloat16):
    result = jax.random.normal(rng, shape, jnp.float32) * scale
    if len(split) > 0:
        result = block_levels(rng, shape, split, -0.22, 0.18) * result
    return jnp.clip(result, min=-bound, max=bound).astype(kind)


def noise_with(rng, extent, width, most, shards, heavy, kind=jnp.bfloat16):
    values = width * jax.random.normal(rng, extent, jnp.float32)
    if shards:
        values = values * block_levels(rng, extent, shards, -0.22, 0.18)
    return jnp.clip(spiked(values, jax.random.fold_in(rng, 3), *heavy), -most, most).astype(kind)


def setup_inputs(seed: int = 0) -> dict:
    arg_keys = jax.random.split(jax.random.key(seed), 8)
    query_rows = draw_query_rows(jax.random.fold_in(arg_keys[7], 71), 0)
    key_rows = draw_key_rows(jax.random.fold_in(arg_keys[7], 71), 0)
    value_rows = centred(arg_keys[2], (TOKENS, D), 2.0, 12.0, ((0, 8), (1, 4)))
    frame_counts = ragged(arg_keys[3], N_TM, 3 * N_TM, FRAMES, 1).astype(jnp.int32)
    history = centred(arg_keys[4], (HIST, D), 0.5, 3.0, ((0, 8), (1, 4)))
    offsets = jax.vmap(lambda own: jax.random.permutation(own, N_TM))(jax.random.split(arg_keys[5], N_TM)).reshape((N_TM, CLIP)).astype(jnp.int32)
    cotangent = noise_with(arg_keys[6], (ROWS_ALL, DH), ROWS_ALL ** -0.5, 0.1875, ((0, 8),), (0, 1, 8, 2.0))
    return dict(query_rows=query_rows, key_rows=key_rows, value_rows=value_rows, frame_counts=frame_counts, history=history, offsets=offsets, cotangent=cotangent)


def reference(query_rows, key_rows, value_rows, frame_counts, history, offsets, cotangent):
    score_scale = 1.0 / math.sqrt(HD)
    query_blocks = query_rows.reshape(N_TM, TOK_DEV, H, HD)
    key_blocks = jnp.concatenate([jnp.zeros((WINB - 1, TOK_DEV, H, HD), key_rows.dtype), key_rows.reshape(N_TM, TOK_DEV, H, HD)], axis=0)
    value_blocks = jnp.concatenate([jnp.zeros((WINB - 1, TOK_DEV, H, HD), value_rows.dtype), value_rows.reshape(N_TM, TOK_DEV, H, HD)], axis=0)
    frame_index = jnp.arange(TOK_DEV, dtype=jnp.int32) // TPF
    kept_blocks = frame_index[None, :] < frame_counts[:, None]
    kept_padded = jnp.concatenate([jnp.zeros((WINB - 1, TOK_DEV), dtype=bool), kept_blocks], axis=0)

    def one_block(block_index):
        key_window = lax.dynamic_slice_in_dim(key_blocks, block_index, WINB, 0).reshape(WINB * TOK_DEV, H, HD)
        value_window = lax.dynamic_slice_in_dim(value_blocks, block_index, WINB, 0).reshape(WINB * TOK_DEV, H, HD)
        kept_window = lax.dynamic_slice_in_dim(kept_padded, block_index, WINB, 0).reshape(WINB * TOK_DEV)
        query_block = query_blocks[block_index]
        scores = jnp.einsum('qhd,khd->hqk', query_block.astype(jnp.float32), key_window.astype(jnp.float32)) * score_scale
        scores = jnp.where(kept_window[None, None, :], scores, -jnp.inf)
        row_max = lax.optimization_barrier(jnp.max(scores, axis=-1, keepdims=True))
        weights = jnp.exp(scores - row_max)
        probs = (weights / lax.optimization_barrier(jnp.sum(weights, axis=-1, keepdims=True))).astype(jnp.bfloat16)
        mixed = jnp.einsum('hqk,khd->qhd', probs.astype(jnp.float32), value_window.astype(jnp.float32))
        return mixed.astype(jnp.bfloat16).reshape(TOK_DEV, H * HD)
    attended = lax.map(one_block, jnp.arange(N_TM, dtype=jnp.int32)).reshape(TOKENS, H * HD)
    owners = jnp.arange(N_TM, dtype=jnp.int32)
    source_tile = (owners[:, None] - offsets) % N_TM
    source_row = (source_tile[:, :, None] * TILE + jnp.arange(TILE, dtype=jnp.int32)[None, None, :]).reshape(N_TM, CLIP_TOK)
    clip_hist = history[source_row]
    disc_clip = jnp.concatenate([clip_hist, attended.reshape(N_TM, TOK_DEV, H * HD)], axis=1).reshape(ROWS_ALL, H * HD)
    disc_grad = jnp.dot(cotangent.T, disc_clip, preferred_element_type=jnp.float32)
    return (attended, disc_grad)
```

```python
import math

import jax
import jax.numpy as jnp
from jax import lax
from jax.experimental import pallas as pl
from jax.experimental.pallas import tpu as pltpu
from jax.sharding import PartitionSpec as P

HD = 128
TPF = 64
WINB = 4
VMEM_LIMIT = 48 * 1024 * 1024


def from_behind(x, axis, by):
    devices = lax.axis_size(axis)
    pairs = [(i, i + by) for i in range(devices) if 0 <= i + by < devices]
    return lax.ppermute(x, axis, pairs)


def window_body(query_rows, key_rows, value_rows, frame_counts, history, offsets, cotangent):
    tok_rows, feat_width = query_rows.shape
    local_heads = feat_width // HD
    block_total = lax.axis_size("tm")
    own_block = lax.axis_index("tm")
    score_scale = 1.0 / math.sqrt(HD)
    key_value = jnp.stack([key_rows, value_rows])
    pieces = []
    for distance in range(WINB - 1, 0, -1):
        pieces.append(from_behind(key_value, "tm", distance))
    window = jnp.concatenate(pieces + [key_value], axis=1)
    source_block = own_block - (WINB - 1) + jnp.arange(WINB, dtype=jnp.int32)
    block_match = jnp.arange(block_total, dtype=jnp.int32)[None, :] == source_block[:, None]
    block_count = jnp.sum(jnp.where(block_match, frame_counts[None, :], 0), axis=1)
    frame_index = jnp.arange(tok_rows, dtype=jnp.int32) // TPF
    kept_mask = (
        (source_block[:, None] >= 0) & (frame_index[None, :] < block_count[:, None])
    ).reshape(WINB * tok_rows)
    key_window = window[0].reshape(WINB * tok_rows, local_heads, HD)
    value_window = window[1].reshape(WINB * tok_rows, local_heads, HD)
    query_heads = query_rows.reshape(tok_rows, local_heads, HD)
    scores = (
        jnp.einsum("qhd,khd->hqk", query_heads, key_window, preferred_element_type=jnp.float32)
        * score_scale
    )
    scores = jnp.where(kept_mask[None, None, :], scores, -jnp.inf)
    row_max = jnp.max(scores, axis=-1, keepdims=True)
    weights = jnp.exp(scores - row_max)
    probs = (weights / jnp.sum(weights, axis=-1, keepdims=True)).astype(jnp.bfloat16)
    mixed = jnp.einsum("hqk,khd->qhd", probs, value_window, preferred_element_type=jnp.float32)
    attended = mixed.astype(jnp.bfloat16).reshape(tok_rows, feat_width)
    tile_rows = history.shape[0]
    source_tile = (own_block - offsets[0]) % block_total
    source_row = (
        source_tile[:, None] * tile_rows + jnp.arange(tile_rows, dtype=jnp.int32)[None, :]
    ).reshape(-1)
    incoming = lax.all_gather(history, "tm", axis=0, tiled=True)
    piece_rows = incoming.shape[0]
    selector = (source_row[:, None] == jnp.arange(piece_rows, dtype=jnp.int32)[None, :]).astype(
        jnp.bfloat16
    )
    clip_hist = jnp.dot(selector, incoming, preferred_element_type=jnp.float32).astype(jnp.bfloat16)
    disc_clip = jnp.concatenate([clip_hist, attended], axis=0)
    disc_grad = lax.psum_scatter(
        lax.dot_general(
            cotangent, disc_clip, (((0,), (0,)), ((), ())), preferred_element_type=jnp.float32
        ),
        "tm",
        scatter_dimension=0,
        tiled=True,
    )
    return (attended, disc_grad)


def pack_kernel(n, off_ref, q_ref, k_ref, v_ref, hist_ref, cot_ref, out_ref):
    own = lax.axis_index("tm")
    tok = q_ref.shape[0]
    tile = hist_ref.shape[0]
    clip_rows = n * tile
    cot_rows = cot_ref.shape[0]
    cols = cot_ref.shape[1] // n
    for h in range(n):
        lanes = slice(h * HD, (h + 1) * HD)
        out_ref[h, 0:tok, :] = q_ref[:, lanes]
        out_ref[h, tok : 2 * tok, :] = k_ref[:, lanes]
        out_ref[h, 2 * tok : 3 * tok, :] = v_ref[:, lanes]
    base = 3 * tok
    hist = hist_ref[...].astype(jnp.float32)
    row = lax.broadcasted_iota(jnp.int32, (clip_rows, n * HD), 0)
    placed = jnp.zeros((clip_rows, n * HD), jnp.float32)
    for t in range(tile):
        placed = jnp.where(row == own * tile + t, hist[t : t + 1, :], placed)
    placed = placed.astype(jnp.bfloat16)
    for h in range(n):
        out_ref[h, base : base + clip_rows, :] = placed[:, h * HD : (h + 1) * HD]
    base += clip_rows
    r = lax.broadcasted_iota(jnp.int32, (clip_rows, clip_rows), 0)
    c = lax.broadcasted_iota(jnp.int32, (clip_rows, clip_rows), 1)
    select = jnp.zeros((clip_rows, clip_rows), jnp.float32)
    for j in range(n):
        src = lax.rem(own - off_ref[0, j] + 2 * n, n)
        for t in range(tile):
            select = jnp.where((c == j * tile + t) & (r == src * tile + t), 1.0, select)
    by_row = jnp.dot(
        select.astype(jnp.bfloat16), cot_ref[0:clip_rows, :], preferred_element_type=jnp.float32
    ).astype(jnp.bfloat16)
    for d in range(n):
        for u in range(cols // HD):
            lanes = slice(d * cols + u * HD, d * cols + (u + 1) * HD)
            at = base + u * cot_rows
            out_ref[d, at : at + clip_rows, :] = by_row[:, lanes]
            out_ref[d, at + clip_rows : at + cot_rows, :] = cot_ref[clip_rows:cot_rows, lanes]


def attend_kernel(n, tok, counts_ref, x_ref, out_ref):
    half = n // 2
    rate = math.log2(math.e) / math.sqrt(HD)
    token = lax.broadcasted_iota(jnp.int32, (1, tok), 1)
    bias = [
        jnp.where(token < counts_ref[s] * TPF, 0.0, -jnp.inf).astype(jnp.float32) for s in range(n)
    ]
    for b in range(n):
        first = max(0, b - (WINB - 1))
        q = x_ref[b, 0:tok, :]
        scores = [
            lax.dot_general(
                q,
                x_ref[s, tok : 2 * tok, :],
                (((1,), (1,)), ((), ())),
                preferred_element_type=jnp.float32,
            )
            + bias[s]
            for s in range(first, b + 1)
        ]
        top = jnp.max(scores[0], axis=1, keepdims=True)
        for s in scores[1:]:
            top = jnp.maximum(top, jnp.max(s, axis=1, keepdims=True))
        weights = [jnp.exp2((s - top) * rate) for s in scores]
        total = jnp.sum(weights[0], axis=1, keepdims=True)
        for w in weights[1:]:
            total = total + jnp.sum(w, axis=1, keepdims=True)
        share = 1.0 / total
        mixed = jnp.zeros((tok, HD), jnp.float32)
        for s, w in zip(range(first, b + 1), weights):
            mixed = mixed + jnp.dot(
                (w * share).astype(jnp.bfloat16),
                x_ref[s, 2 * tok : 3 * tok, :],
                preferred_element_type=jnp.float32,
            )
        mixed = mixed.astype(jnp.bfloat16)
        at = (b // 2) * tok
        for c in range(half):
            out_ref[2 * c + b % 2, at : at + tok, :] = mixed
    clip_rows = out_ref.shape[1] - half * tok
    hist = jnp.zeros((clip_rows, HD), jnp.float32)
    for s in range(n):
        hist = hist + x_ref[s, 3 * tok : 3 * tok + clip_rows, :].astype(jnp.float32)
    hist = hist.astype(jnp.bfloat16)
    for d in range(n):
        out_ref[d, half * tok :, :] = hist


def grad_rows(cot, a_ref, tok, clip_rows):
    n = a_ref.shape[0]
    half = len(cot)
    rows = jnp.concatenate([a_ref[h, 0 : half * tok, :] for h in range(n)], axis=1)
    hist = jnp.concatenate([a_ref[h, half * tok :, :] for h in range(n)], axis=1)
    dims = (((0,), (0,)), ((), ()))
    left = jnp.concatenate([x[clip_rows:] for x in cot], axis=0)
    left_hist = jnp.concatenate([x[:clip_rows] for x in cot], axis=0)
    out = lax.dot_general(left, rows, dims, preferred_element_type=jnp.float32)
    return out + lax.dot_general(
        left_hist, jnp.concatenate([hist] * half, axis=0), dims, preferred_element_type=jnp.float32
    )


def other_kernel(tok, clip_rows, cot_ref, a_ref, out_ref):
    cot_rows = clip_rows + tok
    units = cot_ref.shape[1] // cot_rows
    cot = [
        jnp.concatenate(
            [cot_ref[c, u * cot_rows : (u + 1) * cot_rows, :] for u in range(units)], axis=1
        )
        for c in range(cot_ref.shape[0])
    ]
    out_ref[...] = grad_rows(cot, a_ref, tok, clip_rows).astype(jnp.bfloat16)


def own_kernel(tok, clip_rows, x_ref, a_ref, att_ref, out_ref):
    n = a_ref.shape[0]
    own = lax.axis_index("tm")
    chip = own // 2
    side = lax.rem(own, 2)
    cot_rows = clip_rows + tok
    base = 3 * tok + clip_rows
    units = (x_ref.shape[1] - base) // cot_rows
    cot = [
        jnp.concatenate(
            [
                x_ref[2 * c + side, base + u * cot_rows : base + (u + 1) * cot_rows, :]
                for u in range(units)
            ],
            axis=1,
        )
        for c in range(n // 2)
    ]
    out_ref[...] = grad_rows(cot, a_ref, tok, clip_rows)
    at = pl.multiple_of(chip * tok, tok)
    for h in range(n):
        att_ref[:, h * HD : (h + 1) * HD] = a_ref[h, pl.ds(at, tok), :]


def head_body(query_rows, key_rows, value_rows, frame_counts, history, offsets, cotangent):
    n = lax.axis_size("tm")
    half = n // 2
    tok, width = query_rows.shape
    clip_rows = n * history.shape[0]
    cot_rows, all_cols = cotangent.shape
    cols = all_cols // n
    base = 3 * tok + clip_rows
    length = base + (cols // HD) * cot_rows
    vmem = pl.BlockSpec(memory_space=pltpu.VMEM)
    smem = pl.BlockSpec(memory_space=pltpu.SMEM)
    params = pltpu.CompilerParams(vmem_limit_bytes=VMEM_LIMIT)
    side = lax.rem(lax.axis_index("tm"), 2)
    swap = [(i, i ^ 1) for i in range(n)]

    packed = pl.pallas_call(
        lambda *refs: pack_kernel(n, *refs),
        out_shape=jax.ShapeDtypeStruct((n, length, HD), jnp.bfloat16),
        in_specs=[smem] + [vmem] * 5,
        out_specs=vmem,
        compiler_params=params,
        name="pack",
    )(offsets, query_rows, key_rows, value_rows, history, cotangent)
    by_head = lax.all_to_all(packed, "tm", 0, 0)

    for_other = lax.dynamic_slice(
        by_head.reshape(half, 2, length, HD), (0, 1 - side, base, 0), (half, 1, length - base, HD)
    ).reshape(half, length - base, HD)
    from_other = lax.ppermute(for_other, "tm", swap)

    spread = pl.pallas_call(
        lambda *refs: attend_kernel(n, tok, *refs),
        out_shape=jax.ShapeDtypeStruct((n, half * tok + clip_rows, HD), jnp.bfloat16),
        in_specs=[smem, vmem],
        out_specs=vmem,
        compiler_params=params,
        cost_estimate=pl.CostEstimate(
            flops=4 * n * tok * WINB * tok * HD,
            bytes_accessed=2 * 2 * n * length * HD,
            transcendentals=n * tok * WINB * tok,
        ),
        name="attend",
    )(frame_counts, by_head)
    gathered = lax.all_to_all(spread, "tm", 0, 0)

    grad_cost = pl.CostEstimate(
        flops=2 * cols * half * cot_rows * width,
        bytes_accessed=2 * n * (half * tok + clip_rows) * HD + 4 * cols * width,
        transcendentals=0,
    )
    other = pl.pallas_call(
        lambda *refs: other_kernel(tok, clip_rows, *refs),
        out_shape=jax.ShapeDtypeStruct((cols, width), jnp.bfloat16),
        in_specs=[vmem, vmem],
        out_specs=vmem,
        compiler_params=params,
        cost_estimate=grad_cost,
        name="grad_other",
    )(from_other, gathered)
    arrived = lax.ppermute(other, "tm", swap)
    attended, own = pl.pallas_call(
        lambda *refs: own_kernel(tok, clip_rows, *refs),
        out_shape=(
            jax.ShapeDtypeStruct((tok, width), jnp.bfloat16),
            jax.ShapeDtypeStruct((cols, width), jnp.float32),
        ),
        in_specs=[vmem, vmem],
        out_specs=(vmem, vmem),
        compiler_params=params,
        cost_estimate=grad_cost,
        name="grad_own",
    )(by_head, gathered)
    return attended, own + arrived.astype(jnp.float32)


def body(query_rows, key_rows, value_rows, frame_counts, history, offsets, cotangent):
    n = lax.axis_size("tm")
    tok, width = query_rows.shape
    by_heads = (
        n % 2 == 0
        and width == n * HD
        and offsets.shape[1] == n
        and cotangent.shape[0] == tok + n * history.shape[0]
        and cotangent.shape[1] % (n * HD) == 0
        and tok % 16 == 0
        and (n * history.shape[0]) % 16 == 0
    )
    plan = head_body if by_heads else window_body
    return plan(query_rows, key_rows, value_rows, frame_counts, history, offsets, cotangent)


def solution(mesh):
    in_specs = (
        P("tm", "head"),
        P("tm", "head"),
        P("tm", "head"),
        P(),
        P("tm", "head"),
        P("tm", None),
        P("tm", None),
    )
    out_specs = (P("tm", "head"), P("tm", "head"))
    return jax.shard_map(body, mesh=mesh, in_specs=in_specs, out_specs=out_specs, check_vma=False)
```

```python
import math

import jax
import jax.numpy as jnp
from jax import lax
from jax.experimental import pallas as pl
from jax.experimental.pallas import tpu as pltpu
from jax.sharding import PartitionSpec as P

HD = 128
TPF = 64
WINB = 4
VMEM_LIMIT = 32 * 1024 * 1024
PACK_LIMIT = 63 * 1024 * 1024


def from_behind(x, axis, by):
    devices = lax.axis_size(axis)
    pairs = [(i, i + by) for i in range(devices) if 0 <= i + by < devices]
    return lax.ppermute(x, axis, pairs)


def window_body(query_rows, key_rows, value_rows, frame_counts, history, offsets, cotangent):
    tok_rows, feat_width = query_rows.shape
    local_heads = feat_width // HD
    block_total = lax.axis_size("tm")
    own_block = lax.axis_index("tm")
    score_scale = 1.0 / math.sqrt(HD)
    key_value = jnp.stack([key_rows, value_rows])
    pieces = []
    for distance in range(WINB - 1, 0, -1):
        pieces.append(from_behind(key_value, "tm", distance))
    window = jnp.concatenate(pieces + [key_value], axis=1)
    source_block = own_block - (WINB - 1) + jnp.arange(WINB, dtype=jnp.int32)
    block_match = jnp.arange(block_total, dtype=jnp.int32)[None, :] == source_block[:, None]
    block_count = jnp.sum(jnp.where(block_match, frame_counts[None, :], 0), axis=1)
    frame_index = jnp.arange(tok_rows, dtype=jnp.int32) // TPF
    kept_mask = (
        (source_block[:, None] >= 0) & (frame_index[None, :] < block_count[:, None])
    ).reshape(WINB * tok_rows)
    key_window = window[0].reshape(WINB * tok_rows, local_heads, HD)
    value_window = window[1].reshape(WINB * tok_rows, local_heads, HD)
    query_heads = query_rows.reshape(tok_rows, local_heads, HD)
    scores = (
        jnp.einsum("qhd,khd->hqk", query_heads, key_window, preferred_element_type=jnp.float32)
        * score_scale
    )
    scores = jnp.where(kept_mask[None, None, :], scores, -jnp.inf)
    row_max = jnp.max(scores, axis=-1, keepdims=True)
    weights = jnp.exp(scores - row_max)
    probs = (weights / jnp.sum(weights, axis=-1, keepdims=True)).astype(jnp.bfloat16)
    mixed = jnp.einsum("hqk,khd->qhd", probs, value_window, preferred_element_type=jnp.float32)
    attended = mixed.astype(jnp.bfloat16).reshape(tok_rows, feat_width)
    tile_rows = history.shape[0]
    source_tile = (own_block - offsets[0]) % block_total
    source_row = (
        source_tile[:, None] * tile_rows + jnp.arange(tile_rows, dtype=jnp.int32)[None, :]
    ).reshape(-1)
    incoming = lax.all_gather(history, "tm", axis=0, tiled=True)
    piece_rows = incoming.shape[0]
    selector = (source_row[:, None] == jnp.arange(piece_rows, dtype=jnp.int32)[None, :]).astype(
        jnp.bfloat16
    )
    clip_hist = jnp.dot(selector, incoming, preferred_element_type=jnp.float32).astype(jnp.bfloat16)
    disc_clip = jnp.concatenate([clip_hist, attended], axis=0)
    disc_grad = lax.psum_scatter(
        lax.dot_general(
            cotangent, disc_clip, (((0,), (0,)), ((), ())), preferred_element_type=jnp.float32
        ),
        "tm",
        scatter_dimension=0,
        tiled=True,
    )
    return (attended, disc_grad)


def pack_kernel(n, lo, off_hbm, q_hbm, k_hbm, v_hbm, hist_hbm, cot_hbm, out_hbm, off, hist, clip, placed, by_row, sems):
    own = lax.axis_index("tm")
    plane = lax.rem(lax.axis_index("head"), 2)
    tok = q_hbm.shape[0]
    tile = hist.shape[0]
    clip_rows = n * tile
    cols = cot_hbm.shape[1] // n
    units = cols // HD
    part = cot_hbm.shape[0] - lo
    base = 3 * tok + clip_rows
    bulk, small = [], []
    low = pl.multiple_of(plane * lo, 16)
    for h in range(n):
        for i, x in enumerate((q_hbm, k_hbm, v_hbm)):
            bulk.append((x.at[:, pl.ds(h * HD, HD)], out_hbm.at[h, pl.ds(i * tok, tok), :]))
        for u in range(units):
            lanes = pl.ds(h * cols + u * HD, HD)
            at = base + u * part
            bulk.append(
                (
                    cot_hbm.at[pl.ds(low + clip_rows, part - clip_rows), lanes],
                    out_hbm.at[h, pl.ds(at + clip_rows, part - clip_rows), :],
                )
            )
            small.append((by_row.at[:, lanes], out_hbm.at[h, pl.ds(at, clip_rows), :]))
        small.append((placed.at[:, pl.ds(h * HD, HD)], out_hbm.at[h, pl.ds(3 * tok, clip_rows), :]))
    fetch = [(off_hbm, off), (hist_hbm, hist), (cot_hbm.at[pl.ds(low, clip_rows), :], clip)]
    copies = [
        pltpu.make_async_copy(a, b, sems.at[i]) for i, (a, b) in enumerate(fetch + bulk + small)
    ]
    fetch, rest = copies[: len(fetch)], copies[len(fetch) :]
    bulk, small = rest[: len(bulk)], rest[len(bulk) :]
    for copy in fetch + bulk:
        copy.start()
    for copy in fetch:
        copy.wait()
    tiles = hist[...].astype(jnp.float32)
    row = lax.broadcasted_iota(jnp.int32, (clip_rows, n * HD), 0)
    total = jnp.zeros((clip_rows, n * HD), jnp.float32)
    for t in range(tile):
        total = jnp.where(row == own * tile + t, tiles[t : t + 1, :], total)
    placed[...] = total.astype(jnp.bfloat16)
    r = lax.broadcasted_iota(jnp.int32, (clip_rows, clip_rows), 0)
    c = lax.broadcasted_iota(jnp.int32, (clip_rows, clip_rows), 1)
    select = jnp.where((r == c) & (plane != 0), 1.0, 0.0)
    for j in range(n):
        src = lax.rem(own - off[0, j] + 2 * n, n)
        for t in range(tile):
            hit = (c == j * tile + t) & (r == src * tile + t) & (plane == 0)
            select = jnp.where(hit, 1.0, select)
    by_row[...] = jnp.dot(
        select.astype(jnp.bfloat16), clip[...], preferred_element_type=jnp.float32
    ).astype(jnp.bfloat16)
    for copy in small:
        copy.start()
    for copy in bulk + small:
        copy.wait()


def attend_blocks(n, tok, parity, counts, x_ref, out_ref):
    rate = math.log2(math.e) / math.sqrt(HD)
    token = lax.broadcasted_iota(jnp.int32, (1, tok), 1)
    for i in range(n // 2):
        block = 2 * i + parity
        keys = min(WINB, 2 * i + 2)
        sources = [block - (keys - 1) + k for k in range(keys)]
        q = x_ref[block, 0:tok, :]
        scores = []
        for s in sources:
            at = jnp.maximum(s, 0)
            kept = jnp.where(s >= 0, counts[at], 0) * TPF
            scores.append(
                lax.dot_general(
                    q,
                    x_ref[at, tok : 2 * tok, :],
                    (((1,), (1,)), ((), ())),
                    preferred_element_type=jnp.float32,
                )
                + jnp.where(token < kept, 0.0, -jnp.inf).astype(jnp.float32)
            )
        top = jnp.max(scores[0], axis=1, keepdims=True)
        for s in scores[1:]:
            top = jnp.maximum(top, jnp.max(s, axis=1, keepdims=True))
        weights = [jnp.exp2((s - top) * rate) for s in scores]
        total = jnp.sum(weights[0], axis=1, keepdims=True)
        for w in weights[1:]:
            total = total + jnp.sum(w, axis=1, keepdims=True)
        share = 1.0 / total
        mixed = jnp.zeros((tok, HD), jnp.float32)
        for s, w in zip(sources, weights):
            mixed = mixed + jnp.dot(
                (w * share).astype(jnp.bfloat16),
                x_ref[jnp.maximum(s, 0), 2 * tok : 3 * tok, :],
                preferred_element_type=jnp.float32,
            )
        out_ref[i * tok : (i + 1) * tok, :] = mixed.astype(jnp.bfloat16)
    rows = n // 2 * tok
    clip_rows = out_ref.shape[0] - rows
    hist = jnp.zeros((clip_rows, HD), jnp.float32)
    for s in range(n):
        hist = hist + x_ref[s, 3 * tok : 3 * tok + clip_rows, :].astype(jnp.float32)
    out_ref[rows:, :] = hist.astype(jnp.bfloat16)


def attend_same_kernel(n, tok, counts_hbm, x_ref, out_ref, cot_ref, cot_other_ref, counts, sem):
    copy = pltpu.make_async_copy(counts_hbm, counts, sem)
    copy.start()
    side = lax.rem(lax.axis_index("tm"), 2)
    length = x_ref.shape[1]
    part = cot_ref.shape[1]
    for c in range(n // 2):
        cot_ref[c] = x_ref[2 * c + side, length - part : length, :]
        cot_other_ref[c] = x_ref[2 * c + 1 - side, length - part : length, :]
    copy.wait()
    attend_blocks(n, tok, side, counts, x_ref, out_ref)


def attend_cross_kernel(n, tok, counts_hbm, x_ref, out_ref, counts, sem):
    copy = pltpu.make_async_copy(counts_hbm, counts, sem)
    copy.start()
    copy.wait()
    attend_blocks(n, tok, 1 - lax.rem(lax.axis_index("tm"), 2), counts, x_ref, out_ref)


def turn_kernel(lo, clip_rows, mine_ref, swapped_ref, out_ref):
    plane = lax.rem(lax.axis_index("head"), 2)
    blocks, length, _ = mine_ref.shape
    part = out_ref.shape[1] // blocks - lo
    units = length // part
    token_pieces, clip_pieces = [], []
    for c in range(blocks):
        pieces = []
        for u in range(units):
            a = mine_ref[c, u * part : (u + 1) * part, :]
            b = swapped_ref[c, u * part : (u + 1) * part, :]
            low = jnp.where(plane == 0, a, b)
            high = jnp.where(plane == 0, b, a)
            pieces.append(jnp.concatenate([low[:lo], high], axis=0))
        whole = jnp.concatenate(pieces, axis=1)
        clip_pieces.append(whole[:clip_rows])
        token_pieces.append(whole[clip_rows:])
    out_ref[...] = jnp.concatenate(token_pieces + clip_pieces, axis=0).T


def grad_part(turned_ref, head_refs, rows):
    right = jnp.concatenate([x[0:rows, :] for x in head_refs], axis=1)
    hist = jnp.concatenate([x[rows:, :] for x in head_refs], axis=1)
    copies = (turned_ref.shape[1] - rows) // hist.shape[0]
    out = jnp.dot(turned_ref[:, 0:rows], right, preferred_element_type=jnp.float32)
    return out + jnp.dot(
        turned_ref[:, rows:],
        jnp.concatenate([hist] * copies, axis=0),
        preferred_element_type=jnp.float32,
    )


def grad_kernel(rows, turned_ref, *refs):
    out_ref = refs[-1]
    out_ref[...] = grad_part(turned_ref, refs[:-1], rows).astype(out_ref.dtype)


def finish_kernel(n, tok, own_near, own_far, got_near, got_far, *refs):
    heads, att_ref, out_ref = refs[:n], refs[n], refs[n + 1]
    own = lax.axis_index("tm")
    at = pl.multiple_of(own // 2 * tok, tok)
    near = own_near.shape[1] // HD
    for k in range(n):
        lanes = pl.ds(pl.multiple_of((own ^ k) * HD, HD), HD)
        att_ref[:, lanes] = heads[k][pl.ds(at, tok), :]
        mine, got, a = (own_near, got_near, k) if k < near else (own_far, got_far, k - near)
        b = a ^ 1
        out_ref[:, lanes] = mine[:, a * HD : (a + 1) * HD] + got[:, b * HD : (b + 1) * HD].astype(
            jnp.float32
        )


def head_body(query_rows, key_rows, value_rows, frame_counts, history, offsets, cotangent):
    n = lax.axis_size("tm")
    planes = lax.axis_size("head")
    half = n // 2
    tok, width = query_rows.shape
    tile = history.shape[0]
    clip_rows = n * tile
    cot_rows, all_cols = cotangent.shape
    cols = all_cols // n
    units = cols // HD
    lo = cot_rows // 32 * 16
    part = cot_rows - lo
    base = 3 * tok + clip_rows
    length = base + units * part
    rows = half * tok
    vmem = pl.BlockSpec(memory_space=pltpu.VMEM)
    hbm = pl.BlockSpec(memory_space=pl.ANY)
    bf16 = jnp.bfloat16

    def swap(x, bit):
        return lax.ppermute(x, "tm", [(i, i ^ bit) for i in range(n)])

    def swap_plane(x, bit):
        pairs = [
            (i * planes + p, (i ^ bit) * planes + (p ^ 1)) for i in range(n) for p in range(planes)
        ]
        return lax.ppermute(x, ("tm", "head"), pairs)

    def call(
        kernel, name, outs, specs, flops, scratch=(), exps=0, out_spec=vmem, limit=VMEM_LIMIT
    ):
        shapes = [jax.ShapeDtypeStruct(s, d) for s, d in outs]
        moved = 2 * sum(math.prod(s.shape) * s.dtype.itemsize for s in shapes)
        return pl.pallas_call(
            kernel,
            out_shape=tuple(shapes),
            in_specs=specs,
            out_specs=tuple([out_spec] * len(shapes)),
            scratch_shapes=scratch,
            compiler_params=pltpu.CompilerParams(vmem_limit_bytes=limit),
            cost_estimate=pl.CostEstimate(flops=flops, bytes_accessed=moved, transcendentals=exps),
            name=name,
        )

    (packed,) = call(
        lambda *refs: pack_kernel(n, lo, *refs),
        "pack",
        [((n, length, HD), bf16)],
        [hbm] * 6,
        0,
        (
            pltpu.SMEM(offsets.shape, jnp.int32),
            pltpu.VMEM(history.shape, bf16),
            pltpu.VMEM((clip_rows, all_cols), bf16),
            pltpu.VMEM((clip_rows, width), bf16),
            pltpu.VMEM((clip_rows, all_cols), bf16),
            pltpu.SemaphoreType.DMA((3 + n * (4 + 2 * units),)),
        ),
        out_spec=hbm,
        limit=PACK_LIMIT,
    )(offsets, query_rows, key_rows, value_rows, history, cotangent)
    by_head = lax.all_to_all(packed, "tm", 0, 0)

    counts = (pltpu.SMEM(frame_counts.shape, jnp.int32), pltpu.SemaphoreType.DMA)
    pairs = half * tok * WINB * tok
    head_shape = ((rows + clip_rows, HD), bf16)
    cot_shape = ((half, units * part, HD), bf16)
    same, cot_mine, cot_other = call(
        lambda *refs: attend_same_kernel(n, tok, *refs),
        "attend_same",
        [head_shape, cot_shape, cot_shape],
        [hbm, vmem],
        4 * pairs * HD,
        counts,
        pairs,
    )(frame_counts, by_head)
    x_same, y_same = swap(same, 2), swap(same, 4)
    (cross,) = call(
        lambda *refs: attend_cross_kernel(n, tok, *refs),
        "attend_cross",
        [head_shape],
        [hbm, vmem],
        4 * pairs * HD,
        counts,
        pairs,
    )(frame_counts, by_head)
    x_cross, y_cross, c_cross = swap(cross, 2 ^ 1), swap(cross, 4 ^ 1), swap(cross, 1)
    mine_up = swap_plane(cot_mine, 0)
    other, other_up = swap(cot_other, 1), swap_plane(cot_other, 1)
    far_same, far_cross = swap(x_same, 4), swap(y_cross, 2)

    def turn(a, b, name):
        (out,) = call(
            lambda *refs: turn_kernel(lo, clip_rows, *refs),
            name,
            [((cols, half * cot_rows), bf16)],
            [vmem] * 2,
            0,
        )(a, b)
        return out

    def grad(turned, heads, dtype, name):
        (out,) = call(
            lambda *refs: grad_kernel(rows, *refs),
            name,
            [((cols, len(heads) * HD), dtype)],
            [vmem] * (1 + len(heads)),
            2 * cols * half * cot_rows * len(heads) * HD,
        )(turned, *heads)
        return out

    turned_other = turn(other, other_up, "turn_other")
    turned_own = turn(cot_mine, mine_up, "turn_own")
    near = [same, c_cross, x_same, x_cross, y_same, y_cross]
    far = [far_same, far_cross]
    got_near = swap(grad(turned_other, near, bf16, "grad_other_near"), 1)
    own_near = grad(turned_own, near, jnp.float32, "grad_own_near")
    got_far = swap(grad(turned_other, far, bf16, "grad_other_far"), 1)
    own_far = grad(turned_own, far, jnp.float32, "grad_own_far")
    return call(
        lambda *refs: finish_kernel(n, tok, *refs),
        "finish",
        [((tok, width), bf16), ((cols, width), jnp.float32)],
        [vmem] * (4 + n),
        0,
    )(own_near, own_far, got_near, got_far, *near, *far)


def body(query_rows, key_rows, value_rows, frame_counts, history, offsets, cotangent):
    n = lax.axis_size("tm")
    tok, width = query_rows.shape
    by_heads = (
        n == 8
        and lax.axis_size("head") % 2 == 0
        and width == n * HD
        and offsets.shape[1] == n
        and cotangent.shape[0] == tok + n * history.shape[0]
        and cotangent.shape[1] % (n * HD) == 0
        and tok % 16 == 0
        and (n * history.shape[0]) % 16 == 0
    )
    plan = head_body if by_heads else window_body
    return plan(query_rows, key_rows, value_rows, frame_counts, history, offsets, cotangent)


def solution(mesh):
    in_specs = (
        P("tm", "head"),
        P("tm", "head"),
        P("tm", "head"),
        P(),
        P("tm", "head"),
        P("tm", None),
        P("tm", None),
    )
    out_specs = (P("tm", "head"), P("tm", "head"))
    return jax.shard_map(body, mesh=mesh, in_specs=in_specs, out_specs=out_specs, check_vma=False)
```

```python
import math

import jax
import jax.numpy as jnp
from jax import lax
from jax.experimental import pallas as pl
from jax.experimental.pallas import tpu as pltpu
from jax.sharding import PartitionSpec as P

HD = 128
TPF = 64
WINB = 4
VMEM_LIMIT = 32 * 1024 * 1024
PACK_LIMIT = 63 * 1024 * 1024


def from_behind(x, axis, by):
    devices = lax.axis_size(axis)
    pairs = [(i, i + by) for i in range(devices) if 0 <= i + by < devices]
    return lax.ppermute(x, axis, pairs)


def window_body(query_rows, key_rows, value_rows, frame_counts, history, offsets, cotangent):
    tok_rows, feat_width = query_rows.shape
    local_heads = feat_width // HD
    block_total = lax.axis_size("tm")
    own_block = lax.axis_index("tm")
    score_scale = 1.0 / math.sqrt(HD)
    key_value = jnp.stack([key_rows, value_rows])
    pieces = []
    for distance in range(WINB - 1, 0, -1):
        pieces.append(from_behind(key_value, "tm", distance))
    window = jnp.concatenate(pieces + [key_value], axis=1)
    source_block = own_block - (WINB - 1) + jnp.arange(WINB, dtype=jnp.int32)
    block_match = jnp.arange(block_total, dtype=jnp.int32)[None, :] == source_block[:, None]
    block_count = jnp.sum(jnp.where(block_match, frame_counts[None, :], 0), axis=1)
    frame_index = jnp.arange(tok_rows, dtype=jnp.int32) // TPF
    kept_mask = (
        (source_block[:, None] >= 0) & (frame_index[None, :] < block_count[:, None])
    ).reshape(WINB * tok_rows)
    key_window = window[0].reshape(WINB * tok_rows, local_heads, HD)
    value_window = window[1].reshape(WINB * tok_rows, local_heads, HD)
    query_heads = query_rows.reshape(tok_rows, local_heads, HD)
    scores = (
        jnp.einsum("qhd,khd->hqk", query_heads, key_window, preferred_element_type=jnp.float32)
        * score_scale
    )
    scores = jnp.where(kept_mask[None, None, :], scores, -jnp.inf)
    row_max = jnp.max(scores, axis=-1, keepdims=True)
    weights = jnp.exp(scores - row_max)
    probs = (weights / jnp.sum(weights, axis=-1, keepdims=True)).astype(jnp.bfloat16)
    mixed = jnp.einsum("hqk,khd->qhd", probs, value_window, preferred_element_type=jnp.float32)
    attended = mixed.astype(jnp.bfloat16).reshape(tok_rows, feat_width)
    tile_rows = history.shape[0]
    source_tile = (own_block - offsets[0]) % block_total
    source_row = (
        source_tile[:, None] * tile_rows + jnp.arange(tile_rows, dtype=jnp.int32)[None, :]
    ).reshape(-1)
    incoming = lax.all_gather(history, "tm", axis=0, tiled=True)
    piece_rows = incoming.shape[0]
    selector = (source_row[:, None] == jnp.arange(piece_rows, dtype=jnp.int32)[None, :]).astype(
        jnp.bfloat16
    )
    clip_hist = jnp.dot(selector, incoming, preferred_element_type=jnp.float32).astype(jnp.bfloat16)
    disc_clip = jnp.concatenate([clip_hist, attended], axis=0)
    disc_grad = lax.psum_scatter(
        lax.dot_general(
            cotangent, disc_clip, (((0,), (0,)), ((), ())), preferred_element_type=jnp.float32
        ),
        "tm",
        scatter_dimension=0,
        tiled=True,
    )
    return (attended, disc_grad)


def pack_kernel(n, lo, off_hbm, q_hbm, k_hbm, v_hbm, hist_hbm, cot_hbm, out_hbm, off, hist, q, k, v, cot, out, sems):
    own = lax.axis_index("tm")
    plane = lax.rem(lax.axis_index("head"), 2)
    tok = q.shape[0]
    tile = hist.shape[0]
    clip_rows = n * tile
    part, all_cols = cot.shape
    cols = all_cols // n
    base = 3 * tok + clip_rows
    low = pl.multiple_of(plane * lo, 16)
    fetched = [
        (q_hbm, q),
        (k_hbm, k),
        (v_hbm, v),
        (cot_hbm.at[pl.ds(low, part), :], cot),
        (hist_hbm, hist),
        (off_hbm, off),
    ]
    fetches = [pltpu.make_async_copy(a, b, sems.at[i]) for i, (a, b) in enumerate(fetched)]
    cuts = [0, tok, 2 * tok, base, out.shape[1]]
    stores = []
    for i in range(4):
        rows = pl.ds(cuts[i], cuts[i + 1] - cuts[i])
        at = len(fetches) + i
        stores.append(
            pltpu.make_async_copy(out.at[:, rows, :], out_hbm.at[:, rows, :], sems.at[at])
        )
    for fetch in fetches:
        fetch.start()
    fetches[4].wait()
    fetches[5].wait()
    tiles = hist[...].astype(jnp.float32)
    row = lax.broadcasted_iota(jnp.int32, (clip_rows, n * HD), 0)
    placed = jnp.zeros((clip_rows, n * HD), jnp.float32)
    for t in range(tile):
        placed = jnp.where(row == own * tile + t, tiles[t : t + 1, :], placed)
    placed = placed.astype(jnp.bfloat16)
    for h in range(n):
        out[h, 3 * tok : base, :] = placed[:, h * HD : (h + 1) * HD]
    for i, x in enumerate((q, k, v)):
        fetches[i].wait()
        for h in range(n):
            out[h, i * tok : (i + 1) * tok, :] = x[:, h * HD : (h + 1) * HD]
        stores[i].start()
    r = lax.broadcasted_iota(jnp.int32, (clip_rows, clip_rows), 0)
    c = lax.broadcasted_iota(jnp.int32, (clip_rows, clip_rows), 1)
    select = jnp.where((r == c) & (plane != 0), 1.0, 0.0)
    for j in range(n):
        src = lax.rem(own - off[0, j] + 2 * n, n)
        for t in range(tile):
            hit = (c == j * tile + t) & (r == src * tile + t) & (plane == 0)
            select = jnp.where(hit, 1.0, select)
    fetches[3].wait()
    by_row = jnp.dot(
        select.astype(jnp.bfloat16), cot[0:clip_rows, :], preferred_element_type=jnp.float32
    ).astype(jnp.bfloat16)
    for h in range(n):
        for u in range(cols // HD):
            at = base + u * part
            lanes = slice(h * cols + u * HD, h * cols + (u + 1) * HD)
            out[h, at : at + clip_rows, :] = by_row[:, lanes]
            out[h, at + clip_rows : at + part, :] = cot[clip_rows:part, lanes]
    stores[3].start()
    for store in stores:
        store.wait()


def attend_blocks(n, tok, parity, counts, x_ref, out_ref):
    rate = math.log2(math.e) / math.sqrt(HD)
    token = lax.broadcasted_iota(jnp.int32, (1, tok), 1)
    for i in range(n // 2):
        block = 2 * i + parity
        keys = min(WINB, 2 * i + 2)
        sources = [block - (keys - 1) + k for k in range(keys)]
        q = x_ref[block, 0:tok, :]
        scores = []
        for s in sources:
            at = jnp.maximum(s, 0)
            kept = jnp.where(s >= 0, counts[at], 0) * TPF
            scores.append(
                lax.dot_general(
                    q,
                    x_ref[at, tok : 2 * tok, :],
                    (((1,), (1,)), ((), ())),
                    preferred_element_type=jnp.float32,
                )
                + jnp.where(token < kept, 0.0, -jnp.inf).astype(jnp.float32)
            )
        top = jnp.max(scores[0], axis=1, keepdims=True)
        for s in scores[1:]:
            top = jnp.maximum(top, jnp.max(s, axis=1, keepdims=True))
        weights = [jnp.exp2((s - top) * rate) for s in scores]
        total = jnp.sum(weights[0], axis=1, keepdims=True)
        for w in weights[1:]:
            total = total + jnp.sum(w, axis=1, keepdims=True)
        share = 1.0 / total
        mixed = jnp.zeros((tok, HD), jnp.float32)
        for s, w in zip(sources, weights):
            mixed = mixed + jnp.dot(
                (w * share).astype(jnp.bfloat16),
                x_ref[jnp.maximum(s, 0), 2 * tok : 3 * tok, :],
                preferred_element_type=jnp.float32,
            )
        out_ref[i * tok : (i + 1) * tok, :] = mixed.astype(jnp.bfloat16)
    rows = n // 2 * tok
    clip_rows = out_ref.shape[0] - rows
    hist = jnp.zeros((clip_rows, HD), jnp.float32)
    for s in range(n):
        hist = hist + x_ref[s, 3 * tok : 3 * tok + clip_rows, :].astype(jnp.float32)
    out_ref[rows:, :] = hist.astype(jnp.bfloat16)


def attend_kernel(n, tok, counts_hbm, x_ref, same_ref, cross_ref, cot_ref, counts, sem):
    copy = pltpu.make_async_copy(counts_hbm, counts, sem)
    copy.start()
    side = lax.rem(lax.axis_index("tm"), 2)
    length = x_ref.shape[1]
    part = cot_ref.shape[1]
    for s in range(n):
        cot_ref[s] = x_ref[s, length - part : length, :]
    copy.wait()
    attend_blocks(n, tok, side, counts, x_ref, same_ref)
    attend_blocks(n, tok, 1 - side, counts, x_ref, cross_ref)


def whole_cot(lo, part, plane, mine, swapped):
    pieces = []
    for u in range(mine.shape[0] // part):
        a = mine[u * part : (u + 1) * part, :]
        b = swapped[u * part : (u + 1) * part, :]
        low = jnp.where(plane == 0, a, b)
        high = jnp.where(plane == 0, b, a)
        pieces.append(jnp.concatenate([low[:lo], high], axis=0))
    return jnp.concatenate(pieces, axis=1)


def turn(wholes, clip_rows):
    pieces = [x[clip_rows:] for x in wholes] + [x[:clip_rows] for x in wholes]
    return jnp.concatenate(pieces, axis=0).T


def turn_kernel(lo, clip_rows, cot_rows, mine_ref, swapped_ref, *refs):
    own_ref, give_ref = refs[-2:]
    plane = lax.rem(lax.axis_index("head"), 2)
    side = lax.rem(lax.axis_index("tm"), 2)
    half = mine_ref.shape[0] // 2
    part = cot_rows - lo
    filled = half * cot_rows
    for out_ref, first in ((own_ref, side), (give_ref, 1 - side)):
        wholes = []
        for c in range(half):
            s = 2 * c + first
            wholes.append(whole_cot(lo, part, plane, mine_ref[s], swapped_ref[s]))
        out_ref[:, 0:filled] = turn(wholes, clip_rows)
        if filled < out_ref.shape[1]:
            out_ref[:, filled:] = jnp.zeros_like(out_ref[:, filled:])


def grad_part(turned_ref, head_refs, rows, copies):
    right = jnp.concatenate([x[0:rows, :] for x in head_refs], axis=1)
    hist = jnp.concatenate([x[rows:, :] for x in head_refs], axis=1)
    clip = copies * hist.shape[0]
    out = jnp.dot(turned_ref[:, 0:rows], right, preferred_element_type=jnp.float32)
    return out + jnp.dot(
        turned_ref[:, rows : rows + clip],
        jnp.concatenate([hist] * copies, axis=0),
        preferred_element_type=jnp.float32,
    )


def grad_kernel(rows, copies, turned_ref, *refs):
    out_ref = refs[-1]
    out_ref[...] = grad_part(turned_ref, refs[:-1], rows, copies).astype(out_ref.dtype)


def finish_kernel(n, tok, own_near, own_far, got_near, got_far, *refs):
    heads, att_ref, out_ref = refs[:n], refs[n], refs[n + 1]
    own = lax.axis_index("tm")
    at = pl.multiple_of(own // 2 * tok, tok)
    near = own_near.shape[1] // HD
    for k in range(n):
        lanes = pl.ds(pl.multiple_of((own ^ k) * HD, HD), HD)
        att_ref[:, lanes] = heads[k][pl.ds(at, tok), :]
        mine, got, a = (own_near, got_near, k) if k < near else (own_far, got_far, k - near)
        b = a ^ 1
        out_ref[:, lanes] = mine[:, a * HD : (a + 1) * HD] + got[:, b * HD : (b + 1) * HD].astype(
            jnp.float32
        )


def head_body(query_rows, key_rows, value_rows, frame_counts, history, offsets, cotangent):
    n = lax.axis_size("tm")
    planes = lax.axis_size("head")
    half = n // 2
    tok, width = query_rows.shape
    tile = history.shape[0]
    clip_rows = n * tile
    cot_rows, all_cols = cotangent.shape
    cols = all_cols // n
    units = cols // HD
    lo = cot_rows // 32 * 16
    part = cot_rows - lo
    base = 3 * tok + clip_rows
    length = base + units * part
    rows = half * tok
    vmem = pl.BlockSpec(memory_space=pltpu.VMEM)
    hbm = pl.BlockSpec(memory_space=pl.ANY)
    bf16 = jnp.bfloat16

    def swap(x, bit):
        return lax.ppermute(x, "tm", [(i, i ^ bit) for i in range(n)])

    def swap_plane(x, bit):
        pairs = [
            (i * planes + p, (i ^ bit) * planes + (p ^ 1)) for i in range(n) for p in range(planes)
        ]
        return lax.ppermute(x, ("tm", "head"), pairs)

    def call(
        kernel, name, outs, specs, flops, scratch=(), exps=0, out_spec=vmem, limit=VMEM_LIMIT
    ):
        shapes = [jax.ShapeDtypeStruct(s, d) for s, d in outs]
        moved = 2 * sum(math.prod(s.shape) * s.dtype.itemsize for s in shapes)
        return pl.pallas_call(
            kernel,
            out_shape=tuple(shapes),
            in_specs=specs,
            out_specs=tuple([out_spec] * len(shapes)),
            scratch_shapes=scratch,
            compiler_params=pltpu.CompilerParams(vmem_limit_bytes=limit),
            cost_estimate=pl.CostEstimate(flops=flops, bytes_accessed=moved, transcendentals=exps),
            name=name,
        )

    (packed,) = call(
        lambda *refs: pack_kernel(n, lo, *refs),
        "pack",
        [((n, length, HD), bf16)],
        [hbm] * 6,
        0,
        (
            pltpu.SMEM(offsets.shape, jnp.int32),
            pltpu.VMEM(history.shape, bf16),
            pltpu.VMEM((tok, width), bf16),
            pltpu.VMEM((tok, width), bf16),
            pltpu.VMEM((tok, width), bf16),
            pltpu.VMEM((part, all_cols), bf16),
            pltpu.VMEM((n, length, HD), bf16),
            pltpu.SemaphoreType.DMA((10,)),
        ),
        out_spec=hbm,
        limit=PACK_LIMIT,
    )(offsets, query_rows, key_rows, value_rows, history, cotangent)
    by_head = lax.all_to_all(packed, "tm", 0, 0)

    counts = (pltpu.SMEM(frame_counts.shape, jnp.int32), pltpu.SemaphoreType.DMA)
    pairs = half * tok * WINB * tok
    head_shape = ((rows + clip_rows, HD), bf16)
    same, cross, cot_mine = call(
        lambda *refs: attend_kernel(n, tok, *refs),
        "attend",
        [head_shape, head_shape, ((n, units * part, HD), bf16)],
        [hbm, vmem],
        8 * pairs * HD,
        counts,
        2 * pairs,
    )(frame_counts, by_head)
    cot_swapped = swap_plane(cot_mine, 0)
    x_same, y_cross = swap(same, 2), swap(cross, 4 ^ 1)
    y_same, x_cross, c_cross = swap(same, 4), swap(cross, 2 ^ 1), swap(cross, 1)
    far_same, far_cross = swap(x_same, 4), swap(y_cross, 2)

    turned_shape = ((cols, -(-half * cot_rows // HD) * HD), bf16)
    turned_own, turned_give = call(
        lambda *refs: turn_kernel(lo, clip_rows, cot_rows, *refs),
        "turn",
        [turned_shape] * 2,
        [vmem] * 2 + [hbm] * 4,
        0,
    )(cot_mine, cot_swapped, x_same, y_cross, x_cross, y_same)
    turned_other = swap(turned_give, 1)

    def grad(turned, heads, dtype, name):
        (out,) = call(
            lambda *refs: grad_kernel(rows, half, *refs),
            name,
            [((cols, len(heads) * HD), dtype)],
            [vmem] * (1 + len(heads)),
            2 * cols * half * cot_rows * len(heads) * HD,
        )(turned, *heads)
        return out

    near = [same, c_cross, x_same, x_cross, y_same, y_cross]
    far = [far_same, far_cross]
    got_near = swap(grad(turned_other, near, bf16, "grad_other_near"), 1)
    own_near = grad(turned_own, near, jnp.float32, "grad_own_near")
    got_far = swap(grad(turned_other, far, bf16, "grad_other_far"), 1)
    own_far = grad(turned_own, far, jnp.float32, "grad_own_far")
    return call(
        lambda *refs: finish_kernel(n, tok, *refs),
        "finish",
        [((tok, width), bf16), ((cols, width), jnp.float32)],
        [vmem] * (4 + n),
        0,
    )(own_near, own_far, got_near, got_far, *near, *far)


def body(query_rows, key_rows, value_rows, frame_counts, history, offsets, cotangent):
    n = lax.axis_size("tm")
    tok, width = query_rows.shape
    by_heads = (
        n == 8
        and lax.axis_size("head") % 2 == 0
        and width == n * HD
        and offsets.shape[1] == n
        and cotangent.shape[0] == tok + n * history.shape[0]
        and cotangent.shape[1] % (n * HD) == 0
        and tok % 16 == 0
        and (n * history.shape[0]) % 16 == 0
    )
    plan = head_body if by_heads else window_body
    return plan(query_rows, key_rows, value_rows, frame_counts, history, offsets, cotangent)


def solution(mesh):
    in_specs = (
        P("tm", "head"),
        P("tm", "head"),
        P("tm", "head"),
        P(),
        P("tm", "head"),
        P("tm", None),
        P("tm", None),
    )
    out_specs = (P("tm", "head"), P("tm", "head"))
    return jax.shard_map(body, mesh=mesh, in_specs=in_specs, out_specs=out_specs, check_vma=False)
```

```python
import math

import jax
import jax.numpy as jnp
from jax import lax
from jax.experimental import pallas as pl
from jax.experimental.pallas import tpu as pltpu
from jax.sharding import PartitionSpec as P

HD = 128
TPF = 64
WINB = 4
VMEM_LIMIT = 32 * 1024 * 1024
PACK_LIMIT = 63 * 1024 * 1024


def from_behind(x, axis, by):
    devices = lax.axis_size(axis)
    pairs = [(i, i + by) for i in range(devices) if 0 <= i + by < devices]
    return lax.ppermute(x, axis, pairs)


def window_body(query_rows, key_rows, value_rows, frame_counts, history, offsets, cotangent):
    tok_rows, feat_width = query_rows.shape
    local_heads = feat_width // HD
    block_total = lax.axis_size("tm")
    own_block = lax.axis_index("tm")
    score_scale = 1.0 / math.sqrt(HD)
    key_value = jnp.stack([key_rows, value_rows])
    pieces = []
    for distance in range(WINB - 1, 0, -1):
        pieces.append(from_behind(key_value, "tm", distance))
    window = jnp.concatenate(pieces + [key_value], axis=1)
    source_block = own_block - (WINB - 1) + jnp.arange(WINB, dtype=jnp.int32)
    block_match = jnp.arange(block_total, dtype=jnp.int32)[None, :] == source_block[:, None]
    block_count = jnp.sum(jnp.where(block_match, frame_counts[None, :], 0), axis=1)
    frame_index = jnp.arange(tok_rows, dtype=jnp.int32) // TPF
    kept_mask = (
        (source_block[:, None] >= 0) & (frame_index[None, :] < block_count[:, None])
    ).reshape(WINB * tok_rows)
    key_window = window[0].reshape(WINB * tok_rows, local_heads, HD)
    value_window = window[1].reshape(WINB * tok_rows, local_heads, HD)
    query_heads = query_rows.reshape(tok_rows, local_heads, HD)
    scores = (
        jnp.einsum("qhd,khd->hqk", query_heads, key_window, preferred_element_type=jnp.float32)
        * score_scale
    )
    scores = jnp.where(kept_mask[None, None, :], scores, -jnp.inf)
    row_max = jnp.max(scores, axis=-1, keepdims=True)
    weights = jnp.exp(scores - row_max)
    probs = (weights / jnp.sum(weights, axis=-1, keepdims=True)).astype(jnp.bfloat16)
    mixed = jnp.einsum("hqk,khd->qhd", probs, value_window, preferred_element_type=jnp.float32)
    attended = mixed.astype(jnp.bfloat16).reshape(tok_rows, feat_width)
    tile_rows = history.shape[0]
    source_tile = (own_block - offsets[0]) % block_total
    source_row = (
        source_tile[:, None] * tile_rows + jnp.arange(tile_rows, dtype=jnp.int32)[None, :]
    ).reshape(-1)
    incoming = lax.all_gather(history, "tm", axis=0, tiled=True)
    piece_rows = incoming.shape[0]
    selector = (source_row[:, None] == jnp.arange(piece_rows, dtype=jnp.int32)[None, :]).astype(
        jnp.bfloat16
    )
    clip_hist = jnp.dot(selector, incoming, preferred_element_type=jnp.float32).astype(jnp.bfloat16)
    disc_clip = jnp.concatenate([clip_hist, attended], axis=0)
    disc_grad = lax.psum_scatter(
        lax.dot_general(
            cotangent, disc_clip, (((0,), (0,)), ((), ())), preferred_element_type=jnp.float32
        ),
        "tm",
        scatter_dimension=0,
        tiled=True,
    )
    return (attended, disc_grad)


def cot_kernel(n, tile, lo, off_hbm, cot_hbm, *refs):
    outs, (off, cot, sems) = refs[:-3], refs[-3:]
    own = lax.axis_index("tm")
    chip, side = own // 2, lax.rem(own, 2)
    plane = lax.rem(lax.axis_index("head"), 2)
    clip_rows = n * tile
    part, all_cols = cot.shape
    cols = all_cols // n
    low = pl.multiple_of(plane * lo, 16)
    fetch_off = pltpu.make_async_copy(off_hbm, off, sems.at[0])
    fetch_cot = pltpu.make_async_copy(cot_hbm.at[pl.ds(low, part), :], cot, sems.at[1])
    fetch_off.start()
    fetch_cot.start()
    fetch_off.wait()
    r = lax.broadcasted_iota(jnp.int32, (clip_rows, clip_rows), 0)
    c = lax.broadcasted_iota(jnp.int32, (clip_rows, clip_rows), 1)
    select = jnp.where((r == c) & (plane != 0), 1.0, 0.0)
    for j in range(n):
        src = lax.rem(own - off[0, j] + 2 * n, n)
        for t in range(tile):
            hit = (c == j * tile + t) & (r == src * tile + t) & (plane == 0)
            select = jnp.where(hit, 1.0, select)
    fetch_cot.wait()
    cot[0:clip_rows, :] = jnp.dot(
        select.astype(jnp.bfloat16), cot[0:clip_rows, :], preferred_element_type=jnp.float32
    ).astype(jnp.bfloat16)
    units = cols // HD
    for m, out_ref in enumerate(outs):
        for i, block in enumerate((2 * (chip ^ m) + side, 2 * (chip ^ m) + 1 - side)):
            for u in range(units):
                at = (i * units + u) * part
                lanes = pl.ds(pl.multiple_of(block * cols + u * HD, HD), HD)
                out_ref[at : at + part, :] = cot[:, lanes]


def pack_kernel(n, q_hbm, k_hbm, v_hbm, hist_hbm, *refs):
    outs, (q, k, v, hist, sems) = refs[:n], refs[n:]
    own = lax.axis_index("tm")
    tok = q.shape[0]
    tile = hist.shape[0]
    clip_rows = n * tile
    pairs = [(hist_hbm, hist), (q_hbm, q), (k_hbm, k), (v_hbm, v)]
    copies = [pltpu.make_async_copy(a, b, sems.at[i]) for i, (a, b) in enumerate(pairs)]
    for copy in copies:
        copy.start()
    copies[0].wait()
    for d, out_ref in enumerate(outs):
        lanes = pl.ds(pl.multiple_of((own ^ d) * HD, HD), HD)
        tiles = hist[:, lanes].astype(jnp.float32)
        row = lax.broadcasted_iota(jnp.int32, (clip_rows, HD), 0)
        placed = jnp.zeros((clip_rows, HD), jnp.float32)
        for t in range(tile):
            placed = jnp.where(row == own * tile + t, tiles[t : t + 1, :], placed)
        out_ref[3 * tok : 3 * tok + clip_rows, :] = placed.astype(jnp.bfloat16)
    for i, x in enumerate((q, k, v)):
        copies[1 + i].wait()
        for d, out_ref in enumerate(outs):
            lanes = pl.ds(pl.multiple_of((own ^ d) * HD, HD), HD)
            out_ref[i * tok : (i + 1) * tok, :] = x[:, lanes]


def attend_blocks(n, tok, parity, counts, x_ref, out_ref):
    rate = math.log2(math.e) / math.sqrt(HD)
    token = lax.broadcasted_iota(jnp.int32, (1, tok), 1)
    for i in range(n // 2):
        block = 2 * i + parity
        keys = min(WINB, 2 * i + 2)
        sources = [block - (keys - 1) + k for k in range(keys)]
        q = x_ref[block, 0:tok, :]
        scores = []
        for s in sources:
            at = jnp.maximum(s, 0)
            kept = jnp.where(s >= 0, counts[at], 0) * TPF
            scores.append(
                lax.dot_general(
                    q,
                    x_ref[at, tok : 2 * tok, :],
                    (((1,), (1,)), ((), ())),
                    preferred_element_type=jnp.float32,
                )
                + jnp.where(token < kept, 0.0, -jnp.inf).astype(jnp.float32)
            )
        top = jnp.max(scores[0], axis=1, keepdims=True)
        for s in scores[1:]:
            top = jnp.maximum(top, jnp.max(s, axis=1, keepdims=True))
        weights = [jnp.exp2((s - top) * rate) for s in scores]
        total = jnp.sum(weights[0], axis=1, keepdims=True)
        for w in weights[1:]:
            total = total + jnp.sum(w, axis=1, keepdims=True)
        share = 1.0 / total
        mixed = jnp.zeros((tok, HD), jnp.float32)
        for s, w in zip(sources, weights):
            mixed = mixed + jnp.dot(
                (w * share).astype(jnp.bfloat16),
                x_ref[jnp.maximum(s, 0), 2 * tok : 3 * tok, :],
                preferred_element_type=jnp.float32,
            )
        out_ref[i * tok : (i + 1) * tok, :] = mixed.astype(jnp.bfloat16)
    rows = n // 2 * tok
    clip_rows = out_ref.shape[0] - rows
    hist = jnp.zeros((clip_rows, HD), jnp.float32)
    for s in range(n):
        hist = hist + x_ref[s, 3 * tok : 3 * tok + clip_rows, :].astype(jnp.float32)
    out_ref[rows:, :] = hist.astype(jnp.bfloat16)


def attend_kernel(n, tok, counts_hbm, *refs):
    parts, (same_ref, cross_ref, x_ref, counts, sem) = refs[:n], refs[n:]
    copy = pltpu.make_async_copy(counts_hbm, counts, sem)
    copy.start()
    own = lax.axis_index("tm")
    side = lax.rem(own, 2)
    for k, part in enumerate(parts):
        x_ref[own ^ k] = part[...]
    copy.wait()
    attend_blocks(n, tok, side, counts, x_ref, same_ref)
    attend_blocks(n, tok, 1 - side, counts, x_ref, cross_ref)


def stack_kernel(*refs):
    out_ref = refs[-1]
    for i, x in enumerate(refs[:-1]):
        out_ref[i] = x[...]


def whole_cot(lo, part, plane, mine, swapped):
    pieces = []
    for u in range(mine.shape[0] // part):
        a = mine[u * part : (u + 1) * part, :]
        b = swapped[u * part : (u + 1) * part, :]
        low = jnp.where(plane == 0, a, b)
        high = jnp.where(plane == 0, b, a)
        pieces.append(jnp.concatenate([low[:lo], high], axis=0))
    return jnp.concatenate(pieces, axis=1)


def turn(wholes, clip_rows):
    pieces = [x[clip_rows:] for x in wholes] + [x[:clip_rows] for x in wholes]
    return jnp.concatenate(pieces, axis=0).T


def turn_kernel(lo, clip_rows, cot_rows, mine_ref, swapped_ref, own_ref, other_ref):
    plane = lax.rem(lax.axis_index("head"), 2)
    chip = lax.axis_index("tm") // 2
    chips, length, _ = mine_ref.shape
    for i, out_ref in enumerate((own_ref, other_ref)):
        rows = slice(i * length // 2, (i + 1) * length // 2)
        wholes = [
            whole_cot(
                lo, cot_rows - lo, plane, mine_ref[chip ^ c, rows], swapped_ref[chip ^ c, rows]
            )
            for c in range(chips)
        ]
        out_ref[...] = turn(wholes, clip_rows)


def grad_part(turned_ref, head_refs, rows, copies):
    right = jnp.concatenate([x[0:rows, :] for x in head_refs], axis=1)
    hist = jnp.concatenate([x[rows:, :] for x in head_refs], axis=1)
    clip = copies * hist.shape[0]
    out = jnp.dot(turned_ref[:, 0:rows], right, preferred_element_type=jnp.float32)
    return out + jnp.dot(
        turned_ref[:, rows : rows + clip],
        jnp.concatenate([hist] * copies, axis=0),
        preferred_element_type=jnp.float32,
    )


def grad_kernel(rows, copies, turned_ref, *refs):
    out_ref = refs[-1]
    out_ref[...] = grad_part(turned_ref, refs[:-1], rows, copies).astype(out_ref.dtype)


def finish_kernel(n, tok, own_near, own_far, got_near, got_far, *refs):
    heads, att_ref, out_ref = refs[:n], refs[n], refs[n + 1]
    own = lax.axis_index("tm")
    at = pl.multiple_of(own // 2 * tok, tok)
    near = own_near.shape[1] // HD
    for k in range(n):
        lanes = pl.ds(pl.multiple_of((own ^ k) * HD, HD), HD)
        att_ref[:, lanes] = heads[k][pl.ds(at, tok), :]
        mine, got, a = (own_near, got_near, k) if k < near else (own_far, got_far, k - near)
        b = a ^ 1
        out_ref[:, lanes] = mine[:, a * HD : (a + 1) * HD] + got[:, b * HD : (b + 1) * HD].astype(
            jnp.float32
        )


def head_body(query_rows, key_rows, value_rows, frame_counts, history, offsets, cotangent):
    n = lax.axis_size("tm")
    planes = lax.axis_size("head")
    half = n // 2
    tok, width = query_rows.shape
    tile = history.shape[0]
    clip_rows = n * tile
    cot_rows, all_cols = cotangent.shape
    cols = all_cols // n
    units = cols // HD
    lo = cot_rows // 32 * 16
    part = cot_rows - lo
    base = 3 * tok + clip_rows
    length = base
    rows = half * tok
    vmem = pl.BlockSpec(memory_space=pltpu.VMEM)
    hbm = pl.BlockSpec(memory_space=pl.ANY)
    bf16 = jnp.bfloat16

    def swap(x, bit):
        return lax.ppermute(x, "tm", [(i, i ^ bit) for i in range(n)])

    def swap_plane(x, bit):
        pairs = [
            (i * planes + p, (i ^ bit) * planes + (p ^ 1)) for i in range(n) for p in range(planes)
        ]
        return lax.ppermute(x, ("tm", "head"), pairs)

    def call(
        kernel, name, outs, specs, flops, scratch=(), exps=0, out_spec=vmem, limit=VMEM_LIMIT
    ):
        shapes = [jax.ShapeDtypeStruct(s, d) for s, d in outs]
        moved = 2 * sum(math.prod(s.shape) * s.dtype.itemsize for s in shapes)
        return pl.pallas_call(
            kernel,
            out_shape=tuple(shapes),
            in_specs=specs,
            out_specs=tuple([out_spec] * len(shapes)),
            scratch_shapes=scratch,
            compiler_params=pltpu.CompilerParams(vmem_limit_bytes=limit),
            cost_estimate=pl.CostEstimate(flops=flops, bytes_accessed=moved, transcendentals=exps),
            name=name,
        )

    chips = range(half)
    cots = call(
        lambda *refs: cot_kernel(n, tile, lo, *refs),
        "cot",
        [((2 * units * part, HD), bf16)] * half,
        [hbm] * 2,
        0,
        (
            pltpu.SMEM(offsets.shape, jnp.int32),
            pltpu.VMEM((part, all_cols), bf16),
            pltpu.SemaphoreType.DMA((2,)),
        ),
        limit=PACK_LIMIT,
    )(offsets, cotangent)
    cots = [cots[0]] + [swap(cots[m], 2 * m) for m in chips[1:]]
    packed = call(
        lambda *refs: pack_kernel(n, *refs),
        "pack",
        [((length, HD), bf16)] * n,
        [hbm] * 4,
        0,
        (
            pltpu.VMEM((tok, width), bf16),
            pltpu.VMEM((tok, width), bf16),
            pltpu.VMEM((tok, width), bf16),
            pltpu.VMEM(history.shape, bf16),
            pltpu.SemaphoreType.DMA((4,)),
        ),
        limit=PACK_LIMIT,
    )(query_rows, key_rows, value_rows, history)
    by_head = [packed[0]] + [swap(packed[k], k) for k in range(1, n)]
    (cot_mine,) = call(
        stack_kernel, "stack", [((half, 2 * units * part, HD), bf16)], [vmem] * half, 0
    )(*cots)
    cot_swapped = swap_plane(cot_mine, 0)

    counts = (
        pltpu.VMEM((n, length, HD), bf16),
        pltpu.SMEM(frame_counts.shape, jnp.int32),
        pltpu.SemaphoreType.DMA,
    )
    pairs = half * tok * WINB * tok
    head_shape = ((rows + clip_rows, HD), bf16)
    same, cross = call(
        lambda *refs: attend_kernel(n, tok, *refs),
        "attend",
        [head_shape, head_shape],
        [hbm] + [vmem] * n,
        8 * pairs * HD,
        counts,
        2 * pairs,
    )(frame_counts, *by_head)
    x_same, y_cross = swap(same, 2), swap(cross, 4 ^ 1)
    y_same, x_cross, c_cross = swap(same, 4), swap(cross, 2 ^ 1), swap(cross, 1)
    far_same, far_cross = swap(x_same, 4), swap(y_cross, 2)

    turned_own, turned_other = call(
        lambda *refs: turn_kernel(lo, clip_rows, cot_rows, *refs),
        "turn",
        [((cols, half * cot_rows), bf16)] * 2,
        [vmem] * 2,
        0,
    )(cot_mine, cot_swapped)

    def grad(turned, heads, dtype, name):
        (out,) = call(
            lambda *refs: grad_kernel(rows, half, *refs),
            name,
            [((cols, len(heads) * HD), dtype)],
            [vmem] * (1 + len(heads)),
            2 * cols * half * cot_rows * len(heads) * HD,
        )(turned, *heads)
        return out

    near = [same, c_cross, x_same, x_cross, y_same, y_cross]
    far = [far_same, far_cross]
    got_near = swap(grad(turned_other, near, bf16, "grad_other_near"), 1)
    own_near = grad(turned_own, near, jnp.float32, "grad_own_near")
    got_far = swap(grad(turned_other, far, bf16, "grad_other_far"), 1)
    own_far = grad(turned_own, far, jnp.float32, "grad_own_far")
    return call(
        lambda *refs: finish_kernel(n, tok, *refs),
        "finish",
        [((tok, width), bf16), ((cols, width), jnp.float32)],
        [vmem] * (4 + n),
        0,
    )(own_near, own_far, got_near, got_far, *near, *far)


def body(query_rows, key_rows, value_rows, frame_counts, history, offsets, cotangent):
    n = lax.axis_size("tm")
    tok, width = query_rows.shape
    by_heads = (
        n == 8
        and lax.axis_size("head") % 2 == 0
        and width == n * HD
        and offsets.shape[1] == n
        and cotangent.shape[0] == tok + n * history.shape[0]
        and cotangent.shape[1] % (n * HD) == 0
        and tok % 16 == 0
        and (n * history.shape[0]) % 16 == 0
    )
    plan = head_body if by_heads else window_body
    return plan(query_rows, key_rows, value_rows, frame_counts, history, offsets, cotangent)


def solution(mesh):
    in_specs = (
        P("tm", "head"),
        P("tm", "head"),
        P("tm", "head"),
        P(),
        P("tm", "head"),
        P("tm", None),
        P("tm", None),
    )
    out_specs = (P("tm", "head"), P("tm", "head"))
    return jax.shard_map(body, mesh=mesh, in_specs=in_specs, out_specs=out_specs, check_vma=False)
```

```python
import math

import jax
import jax.numpy as jnp
from jax import lax
from jax.experimental import pallas as pl
from jax.experimental.pallas import tpu as pltpu
from jax.sharding import PartitionSpec as P

HD = 128
TPF = 64
WINB = 4
VMEM_LIMIT = 24 * 1024 * 1024
PACK_LIMIT = 63 * 1024 * 1024


def from_behind(x, axis, by):
    devices = lax.axis_size(axis)
    pairs = [(i, i + by) for i in range(devices) if 0 <= i + by < devices]
    return lax.ppermute(x, axis, pairs)


def window_body(query_rows, key_rows, value_rows, frame_counts, history, offsets, cotangent):
    tok_rows, feat_width = query_rows.shape
    local_heads = feat_width // HD
    block_total = lax.axis_size("tm")
    own_block = lax.axis_index("tm")
    score_scale = 1.0 / math.sqrt(HD)
    key_value = jnp.stack([key_rows, value_rows])
    pieces = []
    for distance in range(WINB - 1, 0, -1):
        pieces.append(from_behind(key_value, "tm", distance))
    window = jnp.concatenate(pieces + [key_value], axis=1)
    source_block = own_block - (WINB - 1) + jnp.arange(WINB, dtype=jnp.int32)
    block_match = jnp.arange(block_total, dtype=jnp.int32)[None, :] == source_block[:, None]
    block_count = jnp.sum(jnp.where(block_match, frame_counts[None, :], 0), axis=1)
    frame_index = jnp.arange(tok_rows, dtype=jnp.int32) // TPF
    kept_mask = (
        (source_block[:, None] >= 0) & (frame_index[None, :] < block_count[:, None])
    ).reshape(WINB * tok_rows)
    key_window = window[0].reshape(WINB * tok_rows, local_heads, HD)
    value_window = window[1].reshape(WINB * tok_rows, local_heads, HD)
    query_heads = query_rows.reshape(tok_rows, local_heads, HD)
    scores = (
        jnp.einsum("qhd,khd->hqk", query_heads, key_window, preferred_element_type=jnp.float32)
        * score_scale
    )
    scores = jnp.where(kept_mask[None, None, :], scores, -jnp.inf)
    row_max = jnp.max(scores, axis=-1, keepdims=True)
    weights = jnp.exp(scores - row_max)
    probs = (weights / jnp.sum(weights, axis=-1, keepdims=True)).astype(jnp.bfloat16)
    mixed = jnp.einsum("hqk,khd->qhd", probs, value_window, preferred_element_type=jnp.float32)
    attended = mixed.astype(jnp.bfloat16).reshape(tok_rows, feat_width)
    tile_rows = history.shape[0]
    source_tile = (own_block - offsets[0]) % block_total
    source_row = (
        source_tile[:, None] * tile_rows + jnp.arange(tile_rows, dtype=jnp.int32)[None, :]
    ).reshape(-1)
    incoming = lax.all_gather(history, "tm", axis=0, tiled=True)
    piece_rows = incoming.shape[0]
    selector = (source_row[:, None] == jnp.arange(piece_rows, dtype=jnp.int32)[None, :]).astype(
        jnp.bfloat16
    )
    clip_hist = jnp.dot(selector, incoming, preferred_element_type=jnp.float32).astype(jnp.bfloat16)
    disc_clip = jnp.concatenate([clip_hist, attended], axis=0)
    disc_grad = lax.psum_scatter(
        lax.dot_general(
            cotangent, disc_clip, (((0,), (0,)), ((), ())), preferred_element_type=jnp.float32
        ),
        "tm",
        scatter_dimension=0,
        tiled=True,
    )
    return (attended, disc_grad)


def cot_kernel(n, tile, lo, off_hbm, cot_hbm, behind_a, behind_b, *refs):
    outs, (off, cot, sems) = refs[:-3], refs[-3:]
    own = lax.axis_index("tm")
    chip, side = own // 2, lax.rem(own, 2)
    plane = lax.rem(lax.axis_index("head"), 2)
    clip_rows = n * tile
    part, all_cols = cot.shape
    cols = all_cols // n
    low = pl.multiple_of(plane * lo, 16)
    fetch_off = pltpu.make_async_copy(off_hbm, off, sems.at[0])
    fetch_cot = pltpu.make_async_copy(cot_hbm.at[pl.ds(low, part), :], cot, sems.at[1])
    fetch_off.start()
    fetch_cot.start()
    fetch_off.wait()
    r = lax.broadcasted_iota(jnp.int32, (clip_rows, clip_rows), 0)
    c = lax.broadcasted_iota(jnp.int32, (clip_rows, clip_rows), 1)
    select = jnp.where((r == c) & (plane != 0), 1.0, 0.0)
    for j in range(n):
        src = lax.rem(own - off[0, j] + 2 * n, n)
        for t in range(tile):
            hit = (c == j * tile + t) & (r == src * tile + t) & (plane == 0)
            select = jnp.where(hit, 1.0, select)
    fetch_cot.wait()
    cot[0:clip_rows, :] = jnp.dot(
        select.astype(jnp.bfloat16), cot[0:clip_rows, :], preferred_element_type=jnp.float32
    ).astype(jnp.bfloat16)
    units = cols // HD
    for m, out_ref in enumerate(outs):
        for i, block in enumerate((2 * (chip ^ m) + side, 2 * (chip ^ m) + 1 - side)):
            for u in range(units):
                at = (i * units + u) * part
                lanes = pl.ds(pl.multiple_of(block * cols + u * HD, HD), HD)
                out_ref[at : at + part, :] = cot[:, lanes]


def pack_kernel(n, q_hbm, k_hbm, v_hbm, hist_hbm, *refs):
    outs, (q, k, v, hist, sems) = refs[:n], refs[n:]
    own = lax.axis_index("tm")
    tok = q.shape[0]
    tile = hist.shape[0]
    clip_rows = n * tile
    pairs = [(hist_hbm, hist), (q_hbm, q), (k_hbm, k), (v_hbm, v)]
    copies = [pltpu.make_async_copy(a, b, sems.at[i]) for i, (a, b) in enumerate(pairs)]
    for copy in copies:
        copy.start()
    copies[0].wait()
    for d, out_ref in enumerate(outs):
        lanes = pl.ds(pl.multiple_of((own ^ d) * HD, HD), HD)
        tiles = hist[:, lanes].astype(jnp.float32)
        row = lax.broadcasted_iota(jnp.int32, (clip_rows, HD), 0)
        placed = jnp.zeros((clip_rows, HD), jnp.float32)
        for t in range(tile):
            placed = jnp.where(row == own * tile + t, tiles[t : t + 1, :], placed)
        out_ref[3 * tok : 3 * tok + clip_rows, :] = placed.astype(jnp.bfloat16)
    for i, x in enumerate((q, k, v)):
        copies[1 + i].wait()
        for d, out_ref in enumerate(outs):
            lanes = pl.ds(pl.multiple_of((own ^ d) * HD, HD), HD)
            out_ref[i * tok : (i + 1) * tok, :] = x[:, lanes]


def attend_blocks(n, tok, parity, counts, x_ref, out_ref):
    rate = math.log2(math.e) / math.sqrt(HD)
    token = lax.broadcasted_iota(jnp.int32, (1, tok), 1)
    for i in range(n // 2):
        block = 2 * i + parity
        keys = min(WINB, 2 * i + 2)
        sources = [block - (keys - 1) + k for k in range(keys)]
        q = x_ref[block, 0:tok, :]
        scores = []
        for s in sources:
            at = jnp.maximum(s, 0)
            kept = jnp.where(s >= 0, counts[at], 0) * TPF
            scores.append(
                lax.dot_general(
                    q,
                    x_ref[at, tok : 2 * tok, :],
                    (((1,), (1,)), ((), ())),
                    preferred_element_type=jnp.float32,
                )
                + jnp.where(token < kept, 0.0, -jnp.inf).astype(jnp.float32)
            )
        top = jnp.max(scores[0], axis=1, keepdims=True)
        for s in scores[1:]:
            top = jnp.maximum(top, jnp.max(s, axis=1, keepdims=True))
        weights = [jnp.exp2((s - top) * rate) for s in scores]
        total = jnp.sum(weights[0], axis=1, keepdims=True)
        for w in weights[1:]:
            total = total + jnp.sum(w, axis=1, keepdims=True)
        share = 1.0 / total
        mixed = jnp.zeros((tok, HD), jnp.float32)
        for s, w in zip(sources, weights):
            mixed = mixed + jnp.dot(
                (w * share).astype(jnp.bfloat16),
                x_ref[jnp.maximum(s, 0), 2 * tok : 3 * tok, :],
                preferred_element_type=jnp.float32,
            )
        out_ref[i * tok : (i + 1) * tok, :] = mixed.astype(jnp.bfloat16)
    rows = n // 2 * tok
    clip_rows = out_ref.shape[0] - rows
    hist = jnp.zeros((clip_rows, HD), jnp.float32)
    for s in range(n):
        hist = hist + x_ref[s, 3 * tok : 3 * tok + clip_rows, :].astype(jnp.float32)
    out_ref[rows:, :] = hist.astype(jnp.bfloat16)


def attend_kernel(n, tok, order, counts_hbm, *refs):
    parts, (same_ref, cross_ref, x_ref, counts, sem) = refs[:n], refs[n:]
    copy = pltpu.make_async_copy(counts_hbm, counts, sem)
    copy.start()
    own = lax.axis_index("tm")
    side = lax.rem(own, 2)
    for k, part in zip(order, parts):
        x_ref[own ^ k] = part[...]
    copy.wait()
    attend_blocks(n, tok, side, counts, x_ref, same_ref)
    attend_blocks(n, tok, 1 - side, counts, x_ref, cross_ref)


def stack_kernel(*refs):
    out_ref = refs[-1]
    for i, x in enumerate(refs[:-2]):
        out_ref[i] = x[...]


def late_kernel(x_ref, behind, out_ref):
    out_ref[...] = x_ref[...]


def whole_cot(lo, part, plane, mine, swapped):
    pieces = []
    for u in range(mine.shape[0] // part):
        a = mine[u * part : (u + 1) * part, :]
        b = swapped[u * part : (u + 1) * part, :]
        low = jnp.where(plane == 0, a, b)
        high = jnp.where(plane == 0, b, a)
        pieces.append(jnp.concatenate([low[:lo], high], axis=0))
    return jnp.concatenate(pieces, axis=1)


def turn(wholes, clip_rows):
    pieces = [x[clip_rows:] for x in wholes] + [x[:clip_rows] for x in wholes]
    return jnp.concatenate(pieces, axis=0).T


def turn_kernel(lo, clip_rows, cot_rows, mine_ref, swapped_ref, own_ref, other_ref):
    plane = lax.rem(lax.axis_index("head"), 2)
    chip = lax.axis_index("tm") // 2
    chips, length, _ = mine_ref.shape
    for i, out_ref in enumerate((own_ref, other_ref)):
        rows = slice(i * length // 2, (i + 1) * length // 2)
        wholes = [
            whole_cot(
                lo, cot_rows - lo, plane, mine_ref[chip ^ c, rows], swapped_ref[chip ^ c, rows]
            )
            for c in range(chips)
        ]
        out_ref[...] = turn(wholes, clip_rows)


def grad_part(turned_ref, head_refs, rows, copies):
    right = jnp.concatenate([x[0:rows, :] for x in head_refs], axis=1)
    hist = jnp.concatenate([x[rows:, :] for x in head_refs], axis=1)
    clip = copies * hist.shape[0]
    out = jnp.dot(turned_ref[:, 0:rows], right, preferred_element_type=jnp.float32)
    return out + jnp.dot(
        turned_ref[:, rows : rows + clip],
        jnp.concatenate([hist] * copies, axis=0),
        preferred_element_type=jnp.float32,
    )


def grad_kernel(rows, copies, turned_ref, *refs):
    out_ref = refs[-1]
    out_ref[...] = grad_part(turned_ref, refs[:-1], rows, copies).astype(out_ref.dtype)


def finish_kernel(order, tok, own_near, own_far, got_near, got_far, *refs):
    n = len(order)
    heads, att_ref, out_ref = refs[:n], refs[n], refs[n + 1]
    own = lax.axis_index("tm")
    at = pl.multiple_of(own // 2 * tok, tok)
    near = own_near.shape[1] // HD

    def column(near_ref, far_ref, i):
        ref, i = (near_ref, i) if i < near else (far_ref, i - near)
        return ref[:, i * HD : (i + 1) * HD]

    for i, k in enumerate(order):
        lanes = pl.ds(pl.multiple_of((own ^ k) * HD, HD), HD)
        att_ref[:, lanes] = heads[i][pl.ds(at, tok), :]
        got = column(got_near, got_far, order.index(k ^ 1))
        out_ref[:, lanes] = column(own_near, own_far, i) + got.astype(jnp.float32)


def head_body(query_rows, key_rows, value_rows, frame_counts, history, offsets, cotangent):
    n = lax.axis_size("tm")
    planes = lax.axis_size("head")
    half = n // 2
    tok, width = query_rows.shape
    tile = history.shape[0]
    clip_rows = n * tile
    cot_rows, all_cols = cotangent.shape
    cols = all_cols // n
    units = cols // HD
    lo = cot_rows // 32 * 16
    part = cot_rows - lo
    base = 3 * tok + clip_rows
    length = base
    rows = half * tok
    vmem = pl.BlockSpec(memory_space=pltpu.VMEM)
    hbm = pl.BlockSpec(memory_space=pl.ANY)
    bf16 = jnp.bfloat16

    def swap(x, bit):
        return lax.ppermute(x, "tm", [(i, i ^ bit) for i in range(n)])

    def swap_plane(x, bit):
        pairs = [
            (i * planes + p, (i ^ bit) * planes + (p ^ 1)) for i in range(n) for p in range(planes)
        ]
        return lax.ppermute(x, ("tm", "head"), pairs)

    def call(
        kernel, name, outs, specs, flops, scratch=(), exps=0, out_spec=vmem, limit=VMEM_LIMIT
    ):
        shapes = [jax.ShapeDtypeStruct(s, d) for s, d in outs]
        moved = 2 * sum(math.prod(s.shape) * s.dtype.itemsize for s in shapes)
        return pl.pallas_call(
            kernel,
            out_shape=tuple(shapes),
            in_specs=specs,
            out_specs=tuple([out_spec] * len(shapes)),
            scratch_shapes=scratch,
            compiler_params=pltpu.CompilerParams(vmem_limit_bytes=limit),
            cost_estimate=pl.CostEstimate(flops=flops, bytes_accessed=moved, transcendentals=exps),
            name=name,
        )

    packed = call(
        lambda *refs: pack_kernel(n, *refs),
        "pack",
        [((length, HD), bf16)] * n,
        [hbm] * 4,
        0,
        (
            pltpu.VMEM((tok, width), bf16),
            pltpu.VMEM((tok, width), bf16),
            pltpu.VMEM((tok, width), bf16),
            pltpu.VMEM(history.shape, bf16),
            pltpu.SemaphoreType.DMA((4,)),
        ),
        limit=PACK_LIMIT,
    )(query_rows, key_rows, value_rows, history)
    order = [6, 7, 2, 4, 3, 5, 1]
    arrived = {k: swap(packed[k], k) for k in order}
    by_head = [packed[0]] + [arrived[k] for k in order]
    chips = range(half)
    cots = call(
        lambda *refs: cot_kernel(n, tile, lo, *refs),
        "cot",
        [((2 * units * part, HD), bf16)] * half,
        [hbm] * 4,
        0,
        (
            pltpu.SMEM(offsets.shape, jnp.int32),
            pltpu.VMEM((part, all_cols), bf16),
            pltpu.SemaphoreType.DMA((2,)),
        ),
    )(offsets, cotangent, arrived[6], arrived[7])
    cots = [cots[0]] + [swap(cots[m], 2 * m) for m in chips[1:]]
    counts = (
        pltpu.VMEM((n, length, HD), bf16),
        pltpu.SMEM(frame_counts.shape, jnp.int32),
        pltpu.SemaphoreType.DMA,
    )
    pairs = half * tok * WINB * tok
    head_shape = ((rows + clip_rows, HD), bf16)
    same, cross = call(
        lambda *refs: attend_kernel(n, tok, [0] + order, *refs),
        "attend",
        [head_shape, head_shape],
        [hbm] + [vmem] * n,
        8 * pairs * HD,
        counts,
        2 * pairs,
    )(frame_counts, *by_head)
    (cot_mine,) = call(
        stack_kernel, "stack", [((half, 2 * units * part, HD), bf16)], [vmem] * half + [hbm], 0
    )(*cots, same)
    cot_swapped = swap_plane(cot_mine, 0)

    x_same, y_cross = swap(same, 2), swap(cross, 4 ^ 1)
    y_same, x_cross = swap(same, 4), swap(cross, 2 ^ 1)
    far_same, far_cross = swap(x_same, 4), swap(y_cross, 2)
    (late_cross,) = call(late_kernel, "late", [head_shape], [vmem, hbm], 0)(cross, x_same)
    c_cross = swap(late_cross, 1)

    turned_own, turned_other = call(
        lambda *refs: turn_kernel(lo, clip_rows, cot_rows, *refs),
        "turn",
        [((cols, half * cot_rows), bf16)] * 2,
        [vmem] * 2,
        0,
    )(cot_mine, cot_swapped)

    def grad(turned, heads, dtype, name):
        (out,) = call(
            lambda *refs: grad_kernel(rows, half, *refs),
            name,
            [((cols, len(heads) * HD), dtype)],
            [vmem] * (1 + len(heads)),
            2 * cols * half * cot_rows * len(heads) * HD,
        )(turned, *heads)
        return out

    near = [same, c_cross, x_cross, y_same, x_same, y_cross]
    heads = [0, 1, 3, 4, 2, 5, 6, 7]
    far = [far_same, far_cross]
    got_near = swap(grad(turned_other, near, bf16, "grad_other_near"), 1)
    own_near = grad(turned_own, near, jnp.float32, "grad_own_near")
    got_far = swap(grad(turned_other, far, bf16, "grad_other_far"), 1)
    own_far = grad(turned_own, far, jnp.float32, "grad_own_far")
    return call(
        lambda *refs: finish_kernel(heads, tok, *refs),
        "finish",
        [((tok, width), bf16), ((cols, width), jnp.float32)],
        [vmem] * (4 + n),
        0,
    )(own_near, own_far, got_near, got_far, *near, *far)


def body(query_rows, key_rows, value_rows, frame_counts, history, offsets, cotangent):
    n = lax.axis_size("tm")
    tok, width = query_rows.shape
    by_heads = (
        n == 8
        and lax.axis_size("head") % 2 == 0
        and width == n * HD
        and offsets.shape[1] == n
        and cotangent.shape[0] == tok + n * history.shape[0]
        and cotangent.shape[1] % (n * HD) == 0
        and tok % 16 == 0
        and (n * history.shape[0]) % 16 == 0
    )
    plan = head_body if by_heads else window_body
    return plan(query_rows, key_rows, value_rows, frame_counts, history, offsets, cotangent)


def solution(mesh):
    in_specs = (
        P("tm", "head"),
        P("tm", "head"),
        P("tm", "head"),
        P(),
        P("tm", "head"),
        P("tm", None),
        P("tm", None),
    )
    out_specs = (P("tm", "head"), P("tm", "head"))
    return jax.shard_map(body, mesh=mesh, in_specs=in_specs, out_specs=out_specs, check_vma=False)
```

```python
import math

import jax
import jax.numpy as jnp
from jax import lax
from jax.experimental import pallas as pl
from jax.experimental.pallas import tpu as pltpu
from jax.sharding import PartitionSpec as P

HD = 128
TPF = 64
WINB = 4
VMEM_LIMIT = 24 * 1024 * 1024
PACK_LIMIT = 63 * 1024 * 1024


def from_behind(x, axis, by):
    devices = lax.axis_size(axis)
    pairs = [(i, i + by) for i in range(devices) if 0 <= i + by < devices]
    return lax.ppermute(x, axis, pairs)


def window_body(query_rows, key_rows, value_rows, frame_counts, history, offsets, cotangent):
    tok_rows, feat_width = query_rows.shape
    local_heads = feat_width // HD
    block_total = lax.axis_size("tm")
    own_block = lax.axis_index("tm")
    score_scale = 1.0 / math.sqrt(HD)
    key_value = jnp.stack([key_rows, value_rows])
    pieces = []
    for distance in range(WINB - 1, 0, -1):
        pieces.append(from_behind(key_value, "tm", distance))
    window = jnp.concatenate(pieces + [key_value], axis=1)
    source_block = own_block - (WINB - 1) + jnp.arange(WINB, dtype=jnp.int32)
    block_match = jnp.arange(block_total, dtype=jnp.int32)[None, :] == source_block[:, None]
    block_count = jnp.sum(jnp.where(block_match, frame_counts[None, :], 0), axis=1)
    frame_index = jnp.arange(tok_rows, dtype=jnp.int32) // TPF
    kept_mask = (
        (source_block[:, None] >= 0) & (frame_index[None, :] < block_count[:, None])
    ).reshape(WINB * tok_rows)
    key_window = window[0].reshape(WINB * tok_rows, local_heads, HD)
    value_window = window[1].reshape(WINB * tok_rows, local_heads, HD)
    query_heads = query_rows.reshape(tok_rows, local_heads, HD)
    scores = (
        jnp.einsum("qhd,khd->hqk", query_heads, key_window, preferred_element_type=jnp.float32)
        * score_scale
    )
    scores = jnp.where(kept_mask[None, None, :], scores, -jnp.inf)
    row_max = jnp.max(scores, axis=-1, keepdims=True)
    weights = jnp.exp(scores - row_max)
    probs = (weights / jnp.sum(weights, axis=-1, keepdims=True)).astype(jnp.bfloat16)
    mixed = jnp.einsum("hqk,khd->qhd", probs, value_window, preferred_element_type=jnp.float32)
    attended = mixed.astype(jnp.bfloat16).reshape(tok_rows, feat_width)
    tile_rows = history.shape[0]
    source_tile = (own_block - offsets[0]) % block_total
    source_row = (
        source_tile[:, None] * tile_rows + jnp.arange(tile_rows, dtype=jnp.int32)[None, :]
    ).reshape(-1)
    incoming = lax.all_gather(history, "tm", axis=0, tiled=True)
    piece_rows = incoming.shape[0]
    selector = (source_row[:, None] == jnp.arange(piece_rows, dtype=jnp.int32)[None, :]).astype(
        jnp.bfloat16
    )
    clip_hist = jnp.dot(selector, incoming, preferred_element_type=jnp.float32).astype(jnp.bfloat16)
    disc_clip = jnp.concatenate([clip_hist, attended], axis=0)
    disc_grad = lax.psum_scatter(
        lax.dot_general(
            cotangent, disc_clip, (((0,), (0,)), ((), ())), preferred_element_type=jnp.float32
        ),
        "tm",
        scatter_dimension=0,
        tiled=True,
    )
    return (attended, disc_grad)


def cot_kernel(n, tile, lo, off_hbm, cot_hbm, behind_a, behind_b, *refs):
    outs, (off, cot, sems) = refs[:-3], refs[-3:]
    own = lax.axis_index("tm")
    chip, side = own // 2, lax.rem(own, 2)
    plane = lax.rem(lax.axis_index("head"), 2)
    clip_rows = n * tile
    part, all_cols = cot.shape
    cols = all_cols // n
    low = pl.multiple_of(plane * lo, 16)
    fetch_off = pltpu.make_async_copy(off_hbm, off, sems.at[0])
    fetch_cot = pltpu.make_async_copy(cot_hbm.at[pl.ds(low, part), :], cot, sems.at[1])
    fetch_off.start()
    fetch_cot.start()
    fetch_off.wait()
    r = lax.broadcasted_iota(jnp.int32, (clip_rows, clip_rows), 0)
    c = lax.broadcasted_iota(jnp.int32, (clip_rows, clip_rows), 1)
    select = jnp.where((r == c) & (plane != 0), 1.0, 0.0)
    for j in range(n):
        src = lax.rem(own - off[0, j] + 2 * n, n)
        for t in range(tile):
            hit = (c == j * tile + t) & (r == src * tile + t) & (plane == 0)
            select = jnp.where(hit, 1.0, select)
    fetch_cot.wait()
    cot[0:clip_rows, :] = jnp.dot(
        select.astype(jnp.bfloat16), cot[0:clip_rows, :], preferred_element_type=jnp.float32
    ).astype(jnp.bfloat16)
    units = cols // HD
    for m, out_ref in enumerate(outs):
        for i, block in enumerate((2 * (chip ^ m) + side, 2 * (chip ^ m) + 1 - side)):
            for u in range(units):
                at = (i * units + u) * part
                lanes = pl.ds(pl.multiple_of(block * cols + u * HD, HD), HD)
                out_ref[at : at + part, :] = cot[:, lanes]


def pack_kernel(n, heads, q_hbm, k_hbm, v_hbm, hist_hbm, *refs):
    outs, (q, k, v, hist, sems) = refs[:-5], refs[-5:]
    own = lax.axis_index("tm")
    tok, width = q.shape
    tile = hist.shape[0]
    clip_rows = n * tile
    start = 0 if width == n * HD else pl.multiple_of(((own ^ heads[0]) // 2) * width, width)
    pairs = [(hist_hbm, hist)] + [
        (x.at[:, pl.ds(start, width)], y) for x, y in ((q_hbm, q), (k_hbm, k), (v_hbm, v))
    ]
    copies = [pltpu.make_async_copy(a, b, sems.at[i]) for i, (a, b) in enumerate(pairs)]
    for copy in copies:
        copy.start()
    copies[0].wait()
    for d, out_ref in zip(heads, outs):
        lanes = pl.ds(pl.multiple_of((own ^ d) * HD, HD), HD)
        tiles = hist[:, lanes].astype(jnp.float32)
        row = lax.broadcasted_iota(jnp.int32, (clip_rows, HD), 0)
        placed = jnp.zeros((clip_rows, HD), jnp.float32)
        for t in range(tile):
            placed = jnp.where(row == own * tile + t, tiles[t : t + 1, :], placed)
        out_ref[3 * tok : 3 * tok + clip_rows, :] = placed.astype(jnp.bfloat16)
    for i, x in enumerate((q, k, v)):
        copies[1 + i].wait()
        for d, out_ref in zip(heads, outs):
            lanes = pl.ds(pl.multiple_of((own ^ d) * HD - start, HD), HD)
            out_ref[i * tok : (i + 1) * tok, :] = x[:, lanes]


def attend_blocks(n, tok, parity, counts, x_ref, out_ref):
    rate = math.log2(math.e) / math.sqrt(HD)
    token = lax.broadcasted_iota(jnp.int32, (1, tok), 1)
    for i in range(n // 2):
        block = 2 * i + parity
        keys = min(WINB, 2 * i + 2)
        sources = [block - (keys - 1) + k for k in range(keys)]
        q = x_ref[block, 0:tok, :]
        scores = []
        for s in sources:
            at = jnp.maximum(s, 0)
            kept = jnp.where(s >= 0, counts[at], 0) * TPF
            scores.append(
                lax.dot_general(
                    q,
                    x_ref[at, tok : 2 * tok, :],
                    (((1,), (1,)), ((), ())),
                    preferred_element_type=jnp.float32,
                )
                + jnp.where(token < kept, 0.0, -jnp.inf).astype(jnp.float32)
            )
        top = jnp.max(scores[0], axis=1, keepdims=True)
        for s in scores[1:]:
            top = jnp.maximum(top, jnp.max(s, axis=1, keepdims=True))
        weights = [jnp.exp2((s - top) * rate) for s in scores]
        total = jnp.sum(weights[0], axis=1, keepdims=True)
        for w in weights[1:]:
            total = total + jnp.sum(w, axis=1, keepdims=True)
        share = 1.0 / total
        mixed = jnp.zeros((tok, HD), jnp.float32)
        for s, w in zip(sources, weights):
            mixed = mixed + jnp.dot(
                (w * share).astype(jnp.bfloat16),
                x_ref[jnp.maximum(s, 0), 2 * tok : 3 * tok, :],
                preferred_element_type=jnp.float32,
            )
        out_ref[i * tok : (i + 1) * tok, :] = mixed.astype(jnp.bfloat16)
    rows = n // 2 * tok
    clip_rows = out_ref.shape[0] - rows
    hist = jnp.zeros((clip_rows, HD), jnp.float32)
    for s in range(n):
        hist = hist + x_ref[s, 3 * tok : 3 * tok + clip_rows, :].astype(jnp.float32)
    out_ref[rows:, :] = hist.astype(jnp.bfloat16)


def attend_kernel(n, tok, order, counts_hbm, *refs):
    parts, (same_ref, cross_ref, x_ref, counts, sem) = refs[:n], refs[n:]
    copy = pltpu.make_async_copy(counts_hbm, counts, sem)
    copy.start()
    own = lax.axis_index("tm")
    side = lax.rem(own, 2)
    for k, part in zip(order, parts):
        x_ref[own ^ k] = part[...]
    copy.wait()
    attend_blocks(n, tok, side, counts, x_ref, same_ref)
    attend_blocks(n, tok, 1 - side, counts, x_ref, cross_ref)


def stack_kernel(*refs):
    out_ref = refs[-1]
    for i, x in enumerate(refs[:-2]):
        out_ref[i] = x[...]


def late_kernel(x_ref, behind, out_ref):
    out_ref[...] = x_ref[...]


def whole_cot(lo, part, plane, mine, swapped):
    pieces = []
    for u in range(mine.shape[0] // part):
        a = mine[u * part : (u + 1) * part, :]
        b = swapped[u * part : (u + 1) * part, :]
        low = jnp.where(plane == 0, a, b)
        high = jnp.where(plane == 0, b, a)
        pieces.append(jnp.concatenate([low[:lo], high], axis=0))
    return jnp.concatenate(pieces, axis=1)


def turn(wholes, clip_rows):
    pieces = [x[clip_rows:] for x in wholes] + [x[:clip_rows] for x in wholes]
    return jnp.concatenate(pieces, axis=0).T


def turn_kernel(lo, clip_rows, cot_rows, mine_ref, swapped_ref, own_ref, other_ref):
    plane = lax.rem(lax.axis_index("head"), 2)
    chip = lax.axis_index("tm") // 2
    chips, length, _ = mine_ref.shape
    for i, out_ref in enumerate((own_ref, other_ref)):
        rows = slice(i * length // 2, (i + 1) * length // 2)
        wholes = [
            whole_cot(
                lo, cot_rows - lo, plane, mine_ref[chip ^ c, rows], swapped_ref[chip ^ c, rows]
            )
            for c in range(chips)
        ]
        out_ref[...] = turn(wholes, clip_rows)


def grad_part(turned_ref, head_refs, rows, copies):
    right = jnp.concatenate([x[0:rows, :] for x in head_refs], axis=1)
    hist = jnp.concatenate([x[rows:, :] for x in head_refs], axis=1)
    clip = copies * hist.shape[0]
    out = jnp.dot(turned_ref[:, 0:rows], right, preferred_element_type=jnp.float32)
    return out + jnp.dot(
        turned_ref[:, rows : rows + clip],
        jnp.concatenate([hist] * copies, axis=0),
        preferred_element_type=jnp.float32,
    )


def grad_kernel(rows, copies, turned_ref, *refs):
    out_ref = refs[-1]
    out_ref[...] = grad_part(turned_ref, refs[:-1], rows, copies).astype(out_ref.dtype)


def finish_kernel(order, tok, own_near, own_far, got_near, got_far, *refs):
    n = len(order)
    heads, att_ref, out_ref = refs[:n], refs[n], refs[n + 1]
    own = lax.axis_index("tm")
    at = pl.multiple_of(own // 2 * tok, tok)
    near = own_near.shape[1] // HD

    def column(near_ref, far_ref, i):
        ref, i = (near_ref, i) if i < near else (far_ref, i - near)
        return ref[:, i * HD : (i + 1) * HD]

    for i, k in enumerate(order):
        lanes = pl.ds(pl.multiple_of((own ^ k) * HD, HD), HD)
        att_ref[:, lanes] = heads[i][pl.ds(at, tok), :]
        got = column(got_near, got_far, order.index(k ^ 1))
        out_ref[:, lanes] = column(own_near, own_far, i) + got.astype(jnp.float32)


def head_body(query_rows, key_rows, value_rows, frame_counts, history, offsets, cotangent):
    n = lax.axis_size("tm")
    planes = lax.axis_size("head")
    half = n // 2
    tok, width = query_rows.shape
    tile = history.shape[0]
    clip_rows = n * tile
    cot_rows, all_cols = cotangent.shape
    cols = all_cols // n
    units = cols // HD
    lo = cot_rows // 32 * 16
    part = cot_rows - lo
    base = 3 * tok + clip_rows
    length = base
    rows = half * tok
    vmem = pl.BlockSpec(memory_space=pltpu.VMEM)
    hbm = pl.BlockSpec(memory_space=pl.ANY)
    bf16 = jnp.bfloat16

    def swap(x, bit):
        return lax.ppermute(x, "tm", [(i, i ^ bit) for i in range(n)])

    def swap_plane(x, bit):
        pairs = [
            (i * planes + p, (i ^ bit) * planes + (p ^ 1)) for i in range(n) for p in range(planes)
        ]
        return lax.ppermute(x, ("tm", "head"), pairs)

    def call(
        kernel, name, outs, specs, flops, scratch=(), exps=0, out_spec=vmem, limit=VMEM_LIMIT
    ):
        shapes = [jax.ShapeDtypeStruct(s, d) for s, d in outs]
        moved = 2 * sum(math.prod(s.shape) * s.dtype.itemsize for s in shapes)
        return pl.pallas_call(
            kernel,
            out_shape=tuple(shapes),
            in_specs=specs,
            out_specs=tuple([out_spec] * len(shapes)),
            scratch_shapes=scratch,
            compiler_params=pltpu.CompilerParams(vmem_limit_bytes=limit),
            cost_estimate=pl.CostEstimate(flops=flops, bytes_accessed=moved, transcendentals=exps),
            name=name,
        )

    def pack(heads, lanes, name):
        return call(
            lambda *refs: pack_kernel(n, heads, *refs),
            name,
            [((length, HD), bf16)] * len(heads),
            [hbm] * 4,
            0,
            (
                pltpu.VMEM((tok, lanes), bf16),
                pltpu.VMEM((tok, lanes), bf16),
                pltpu.VMEM((tok, lanes), bf16),
                pltpu.VMEM(history.shape, bf16),
                pltpu.SemaphoreType.DMA((4,)),
            ),
            limit=PACK_LIMIT,
        )(query_rows, key_rows, value_rows, history)

    first, rest = [6, 7], [0, 1, 2, 3, 4, 5]
    packed = dict(zip(first, pack(first, 2 * HD, "pack_first")))
    packed.update(zip(rest, pack(rest, width, "pack_rest")))
    order = [6, 7, 2, 4, 3, 5, 1]
    arrived = {k: swap(packed[k], k) for k in order}
    by_head = [packed[0]] + [arrived[k] for k in order]
    chips = range(half)
    cots = call(
        lambda *refs: cot_kernel(n, tile, lo, *refs),
        "cot",
        [((2 * units * part, HD), bf16)] * half,
        [hbm] * 4,
        0,
        (
            pltpu.SMEM(offsets.shape, jnp.int32),
            pltpu.VMEM((part, all_cols), bf16),
            pltpu.SemaphoreType.DMA((2,)),
        ),
    )(offsets, cotangent, arrived[6], arrived[7])
    cots = [cots[0]] + [swap(cots[m], 2 * m) for m in chips[1:]]
    counts = (
        pltpu.VMEM((n, length, HD), bf16),
        pltpu.SMEM(frame_counts.shape, jnp.int32),
        pltpu.SemaphoreType.DMA,
    )
    pairs = half * tok * WINB * tok
    head_shape = ((rows + clip_rows, HD), bf16)
    same, cross = call(
        lambda *refs: attend_kernel(n, tok, [0] + order, *refs),
        "attend",
        [head_shape, head_shape],
        [hbm] + [vmem] * n,
        8 * pairs * HD,
        counts,
        2 * pairs,
    )(frame_counts, *by_head)
    (cot_mine,) = call(
        stack_kernel, "stack", [((half, 2 * units * part, HD), bf16)], [vmem] * half + [hbm], 0
    )(*cots, same)
    cot_swapped = swap_plane(cot_mine, 0)

    x_same, y_cross = swap(same, 2), swap(cross, 4 ^ 1)
    y_same, x_cross = swap(same, 4), swap(cross, 2 ^ 1)
    far_same, far_cross = swap(x_same, 4), swap(y_cross, 2)
    (late_cross,) = call(late_kernel, "late", [head_shape], [vmem, hbm], 0)(cross, x_cross)
    c_cross = swap(late_cross, 1)

    turned_own, turned_other = call(
        lambda *refs: turn_kernel(lo, clip_rows, cot_rows, *refs),
        "turn",
        [((cols, half * cot_rows), bf16)] * 2,
        [vmem] * 2,
        0,
    )(cot_mine, cot_swapped)

    def grad(turned, heads, dtype, name):
        (out,) = call(
            lambda *refs: grad_kernel(rows, half, *refs),
            name,
            [((cols, len(heads) * HD), dtype)],
            [vmem] * (1 + len(heads)),
            2 * cols * half * cot_rows * len(heads) * HD,
        )(turned, *heads)
        return out

    near = [same, c_cross, x_cross, y_same, x_same, y_cross]
    heads = [0, 1, 3, 4, 2, 5, 6, 7]
    far = [far_same, far_cross]
    got_near = swap(grad(turned_other, near, bf16, "grad_other_near"), 1)
    own_near = grad(turned_own, near, jnp.float32, "grad_own_near")
    got_far = swap(grad(turned_other, far, bf16, "grad_other_far"), 1)
    own_far = grad(turned_own, far, jnp.float32, "grad_own_far")
    return call(
        lambda *refs: finish_kernel(heads, tok, *refs),
        "finish",
        [((tok, width), bf16), ((cols, width), jnp.float32)],
        [vmem] * (4 + n),
        0,
    )(own_near, own_far, got_near, got_far, *near, *far)


def body(query_rows, key_rows, value_rows, frame_counts, history, offsets, cotangent):
    n = lax.axis_size("tm")
    tok, width = query_rows.shape
    by_heads = (
        n == 8
        and lax.axis_size("head") % 2 == 0
        and width == n * HD
        and offsets.shape[1] == n
        and cotangent.shape[0] == tok + n * history.shape[0]
        and cotangent.shape[1] % (n * HD) == 0
        and tok % 16 == 0
        and (n * history.shape[0]) % 16 == 0
    )
    plan = head_body if by_heads else window_body
    return plan(query_rows, key_rows, value_rows, frame_counts, history, offsets, cotangent)


def solution(mesh):
    in_specs = (
        P("tm", "head"),
        P("tm", "head"),
        P("tm", "head"),
        P(),
        P("tm", "head"),
        P("tm", None),
        P("tm", None),
    )
    out_specs = (P("tm", "head"), P("tm", "head"))
    return jax.shard_map(body, mesh=mesh, in_specs=in_specs, out_specs=out_specs, check_vma=False)
```

```python
import math

import jax
import jax.numpy as jnp
from jax import lax
from jax.experimental import pallas as pl
from jax.experimental.pallas import tpu as pltpu
from jax.sharding import PartitionSpec as P

HD = 128
TPF = 64
WINB = 4
VMEM_LIMIT = 24 * 1024 * 1024
PACK_LIMIT = 63 * 1024 * 1024


def from_behind(x, axis, by):
    devices = lax.axis_size(axis)
    pairs = [(i, i + by) for i in range(devices) if 0 <= i + by < devices]
    return lax.ppermute(x, axis, pairs)


def window_body(query_rows, key_rows, value_rows, frame_counts, history, offsets, cotangent):
    tok_rows, feat_width = query_rows.shape
    local_heads = feat_width // HD
    block_total = lax.axis_size("tm")
    own_block = lax.axis_index("tm")
    score_scale = 1.0 / math.sqrt(HD)
    key_value = jnp.stack([key_rows, value_rows])
    pieces = []
    for distance in range(WINB - 1, 0, -1):
        pieces.append(from_behind(key_value, "tm", distance))
    window = jnp.concatenate(pieces + [key_value], axis=1)
    source_block = own_block - (WINB - 1) + jnp.arange(WINB, dtype=jnp.int32)
    block_match = jnp.arange(block_total, dtype=jnp.int32)[None, :] == source_block[:, None]
    block_count = jnp.sum(jnp.where(block_match, frame_counts[None, :], 0), axis=1)
    frame_index = jnp.arange(tok_rows, dtype=jnp.int32) // TPF
    kept_mask = (
        (source_block[:, None] >= 0) & (frame_index[None, :] < block_count[:, None])
    ).reshape(WINB * tok_rows)
    key_window = window[0].reshape(WINB * tok_rows, local_heads, HD)
    value_window = window[1].reshape(WINB * tok_rows, local_heads, HD)
    query_heads = query_rows.reshape(tok_rows, local_heads, HD)
    scores = (
        jnp.einsum("qhd,khd->hqk", query_heads, key_window, preferred_element_type=jnp.float32)
        * score_scale
    )
    scores = jnp.where(kept_mask[None, None, :], scores, -jnp.inf)
    row_max = jnp.max(scores, axis=-1, keepdims=True)
    weights = jnp.exp(scores - row_max)
    probs = (weights / jnp.sum(weights, axis=-1, keepdims=True)).astype(jnp.bfloat16)
    mixed = jnp.einsum("hqk,khd->qhd", probs, value_window, preferred_element_type=jnp.float32)
    attended = mixed.astype(jnp.bfloat16).reshape(tok_rows, feat_width)
    tile_rows = history.shape[0]
    source_tile = (own_block - offsets[0]) % block_total
    source_row = (
        source_tile[:, None] * tile_rows + jnp.arange(tile_rows, dtype=jnp.int32)[None, :]
    ).reshape(-1)
    incoming = lax.all_gather(history, "tm", axis=0, tiled=True)
    piece_rows = incoming.shape[0]
    selector = (source_row[:, None] == jnp.arange(piece_rows, dtype=jnp.int32)[None, :]).astype(
        jnp.bfloat16
    )
    clip_hist = jnp.dot(selector, incoming, preferred_element_type=jnp.float32).astype(jnp.bfloat16)
    disc_clip = jnp.concatenate([clip_hist, attended], axis=0)
    disc_grad = lax.psum_scatter(
        lax.dot_general(
            cotangent, disc_clip, (((0,), (0,)), ((), ())), preferred_element_type=jnp.float32
        ),
        "tm",
        scatter_dimension=0,
        tiled=True,
    )
    return (attended, disc_grad)


def cot_kernel(n, tile, lo, off_hbm, cot_hbm, behind_a, behind_b, *refs):
    outs, (off, cot, sems) = refs[:-3], refs[-3:]
    own = lax.axis_index("tm")
    chip, side = own // 2, lax.rem(own, 2)
    plane = lax.rem(lax.axis_index("head"), 2)
    clip_rows = n * tile
    part, all_cols = cot.shape
    cols = all_cols // n
    low = pl.multiple_of(plane * lo, 16)
    fetch_off = pltpu.make_async_copy(off_hbm, off, sems.at[0])
    fetch_cot = pltpu.make_async_copy(cot_hbm.at[pl.ds(low, part), :], cot, sems.at[1])
    fetch_off.start()
    fetch_cot.start()
    fetch_off.wait()
    r = lax.broadcasted_iota(jnp.int32, (clip_rows, clip_rows), 0)
    c = lax.broadcasted_iota(jnp.int32, (clip_rows, clip_rows), 1)
    select = jnp.where((r == c) & (plane != 0), 1.0, 0.0)
    for j in range(n):
        src = lax.rem(own - off[0, j] + 2 * n, n)
        for t in range(tile):
            hit = (c == j * tile + t) & (r == src * tile + t) & (plane == 0)
            select = jnp.where(hit, 1.0, select)
    fetch_cot.wait()
    cot[0:clip_rows, :] = jnp.dot(
        select.astype(jnp.bfloat16), cot[0:clip_rows, :], preferred_element_type=jnp.float32
    ).astype(jnp.bfloat16)
    units = cols // HD
    for m, out_ref in enumerate(outs):
        for i, block in enumerate((2 * (chip ^ m) + side, 2 * (chip ^ m) + 1 - side)):
            for u in range(units):
                at = (i * units + u) * part
                lanes = pl.ds(pl.multiple_of(block * cols + u * HD, HD), HD)
                out_ref[at : at + part, :] = cot[:, lanes]


def pack_kernel(n, heads, q_hbm, k_hbm, v_hbm, hist_hbm, *refs):
    outs, (q, k, v, hist, sems) = refs[:-5], refs[-5:]
    own = lax.axis_index("tm")
    tok, width = q.shape
    tile = hist.shape[0]
    clip_rows = n * tile
    start = 0 if width == n * HD else pl.multiple_of(((own ^ heads[0]) // 2) * width, width)
    pairs = [(hist_hbm, hist)] + [
        (x.at[:, pl.ds(start, width)], y) for x, y in ((q_hbm, q), (k_hbm, k), (v_hbm, v))
    ]
    copies = [pltpu.make_async_copy(a, b, sems.at[i]) for i, (a, b) in enumerate(pairs)]
    for copy in copies:
        copy.start()
    copies[0].wait()
    for d, out_ref in zip(heads, outs):
        lanes = pl.ds(pl.multiple_of((own ^ d) * HD, HD), HD)
        tiles = hist[:, lanes].astype(jnp.float32)
        row = lax.broadcasted_iota(jnp.int32, (clip_rows, HD), 0)
        placed = jnp.zeros((clip_rows, HD), jnp.float32)
        for t in range(tile):
            placed = jnp.where(row == own * tile + t, tiles[t : t + 1, :], placed)
        out_ref[3 * tok : 3 * tok + clip_rows, :] = placed.astype(jnp.bfloat16)
    for i, x in enumerate((q, k, v)):
        copies[1 + i].wait()
        for d, out_ref in zip(heads, outs):
            lanes = pl.ds(pl.multiple_of((own ^ d) * HD - start, HD), HD)
            out_ref[i * tok : (i + 1) * tok, :] = x[:, lanes]


def attend_blocks(n, tok, parity, counts, x_ref, out_ref):
    rate = math.log2(math.e) / math.sqrt(HD)
    token = lax.broadcasted_iota(jnp.int32, (1, tok), 1)
    for i in range(n // 2):
        block = 2 * i + parity
        keys = min(WINB, 2 * i + 2)
        sources = [block - (keys - 1) + k for k in range(keys)]
        q = x_ref[block, 0:tok, :]
        scores = []
        for s in sources:
            at = jnp.maximum(s, 0)
            kept = jnp.where(s >= 0, counts[at], 0) * TPF
            scores.append(
                lax.dot_general(
                    q,
                    x_ref[at, tok : 2 * tok, :],
                    (((1,), (1,)), ((), ())),
                    preferred_element_type=jnp.float32,
                )
                + jnp.where(token < kept, 0.0, -jnp.inf).astype(jnp.float32)
            )
        top = jnp.max(scores[0], axis=1, keepdims=True)
        for s in scores[1:]:
            top = jnp.maximum(top, jnp.max(s, axis=1, keepdims=True))
        weights = [jnp.exp2((s - top) * rate) for s in scores]
        total = jnp.sum(weights[0], axis=1, keepdims=True)
        for w in weights[1:]:
            total = total + jnp.sum(w, axis=1, keepdims=True)
        share = 1.0 / total
        mixed = jnp.zeros((tok, HD), jnp.float32)
        for s, w in zip(sources, weights):
            mixed = mixed + jnp.dot(
                (w * share).astype(jnp.bfloat16),
                x_ref[jnp.maximum(s, 0), 2 * tok : 3 * tok, :],
                preferred_element_type=jnp.float32,
            )
        out_ref[i * tok : (i + 1) * tok, :] = mixed.astype(jnp.bfloat16)
    rows = n // 2 * tok
    clip_rows = out_ref.shape[0] - rows
    hist = jnp.zeros((clip_rows, HD), jnp.float32)
    for s in range(n):
        hist = hist + x_ref[s, 3 * tok : 3 * tok + clip_rows, :].astype(jnp.float32)
    out_ref[rows:, :] = hist.astype(jnp.bfloat16)


def attend_kernel(n, tok, order, counts_hbm, *refs):
    parts, (same_ref, cross_ref, x_ref, counts, sem) = refs[:n], refs[n:]
    copy = pltpu.make_async_copy(counts_hbm, counts, sem)
    copy.start()
    own = lax.axis_index("tm")
    side = lax.rem(own, 2)
    for k, part in zip(order, parts):
        x_ref[own ^ k] = part[...]
    copy.wait()
    attend_blocks(n, tok, side, counts, x_ref, same_ref)
    attend_blocks(n, tok, 1 - side, counts, x_ref, cross_ref)


def stack_kernel(order, *refs):
    out_ref = refs[-1]
    for i, x in zip(order, refs):
        out_ref[i] = x[...]


def late_kernel(x_ref, *refs):
    refs[-1][...] = x_ref[...]


def whole_cot(lo, part, plane, mine, swapped):
    pieces = []
    for u in range(mine.shape[0] // part):
        a = mine[u * part : (u + 1) * part, :]
        b = swapped[u * part : (u + 1) * part, :]
        low = jnp.where(plane == 0, a, b)
        high = jnp.where(plane == 0, b, a)
        pieces.append(jnp.concatenate([low[:lo], high], axis=0))
    return jnp.concatenate(pieces, axis=1)


def turn(wholes, clip_rows):
    pieces = [x[clip_rows:] for x in wholes] + [x[:clip_rows] for x in wholes]
    return jnp.concatenate(pieces, axis=0).T


def turn_kernel(lo, clip_rows, cot_rows, mine_ref, swapped_ref, own_ref, other_ref):
    plane = lax.rem(lax.axis_index("head"), 2)
    chip = lax.axis_index("tm") // 2
    chips, length, _ = mine_ref.shape
    for i, out_ref in enumerate((own_ref, other_ref)):
        rows = slice(i * length // 2, (i + 1) * length // 2)
        wholes = [
            whole_cot(
                lo, cot_rows - lo, plane, mine_ref[chip ^ c, rows], swapped_ref[chip ^ c, rows]
            )
            for c in range(chips)
        ]
        out_ref[...] = turn(wholes, clip_rows)


def grad_part(turned_ref, head_refs, rows, copies):
    right = jnp.concatenate([x[0:rows, :] for x in head_refs], axis=1)
    hist = jnp.concatenate([x[rows:, :] for x in head_refs], axis=1)
    clip = copies * hist.shape[0]
    out = jnp.dot(turned_ref[:, 0:rows], right, preferred_element_type=jnp.float32)
    return out + jnp.dot(
        turned_ref[:, rows : rows + clip],
        jnp.concatenate([hist] * copies, axis=0),
        preferred_element_type=jnp.float32,
    )


def grad_kernel(rows, copies, turned_ref, *refs):
    out_ref = refs[-1]
    out_ref[...] = grad_part(turned_ref, refs[:-1], rows, copies).astype(out_ref.dtype)


def finish_kernel(order, tok, own_near, own_far, got_near, got_far, *refs):
    n = len(order)
    heads, (att_hbm, out_hbm, total, sems) = refs[:n], refs[n:]
    own = lax.axis_index("tm")
    at = pl.multiple_of(own // 2 * tok, tok)
    near = own_near.shape[1] // HD

    def column(near_ref, far_ref, i):
        ref, i = (near_ref, i) if i < near else (far_ref, i - near)
        return ref[:, i * HD : (i + 1) * HD]

    moves = []

    def move(a, b):
        moves.append(pltpu.make_async_copy(a, b, sems.at[len(moves)]))
        moves[-1].start()

    lanes = [pl.ds(pl.multiple_of((own ^ k) * HD, HD), HD) for k in order]
    for i in range(n):
        move(heads[i].at[pl.ds(at, tok), :], att_hbm.at[:, lanes[i]])
    for i, k in enumerate(order):
        got = column(got_near, got_far, order.index(k ^ 1))
        total[i] = column(own_near, own_far, i) + got.astype(jnp.float32)
        move(total.at[i], out_hbm.at[:, lanes[i]])
    for x in moves:
        x.wait()


def head_body(query_rows, key_rows, value_rows, frame_counts, history, offsets, cotangent):
    n = lax.axis_size("tm")
    planes = lax.axis_size("head")
    half = n // 2
    tok, width = query_rows.shape
    tile = history.shape[0]
    clip_rows = n * tile
    cot_rows, all_cols = cotangent.shape
    cols = all_cols // n
    units = cols // HD
    lo = cot_rows // 32 * 16
    part = cot_rows - lo
    base = 3 * tok + clip_rows
    length = base
    rows = half * tok
    vmem = pl.BlockSpec(memory_space=pltpu.VMEM)
    hbm = pl.BlockSpec(memory_space=pl.ANY)
    bf16 = jnp.bfloat16

    def swap(x, bit):
        return lax.ppermute(x, "tm", [(i, i ^ bit) for i in range(n)])

    def swap_plane(x, bit):
        pairs = [
            (i * planes + p, (i ^ bit) * planes + (p ^ 1)) for i in range(n) for p in range(planes)
        ]
        return lax.ppermute(x, ("tm", "head"), pairs)

    def call(
        kernel, name, outs, specs, flops, scratch=(), exps=0, out_spec=vmem, limit=VMEM_LIMIT
    ):
        shapes = [jax.ShapeDtypeStruct(s, d) for s, d in outs]
        moved = 2 * sum(math.prod(s.shape) * s.dtype.itemsize for s in shapes)
        return pl.pallas_call(
            kernel,
            out_shape=tuple(shapes),
            in_specs=specs,
            out_specs=tuple([out_spec] * len(shapes)),
            scratch_shapes=scratch,
            compiler_params=pltpu.CompilerParams(vmem_limit_bytes=limit),
            cost_estimate=pl.CostEstimate(flops=flops, bytes_accessed=moved, transcendentals=exps),
            name=name,
        )

    def pack(heads, lanes, name):
        return call(
            lambda *refs: pack_kernel(n, heads, *refs),
            name,
            [((length, HD), bf16)] * len(heads),
            [hbm] * 4,
            0,
            (
                pltpu.VMEM((tok, lanes), bf16),
                pltpu.VMEM((tok, lanes), bf16),
                pltpu.VMEM((tok, lanes), bf16),
                pltpu.VMEM(history.shape, bf16),
                pltpu.SemaphoreType.DMA((4,)),
            ),
            limit=PACK_LIMIT,
        )(query_rows, key_rows, value_rows, history)

    first, rest = [6, 7], [0, 1, 2, 3, 4, 5]
    packed = dict(zip(first, pack(first, 2 * HD, "pack_first")))
    packed.update(zip(rest, pack(rest, width, "pack_rest")))
    order = [6, 7, 2, 4, 3, 5, 1]
    arrived = {k: swap(packed[k], k) for k in order}
    by_head = [packed[0]] + [arrived[k] for k in order]
    chips = range(half)
    cots = call(
        lambda *refs: cot_kernel(n, tile, lo, *refs),
        "cot",
        [((2 * units * part, HD), bf16)] * half,
        [hbm] * 4,
        0,
        (
            pltpu.SMEM(offsets.shape, jnp.int32),
            pltpu.VMEM((part, all_cols), bf16),
            pltpu.SemaphoreType.DMA((2,)),
        ),
    )(offsets, cotangent, arrived[6], arrived[7])
    moved = {m: swap(cots[m], 2 * m) for m in reversed(chips[1:])}
    cots = [cots[0]] + [moved[m] for m in chips[1:]]
    counts = (
        pltpu.VMEM((n, length, HD), bf16),
        pltpu.SMEM(frame_counts.shape, jnp.int32),
        pltpu.SemaphoreType.DMA,
    )
    pairs = half * tok * WINB * tok
    head_shape = ((rows + clip_rows, HD), bf16)
    same, cross = call(
        lambda *refs: attend_kernel(n, tok, [0] + order, *refs),
        "attend",
        [head_shape, head_shape],
        [hbm] + [vmem] * n,
        8 * pairs * HD,
        counts,
        2 * pairs,
    )(frame_counts, *by_head)
    stack_order = [3, 1, 2, 0]
    (cot_mine,) = call(
        lambda *refs: stack_kernel(stack_order, *refs),
        "stack",
        [((half, 2 * units * part, HD), bf16)],
        [vmem] * half + [hbm],
        0,
    )(*[cots[m] for m in stack_order], same)
    cot_swapped = swap_plane(cot_mine, 0)

    x_same, y_cross = swap(same, 2), swap(cross, 4 ^ 1)
    y_same, x_cross = swap(same, 4), swap(cross, 2 ^ 1)
    far_same, far_cross = swap(x_same, 4), swap(y_cross, 2)
    (late_cross,) = call(late_kernel, "late", [head_shape], [vmem] + [hbm] * 2, 0)(cross, x_cross, y_same)
    c_cross = swap(late_cross, 1)

    turned_own, turned_other = call(
        lambda *refs: turn_kernel(lo, clip_rows, cot_rows, *refs),
        "turn",
        [((cols, half * cot_rows), bf16)] * 2,
        [vmem] * 2,
        0,
    )(cot_mine, cot_swapped)

    def grad(turned, heads, dtype, name):
        (out,) = call(
            lambda *refs: grad_kernel(rows, half, *refs),
            name,
            [((cols, len(heads) * HD), dtype)],
            [vmem] * (1 + len(heads)),
            2 * cols * half * cot_rows * len(heads) * HD,
        )(turned, *heads)
        return out

    near = [same, x_cross, y_same, x_same, y_cross]
    far = [c_cross, far_same, far_cross]
    heads = [0, 3, 4, 2, 5, 1, 6, 7]
    got_near = swap(grad(turned_other, near, bf16, "grad_other_near"), 1)
    own_near = grad(turned_own, near, jnp.float32, "grad_own_near")
    got_far = swap(grad(turned_other, far, bf16, "grad_other_far"), 1)
    own_far = grad(turned_own, far, jnp.float32, "grad_own_far")
    return call(
        lambda *refs: finish_kernel(heads, tok, *refs),
        "finish",
        [((tok, width), bf16), ((cols, width), jnp.float32)],
        [vmem] * (4 + n),
        0,
        (pltpu.VMEM((n, cols, HD), jnp.float32), pltpu.SemaphoreType.DMA((2 * n,))),
        out_spec=hbm,
    )(own_near, own_far, got_near, got_far, *near, *far)


def body(query_rows, key_rows, value_rows, frame_counts, history, offsets, cotangent):
    n = lax.axis_size("tm")
    tok, width = query_rows.shape
    by_heads = (
        n == 8
        and lax.axis_size("head") % 2 == 0
        and width == n * HD
        and offsets.shape[1] == n
        and cotangent.shape[0] == tok + n * history.shape[0]
        and cotangent.shape[1] % (n * HD) == 0
        and tok % 16 == 0
        and (n * history.shape[0]) % 16 == 0
    )
    plan = head_body if by_heads else window_body
    return plan(query_rows, key_rows, value_rows, frame_counts, history, offsets, cotangent)


def solution(mesh):
    in_specs = (
        P("tm", "head"),
        P("tm", "head"),
        P("tm", "head"),
        P(),
        P("tm", "head"),
        P("tm", None),
        P("tm", None),
    )
    out_specs = (P("tm", "head"), P("tm", "head"))
    return jax.shard_map(body, mesh=mesh, in_specs=in_specs, out_specs=out_specs, check_vma=False)
```

```python
import math

import jax
import jax.numpy as jnp
from jax import lax
from jax.experimental import pallas as pl
from jax.experimental.pallas import tpu as pltpu
from jax.sharding import PartitionSpec as P

HD = 128
TPF = 64
WINB = 4
VMEM_LIMIT = 24 * 1024 * 1024
PACK_LIMIT = 58 * 1024 * 1024


def from_behind(x, axis, by):
    devices = lax.axis_size(axis)
    pairs = [(i, i + by) for i in range(devices) if 0 <= i + by < devices]
    return lax.ppermute(x, axis, pairs)


def window_body(query_rows, key_rows, value_rows, frame_counts, history, offsets, cotangent):
    tok_rows, feat_width = query_rows.shape
    local_heads = feat_width // HD
    block_total = lax.axis_size("tm")
    own_block = lax.axis_index("tm")
    score_scale = 1.0 / math.sqrt(HD)
    key_value = jnp.stack([key_rows, value_rows])
    pieces = []
    for distance in range(WINB - 1, 0, -1):
        pieces.append(from_behind(key_value, "tm", distance))
    window = jnp.concatenate(pieces + [key_value], axis=1)
    source_block = own_block - (WINB - 1) + jnp.arange(WINB, dtype=jnp.int32)
    block_match = jnp.arange(block_total, dtype=jnp.int32)[None, :] == source_block[:, None]
    block_count = jnp.sum(jnp.where(block_match, frame_counts[None, :], 0), axis=1)
    frame_index = jnp.arange(tok_rows, dtype=jnp.int32) // TPF
    kept_mask = (
        (source_block[:, None] >= 0) & (frame_index[None, :] < block_count[:, None])
    ).reshape(WINB * tok_rows)
    key_window = window[0].reshape(WINB * tok_rows, local_heads, HD)
    value_window = window[1].reshape(WINB * tok_rows, local_heads, HD)
    query_heads = query_rows.reshape(tok_rows, local_heads, HD)
    scores = (
        jnp.einsum("qhd,khd->hqk", query_heads, key_window, preferred_element_type=jnp.float32)
        * score_scale
    )
    scores = jnp.where(kept_mask[None, None, :], scores, -jnp.inf)
    row_max = jnp.max(scores, axis=-1, keepdims=True)
    weights = jnp.exp(scores - row_max)
    probs = (weights / jnp.sum(weights, axis=-1, keepdims=True)).astype(jnp.bfloat16)
    mixed = jnp.einsum("hqk,khd->qhd", probs, value_window, preferred_element_type=jnp.float32)
    attended = mixed.astype(jnp.bfloat16).reshape(tok_rows, feat_width)
    tile_rows = history.shape[0]
    source_tile = (own_block - offsets[0]) % block_total
    source_row = (
        source_tile[:, None] * tile_rows + jnp.arange(tile_rows, dtype=jnp.int32)[None, :]
    ).reshape(-1)
    incoming = lax.all_gather(history, "tm", axis=0, tiled=True)
    piece_rows = incoming.shape[0]
    selector = (source_row[:, None] == jnp.arange(piece_rows, dtype=jnp.int32)[None, :]).astype(
        jnp.bfloat16
    )
    clip_hist = jnp.dot(selector, incoming, preferred_element_type=jnp.float32).astype(jnp.bfloat16)
    disc_clip = jnp.concatenate([clip_hist, attended], axis=0)
    disc_grad = lax.psum_scatter(
        lax.dot_general(
            cotangent, disc_clip, (((0,), (0,)), ((), ())), preferred_element_type=jnp.float32
        ),
        "tm",
        scatter_dimension=0,
        tiled=True,
    )
    return (attended, disc_grad)


def cot_kernel(n, tile, lo, off_hbm, cot_hbm, behind_a, behind_b, *refs):
    outs, (off, cot, sems) = refs[:-3], refs[-3:]
    own = lax.axis_index("tm")
    chip, side = own // 2, lax.rem(own, 2)
    plane = lax.rem(lax.axis_index("head"), 2)
    clip_rows = n * tile
    part, all_cols = cot.shape
    cols = all_cols // n
    low = pl.multiple_of(plane * lo, 16)
    fetch_off = pltpu.make_async_copy(off_hbm, off, sems.at[0])
    fetch_cot = pltpu.make_async_copy(cot_hbm.at[pl.ds(low, part), :], cot, sems.at[1])
    fetch_off.start()
    fetch_cot.start()
    fetch_off.wait()
    r = lax.broadcasted_iota(jnp.int32, (clip_rows, clip_rows), 0)
    c = lax.broadcasted_iota(jnp.int32, (clip_rows, clip_rows), 1)
    select = jnp.where((r == c) & (plane != 0), 1.0, 0.0)
    for j in range(n):
        src = lax.rem(own - off[0, j] + 2 * n, n)
        for t in range(tile):
            hit = (c == j * tile + t) & (r == src * tile + t) & (plane == 0)
            select = jnp.where(hit, 1.0, select)
    fetch_cot.wait()
    cot[0:clip_rows, :] = jnp.dot(
        select.astype(jnp.bfloat16), cot[0:clip_rows, :], preferred_element_type=jnp.float32
    ).astype(jnp.bfloat16)
    units = cols // HD
    for m, out_ref in enumerate(outs):
        for i, block in enumerate((2 * (chip ^ m) + side, 2 * (chip ^ m) + 1 - side)):
            for u in range(units):
                at = (i * units + u) * part
                lanes = pl.ds(pl.multiple_of(block * cols + u * HD, HD), HD)
                out_ref[at : at + part, :] = cot[:, lanes]


def pack_kernel(n, heads, q_hbm, k_hbm, v_hbm, hist_hbm, *refs):
    outs, (q, k, v, hist, sems) = refs[:-5], refs[-5:]
    own = lax.axis_index("tm")
    tok, width = q.shape
    tile = hist.shape[0]
    clip_rows = n * tile
    start = 0 if width == n * HD else pl.multiple_of(((own ^ heads[0]) // 2) * width, width)
    pairs = [(hist_hbm, hist)] + [
        (x.at[:, pl.ds(start, width)], y) for x, y in ((q_hbm, q), (k_hbm, k), (v_hbm, v))
    ]
    copies = [pltpu.make_async_copy(a, b, sems.at[i]) for i, (a, b) in enumerate(pairs)]
    for copy in copies:
        copy.start()
    copies[0].wait()
    for d, out_ref in zip(heads, outs):
        lanes = pl.ds(pl.multiple_of((own ^ d) * HD, HD), HD)
        tiles = hist[:, lanes].astype(jnp.float32)
        row = lax.broadcasted_iota(jnp.int32, (clip_rows, HD), 0)
        placed = jnp.zeros((clip_rows, HD), jnp.float32)
        for t in range(tile):
            placed = jnp.where(row == own * tile + t, tiles[t : t + 1, :], placed)
        out_ref[3 * tok : 3 * tok + clip_rows, :] = placed.astype(jnp.bfloat16)
    for i, x in enumerate((q, k, v)):
        copies[1 + i].wait()
        for d, out_ref in zip(heads, outs):
            lanes = pl.ds(pl.multiple_of((own ^ d) * HD - start, HD), HD)
            out_ref[i * tok : (i + 1) * tok, :] = x[:, lanes]


def attend_blocks(n, tok, parity, counts, x_ref, out_ref):
    rate = math.log2(math.e) / math.sqrt(HD)
    token = lax.broadcasted_iota(jnp.int32, (1, tok), 1)
    for i in range(n // 2):
        block = 2 * i + parity
        keys = min(WINB, 2 * i + 2)
        sources = [block - (keys - 1) + k for k in range(keys)]
        q = x_ref[block, 0:tok, :]
        scores = []
        for s in sources:
            at = jnp.maximum(s, 0)
            kept = jnp.where(s >= 0, counts[at], 0) * TPF
            scores.append(
                lax.dot_general(
                    q,
                    x_ref[at, tok : 2 * tok, :],
                    (((1,), (1,)), ((), ())),
                    preferred_element_type=jnp.float32,
                )
                + jnp.where(token < kept, 0.0, -jnp.inf).astype(jnp.float32)
            )
        top = jnp.max(scores[0], axis=1, keepdims=True)
        for s in scores[1:]:
            top = jnp.maximum(top, jnp.max(s, axis=1, keepdims=True))
        weights = [jnp.exp2((s - top) * rate) for s in scores]
        total = jnp.sum(weights[0], axis=1, keepdims=True)
        for w in weights[1:]:
            total = total + jnp.sum(w, axis=1, keepdims=True)
        share = 1.0 / total
        mixed = jnp.zeros((tok, HD), jnp.float32)
        for s, w in zip(sources, weights):
            mixed = mixed + jnp.dot(
                (w * share).astype(jnp.bfloat16),
                x_ref[jnp.maximum(s, 0), 2 * tok : 3 * tok, :],
                preferred_element_type=jnp.float32,
            )
        out_ref[i * tok : (i + 1) * tok, :] = mixed.astype(jnp.bfloat16)
    rows = n // 2 * tok
    clip_rows = out_ref.shape[0] - rows
    hist = jnp.zeros((clip_rows, HD), jnp.float32)
    for s in range(n):
        hist = hist + x_ref[s, 3 * tok : 3 * tok + clip_rows, :].astype(jnp.float32)
    out_ref[rows:, :] = hist.astype(jnp.bfloat16)


def attend_kernel(n, tok, order, counts_hbm, *refs):
    parts, (same_ref, cross_ref, x_ref, counts, sem) = refs[:n], refs[n:]
    copy = pltpu.make_async_copy(counts_hbm, counts, sem)
    copy.start()
    own = lax.axis_index("tm")
    side = lax.rem(own, 2)
    for k, part in zip(order, parts):
        x_ref[own ^ k] = part[...]
    copy.wait()
    attend_blocks(n, tok, side, counts, x_ref, same_ref)
    attend_blocks(n, tok, 1 - side, counts, x_ref, cross_ref)


def stack_kernel(order, *refs):
    out_ref = refs[-1]
    for i, x in zip(order, refs):
        out_ref[i] = x[...]


def late_kernel(x_ref, *refs):
    refs[-1][...] = x_ref[...]


def whole_cot(lo, part, plane, mine, swapped):
    pieces = []
    for u in range(mine.shape[0] // part):
        a = mine[u * part : (u + 1) * part, :]
        b = swapped[u * part : (u + 1) * part, :]
        low = jnp.where(plane == 0, a, b)
        high = jnp.where(plane == 0, b, a)
        pieces.append(jnp.concatenate([low[:lo], high], axis=0))
    return jnp.concatenate(pieces, axis=1)


def turn(wholes, clip_rows):
    pieces = [x[clip_rows:] for x in wholes] + [x[:clip_rows] for x in wholes]
    return jnp.concatenate(pieces, axis=0).T


def turn_kernel(lo, clip_rows, cot_rows, mine_ref, swapped_ref, own_ref, other_ref):
    plane = lax.rem(lax.axis_index("head"), 2)
    chip = lax.axis_index("tm") // 2
    chips, length, _ = mine_ref.shape
    for i, out_ref in enumerate((own_ref, other_ref)):
        rows = slice(i * length // 2, (i + 1) * length // 2)
        wholes = [
            whole_cot(
                lo, cot_rows - lo, plane, mine_ref[chip ^ c, rows], swapped_ref[chip ^ c, rows]
            )
            for c in range(chips)
        ]
        out_ref[...] = turn(wholes, clip_rows)


def grad_part(turned_ref, head_refs, rows, copies):
    right = jnp.concatenate([x[0:rows, :] for x in head_refs], axis=1)
    hist = jnp.concatenate([x[rows:, :] for x in head_refs], axis=1)
    clip = copies * hist.shape[0]
    out = jnp.dot(turned_ref[:, 0:rows], right, preferred_element_type=jnp.float32)
    return out + jnp.dot(
        turned_ref[:, rows : rows + clip],
        jnp.concatenate([hist] * copies, axis=0),
        preferred_element_type=jnp.float32,
    )


def grad_kernel(rows, copies, turned_ref, *refs):
    out_ref = refs[-1]
    out_ref[...] = grad_part(turned_ref, refs[:-1], rows, copies).astype(out_ref.dtype)


def finish_kernel(order, tok, own_near, own_far, got_near, got_far, *refs):
    n = len(order)
    heads, (att_hbm, out_hbm, total, sems) = refs[:n], refs[n:]
    own = lax.axis_index("tm")
    at = pl.multiple_of(own // 2 * tok, tok)
    near = own_near.shape[1] // HD

    def column(near_ref, far_ref, i):
        ref, i = (near_ref, i) if i < near else (far_ref, i - near)
        return ref[:, i * HD : (i + 1) * HD]

    moves = []

    def move(a, b):
        moves.append(pltpu.make_async_copy(a, b, sems.at[len(moves)]))
        moves[-1].start()

    lanes = [pl.ds(pl.multiple_of((own ^ k) * HD, HD), HD) for k in order]
    for i in range(n):
        move(heads[i].at[pl.ds(at, tok), :], att_hbm.at[:, lanes[i]])
    for i, k in enumerate(order):
        got = column(got_near, got_far, order.index(k ^ 1))
        total[i] = column(own_near, own_far, i) + got.astype(jnp.float32)
        move(total.at[i], out_hbm.at[:, lanes[i]])
    for x in moves:
        x.wait()


def head_body(query_rows, key_rows, value_rows, frame_counts, history, offsets, cotangent):
    n = lax.axis_size("tm")
    planes = lax.axis_size("head")
    half = n // 2
    tok, width = query_rows.shape
    tile = history.shape[0]
    clip_rows = n * tile
    cot_rows, all_cols = cotangent.shape
    cols = all_cols // n
    units = cols // HD
    lo = cot_rows // 32 * 16
    part = cot_rows - lo
    base = 3 * tok + clip_rows
    length = base
    rows = half * tok
    vmem = pl.BlockSpec(memory_space=pltpu.VMEM)
    hbm = pl.BlockSpec(memory_space=pl.ANY)
    bf16 = jnp.bfloat16

    def swap(x, bit):
        return lax.ppermute(x, "tm", [(i, i ^ bit) for i in range(n)])

    def swap_plane(x, bit):
        pairs = [
            (i * planes + p, (i ^ bit) * planes + (p ^ 1)) for i in range(n) for p in range(planes)
        ]
        return lax.ppermute(x, ("tm", "head"), pairs)

    def call(
        kernel, name, outs, specs, flops, scratch=(), exps=0, out_spec=vmem, limit=VMEM_LIMIT
    ):
        shapes = [jax.ShapeDtypeStruct(s, d) for s, d in outs]
        moved = 2 * sum(math.prod(s.shape) * s.dtype.itemsize for s in shapes)
        return pl.pallas_call(
            kernel,
            out_shape=tuple(shapes),
            in_specs=specs,
            out_specs=tuple([out_spec] * len(shapes)),
            scratch_shapes=scratch,
            compiler_params=pltpu.CompilerParams(vmem_limit_bytes=limit),
            cost_estimate=pl.CostEstimate(flops=flops, bytes_accessed=moved, transcendentals=exps),
            name=name,
        )

    def pack(heads, lanes, name):
        return call(
            lambda *refs: pack_kernel(n, heads, *refs),
            name,
            [((length, HD), bf16)] * len(heads),
            [hbm] * 4,
            0,
            (
                pltpu.VMEM((tok, lanes), bf16),
                pltpu.VMEM((tok, lanes), bf16),
                pltpu.VMEM((tok, lanes), bf16),
                pltpu.VMEM(history.shape, bf16),
                pltpu.SemaphoreType.DMA((4,)),
            ),
            limit=PACK_LIMIT,
        )(query_rows, key_rows, value_rows, history)

    own = lax.axis_index("tm")
    row = lax.broadcasted_iota(jnp.int32, (clip_rows, 1), 0)
    placed = jnp.zeros((clip_rows, width), jnp.bfloat16)
    for t in range(tile):
        placed = jnp.where(row == own * tile + t, history[t : t + 1], placed)

    def cut(k):
        pieces = (query_rows, key_rows, value_rows, placed)
        return jnp.concatenate(
            [lax.dynamic_slice(x, (0, (own ^ k) * HD), (x.shape[0], HD)) for x in pieces], axis=0
        )

    rest = [0, 1, 2, 3, 4, 5]
    packed = {k: cut(k) for k in (6, 7)}
    packed.update(zip(rest, pack(rest, width, "pack_rest")))
    order = [6, 7, 2, 4, 3, 5, 1]
    arrived = {k: swap(packed[k], k) for k in order}
    by_head = [packed[0]] + [arrived[k] for k in order]
    chips = range(half)
    cots = call(
        lambda *refs: cot_kernel(n, tile, lo, *refs),
        "cot",
        [((2 * units * part, HD), bf16)] * half,
        [hbm] * 4,
        0,
        (
            pltpu.SMEM(offsets.shape, jnp.int32),
            pltpu.VMEM((part, all_cols), bf16),
            pltpu.SemaphoreType.DMA((2,)),
        ),
    )(offsets, cotangent, arrived[6], arrived[1])
    moved = {m: swap(cots[m], 2 * m) for m in reversed(chips[1:])}
    cots = [cots[0]] + [moved[m] for m in chips[1:]]
    counts = (
        pltpu.VMEM((n, length, HD), bf16),
        pltpu.SMEM(frame_counts.shape, jnp.int32),
        pltpu.SemaphoreType.DMA,
    )
    pairs = half * tok * WINB * tok
    head_shape = ((rows + clip_rows, HD), bf16)
    same, cross = call(
        lambda *refs: attend_kernel(n, tok, [0] + order, *refs),
        "attend",
        [head_shape, head_shape],
        [hbm] + [vmem] * n,
        8 * pairs * HD,
        counts,
        2 * pairs,
    )(frame_counts, *by_head)
    stack_order = [3, 1, 2, 0]
    (cot_mine,) = call(
        lambda *refs: stack_kernel(stack_order, *refs),
        "stack",
        [((half, 2 * units * part, HD), bf16)],
        [vmem] * half + [hbm],
        0,
    )(*[cots[m] for m in stack_order], same)
    cot_swapped = swap_plane(cot_mine, 0)

    x_same, y_cross = swap(same, 2), swap(cross, 4 ^ 1)
    y_same, x_cross = swap(same, 4), swap(cross, 2 ^ 1)
    far_same, far_cross = swap(x_same, 4), swap(y_cross, 2)
    (late_cross,) = call(late_kernel, "late", [head_shape], [vmem] + [hbm] * 2, 0)(cross, x_cross, y_same)
    c_cross = swap(late_cross, 1)

    turned_own, turned_other = call(
        lambda *refs: turn_kernel(lo, clip_rows, cot_rows, *refs),
        "turn",
        [((cols, half * cot_rows), bf16)] * 2,
        [vmem] * 2,
        0,
    )(cot_mine, cot_swapped)

    def grad(turned, heads, dtype, name):
        (out,) = call(
            lambda *refs: grad_kernel(rows, half, *refs),
            name,
            [((cols, len(heads) * HD), dtype)],
            [vmem] * (1 + len(heads)),
            2 * cols * half * cot_rows * len(heads) * HD,
        )(turned, *heads)
        return out

    near = [same, x_cross, y_same, x_same, y_cross]
    far = [c_cross, far_same, far_cross]
    heads = [0, 3, 4, 2, 5, 1, 6, 7]
    got_near = swap(grad(turned_other, near, bf16, "grad_other_near"), 1)
    own_near = grad(turned_own, near, jnp.float32, "grad_own_near")
    got_far = swap(grad(turned_other, far, bf16, "grad_other_far"), 1)
    own_far = grad(turned_own, far, jnp.float32, "grad_own_far")
    return call(
        lambda *refs: finish_kernel(heads, tok, *refs),
        "finish",
        [((tok, width), bf16), ((cols, width), jnp.float32)],
        [vmem] * (4 + n),
        0,
        (pltpu.VMEM((n, cols, HD), jnp.float32), pltpu.SemaphoreType.DMA((2 * n,))),
        out_spec=hbm,
    )(own_near, own_far, got_near, got_far, *near, *far)


def body(query_rows, key_rows, value_rows, frame_counts, history, offsets, cotangent):
    n = lax.axis_size("tm")
    tok, width = query_rows.shape
    by_heads = (
        n == 8
        and lax.axis_size("head") % 2 == 0
        and width == n * HD
        and offsets.shape[1] == n
        and cotangent.shape[0] == tok + n * history.shape[0]
        and cotangent.shape[1] % (n * HD) == 0
        and tok % 16 == 0
        and (n * history.shape[0]) % 16 == 0
    )
    plan = head_body if by_heads else window_body
    return plan(query_rows, key_rows, value_rows, frame_counts, history, offsets, cotangent)


def solution(mesh):
    in_specs = (
        P("tm", "head"),
        P("tm", "head"),
        P("tm", "head"),
        P(),
        P("tm", "head"),
        P("tm", None),
        P("tm", None),
    )
    out_specs = (P("tm", "head"), P("tm", "head"))
    return jax.shard_map(body, mesh=mesh, in_specs=in_specs, out_specs=out_specs, check_vma=False)
```

```python
import math

import jax
import jax.numpy as jnp
from jax import lax
from jax.experimental import pallas as pl
from jax.experimental.pallas import tpu as pltpu
from jax.sharding import PartitionSpec as P

HD = 128
TPF = 64
WINB = 4
VMEM_LIMIT = 24 * 1024 * 1024
PACK_LIMIT = 58 * 1024 * 1024


def from_behind(x, axis, by):
    devices = lax.axis_size(axis)
    pairs = [(i, i + by) for i in range(devices) if 0 <= i + by < devices]
    return lax.ppermute(x, axis, pairs)


def window_body(query_rows, key_rows, value_rows, frame_counts, history, offsets, cotangent):
    tok_rows, feat_width = query_rows.shape
    local_heads = feat_width // HD
    block_total = lax.axis_size("tm")
    own_block = lax.axis_index("tm")
    score_scale = 1.0 / math.sqrt(HD)
    key_value = jnp.stack([key_rows, value_rows])
    pieces = []
    for distance in range(WINB - 1, 0, -1):
        pieces.append(from_behind(key_value, "tm", distance))
    window = jnp.concatenate(pieces + [key_value], axis=1)
    source_block = own_block - (WINB - 1) + jnp.arange(WINB, dtype=jnp.int32)
    block_match = jnp.arange(block_total, dtype=jnp.int32)[None, :] == source_block[:, None]
    block_count = jnp.sum(jnp.where(block_match, frame_counts[None, :], 0), axis=1)
    frame_index = jnp.arange(tok_rows, dtype=jnp.int32) // TPF
    kept_mask = (
        (source_block[:, None] >= 0) & (frame_index[None, :] < block_count[:, None])
    ).reshape(WINB * tok_rows)
    key_window = window[0].reshape(WINB * tok_rows, local_heads, HD)
    value_window = window[1].reshape(WINB * tok_rows, local_heads, HD)
    query_heads = query_rows.reshape(tok_rows, local_heads, HD)
    scores = (
        jnp.einsum("qhd,khd->hqk", query_heads, key_window, preferred_element_type=jnp.float32)
        * score_scale
    )
    scores = jnp.where(kept_mask[None, None, :], scores, -jnp.inf)
    row_max = jnp.max(scores, axis=-1, keepdims=True)
    weights = jnp.exp(scores - row_max)
    probs = (weights / jnp.sum(weights, axis=-1, keepdims=True)).astype(jnp.bfloat16)
    mixed = jnp.einsum("hqk,khd->qhd", probs, value_window, preferred_element_type=jnp.float32)
    attended = mixed.astype(jnp.bfloat16).reshape(tok_rows, feat_width)
    tile_rows = history.shape[0]
    source_tile = (own_block - offsets[0]) % block_total
    source_row = (
        source_tile[:, None] * tile_rows + jnp.arange(tile_rows, dtype=jnp.int32)[None, :]
    ).reshape(-1)
    incoming = lax.all_gather(history, "tm", axis=0, tiled=True)
    piece_rows = incoming.shape[0]
    selector = (source_row[:, None] == jnp.arange(piece_rows, dtype=jnp.int32)[None, :]).astype(
        jnp.bfloat16
    )
    clip_hist = jnp.dot(selector, incoming, preferred_element_type=jnp.float32).astype(jnp.bfloat16)
    disc_clip = jnp.concatenate([clip_hist, attended], axis=0)
    disc_grad = lax.psum_scatter(
        lax.dot_general(
            cotangent, disc_clip, (((0,), (0,)), ((), ())), preferred_element_type=jnp.float32
        ),
        "tm",
        scatter_dimension=0,
        tiled=True,
    )
    return (attended, disc_grad)


def mate_bit(i):
    return 4 >> (i % 2)


def sum_bit(i):
    return 2 << (i % 2)


def place():
    own = lax.axis_index("tm")
    side = lax.rem(own, 2)
    return own, side, jnp.where(side == 0, 4, 2), jnp.where(side == 0, 2, 4)


def cot_kernel(n, tile, lo, off_hbm, cot_hbm, *refs):
    outs, (off, cot, sems) = refs[-7:-3], refs[-3:]
    own, side, mate, partner = place()
    plane = lax.rem(lax.axis_index("head"), 2)
    clip_rows = n * tile
    all_rows, all_cols = cot.shape
    cols = all_cols // n
    part = all_rows - lo
    low = pl.multiple_of(plane * lo, 16)
    fetch_off = pltpu.make_async_copy(off_hbm, off, sems.at[0])
    fetch_cot = pltpu.make_async_copy(cot_hbm, cot, sems.at[1])
    fetch_off.start()
    fetch_cot.start()
    fetch_off.wait()
    r = lax.broadcasted_iota(jnp.int32, (clip_rows, clip_rows), 0)
    c = lax.broadcasted_iota(jnp.int32, (clip_rows, clip_rows), 1)
    select = jnp.zeros((clip_rows, clip_rows), jnp.float32)
    for j in range(n):
        src = lax.rem(own - off[0, j] + 2 * n, n)
        for t in range(tile):
            select = jnp.where((c == j * tile + t) & (r == src * tile + t), 1.0, select)
    fetch_cot.wait()
    cot[0:clip_rows, :] = jnp.dot(
        select.astype(jnp.bfloat16), cot[0:clip_rows, :], preferred_element_type=jnp.float32
    ).astype(jnp.bfloat16)
    devices = ((own, partner), (own ^ 1, mate), (own ^ mate, partner), (own ^ partner ^ 1, mate))
    units = cols // HD
    for d, ((device, its_partner), out_ref) in enumerate(zip(devices, outs)):
        rows, first = (all_rows, 0) if d < 2 else (part, low)
        blocks = (device, device ^ 1, device ^ its_partner, device ^ its_partner ^ 1)
        for i, block in enumerate(blocks):
            for u in range(units):
                at = (i * units + u) * rows
                lanes = pl.ds(pl.multiple_of(block * cols + u * HD, HD), HD)
                out_ref[at : at + rows, :] = cot[pl.ds(first, rows), lanes]


def pack_kernel(n, heads, q_hbm, k_hbm, v_hbm, hist_hbm, *refs):
    outs, (q, k, v, hist, sems) = refs[:-5], refs[-5:]
    own = lax.axis_index("tm")
    tok, width = q.shape
    tile = hist.shape[0]
    clip_rows = n * tile
    start = 0 if width == n * HD else pl.multiple_of(((own ^ heads[0]) // 2) * width, width)
    pairs = [(hist_hbm, hist)] + [
        (x.at[:, pl.ds(start, width)], y) for x, y in ((q_hbm, q), (k_hbm, k), (v_hbm, v))
    ]
    copies = [pltpu.make_async_copy(a, b, sems.at[i]) for i, (a, b) in enumerate(pairs)]
    for copy in copies:
        copy.start()
    copies[0].wait()
    for d, out_ref in zip(heads, outs):
        lanes = pl.ds(pl.multiple_of((own ^ d) * HD, HD), HD)
        tiles = hist[:, lanes].astype(jnp.float32)
        row = lax.broadcasted_iota(jnp.int32, (clip_rows, HD), 0)
        placed = jnp.zeros((clip_rows, HD), jnp.float32)
        for t in range(tile):
            placed = jnp.where(row == own * tile + t, tiles[t : t + 1, :], placed)
        out_ref[3 * tok : 3 * tok + clip_rows, :] = placed.astype(jnp.bfloat16)
    for i, x in enumerate((q, k, v)):
        copies[1 + i].wait()
        for d, out_ref in zip(heads, outs):
            lanes = pl.ds(pl.multiple_of((own ^ d) * HD - start, HD), HD)
            out_ref[i * tok : (i + 1) * tok, :] = x[:, lanes]


def attend_kernel(n, tok, order, counts_hbm, *refs):
    parts, (mine_ref, other_ref, x_ref, mixed_ref, counts, sem) = refs[:n], refs[n:]
    copy = pltpu.make_async_copy(counts_hbm, counts, sem)
    copy.start()
    own, side, mate, partner = place()
    for k, part in zip(order, parts):
        x_ref[own ^ k] = part[...]
    copy.wait()
    rate = math.log2(math.e) / math.sqrt(HD)
    token = lax.broadcasted_iota(jnp.int32, (1, tok), 1)
    bias = [
        jnp.where(token < counts[s] * TPF, 0.0, -jnp.inf).astype(jnp.float32) for s in range(n)
    ]
    for block in range(n):
        sources = range(max(0, block - (WINB - 1)), block + 1)
        q = x_ref[block, 0:tok, :]
        scores = [
            lax.dot_general(
                q,
                x_ref[s, tok : 2 * tok, :],
                (((1,), (1,)), ((), ())),
                preferred_element_type=jnp.float32,
            )
            + bias[s]
            for s in sources
        ]
        top = jnp.max(scores[0], axis=1, keepdims=True)
        for s in scores[1:]:
            top = jnp.maximum(top, jnp.max(s, axis=1, keepdims=True))
        weights = [jnp.exp2((s - top) * rate) for s in scores]
        total = jnp.sum(weights[0], axis=1, keepdims=True)
        for w in weights[1:]:
            total = total + jnp.sum(w, axis=1, keepdims=True)
        share = 1.0 / total
        mixed = jnp.zeros((tok, HD), jnp.float32)
        for s, w in zip(sources, weights):
            mixed = mixed + jnp.dot(
                (w * share).astype(jnp.bfloat16),
                x_ref[s, 2 * tok : 3 * tok, :],
                preferred_element_type=jnp.float32,
            )
        mixed_ref[block] = mixed.astype(jnp.bfloat16)
    rows = n // 2 * tok
    clip_rows = mine_ref.shape[0] - rows
    hist = jnp.zeros((clip_rows, HD), jnp.float32)
    for s in range(n):
        hist = hist + x_ref[s, 3 * tok : 3 * tok + clip_rows, :].astype(jnp.float32)
    hist = hist.astype(jnp.bfloat16)
    x, y = lax.rem(own // 2, 2), own // 4
    for flip, out_ref in ((0, mine_ref), (1, other_ref)):
        for p in range(n // 2):
            by_x = 4 * (p // 2) + 2 * (x ^ flip) + p % 2
            by_y = 4 * (y ^ flip) + p
            out_ref[p * tok : (p + 1) * tok, :] = mixed_ref[jnp.where(side == 0, by_x, by_y)]
        out_ref[rows:, :] = hist


def stack_kernel(a_ref, b_ref, behind, out_ref):
    out_ref[0] = a_ref[...]
    out_ref[1] = b_ref[...]


def lay_out(rows, pieces):
    return jnp.concatenate([x[:rows] for x in pieces], axis=1)


def turn_kernel(lo, clip_rows, own_in, core_in, mine_ref, swapped_ref, own_ref, give_ref, whole):
    own, side, mate, partner = place()
    plane = lax.rem(lax.axis_index("head"), 2)
    _, all_rows, width = whole.shape
    tiles = width // HD
    part = all_rows - lo
    for u in range(tiles):
        lanes = slice(u * HD, (u + 1) * HD)
        full = slice(u * all_rows, (u + 1) * all_rows)
        whole[0, :, lanes] = own_in[full, :]
        whole[1, :, lanes] = core_in[full, :]
        for i in range(2):
            a = mine_ref[i, u * part : (u + 1) * part, :]
            b = swapped_ref[i, u * part : (u + 1) * part, :]
            whole[2 + i, 0:lo, lanes] = jnp.where(plane == 0, a, b)[:lo]
            whole[2 + i, lo:all_rows, lanes] = jnp.where(plane == 0, b, a)
    at = lax.rem(own // mate, 2)
    slots = [2 * ((p // 2) ^ at) + ((p % 2) ^ side) for p in range(4)]
    for i, out_ref in enumerate((own_ref, give_ref)):
        lanes = slice(i * width // 2, (i + 1) * width // 2)
        pieces = [whole[s, clip_rows:all_rows, lanes] for s in slots]
        pieces += [whole[s, 0:clip_rows, lanes] for s in slots]
        out_ref[...] = jnp.concatenate(pieces, axis=0).T


def grad_part(turned_ref, head_refs, rows, copies):
    right = jnp.concatenate([x[0:rows, :] for x in head_refs], axis=1)
    hist = jnp.concatenate([x[rows:, :] for x in head_refs], axis=1)
    clip = copies * hist.shape[0]
    out = jnp.dot(turned_ref[:, 0:rows], right, preferred_element_type=jnp.float32)
    return out + jnp.dot(
        turned_ref[:, rows : rows + clip],
        jnp.concatenate([hist] * copies, axis=0),
        preferred_element_type=jnp.float32,
    )


def send_kernel(rows, copies, heads, turned_ref, *refs):
    same_ref, cross_ref = refs[-2:]
    cols = same_ref.shape[0]
    out = grad_part(turned_ref, refs[:heads], rows, copies).astype(jnp.bfloat16)
    same_ref[...] = out[:cols]
    cross_ref[...] = out[cols:]


def keep_kernel(rows, copies, tok, turned_ref, *refs):
    heads, (keep_ref, give_ref) = refs[:-2], refs[-2:]
    own, side, mate, partner = place()
    cols, width = keep_ref.shape
    out = grad_part(turned_ref, heads, rows, copies)
    keep_ref[...] = out[:cols]
    give_ref[0:cols, :] = out[cols:].astype(jnp.bfloat16)
    at = 2 * lax.rem(own // mate, 2) + 1 - side
    for i, x in enumerate(heads):
        give_ref[cols : cols + tok, i * HD : (i + 1) * HD] = x[
            pl.ds(pl.multiple_of(at * tok, tok), tok), :
        ]


def finish_kernel(tok, keep_near, keep_far, same_near, same_far, cross_near, cross_far, core_near, core_far, *refs):
    heads, (att_hbm, out_hbm, total, sems) = refs[:4], refs[4:]
    own, side, mate, partner = place()
    cols = keep_near.shape[0]
    at = 2 * lax.rem(own // mate, 2) + side
    moves = []

    def move(a, b):
        moves.append(pltpu.make_async_copy(a, b, sems.at[len(moves)]))
        moves[-1].start()

    def lanes(head):
        return pl.ds(pl.multiple_of(head * HD, HD), HD)

    def column(near, far, i):
        ref, i = (near, i) if i < 3 else (far, 0)
        return ref[0:cols, i * HD : (i + 1) * HD].astype(jnp.float32)

    mine = [own, own ^ partner, own ^ mate, own ^ 6]
    theirs = [own ^ 1, own ^ 1 ^ mate, own ^ 1 ^ partner, own ^ 7]
    for i, head in enumerate(mine):
        move(heads[i].at[pl.ds(pl.multiple_of(at * tok, tok), tok), :], att_hbm.at[:, lanes(head)])
    for i, head in enumerate(theirs):
        ref, k = (core_near, i) if i < 3 else (core_far, 0)
        move(
            ref.at[pl.ds(cols, tok), pl.ds(k * HD, HD)],
            att_hbm.at[:, lanes(head)],
        )
    there = [1, 0, 3, 2]
    for i, head in enumerate(mine):
        total[i] = column(keep_near, keep_far, i) + column(same_near, same_far, there[i])
        move(total.at[i], out_hbm.at[:, lanes(head)])
    for i, head in enumerate(theirs):
        total[4 + i] = column(core_near, core_far, i) + column(cross_near, cross_far, there[i])
        move(total.at[4 + i], out_hbm.at[:, lanes(head)])
    for x in moves:
        x.wait()


def head_body(query_rows, key_rows, value_rows, frame_counts, history, offsets, cotangent):
    n = lax.axis_size("tm")
    planes = lax.axis_size("head")
    half = n // 2
    tok, width = query_rows.shape
    tile = history.shape[0]
    clip_rows = n * tile
    cot_rows, all_cols = cotangent.shape
    cols = all_cols // n
    units = cols // HD
    lo = cot_rows // 32 * 16
    part = cot_rows - lo
    base = 3 * tok + clip_rows
    length = base
    rows = half * tok
    vmem = pl.BlockSpec(memory_space=pltpu.VMEM)
    hbm = pl.BlockSpec(memory_space=pl.ANY)
    bf16 = jnp.bfloat16

    def swap(x, bit):
        return lax.ppermute(x, "tm", [(i, i ^ bit(i)) for i in range(n)])

    def swap_plane(x):
        return lax.ppermute(x, "head", [(p, p ^ 1) for p in range(planes)])

    def call(
        kernel, name, outs, specs, flops, scratch=(), exps=0, out_spec=vmem, limit=VMEM_LIMIT
    ):
        shapes = [jax.ShapeDtypeStruct(s, d) for s, d in outs]
        moved = 2 * sum(math.prod(s.shape) * s.dtype.itemsize for s in shapes)
        return pl.pallas_call(
            kernel,
            out_shape=tuple(shapes),
            in_specs=specs,
            out_specs=tuple([out_spec] * len(shapes)),
            scratch_shapes=scratch,
            compiler_params=pltpu.CompilerParams(vmem_limit_bytes=limit),
            cost_estimate=pl.CostEstimate(flops=flops, bytes_accessed=moved, transcendentals=exps),
            name=name,
        )

    def pack(heads, lanes, name):
        return call(
            lambda *refs: pack_kernel(n, heads, *refs),
            name,
            [((length, HD), bf16)] * len(heads),
            [hbm] * 4,
            0,
            (
                pltpu.VMEM((tok, lanes), bf16),
                pltpu.VMEM((tok, lanes), bf16),
                pltpu.VMEM((tok, lanes), bf16),
                pltpu.VMEM(history.shape, bf16),
                pltpu.SemaphoreType.DMA((4,)),
            ),
            limit=PACK_LIMIT,
        )(query_rows, key_rows, value_rows, history)

    first, rest = [6, 7], [0, 1, 2, 3, 4, 5]
    packed = dict(zip(first, pack(first, 2 * HD, "pack_first")))
    packed.update(zip(rest, pack(rest, width, "pack_rest")))
    order = [6, 7, 2, 4, 3, 5, 1]
    arrived = {k: swap(packed[k], lambda i: k) for k in order}
    by_head = [packed[0]] + [arrived[k] for k in order]
    tiles = 4 * units
    full, split = ((tiles * cot_rows, HD), bf16), ((tiles * part, HD), bf16)
    cot_own, cot_core, cot_mate, cot_cross = call(
        lambda *refs: cot_kernel(n, tile, lo, *refs),
        "cot",
        [full, full, split, split],
        [hbm] * 4,
        0,
        (
            pltpu.SMEM(offsets.shape, jnp.int32),
            pltpu.VMEM(cotangent.shape, bf16),
            pltpu.SemaphoreType.DMA((2,)),
        ),
    )(offsets, cotangent, arrived[6], arrived[7])
    cot_core = swap(cot_core, lambda i: 1)
    cot_cross = swap(cot_cross, lambda i: sum_bit(i) ^ 1)
    cot_mate = swap(cot_mate, mate_bit)

    pairs = half * tok * WINB * tok
    head_shape = ((rows + clip_rows, HD), bf16)
    mine, others = call(
        lambda *refs: attend_kernel(n, tok, [0] + order, *refs),
        "attend",
        [head_shape, head_shape],
        [hbm] + [vmem] * n,
        8 * pairs * HD,
        (
            pltpu.VMEM((n, length, HD), bf16),
            pltpu.VMEM((n, tok, HD), bf16),
            pltpu.SMEM(frame_counts.shape, jnp.int32),
            pltpu.SemaphoreType.DMA,
        ),
        2 * pairs,
    )(frame_counts, *by_head)
    sum_head, mate_head = swap(others, sum_bit), swap(mine, mate_bit)
    far_head = swap(sum_head, mate_bit)
    (cot_mine,) = call(
        stack_kernel,
        "stack",
        [((2, tiles * part, HD), bf16)],
        [vmem] * 2 + [hbm],
        0,
    )(cot_mate, cot_cross, mine)
    cot_swapped = swap_plane(cot_mine)

    turned_own, turned_give = call(
        lambda *refs: turn_kernel(lo, clip_rows, *refs),
        "turn",
        [((2 * cols, half * cot_rows), bf16)] * 2,
        [vmem] * 4,
        0,
        (pltpu.VMEM((4, cot_rows, tiles * HD), bf16),),
    )(cot_own, cot_core, cot_mine, cot_swapped)

    def share(heads, name, *behind):
        lanes = len(heads) * HD
        flops = 4 * cols * half * cot_rows * lanes
        same, cross = call(
            lambda *refs: send_kernel(rows, half, len(heads), *refs),
            "send_" + name,
            [((cols, lanes), bf16)] * 2,
            [vmem] * (1 + len(heads)) + [hbm] * len(behind),
            flops,
        )(turned_give, *heads, *behind)
        same, cross = swap(same, sum_bit), swap(cross, lambda i: sum_bit(i) ^ 1)
        keep, give = call(
            lambda *refs: keep_kernel(rows, half, tok, *refs),
            "keep_" + name,
            [((cols, lanes), jnp.float32), ((cols + tok, lanes), bf16)],
            [vmem] * (1 + len(heads)),
            flops,
        )(turned_own, *heads)
        return keep, same, cross, swap(give, lambda i: 1)

    near, far = [mine, sum_head, mate_head], [far_head]
    near_sums = share(near, "near")
    far_sums = share(far, "far", near_sums[3])
    sums = [x for pair in zip(near_sums, far_sums) for x in pair]
    return call(
        lambda *refs: finish_kernel(tok, *refs),
        "finish",
        [((tok, width), bf16), ((cols, width), jnp.float32)],
        [vmem] * 12,
        0,
        (pltpu.VMEM((n, cols, HD), jnp.float32), pltpu.SemaphoreType.DMA((2 * n,))),
        out_spec=hbm,
    )(*sums, *near, *far)


def body(query_rows, key_rows, value_rows, frame_counts, history, offsets, cotangent):
    n = lax.axis_size("tm")
    tok, width = query_rows.shape
    by_heads = (
        n == 8
        and lax.axis_size("head") % 2 == 0
        and width == n * HD
        and offsets.shape[1] == n
        and cotangent.shape[0] == tok + n * history.shape[0]
        and cotangent.shape[1] % (n * HD) == 0
        and tok % 16 == 0
        and (n * history.shape[0]) % 16 == 0
    )
    plan = head_body if by_heads else window_body
    return plan(query_rows, key_rows, value_rows, frame_counts, history, offsets, cotangent)


def solution(mesh):
    in_specs = (
        P("tm", "head"),
        P("tm", "head"),
        P("tm", "head"),
        P(),
        P("tm", "head"),
        P("tm", None),
        P("tm", None),
    )
    out_specs = (P("tm", "head"), P("tm", "head"))
    return jax.shard_map(body, mesh=mesh, in_specs=in_specs, out_specs=out_specs, check_vma=False)
```

```python
import math

import jax
import jax.numpy as jnp
from jax import lax
from jax.experimental import pallas as pl
from jax.experimental.pallas import tpu as pltpu
from jax.sharding import PartitionSpec as P

HD = 128
TPF = 64
WINB = 4
VMEM_LIMIT = 24 * 1024 * 1024
PACK_LIMIT = 58 * 1024 * 1024


def from_behind(x, axis, by):
    devices = lax.axis_size(axis)
    pairs = [(i, i + by) for i in range(devices) if 0 <= i + by < devices]
    return lax.ppermute(x, axis, pairs)


def window_body(query_rows, key_rows, value_rows, frame_counts, history, offsets, cotangent):
    tok_rows, feat_width = query_rows.shape
    local_heads = feat_width // HD
    block_total = lax.axis_size("tm")
    own_block = lax.axis_index("tm")
    score_scale = 1.0 / math.sqrt(HD)
    key_value = jnp.stack([key_rows, value_rows])
    pieces = []
    for distance in range(WINB - 1, 0, -1):
        pieces.append(from_behind(key_value, "tm", distance))
    window = jnp.concatenate(pieces + [key_value], axis=1)
    source_block = own_block - (WINB - 1) + jnp.arange(WINB, dtype=jnp.int32)
    block_match = jnp.arange(block_total, dtype=jnp.int32)[None, :] == source_block[:, None]
    block_count = jnp.sum(jnp.where(block_match, frame_counts[None, :], 0), axis=1)
    frame_index = jnp.arange(tok_rows, dtype=jnp.int32) // TPF
    kept_mask = (
        (source_block[:, None] >= 0) & (frame_index[None, :] < block_count[:, None])
    ).reshape(WINB * tok_rows)
    key_window = window[0].reshape(WINB * tok_rows, local_heads, HD)
    value_window = window[1].reshape(WINB * tok_rows, local_heads, HD)
    query_heads = query_rows.reshape(tok_rows, local_heads, HD)
    scores = (
        jnp.einsum("qhd,khd->hqk", query_heads, key_window, preferred_element_type=jnp.float32)
        * score_scale
    )
    scores = jnp.where(kept_mask[None, None, :], scores, -jnp.inf)
    row_max = jnp.max(scores, axis=-1, keepdims=True)
    weights = jnp.exp(scores - row_max)
    probs = (weights / jnp.sum(weights, axis=-1, keepdims=True)).astype(jnp.bfloat16)
    mixed = jnp.einsum("hqk,khd->qhd", probs, value_window, preferred_element_type=jnp.float32)
    attended = mixed.astype(jnp.bfloat16).reshape(tok_rows, feat_width)
    tile_rows = history.shape[0]
    source_tile = (own_block - offsets[0]) % block_total
    source_row = (
        source_tile[:, None] * tile_rows + jnp.arange(tile_rows, dtype=jnp.int32)[None, :]
    ).reshape(-1)
    incoming = lax.all_gather(history, "tm", axis=0, tiled=True)
    piece_rows = incoming.shape[0]
    selector = (source_row[:, None] == jnp.arange(piece_rows, dtype=jnp.int32)[None, :]).astype(
        jnp.bfloat16
    )
    clip_hist = jnp.dot(selector, incoming, preferred_element_type=jnp.float32).astype(jnp.bfloat16)
    disc_clip = jnp.concatenate([clip_hist, attended], axis=0)
    disc_grad = lax.psum_scatter(
        lax.dot_general(
            cotangent, disc_clip, (((0,), (0,)), ((), ())), preferred_element_type=jnp.float32
        ),
        "tm",
        scatter_dimension=0,
        tiled=True,
    )
    return (attended, disc_grad)


def mate_bit(i):
    return 4 >> (i % 2)


def sum_bit(i):
    return 2 << (i % 2)


def place():
    own = lax.axis_index("tm")
    side = lax.rem(own, 2)
    return own, side, jnp.where(side == 0, 4, 2), jnp.where(side == 0, 2, 4)


def cot_kernel(n, tile, lo, off_hbm, cot_hbm, *refs):
    outs, (off, cot, sems) = refs[-7:-3], refs[-3:]
    own, side, mate, partner = place()
    plane = lax.rem(lax.axis_index("head"), 2)
    clip_rows = n * tile
    all_rows, all_cols = cot.shape
    cols = all_cols // n
    part = all_rows - lo
    low = pl.multiple_of(plane * lo, 16)
    fetch_off = pltpu.make_async_copy(off_hbm, off, sems.at[0])
    fetch_cot = pltpu.make_async_copy(cot_hbm, cot, sems.at[1])
    fetch_off.start()
    fetch_cot.start()
    fetch_off.wait()
    r = lax.broadcasted_iota(jnp.int32, (clip_rows, clip_rows), 0)
    c = lax.broadcasted_iota(jnp.int32, (clip_rows, clip_rows), 1)
    select = jnp.zeros((clip_rows, clip_rows), jnp.float32)
    for j in range(n):
        src = lax.rem(own - off[0, j] + 2 * n, n)
        for t in range(tile):
            select = jnp.where((c == j * tile + t) & (r == src * tile + t), 1.0, select)
    fetch_cot.wait()
    cot[0:clip_rows, :] = jnp.dot(
        select.astype(jnp.bfloat16), cot[0:clip_rows, :], preferred_element_type=jnp.float32
    ).astype(jnp.bfloat16)
    devices = ((own, partner), (own ^ 1, mate), (own ^ mate, partner), (own ^ partner ^ 1, mate))
    units = cols // HD
    for d, ((device, its_partner), out_ref) in enumerate(zip(devices, outs)):
        rows, first = (all_rows, 0) if d < 2 else (part, low)
        blocks = (device, device ^ 1, device ^ its_partner, device ^ its_partner ^ 1)
        for i, block in enumerate(blocks):
            for u in range(units):
                at = (i * units + u) * rows
                lanes = pl.ds(pl.multiple_of(block * cols + u * HD, HD), HD)
                out_ref[at : at + rows, :] = cot[pl.ds(first, rows), lanes]


def pack_kernel(n, heads, q_hbm, k_hbm, v_hbm, hist_hbm, *refs):
    outs, (q, k, v, hist, sems) = refs[:-5], refs[-5:]
    own = lax.axis_index("tm")
    tok, width = q.shape
    tile = hist.shape[0]
    clip_rows = n * tile
    start = 0 if width == n * HD else pl.multiple_of(((own ^ heads[0]) // 2) * width, width)
    pairs = [(hist_hbm, hist)] + [
        (x.at[:, pl.ds(start, width)], y) for x, y in ((q_hbm, q), (k_hbm, k), (v_hbm, v))
    ]
    copies = [pltpu.make_async_copy(a, b, sems.at[i]) for i, (a, b) in enumerate(pairs)]
    for copy in copies:
        copy.start()
    copies[0].wait()
    for d, out_ref in zip(heads, outs):
        lanes = pl.ds(pl.multiple_of((own ^ d) * HD, HD), HD)
        tiles = hist[:, lanes].astype(jnp.float32)
        row = lax.broadcasted_iota(jnp.int32, (clip_rows, HD), 0)
        placed = jnp.zeros((clip_rows, HD), jnp.float32)
        for t in range(tile):
            placed = jnp.where(row == own * tile + t, tiles[t : t + 1, :], placed)
        out_ref[3 * tok : 3 * tok + clip_rows, :] = placed.astype(jnp.bfloat16)
    for i, x in enumerate((q, k, v)):
        copies[1 + i].wait()
        for d, out_ref in zip(heads, outs):
            lanes = pl.ds(pl.multiple_of((own ^ d) * HD - start, HD), HD)
            out_ref[i * tok : (i + 1) * tok, :] = x[:, lanes]


def attend_kernel(n, tok, order, counts_hbm, *refs):
    parts, (mine_ref, other_ref, x_ref, mixed_ref, counts, sem) = refs[:n], refs[n:]
    copy = pltpu.make_async_copy(counts_hbm, counts, sem)
    copy.start()
    own, side, mate, partner = place()
    for k, part in zip(order, parts):
        x_ref[own ^ k] = part[...]
    copy.wait()
    rate = math.log2(math.e) / math.sqrt(HD)
    token = lax.broadcasted_iota(jnp.int32, (1, tok), 1)
    bias = [
        jnp.where(token < counts[s] * TPF, 0.0, -jnp.inf).astype(jnp.float32) for s in range(n)
    ]
    for block in range(n):
        sources = range(max(0, block - (WINB - 1)), block + 1)
        q = x_ref[block, 0:tok, :]
        scores = [
            lax.dot_general(
                q,
                x_ref[s, tok : 2 * tok, :],
                (((1,), (1,)), ((), ())),
                preferred_element_type=jnp.float32,
            )
            + bias[s]
            for s in sources
        ]
        top = jnp.max(scores[0], axis=1, keepdims=True)
        for s in scores[1:]:
            top = jnp.maximum(top, jnp.max(s, axis=1, keepdims=True))
        weights = [jnp.exp2((s - top) * rate) for s in scores]
        total = jnp.sum(weights[0], axis=1, keepdims=True)
        for w in weights[1:]:
            total = total + jnp.sum(w, axis=1, keepdims=True)
        share = 1.0 / total
        mixed = jnp.zeros((tok, HD), jnp.float32)
        for s, w in zip(sources, weights):
            mixed = mixed + jnp.dot(
                (w * share).astype(jnp.bfloat16),
                x_ref[s, 2 * tok : 3 * tok, :],
                preferred_element_type=jnp.float32,
            )
        mixed_ref[block] = mixed.astype(jnp.bfloat16)
    rows = n // 2 * tok
    clip_rows = mine_ref.shape[0] - rows
    hist = jnp.zeros((clip_rows, HD), jnp.float32)
    for s in range(n):
        hist = hist + x_ref[s, 3 * tok : 3 * tok + clip_rows, :].astype(jnp.float32)
    hist = hist.astype(jnp.bfloat16)
    x, y = lax.rem(own // 2, 2), own // 4
    for flip, out_ref in ((0, mine_ref), (1, other_ref)):
        for p in range(n // 2):
            by_x = 4 * (p // 2) + 2 * (x ^ flip) + p % 2
            by_y = 4 * (y ^ flip) + p
            out_ref[p * tok : (p + 1) * tok, :] = mixed_ref[jnp.where(side == 0, by_x, by_y)]
        out_ref[rows:, :] = hist


def stack_kernel(tiles, lo, a_ref, b_ref, behind, out_ref):
    plane = lax.rem(lax.axis_index("head"), 2)
    part = a_ref.shape[0] // tiles
    for i, ref in enumerate((a_ref, b_ref)):
        for u in range(tiles):
            first = pl.multiple_of(u * part + plane * (part - lo), 16)
            out_ref[i, u * lo : (u + 1) * lo, :] = ref[pl.ds(first, lo), :]


def turn_kernel(lo, clip_rows, own_in, core_in, mate_in, cross_in, swapped_ref, own_ref, give_ref, whole):
    own, side, mate, partner = place()
    plane = lax.rem(lax.axis_index("head"), 2)
    _, all_rows, width = whole.shape
    tiles = width // HD
    part = all_rows - lo
    for u in range(tiles):
        lanes = slice(u * HD, (u + 1) * HD)
        full = slice(u * all_rows, (u + 1) * all_rows)
        whole[0, :, lanes] = own_in[full, :]
        whole[1, :, lanes] = core_in[full, :]
        for i, ref in enumerate((mate_in, cross_in)):
            a = ref[u * part : (u + 1) * part, :]
            b = swapped_ref[i, u * lo : (u + 1) * lo, :]
            whole[2 + i, 0:lo, lanes] = jnp.where(plane == 0, a[:lo], b)
            whole[2 + i, lo:part, lanes] = jnp.where(plane == 0, a[lo:], a[: part - lo])
            whole[2 + i, part:all_rows, lanes] = jnp.where(plane == 0, b, a[part - lo :])
    at = lax.rem(own // mate, 2)
    slots = [2 * ((p // 2) ^ at) + ((p % 2) ^ side) for p in range(4)]
    for i, out_ref in enumerate((own_ref, give_ref)):
        lanes = slice(i * width // 2, (i + 1) * width // 2)
        pieces = [whole[s, clip_rows:all_rows, lanes] for s in slots]
        pieces += [whole[s, 0:clip_rows, lanes] for s in slots]
        out_ref[...] = jnp.concatenate(pieces, axis=0).T


def grad_part(turned_ref, head_refs, rows, copies):
    right = jnp.concatenate([x[0:rows, :] for x in head_refs], axis=1)
    hist = jnp.concatenate([x[rows:, :] for x in head_refs], axis=1)
    clip = copies * hist.shape[0]
    out = jnp.dot(turned_ref[:, 0:rows], right, preferred_element_type=jnp.float32)
    return out + jnp.dot(
        turned_ref[:, rows : rows + clip],
        jnp.concatenate([hist] * copies, axis=0),
        preferred_element_type=jnp.float32,
    )


def send_kernel(rows, copies, heads, turned_ref, *refs):
    same_ref, cross_ref = refs[-2:]
    cols = same_ref.shape[0]
    out = grad_part(turned_ref, refs[:heads], rows, copies).astype(jnp.bfloat16)
    same_ref[...] = out[:cols]
    cross_ref[...] = out[cols:]


def keep_kernel(rows, copies, tok, before, n, turned_ref, *refs):
    heads, (keep_ref, give_ref) = refs[before : before + n], refs[-2:]
    own, side, mate, partner = place()
    cols, width = keep_ref.shape
    start = give_ref.shape[1] - width
    if before:
        give_ref[:, 0:start] = refs[0][...]
    out = grad_part(turned_ref, heads, rows, copies)
    keep_ref[...] = out[:cols]
    give_ref[0:cols, start:] = out[cols:].astype(jnp.bfloat16)
    at = 2 * lax.rem(own // mate, 2) + 1 - side
    for i, x in enumerate(heads):
        give_ref[cols : cols + tok, start + i * HD : start + (i + 1) * HD] = x[
            pl.ds(pl.multiple_of(at * tok, tok), tok), :
        ]


def finish_kernel(tok, keep_near, keep_far, same_near, same_far, cross_near, cross_far, core, *refs):
    heads, (att_hbm, out_hbm, total, sems) = refs[:4], refs[4:]
    own, side, mate, partner = place()
    cols = keep_near.shape[0]
    at = 2 * lax.rem(own // mate, 2) + side
    moves = []

    def move(a, b):
        moves.append(pltpu.make_async_copy(a, b, sems.at[len(moves)]))
        moves[-1].start()

    def lanes(head):
        return pl.ds(pl.multiple_of(head * HD, HD), HD)

    def column(near, far, i):
        ref, i = (far, 0) if i == 3 and far is not near else (near, i)
        return ref[0:cols, i * HD : (i + 1) * HD].astype(jnp.float32)

    mine = [own, own ^ partner, own ^ mate, own ^ 6]
    theirs = [own ^ 1, own ^ 1 ^ mate, own ^ 1 ^ partner, own ^ 7]
    for i, head in enumerate(mine):
        move(heads[i].at[pl.ds(pl.multiple_of(at * tok, tok), tok), :], att_hbm.at[:, lanes(head)])
    for i, head in enumerate(theirs):
        move(core.at[pl.ds(cols, tok), pl.ds(i * HD, HD)], att_hbm.at[:, lanes(head)])
    there = [1, 0, 3, 2]
    for i, head in enumerate(mine):
        total[i] = column(keep_near, keep_far, i) + column(same_near, same_far, there[i])
        move(total.at[i], out_hbm.at[:, lanes(head)])
    for i, head in enumerate(theirs):
        total[4 + i] = column(core, core, i) + column(cross_near, cross_far, there[i])
        move(total.at[4 + i], out_hbm.at[:, lanes(head)])
    for x in moves:
        x.wait()


def head_body(query_rows, key_rows, value_rows, frame_counts, history, offsets, cotangent):
    n = lax.axis_size("tm")
    planes = lax.axis_size("head")
    half = n // 2
    tok, width = query_rows.shape
    tile = history.shape[0]
    clip_rows = n * tile
    cot_rows, all_cols = cotangent.shape
    cols = all_cols // n
    units = cols // HD
    lo = cot_rows // 64 * 16
    part = cot_rows - lo
    base = 3 * tok + clip_rows
    length = base
    rows = half * tok
    vmem = pl.BlockSpec(memory_space=pltpu.VMEM)
    hbm = pl.BlockSpec(memory_space=pl.ANY)
    bf16 = jnp.bfloat16

    def swap(x, bit):
        return lax.ppermute(x, "tm", [(i, i ^ bit(i)) for i in range(n)])

    def swap_plane(x):
        return lax.ppermute(x, "head", [(p, p ^ 1) for p in range(planes)])

    def call(
        kernel, name, outs, specs, flops, scratch=(), exps=0, out_spec=vmem, limit=VMEM_LIMIT
    ):
        shapes = [jax.ShapeDtypeStruct(s, d) for s, d in outs]
        moved = 2 * sum(math.prod(s.shape) * s.dtype.itemsize for s in shapes)
        return pl.pallas_call(
            kernel,
            out_shape=tuple(shapes),
            in_specs=specs,
            out_specs=tuple([out_spec] * len(shapes)),
            scratch_shapes=scratch,
            compiler_params=pltpu.CompilerParams(vmem_limit_bytes=limit),
            cost_estimate=pl.CostEstimate(flops=flops, bytes_accessed=moved if flops else 0, transcendentals=exps),
            name=name,
        )

    def pack(heads, lanes, name):
        return call(
            lambda *refs: pack_kernel(n, heads, *refs),
            name,
            [((length, HD), bf16)] * len(heads),
            [hbm] * 4,
            0,
            (
                pltpu.VMEM((tok, lanes), bf16),
                pltpu.VMEM((tok, lanes), bf16),
                pltpu.VMEM((tok, lanes), bf16),
                pltpu.VMEM(history.shape, bf16),
                pltpu.SemaphoreType.DMA((4,)),
            ),
            limit=PACK_LIMIT,
        )(query_rows, key_rows, value_rows, history)

    first, rest = [6, 7], [0, 1, 2, 3, 4, 5]
    packed = dict(zip(first, pack(first, 2 * HD, "pack_first")))
    packed.update(zip(rest, pack(rest, width, "pack_rest")))
    order = [6, 7, 2, 4, 3, 5, 1]
    arrived = {k: swap(packed[k], lambda i: k) for k in order}
    by_head = [packed[0]] + [arrived[k] for k in order]
    tiles = 4 * units
    full, split = ((tiles * cot_rows, HD), bf16), ((tiles * part, HD), bf16)
    cot_own, cot_core, cot_mate, cot_cross = call(
        lambda *refs: cot_kernel(n, tile, lo, *refs),
        "cot",
        [full, full, split, split],
        [hbm] * 4,
        0,
        (
            pltpu.SMEM(offsets.shape, jnp.int32),
            pltpu.VMEM(cotangent.shape, bf16),
            pltpu.SemaphoreType.DMA((2,)),
        ),
    )(offsets, cotangent, arrived[6], arrived[7])
    cot_core = swap(cot_core, lambda i: 1)
    cot_cross = swap(cot_cross, lambda i: sum_bit(i) ^ 1)
    cot_mate = swap(cot_mate, mate_bit)

    pairs = half * tok * WINB * tok
    head_shape = ((rows + clip_rows, HD), bf16)
    mine, others = call(
        lambda *refs: attend_kernel(n, tok, [0] + order, *refs),
        "attend",
        [head_shape, head_shape],
        [hbm] + [vmem] * n,
        8 * pairs * HD,
        (
            pltpu.VMEM((n, length, HD), bf16),
            pltpu.VMEM((n, tok, HD), bf16),
            pltpu.SMEM(frame_counts.shape, jnp.int32),
            pltpu.SemaphoreType.DMA,
        ),
        2 * pairs,
    )(frame_counts, *by_head)
    sum_head, mate_head = swap(others, sum_bit), swap(mine, mate_bit)
    far_head = swap(sum_head, mate_bit)
    (cot_rest,) = call(
        lambda *refs: stack_kernel(tiles, lo, *refs),
        "stack",
        [((2, tiles * lo, HD), bf16)],
        [vmem] * 2 + [hbm],
        0,
    )(cot_mate, cot_cross, mine)
    cot_swapped = swap_plane(cot_rest)

    turned_own, turned_give = call(
        lambda *refs: turn_kernel(lo, clip_rows, *refs),
        "turn",
        [((2 * cols, half * cot_rows), bf16)] * 2,
        [vmem] * 5,
        0,
        (pltpu.VMEM((4, cot_rows, tiles * HD), bf16),),
    )(cot_own, cot_core, cot_mate, cot_cross, cot_swapped)

    def send(heads, name):
        lanes = len(heads) * HD
        same, cross = call(
            lambda *refs: send_kernel(rows, half, len(heads), *refs),
            "send_" + name,
            [((cols, lanes), bf16)] * 2,
            [vmem] * (1 + len(heads)),
            0,
        )(turned_give, *heads)
        return same, swap(same, sum_bit), swap(cross, lambda i: sum_bit(i) ^ 1)

    def keep(heads, name, behind, *before):
        lanes = len(heads) * HD
        given = lanes + sum(x.shape[1] for x in before)
        return call(
            lambda *refs: keep_kernel(rows, half, tok, len(before), len(heads), *refs),
            "keep_" + name,
            [((cols, lanes), jnp.float32), ((cols + tok, given), bf16)],
            [vmem] * (1 + len(before) + len(heads)) + [hbm] * len(behind),
            0,
        )(turned_own, *before, *heads, *behind)

    near, far = [mine, sum_head, mate_head], [far_head]
    sent, same_near, cross_near = send(near, "near")
    keep_near, give_near = keep(near, "near", [sent])
    sent, same_far, cross_far = send(far, "far")
    keep_far, give = keep(far, "far", [same_near, cross_near], give_near)
    core = swap(give, lambda i: 1)
    sums = (keep_near, keep_far, same_near, same_far, cross_near, cross_far, core)
    return call(
        lambda *refs: finish_kernel(tok, *refs),
        "finish",
        [((tok, width), bf16), ((cols, width), jnp.float32)],
        [vmem] * 11,
        0,
        (pltpu.VMEM((n, cols, HD), jnp.float32), pltpu.SemaphoreType.DMA((2 * n,))),
        out_spec=hbm,
    )(*sums, *near, *far)


def body(query_rows, key_rows, value_rows, frame_counts, history, offsets, cotangent):
    n = lax.axis_size("tm")
    tok, width = query_rows.shape
    by_heads = (
        n == 8
        and lax.axis_size("head") % 2 == 0
        and width == n * HD
        and offsets.shape[1] == n
        and cotangent.shape[0] == tok + n * history.shape[0]
        and cotangent.shape[1] % (n * HD) == 0
        and tok % 16 == 0
        and (n * history.shape[0]) % 16 == 0
    )
    plan = head_body if by_heads else window_body
    return plan(query_rows, key_rows, value_rows, frame_counts, history, offsets, cotangent)


def solution(mesh):
    in_specs = (
        P("tm", "head"),
        P("tm", "head"),
        P("tm", "head"),
        P(),
        P("tm", "head"),
        P("tm", None),
        P("tm", None),
    )
    out_specs = (P("tm", "head"), P("tm", "head"))
    return jax.shard_map(body, mesh=mesh, in_specs=in_specs, out_specs=out_specs, check_vma=False)
```

```python
import math

import jax
import jax.numpy as jnp
from jax import lax
from jax.experimental import pallas as pl
from jax.experimental.pallas import tpu as pltpu
from jax.sharding import PartitionSpec as P

HD = 128
TPF = 64
WINB = 4
VMEM_LIMIT = 24 * 1024 * 1024
PACK_LIMIT = 58 * 1024 * 1024


def from_behind(x, axis, by):
    devices = lax.axis_size(axis)
    pairs = [(i, i + by) for i in range(devices) if 0 <= i + by < devices]
    return lax.ppermute(x, axis, pairs)


def window_body(query_rows, key_rows, value_rows, frame_counts, history, offsets, cotangent):
    tok_rows, feat_width = query_rows.shape
    local_heads = feat_width // HD
    block_total = lax.axis_size("tm")
    own_block = lax.axis_index("tm")
    score_scale = 1.0 / math.sqrt(HD)
    key_value = jnp.stack([key_rows, value_rows])
    pieces = []
    for distance in range(WINB - 1, 0, -1):
        pieces.append(from_behind(key_value, "tm", distance))
    window = jnp.concatenate(pieces + [key_value], axis=1)
    source_block = own_block - (WINB - 1) + jnp.arange(WINB, dtype=jnp.int32)
    block_match = jnp.arange(block_total, dtype=jnp.int32)[None, :] == source_block[:, None]
    block_count = jnp.sum(jnp.where(block_match, frame_counts[None, :], 0), axis=1)
    frame_index = jnp.arange(tok_rows, dtype=jnp.int32) // TPF
    kept_mask = (
        (source_block[:, None] >= 0) & (frame_index[None, :] < block_count[:, None])
    ).reshape(WINB * tok_rows)
    key_window = window[0].reshape(WINB * tok_rows, local_heads, HD)
    value_window = window[1].reshape(WINB * tok_rows, local_heads, HD)
    query_heads = query_rows.reshape(tok_rows, local_heads, HD)
    scores = (
        jnp.einsum("qhd,khd->hqk", query_heads, key_window, preferred_element_type=jnp.float32)
        * score_scale
    )
    scores = jnp.where(kept_mask[None, None, :], scores, -jnp.inf)
    row_max = jnp.max(scores, axis=-1, keepdims=True)
    weights = jnp.exp(scores - row_max)
    probs = (weights / jnp.sum(weights, axis=-1, keepdims=True)).astype(jnp.bfloat16)
    mixed = jnp.einsum("hqk,khd->qhd", probs, value_window, preferred_element_type=jnp.float32)
    attended = mixed.astype(jnp.bfloat16).reshape(tok_rows, feat_width)
    tile_rows = history.shape[0]
    source_tile = (own_block - offsets[0]) % block_total
    source_row = (
        source_tile[:, None] * tile_rows + jnp.arange(tile_rows, dtype=jnp.int32)[None, :]
    ).reshape(-1)
    incoming = lax.all_gather(history, "tm", axis=0, tiled=True)
    piece_rows = incoming.shape[0]
    selector = (source_row[:, None] == jnp.arange(piece_rows, dtype=jnp.int32)[None, :]).astype(
        jnp.bfloat16
    )
    clip_hist = jnp.dot(selector, incoming, preferred_element_type=jnp.float32).astype(jnp.bfloat16)
    disc_clip = jnp.concatenate([clip_hist, attended], axis=0)
    disc_grad = lax.psum_scatter(
        lax.dot_general(
            cotangent, disc_clip, (((0,), (0,)), ((), ())), preferred_element_type=jnp.float32
        ),
        "tm",
        scatter_dimension=0,
        tiled=True,
    )
    return (attended, disc_grad)


def cot_kernel(n, tile, lo, off_hbm, cot_hbm, *refs):
    outs, (off, cot, sems) = refs[-3 - n // 2 : -3], refs[-3:]
    own = lax.axis_index("tm")
    chip, side = own // 2, lax.rem(own, 2)
    plane = lax.rem(lax.axis_index("head"), 2)
    clip_rows = n * tile
    all_rows, all_cols = cot.shape
    cols = all_cols // n
    part = all_rows - lo
    low = pl.multiple_of(plane * lo, 16)
    fetch_off = pltpu.make_async_copy(off_hbm, off, sems.at[0])
    fetch_cot = pltpu.make_async_copy(cot_hbm, cot, sems.at[1])
    fetch_off.start()
    fetch_cot.start()
    fetch_off.wait()
    r = lax.broadcasted_iota(jnp.int32, (clip_rows, clip_rows), 0)
    c = lax.broadcasted_iota(jnp.int32, (clip_rows, clip_rows), 1)
    select = jnp.zeros((clip_rows, clip_rows), jnp.float32)
    for j in range(n):
        src = lax.rem(own - off[0, j] + 2 * n, n)
        for t in range(tile):
            select = jnp.where((c == j * tile + t) & (r == src * tile + t), 1.0, select)
    fetch_cot.wait()
    cot[0:clip_rows, :] = jnp.dot(
        select.astype(jnp.bfloat16), cot[0:clip_rows, :], preferred_element_type=jnp.float32
    ).astype(jnp.bfloat16)
    units = cols // HD
    for m, out_ref in enumerate(outs):
        rows, first = (part, low) if m else (all_rows, 0)
        for i, block in enumerate((2 * (chip ^ m) + side, 2 * (chip ^ m) + 1 - side)):
            for u in range(units):
                at = (i * units + u) * rows
                lanes = pl.ds(pl.multiple_of(block * cols + u * HD, HD), HD)
                out_ref[at : at + rows, :] = cot[pl.ds(first, rows), lanes]


def pack_kernel(n, heads, q_hbm, k_hbm, v_hbm, hist_hbm, *refs):
    outs, (q, k, v, hist, sems) = refs[:-5], refs[-5:]
    own = lax.axis_index("tm")
    tok, width = q.shape
    tile = hist.shape[0]
    clip_rows = n * tile
    start = 0 if width == n * HD else pl.multiple_of(((own ^ heads[0]) // 2) * width, width)
    pairs = [(hist_hbm, hist)] + [
        (x.at[:, pl.ds(start, width)], y) for x, y in ((q_hbm, q), (k_hbm, k), (v_hbm, v))
    ]
    copies = [pltpu.make_async_copy(a, b, sems.at[i]) for i, (a, b) in enumerate(pairs)]
    for copy in copies:
        copy.start()
    copies[0].wait()
    for d, out_ref in zip(heads, outs):
        lanes = pl.ds(pl.multiple_of((own ^ d) * HD, HD), HD)
        tiles = hist[:, lanes].astype(jnp.float32)
        row = lax.broadcasted_iota(jnp.int32, (clip_rows, HD), 0)
        placed = jnp.zeros((clip_rows, HD), jnp.float32)
        for t in range(tile):
            placed = jnp.where(row == own * tile + t, tiles[t : t + 1, :], placed)
        out_ref[3 * tok : 3 * tok + clip_rows, :] = placed.astype(jnp.bfloat16)
    for i, x in enumerate((q, k, v)):
        copies[1 + i].wait()
        for d, out_ref in zip(heads, outs):
            lanes = pl.ds(pl.multiple_of((own ^ d) * HD - start, HD), HD)
            out_ref[i * tok : (i + 1) * tok, :] = x[:, lanes]


def attend_blocks(n, tok, parity, counts, x_ref, out_ref):
    rate = math.log2(math.e) / math.sqrt(HD)
    token = lax.broadcasted_iota(jnp.int32, (1, tok), 1)
    for i in range(n // 2):
        block = 2 * i + parity
        keys = min(WINB, 2 * i + 2)
        sources = [block - (keys - 1) + k for k in range(keys)]
        q = x_ref[block, 0:tok, :]
        scores = []
        for s in sources:
            at = jnp.maximum(s, 0)
            kept = jnp.where(s >= 0, counts[at], 0) * TPF
            scores.append(
                lax.dot_general(
                    q,
                    x_ref[at, tok : 2 * tok, :],
                    (((1,), (1,)), ((), ())),
                    preferred_element_type=jnp.float32,
                )
                + jnp.where(token < kept, 0.0, -jnp.inf).astype(jnp.float32)
            )
        top = jnp.max(scores[0], axis=1, keepdims=True)
        for s in scores[1:]:
            top = jnp.maximum(top, jnp.max(s, axis=1, keepdims=True))
        weights = [jnp.exp2((s - top) * rate) for s in scores]
        total = jnp.sum(weights[0], axis=1, keepdims=True)
        for w in weights[1:]:
            total = total + jnp.sum(w, axis=1, keepdims=True)
        share = 1.0 / total
        mixed = jnp.zeros((tok, HD), jnp.float32)
        for s, w in zip(sources, weights):
            mixed = mixed + jnp.dot(
                (w * share).astype(jnp.bfloat16),
                x_ref[jnp.maximum(s, 0), 2 * tok : 3 * tok, :],
                preferred_element_type=jnp.float32,
            )
        out_ref[i * tok : (i + 1) * tok, :] = mixed.astype(jnp.bfloat16)
    rows = n // 2 * tok
    clip_rows = out_ref.shape[0] - rows
    hist = jnp.zeros((clip_rows, HD), jnp.float32)
    for s in range(n):
        hist = hist + x_ref[s, 3 * tok : 3 * tok + clip_rows, :].astype(jnp.float32)
    out_ref[rows:, :] = hist.astype(jnp.bfloat16)


def attend_kernel(n, tok, order, counts_hbm, *refs):
    parts, (same_ref, cross_ref, x_ref, counts, sem) = refs[:n], refs[n:]
    copy = pltpu.make_async_copy(counts_hbm, counts, sem)
    copy.start()
    own = lax.axis_index("tm")
    side = lax.rem(own, 2)
    for k, part in zip(order, parts):
        x_ref[own ^ k] = part[...]
    copy.wait()
    attend_blocks(n, tok, side, counts, x_ref, same_ref)
    attend_blocks(n, tok, 1 - side, counts, x_ref, cross_ref)


def stack_kernel(order, lo, tiles, *refs):
    out_ref = refs[-1]
    plane = lax.rem(lax.axis_index("head"), 2)
    for m, ref in zip(order, refs):
        part = ref.shape[0] // tiles
        for u in range(tiles):
            first = pl.multiple_of(u * part + plane * (part - lo), 16)
            out_ref[m - 1, u * lo : (u + 1) * lo, :] = ref[pl.ds(first, lo), :]


def late_kernel(x_ref, *refs):
    refs[-1][...] = x_ref[...]


def turn_kernel(lo, clip_rows, order, own_in, *refs):
    pieces, (swapped_ref, own_ref, other_ref, whole) = refs[:-4], refs[-4:]
    plane = lax.rem(lax.axis_index("head"), 2)
    chip = lax.axis_index("tm") // 2
    chips, all_rows, width = whole.shape
    part = all_rows - lo
    for u in range(width // HD):
        lanes = slice(u * HD, (u + 1) * HD)
        whole[0, :, lanes] = own_in[u * all_rows : (u + 1) * all_rows, :]
        for m, ref in zip(order, pieces):
            a = ref[u * part : (u + 1) * part, :]
            b = swapped_ref[m - 1, u * lo : (u + 1) * lo, :]
            whole[m, 0:lo, lanes] = jnp.where(plane == 0, a[:lo], b)
            whole[m, lo:part, lanes] = jnp.where(plane == 0, a[lo:], a[: part - lo])
            whole[m, part:all_rows, lanes] = jnp.where(plane == 0, b, a[part - lo :])
    for i, out_ref in enumerate((own_ref, other_ref)):
        lanes = slice(i * width // 2, (i + 1) * width // 2)
        rows = [whole[chip ^ c, clip_rows:all_rows, lanes] for c in range(chips)]
        rows += [whole[chip ^ c, 0:clip_rows, lanes] for c in range(chips)]
        out_ref[...] = jnp.concatenate(rows, axis=0).T


def grad_part(turned_ref, head_refs, rows, copies):
    right = jnp.concatenate([x[0:rows, :] for x in head_refs], axis=1)
    hist = jnp.concatenate([x[rows:, :] for x in head_refs], axis=1)
    clip = copies * hist.shape[0]
    out = jnp.dot(turned_ref[:, 0:rows], right, preferred_element_type=jnp.float32)
    return out + jnp.dot(
        turned_ref[:, rows : rows + clip],
        jnp.concatenate([hist] * copies, axis=0),
        preferred_element_type=jnp.float32,
    )


def grad_kernel(rows, copies, turned_ref, *refs):
    out_ref = refs[-1]
    out_ref[...] = grad_part(turned_ref, refs[:-1], rows, copies).astype(out_ref.dtype)


def finish_kernel(order, tok, own_near, own_far, got_near, got_far, *refs):
    n = len(order)
    heads, (att_hbm, out_hbm, total, sems) = refs[:n], refs[n:]
    own = lax.axis_index("tm")
    at = pl.multiple_of(own // 2 * tok, tok)
    near = own_near.shape[1] // HD

    def column(near_ref, far_ref, i):
        ref, i = (near_ref, i) if i < near else (far_ref, i - near)
        return ref[:, i * HD : (i + 1) * HD]

    moves = []

    def move(a, b):
        moves.append(pltpu.make_async_copy(a, b, sems.at[len(moves)]))
        moves[-1].start()

    lanes = [pl.ds(pl.multiple_of((own ^ k) * HD, HD), HD) for k in order]
    for i in range(n):
        move(heads[i].at[pl.ds(at, tok), :], att_hbm.at[:, lanes[i]])
    for i, k in enumerate(order):
        got = column(got_near, got_far, order.index(k ^ 1))
        total[i] = column(own_near, own_far, i) + got.astype(jnp.float32)
        move(total.at[i], out_hbm.at[:, lanes[i]])
    for x in moves:
        x.wait()


def head_body(query_rows, key_rows, value_rows, frame_counts, history, offsets, cotangent):
    n = lax.axis_size("tm")
    planes = lax.axis_size("head")
    half = n // 2
    tok, width = query_rows.shape
    tile = history.shape[0]
    clip_rows = n * tile
    cot_rows, all_cols = cotangent.shape
    cols = all_cols // n
    units = cols // HD
    lo = cot_rows * 7 // 17 // 16 * 16
    part = cot_rows - lo
    base = 3 * tok + clip_rows
    length = base
    rows = half * tok
    vmem = pl.BlockSpec(memory_space=pltpu.VMEM)
    hbm = pl.BlockSpec(memory_space=pl.ANY)
    bf16 = jnp.bfloat16

    def swap(x, bit):
        return lax.ppermute(x, "tm", [(i, i ^ bit) for i in range(n)])

    def swap_plane(x, bit):
        pairs = [
            (i * planes + p, (i ^ bit) * planes + (p ^ 1)) for i in range(n) for p in range(planes)
        ]
        return lax.ppermute(x, ("tm", "head"), pairs)

    def call(
        kernel, name, outs, specs, flops, scratch=(), exps=0, out_spec=vmem, limit=VMEM_LIMIT
    ):
        shapes = [jax.ShapeDtypeStruct(s, d) for s, d in outs]
        moved = 2 * sum(math.prod(s.shape) * s.dtype.itemsize for s in shapes)
        return pl.pallas_call(
            kernel,
            out_shape=tuple(shapes),
            in_specs=specs,
            out_specs=tuple([out_spec] * len(shapes)),
            scratch_shapes=scratch,
            compiler_params=pltpu.CompilerParams(vmem_limit_bytes=limit),
            cost_estimate=pl.CostEstimate(flops=flops, bytes_accessed=moved, transcendentals=exps),
            name=name,
        )

    def pack(heads, lanes, name):
        return call(
            lambda *refs: pack_kernel(n, heads, *refs),
            name,
            [((length, HD), bf16)] * len(heads),
            [hbm] * 4,
            0,
            (
                pltpu.VMEM((tok, lanes), bf16),
                pltpu.VMEM((tok, lanes), bf16),
                pltpu.VMEM((tok, lanes), bf16),
                pltpu.VMEM(history.shape, bf16),
                pltpu.SemaphoreType.DMA((4,)),
            ),
            limit=PACK_LIMIT,
        )(query_rows, key_rows, value_rows, history)

    first, rest = [6, 7], [0, 1, 2, 3, 4, 5]
    packed = dict(zip(first, pack(first, 2 * HD, "pack_first")))
    packed.update(zip(rest, pack(rest, width, "pack_rest")))
    order = [6, 7, 2, 4, 3, 5, 1]
    arrived = {k: swap(packed[k], k) for k in order}
    by_head = [packed[0]] + [arrived[k] for k in order]
    chips = range(half)
    cots = call(
        lambda *refs: cot_kernel(n, tile, lo, *refs),
        "cot",
        [((2 * units * cot_rows, HD), bf16)] + [((2 * units * part, HD), bf16)] * (half - 1),
        [hbm] * 4,
        0,
        (
            pltpu.SMEM(offsets.shape, jnp.int32),
            pltpu.VMEM(cotangent.shape, bf16),
            pltpu.SemaphoreType.DMA((2,)),
        ),
    )(offsets, cotangent, arrived[6], arrived[7])
    moved = {m: swap(cots[m], 2 * m) for m in reversed(chips[1:])}
    cots = [cots[0]] + [moved[m] for m in chips[1:]]
    counts = (
        pltpu.VMEM((n, length, HD), bf16),
        pltpu.SMEM(frame_counts.shape, jnp.int32),
        pltpu.SemaphoreType.DMA,
    )
    pairs = half * tok * WINB * tok
    head_shape = ((rows + clip_rows, HD), bf16)
    same, cross = call(
        lambda *refs: attend_kernel(n, tok, [0] + order, *refs),
        "attend",
        [head_shape, head_shape],
        [hbm] + [vmem] * n,
        8 * pairs * HD,
        counts,
        2 * pairs,
    )(frame_counts, *by_head)
    stack_order = [3, 1, 2]
    (cot_rest,) = call(
        lambda *refs: stack_kernel(stack_order, lo, 2 * units, *refs),
        "stack",
        [((half - 1, 2 * units * lo, HD), bf16)],
        [vmem] * (half - 1) + [hbm],
        0,
    )(*[cots[m] for m in stack_order], same)
    cot_swapped = swap_plane(cot_rest, 0)
    x_same, y_cross = swap(same, 2), swap(cross, 4 ^ 1)
    y_same, x_cross = swap(same, 4), swap(cross, 2 ^ 1)
    far_same, far_cross = swap(x_same, 4), swap(y_cross, 2)
    (late_cross,) = call(late_kernel, "late", [head_shape], [vmem] + [hbm] * 2, 0)(cross, x_cross, y_same)
    c_cross = swap(late_cross, 1)

    turned_own, turned_other = call(
        lambda *refs: turn_kernel(lo, clip_rows, stack_order, *refs),
        "turn",
        [((cols, half * cot_rows), bf16)] * 2,
        [vmem] * (half + 1),
        0,
        (pltpu.VMEM((half, cot_rows, 2 * cols), bf16),),
    )(cots[0], *[cots[m] for m in stack_order], cot_swapped)

    def grad(turned, heads, dtype, name):
        (out,) = call(
            lambda *refs: grad_kernel(rows, half, *refs),
            name,
            [((cols, len(heads) * HD), dtype)],
            [vmem] * (1 + len(heads)),
            2 * cols * half * cot_rows * len(heads) * HD,
        )(turned, *heads)
        return out

    near = [same, x_cross, y_same, x_same, y_cross]
    far = [c_cross, far_same, far_cross]
    heads = [0, 3, 4, 2, 5, 1, 6, 7]
    got_near = swap(grad(turned_other, near, bf16, "grad_other_near"), 1)
    own_near = grad(turned_own, near, jnp.float32, "grad_own_near")
    got_far = swap(grad(turned_other, far, bf16, "grad_other_far"), 1)
    own_far = grad(turned_own, far, jnp.float32, "grad_own_far")
    return call(
        lambda *refs: finish_kernel(heads, tok, *refs),
        "finish",
        [((tok, width), bf16), ((cols, width), jnp.float32)],
        [vmem] * (4 + n),
        0,
        (pltpu.VMEM((n, cols, HD), jnp.float32), pltpu.SemaphoreType.DMA((2 * n,))),
        out_spec=hbm,
    )(own_near, own_far, got_near, got_far, *near, *far)


def body(query_rows, key_rows, value_rows, frame_counts, history, offsets, cotangent):
    n = lax.axis_size("tm")
    tok, width = query_rows.shape
    by_heads = (
        n == 8
        and lax.axis_size("head") % 2 == 0
        and width == n * HD
        and offsets.shape[1] == n
        and cotangent.shape[0] == tok + n * history.shape[0]
        and cotangent.shape[1] % (n * HD) == 0
        and tok % 16 == 0
        and (n * history.shape[0]) % 16 == 0
    )
    plan = head_body if by_heads else window_body
    return plan(query_rows, key_rows, value_rows, frame_counts, history, offsets, cotangent)


def solution(mesh):
    in_specs = (
        P("tm", "head"),
        P("tm", "head"),
        P("tm", "head"),
        P(),
        P("tm", "head"),
        P("tm", None),
        P("tm", None),
    )
    out_specs = (P("tm", "head"), P("tm", "head"))
    return jax.shard_map(body, mesh=mesh, in_specs=in_specs, out_specs=out_specs, check_vma=False)
```

```python
import math

import jax
import jax.numpy as jnp
from jax import lax
from jax.experimental import pallas as pl
from jax.experimental.pallas import tpu as pltpu
from jax.sharding import PartitionSpec as P

HD = 128
TPF = 64
WINB = 4
VMEM_LIMIT = 24 * 1024 * 1024
PACK_LIMIT = 58 * 1024 * 1024


def from_behind(x, axis, by):
    devices = lax.axis_size(axis)
    pairs = [(i, i + by) for i in range(devices) if 0 <= i + by < devices]
    return lax.ppermute(x, axis, pairs)


def window_body(query_rows, key_rows, value_rows, frame_counts, history, offsets, cotangent):
    tok_rows, feat_width = query_rows.shape
    local_heads = feat_width // HD
    block_total = lax.axis_size("tm")
    own_block = lax.axis_index("tm")
    score_scale = 1.0 / math.sqrt(HD)
    key_value = jnp.stack([key_rows, value_rows])
    pieces = []
    for distance in range(WINB - 1, 0, -1):
        pieces.append(from_behind(key_value, "tm", distance))
    window = jnp.concatenate(pieces + [key_value], axis=1)
    source_block = own_block - (WINB - 1) + jnp.arange(WINB, dtype=jnp.int32)
    block_match = jnp.arange(block_total, dtype=jnp.int32)[None, :] == source_block[:, None]
    block_count = jnp.sum(jnp.where(block_match, frame_counts[None, :], 0), axis=1)
    frame_index = jnp.arange(tok_rows, dtype=jnp.int32) // TPF
    kept_mask = (
        (source_block[:, None] >= 0) & (frame_index[None, :] < block_count[:, None])
    ).reshape(WINB * tok_rows)
    key_window = window[0].reshape(WINB * tok_rows, local_heads, HD)
    value_window = window[1].reshape(WINB * tok_rows, local_heads, HD)
    query_heads = query_rows.reshape(tok_rows, local_heads, HD)
    scores = (
        jnp.einsum("qhd,khd->hqk", query_heads, key_window, preferred_element_type=jnp.float32)
        * score_scale
    )
    scores = jnp.where(kept_mask[None, None, :], scores, -jnp.inf)
    row_max = jnp.max(scores, axis=-1, keepdims=True)
    weights = jnp.exp(scores - row_max)
    probs = (weights / jnp.sum(weights, axis=-1, keepdims=True)).astype(jnp.bfloat16)
    mixed = jnp.einsum("hqk,khd->qhd", probs, value_window, preferred_element_type=jnp.float32)
    attended = mixed.astype(jnp.bfloat16).reshape(tok_rows, feat_width)
    tile_rows = history.shape[0]
    source_tile = (own_block - offsets[0]) % block_total
    source_row = (
        source_tile[:, None] * tile_rows + jnp.arange(tile_rows, dtype=jnp.int32)[None, :]
    ).reshape(-1)
    incoming = lax.all_gather(history, "tm", axis=0, tiled=True)
    piece_rows = incoming.shape[0]
    selector = (source_row[:, None] == jnp.arange(piece_rows, dtype=jnp.int32)[None, :]).astype(
        jnp.bfloat16
    )
    clip_hist = jnp.dot(selector, incoming, preferred_element_type=jnp.float32).astype(jnp.bfloat16)
    disc_clip = jnp.concatenate([clip_hist, attended], axis=0)
    disc_grad = lax.psum_scatter(
        lax.dot_general(
            cotangent, disc_clip, (((0,), (0,)), ((), ())), preferred_element_type=jnp.float32
        ),
        "tm",
        scatter_dimension=0,
        tiled=True,
    )
    return (attended, disc_grad)


def cot_kernel(n, tile, lo, off_hbm, cot_hbm, *refs):
    outs, (off, cot, sems) = refs[-3 - n // 2 : -3], refs[-3:]
    own = lax.axis_index("tm")
    chip, side = own // 2, lax.rem(own, 2)
    plane = lax.rem(lax.axis_index("head"), 2)
    clip_rows = n * tile
    all_rows, all_cols = cot.shape
    cols = all_cols // n
    part = all_rows - lo
    low = pl.multiple_of(plane * lo, 16)
    fetch_off = pltpu.make_async_copy(off_hbm, off, sems.at[0])
    fetch_cot = pltpu.make_async_copy(cot_hbm, cot, sems.at[1])
    fetch_off.start()
    fetch_cot.start()
    fetch_off.wait()
    r = lax.broadcasted_iota(jnp.int32, (clip_rows, clip_rows), 0)
    c = lax.broadcasted_iota(jnp.int32, (clip_rows, clip_rows), 1)
    select = jnp.zeros((clip_rows, clip_rows), jnp.float32)
    for j in range(n):
        src = lax.rem(own - off[0, j] + 2 * n, n)
        for t in range(tile):
            select = jnp.where((c == j * tile + t) & (r == src * tile + t), 1.0, select)
    fetch_cot.wait()
    cot[0:clip_rows, :] = jnp.dot(
        select.astype(jnp.bfloat16), cot[0:clip_rows, :], preferred_element_type=jnp.float32
    ).astype(jnp.bfloat16)
    units = cols // HD
    for m, out_ref in enumerate(outs):
        rows, first = (part, low) if m else (all_rows, 0)
        for i, block in enumerate((2 * (chip ^ m) + side, 2 * (chip ^ m) + 1 - side)):
            for u in range(units):
                at = (i * units + u) * rows
                lanes = pl.ds(pl.multiple_of(block * cols + u * HD, HD), HD)
                out_ref[at : at + rows, :] = cot[pl.ds(first, rows), lanes]


def pack_kernel(n, heads, q_hbm, k_hbm, v_hbm, hist_hbm, *refs):
    outs, (q, k, v, hist, sems) = refs[:-5], refs[-5:]
    own = lax.axis_index("tm")
    tok, width = q.shape
    tile = hist.shape[0]
    clip_rows = n * tile
    start = 0 if width == n * HD else pl.multiple_of(((own ^ heads[0]) // 2) * width, width)
    pairs = [(hist_hbm, hist)] + [
        (x.at[:, pl.ds(start, width)], y) for x, y in ((q_hbm, q), (k_hbm, k), (v_hbm, v))
    ]
    copies = [pltpu.make_async_copy(a, b, sems.at[i]) for i, (a, b) in enumerate(pairs)]
    for copy in copies:
        copy.start()
    copies[0].wait()
    for d, out_ref in zip(heads, outs):
        lanes = pl.ds(pl.multiple_of((own ^ d) * HD, HD), HD)
        tiles = hist[:, lanes].astype(jnp.float32)
        row = lax.broadcasted_iota(jnp.int32, (clip_rows, HD), 0)
        placed = jnp.zeros((clip_rows, HD), jnp.float32)
        for t in range(tile):
            placed = jnp.where(row == own * tile + t, tiles[t : t + 1, :], placed)
        out_ref[3 * tok : 3 * tok + clip_rows, :] = placed.astype(jnp.bfloat16)
    for i, x in enumerate((q, k, v)):
        copies[1 + i].wait()
        for d, out_ref in zip(heads, outs):
            lanes = pl.ds(pl.multiple_of((own ^ d) * HD - start, HD), HD)
            out_ref[i * tok : (i + 1) * tok, :] = x[:, lanes]


def attend_kernel(n, tok, order, counts_hbm, *refs):
    parts, (same_ref, cross_ref, x_ref, mixed_ref, counts, sem) = refs[:n], refs[n:]
    copy = pltpu.make_async_copy(counts_hbm, counts, sem)
    copy.start()
    own = lax.axis_index("tm")
    side = lax.rem(own, 2)
    for k, part in zip(order, parts):
        x_ref[own ^ k] = part[...]
    copy.wait()
    rate = math.log2(math.e) / math.sqrt(HD)
    token = lax.broadcasted_iota(jnp.int32, (tok, 1), 0)
    bias = [
        jnp.where(token < counts[s] * TPF, 0.0, -jnp.inf).astype(jnp.float32) for s in range(n)
    ]
    values = [x_ref[s, 2 * tok : 3 * tok, :].T for s in range(n)]
    for block in range(n):
        sources = range(max(0, block - (WINB - 1)), block + 1)
        q = x_ref[block, 0:tok, :]
        scores = [
            lax.dot_general(
                x_ref[s, tok : 2 * tok, :],
                q,
                (((1,), (1,)), ((), ())),
                preferred_element_type=jnp.float32,
            )
            + bias[s]
            for s in sources
        ]
        top = jnp.max(scores[0], axis=0, keepdims=True)
        for s in scores[1:]:
            top = jnp.maximum(top, jnp.max(s, axis=0, keepdims=True))
        weights = [jnp.exp2((s - top) * rate) for s in scores]
        total = jnp.sum(weights[0], axis=0, keepdims=True)
        for w in weights[1:]:
            total = total + jnp.sum(w, axis=0, keepdims=True)
        share = 1.0 / total
        mixed = jnp.zeros((HD, tok), jnp.float32)
        for s, w in zip(sources, weights):
            mixed = mixed + jnp.dot(
                values[s], (w * share).astype(jnp.bfloat16), preferred_element_type=jnp.float32
            )
        mixed_ref[block] = mixed.astype(jnp.bfloat16).T
    rows = n // 2 * tok
    clip_rows = same_ref.shape[0] - rows
    hist = jnp.zeros((clip_rows, HD), jnp.float32)
    for s in range(n):
        hist = hist + x_ref[s, 3 * tok : 3 * tok + clip_rows, :].astype(jnp.float32)
    hist = hist.astype(jnp.bfloat16)
    for flip, out_ref in ((0, same_ref), (1, cross_ref)):
        for i in range(n // 2):
            out_ref[i * tok : (i + 1) * tok, :] = mixed_ref[2 * i + (side ^ flip)]
        out_ref[rows:, :] = hist


def stack_kernel(order, lo, tiles, *refs):
    out_ref = refs[-1]
    plane = lax.rem(lax.axis_index("head"), 2)
    for m, ref in zip(order, refs):
        part = ref.shape[0] // tiles
        for u in range(tiles):
            first = pl.multiple_of(u * part + plane * (part - lo), 16)
            out_ref[m - 1, u * lo : (u + 1) * lo, :] = ref[pl.ds(first, lo), :]


def late_kernel(x_ref, *refs):
    refs[-1][...] = x_ref[...]


def turn_kernel(lo, clip_rows, order, own_in, *refs):
    pieces, (swapped_ref, own_ref, other_ref, whole) = refs[:-4], refs[-4:]
    plane = lax.rem(lax.axis_index("head"), 2)
    chip = lax.axis_index("tm") // 2
    chips, all_rows, width = whole.shape
    part = all_rows - lo
    for u in range(width // HD):
        lanes = slice(u * HD, (u + 1) * HD)
        whole[0, :, lanes] = own_in[u * all_rows : (u + 1) * all_rows, :]
        for m, ref in zip(order, pieces):
            a = ref[u * part : (u + 1) * part, :]
            b = swapped_ref[m - 1, u * lo : (u + 1) * lo, :]
            whole[m, 0:lo, lanes] = jnp.where(plane == 0, a[:lo], b)
            whole[m, lo:part, lanes] = jnp.where(plane == 0, a[lo:], a[: part - lo])
            whole[m, part:all_rows, lanes] = jnp.where(plane == 0, b, a[part - lo :])
    for i, out_ref in enumerate((own_ref, other_ref)):
        lanes = slice(i * width // 2, (i + 1) * width // 2)
        rows = [whole[chip ^ c, clip_rows:all_rows, lanes] for c in range(chips)]
        rows += [whole[chip ^ c, 0:clip_rows, lanes] for c in range(chips)]
        out_ref[...] = jnp.concatenate(rows, axis=0).T


def grad_part(turned_ref, head_refs, rows, copies):
    right = jnp.concatenate([x[0:rows, :] for x in head_refs], axis=1)
    hist = jnp.concatenate([x[rows:, :] for x in head_refs], axis=1)
    clip = copies * hist.shape[0]
    out = jnp.dot(turned_ref[:, 0:rows], right, preferred_element_type=jnp.float32)
    return out + jnp.dot(
        turned_ref[:, rows : rows + clip],
        jnp.concatenate([hist] * copies, axis=0),
        preferred_element_type=jnp.float32,
    )


def grad_kernel(rows, copies, heads, turned_ref, *refs):
    out_ref = refs[-1]
    out_ref[...] = grad_part(turned_ref, refs[:heads], rows, copies).astype(out_ref.dtype)


def store_columns(tok, heads, sums, att_hbm, out_hbm, total, sems):
    own = lax.axis_index("tm")
    at = pl.multiple_of(own // 2 * tok, tok)
    moves = []

    def move(a, b):
        moves.append(pltpu.make_async_copy(a, b, sems.at[len(moves)]))
        moves[-1].start()

    def lanes(k):
        return pl.ds(pl.multiple_of((own ^ k) * HD, HD), HD)

    for k, ref in heads:
        move(ref.at[pl.ds(at, tok), :], att_hbm.at[:, lanes(k)])
    for i, (k, (mine, m), (got, g)) in enumerate(sums):
        columns = got[:, g * HD : (g + 1) * HD].astype(jnp.float32)
        total[i] = mine[:, m * HD : (m + 1) * HD] + columns
        move(total.at[i], out_hbm.at[:, lanes(k)])
    for x in moves:
        x.wait()


def near_kernel(tok, near, own_near, got_near, *refs):
    heads, outs = refs[: len(near)], refs[len(near) :]
    sums = [
        (k, (own_near, i), (got_near, near.index(k ^ 1)))
        for i, k in enumerate(near)
        if k ^ 1 in near
    ]
    store_columns(tok, zip(near, heads), sums, *outs)


def last_kernel(tok, near, far, own_near, got_near, own_far, got_far, *refs):
    heads, outs = refs[: len(far)], refs[len(far) + 2 :]
    sums = [
        (k, (own_near, i), (got_far, far.index(k ^ 1)))
        for i, k in enumerate(near)
        if k ^ 1 in far
    ]
    for i, k in enumerate(far):
        got = (got_far, far.index(k ^ 1)) if k ^ 1 in far else (got_near, near.index(k ^ 1))
        sums.append((k, (own_far, i), got))
    store_columns(tok, zip(far, heads), sums, *outs)


def head_body(query_rows, key_rows, value_rows, frame_counts, history, offsets, cotangent):
    n = lax.axis_size("tm")
    planes = lax.axis_size("head")
    half = n // 2
    tok, width = query_rows.shape
    tile = history.shape[0]
    clip_rows = n * tile
    cot_rows, all_cols = cotangent.shape
    cols = all_cols // n
    units = cols // HD
    lo = cot_rows * 7 // 17 // 16 * 16
    part = cot_rows - lo
    base = 3 * tok + clip_rows
    length = base
    rows = half * tok
    vmem = pl.BlockSpec(memory_space=pltpu.VMEM)
    hbm = pl.BlockSpec(memory_space=pl.ANY)
    bf16 = jnp.bfloat16

    def swap(x, bit):
        return lax.ppermute(x, "tm", [(i, i ^ bit) for i in range(n)])

    def swap_plane(x, bit):
        pairs = [
            (i * planes + p, (i ^ bit) * planes + (p ^ 1)) for i in range(n) for p in range(planes)
        ]
        return lax.ppermute(x, ("tm", "head"), pairs)

    def call(
        kernel, name, outs, specs, flops, scratch=(), exps=0, out_spec=vmem, limit=VMEM_LIMIT, aliases={}
    ):
        shapes = [jax.ShapeDtypeStruct(s, d) for s, d in outs]
        moved = 2 * sum(math.prod(s.shape) * s.dtype.itemsize for s in shapes)
        return pl.pallas_call(
            kernel,
            out_shape=tuple(shapes),
            in_specs=specs,
            out_specs=tuple([out_spec] * len(shapes)),
            scratch_shapes=scratch,
            input_output_aliases=aliases,
            compiler_params=pltpu.CompilerParams(vmem_limit_bytes=limit),
            cost_estimate=pl.CostEstimate(flops=flops, bytes_accessed=moved, transcendentals=exps),
            name=name,
        )

    def pack(heads, lanes, name):
        return call(
            lambda *refs: pack_kernel(n, heads, *refs),
            name,
            [((length, HD), bf16)] * len(heads),
            [hbm] * 4,
            0,
            (
                pltpu.VMEM((tok, lanes), bf16),
                pltpu.VMEM((tok, lanes), bf16),
                pltpu.VMEM((tok, lanes), bf16),
                pltpu.VMEM(history.shape, bf16),
                pltpu.SemaphoreType.DMA((4,)),
            ),
            limit=PACK_LIMIT,
        )(query_rows, key_rows, value_rows, history)

    first, rest = [6, 7], [0, 1, 2, 3, 4, 5]
    packed = dict(zip(first, pack(first, 2 * HD, "pack_first")))
    packed.update(zip(rest, pack(rest, width, "pack_rest")))
    order = [6, 7, 2, 4, 3, 5, 1]
    arrived = {k: swap(packed[k], k) for k in order}
    by_head = [packed[0]] + [arrived[k] for k in order]
    chips = range(half)
    cots = call(
        lambda *refs: cot_kernel(n, tile, lo, *refs),
        "cot",
        [((2 * units * cot_rows, HD), bf16)] + [((2 * units * part, HD), bf16)] * (half - 1),
        [hbm] * 4,
        0,
        (
            pltpu.SMEM(offsets.shape, jnp.int32),
            pltpu.VMEM(cotangent.shape, bf16),
            pltpu.SemaphoreType.DMA((2,)),
        ),
    )(offsets, cotangent, arrived[6], arrived[7])
    moved = {m: swap(cots[m], 2 * m) for m in reversed(chips[1:])}
    cots = [cots[0]] + [moved[m] for m in chips[1:]]
    counts = (
        pltpu.VMEM((n, length, HD), bf16),
        pltpu.VMEM((n, tok, HD), bf16),
        pltpu.SMEM(frame_counts.shape, jnp.int32),
        pltpu.SemaphoreType.DMA,
    )
    pairs = half * tok * WINB * tok
    head_shape = ((rows + clip_rows, HD), bf16)
    same, cross = call(
        lambda *refs: attend_kernel(n, tok, [0] + order, *refs),
        "attend",
        [head_shape, head_shape],
        [hbm] + [vmem] * n,
        8 * pairs * HD,
        counts,
        2 * pairs,
    )(frame_counts, *by_head)
    stack_order = [3, 1, 2]
    (cot_rest,) = call(
        lambda *refs: stack_kernel(stack_order, lo, 2 * units, *refs),
        "stack",
        [((half - 1, 2 * units * lo, HD), bf16)],
        [vmem] * (half - 1) + [hbm],
        0,
    )(*[cots[m] for m in stack_order], same)
    cot_swapped = swap_plane(cot_rest, 0)
    x_same, y_cross = swap(same, 2), swap(cross, 4 ^ 1)
    y_same, x_cross = swap(same, 4), swap(cross, 2 ^ 1)
    far_same, far_cross = swap(x_same, 4), swap(y_cross, 2)
    (late_cross,) = call(late_kernel, "late", [head_shape], [vmem] + [hbm] * 2, 0)(cross, x_cross, y_same)
    c_cross = swap(late_cross, 1)

    turned_own, turned_other = call(
        lambda *refs: turn_kernel(lo, clip_rows, stack_order, *refs),
        "turn",
        [((cols, half * cot_rows), bf16)] * 2,
        [vmem] * (half + 1),
        0,
        (pltpu.VMEM((half, cot_rows, 2 * cols), bf16),),
    )(cots[0], *[cots[m] for m in stack_order], cot_swapped)

    def grad(turned, heads, dtype, name, behind=()):
        (out,) = call(
            lambda *refs: grad_kernel(rows, half, len(heads), *refs),
            name,
            [((cols, len(heads) * HD), dtype)],
            [vmem] * (1 + len(heads)) + [hbm] * len(behind),
            2 * cols * half * cot_rows * len(heads) * HD,
        )(turned, *heads, *behind)
        return out

    near, near_bits = [same, x_cross, y_same, x_same, y_cross], [0, 3, 4, 2, 5]
    far, far_bits = [c_cross, far_same, far_cross], [1, 6, 7]
    whole = [((tok, width), bf16), ((cols, width), jnp.float32)]
    got_near = swap(grad(turned_other, near, bf16, "grad_other_near"), 1)
    own_near = grad(turned_own, near, jnp.float32, "grad_own_near")
    got_far = swap(grad(turned_other, far, bf16, "grad_other_far", (own_near,)), 1)
    own_far = grad(turned_own, far, jnp.float32, "grad_own_far")
    halfway = call(
        lambda *refs: near_kernel(tok, near_bits, *refs),
        "near",
        whole,
        [vmem] * (2 + len(near)),
        0,
        (pltpu.VMEM((4, cols, HD), jnp.float32), pltpu.SemaphoreType.DMA((9,))),
        out_spec=hbm,
    )(own_near, got_near, *near)
    return call(
        lambda *refs: last_kernel(tok, near_bits, far_bits, *refs),
        "last",
        whole,
        [vmem] * (4 + len(far)) + [hbm] * 2,
        0,
        (pltpu.VMEM((4, cols, HD), jnp.float32), pltpu.SemaphoreType.DMA((7,))),
        out_spec=hbm,
        aliases={4 + len(far): 0, 5 + len(far): 1},
    )(own_near, got_near, own_far, got_far, *far, *halfway)


def body(query_rows, key_rows, value_rows, frame_counts, history, offsets, cotangent):
    n = lax.axis_size("tm")
    tok, width = query_rows.shape
    by_heads = (
        n == 8
        and lax.axis_size("head") % 2 == 0
        and width == n * HD
        and offsets.shape[1] == n
        and cotangent.shape[0] == tok + n * history.shape[0]
        and cotangent.shape[1] % (n * HD) == 0
        and tok % 16 == 0
        and (n * history.shape[0]) % 16 == 0
    )
    plan = head_body if by_heads else window_body
    return plan(query_rows, key_rows, value_rows, frame_counts, history, offsets, cotangent)


def solution(mesh):
    in_specs = (
        P("tm", "head"),
        P("tm", "head"),
        P("tm", "head"),
        P(),
        P("tm", "head"),
        P("tm", None),
        P("tm", None),
    )
    out_specs = (P("tm", "head"), P("tm", "head"))
    return jax.shard_map(body, mesh=mesh, in_specs=in_specs, out_specs=out_specs, check_vma=False)
```

```python
import math

import jax
import jax.numpy as jnp
from jax import lax
from jax.experimental import pallas as pl
from jax.experimental.pallas import tpu as pltpu
from jax.sharding import PartitionSpec as P

HD = 128
TPF = 64
WINB = 4
VMEM_LIMIT = 24 * 1024 * 1024
PACK_LIMIT = 58 * 1024 * 1024


def from_behind(x, axis, by):
    devices = lax.axis_size(axis)
    pairs = [(i, i + by) for i in range(devices) if 0 <= i + by < devices]
    return lax.ppermute(x, axis, pairs)


def window_body(query_rows, key_rows, value_rows, frame_counts, history, offsets, cotangent):
    tok_rows, feat_width = query_rows.shape
    local_heads = feat_width // HD
    block_total = lax.axis_size("tm")
    own_block = lax.axis_index("tm")
    score_scale = 1.0 / math.sqrt(HD)
    key_value = jnp.stack([key_rows, value_rows])
    pieces = []
    for distance in range(WINB - 1, 0, -1):
        pieces.append(from_behind(key_value, "tm", distance))
    window = jnp.concatenate(pieces + [key_value], axis=1)
    source_block = own_block - (WINB - 1) + jnp.arange(WINB, dtype=jnp.int32)
    block_match = jnp.arange(block_total, dtype=jnp.int32)[None, :] == source_block[:, None]
    block_count = jnp.sum(jnp.where(block_match, frame_counts[None, :], 0), axis=1)
    frame_index = jnp.arange(tok_rows, dtype=jnp.int32) // TPF
    kept_mask = (
        (source_block[:, None] >= 0) & (frame_index[None, :] < block_count[:, None])
    ).reshape(WINB * tok_rows)
    key_window = window[0].reshape(WINB * tok_rows, local_heads, HD)
    value_window = window[1].reshape(WINB * tok_rows, local_heads, HD)
    query_heads = query_rows.reshape(tok_rows, local_heads, HD)
    scores = (
        jnp.einsum("qhd,khd->hqk", query_heads, key_window, preferred_element_type=jnp.float32)
        * score_scale
    )
    scores = jnp.where(kept_mask[None, None, :], scores, -jnp.inf)
    row_max = jnp.max(scores, axis=-1, keepdims=True)
    weights = jnp.exp(scores - row_max)
    probs = (weights / jnp.sum(weights, axis=-1, keepdims=True)).astype(jnp.bfloat16)
    mixed = jnp.einsum("hqk,khd->qhd", probs, value_window, preferred_element_type=jnp.float32)
    attended = mixed.astype(jnp.bfloat16).reshape(tok_rows, feat_width)
    tile_rows = history.shape[0]
    source_tile = (own_block - offsets[0]) % block_total
    source_row = (
        source_tile[:, None] * tile_rows + jnp.arange(tile_rows, dtype=jnp.int32)[None, :]
    ).reshape(-1)
    incoming = lax.all_gather(history, "tm", axis=0, tiled=True)
    piece_rows = incoming.shape[0]
    selector = (source_row[:, None] == jnp.arange(piece_rows, dtype=jnp.int32)[None, :]).astype(
        jnp.bfloat16
    )
    clip_hist = jnp.dot(selector, incoming, preferred_element_type=jnp.float32).astype(jnp.bfloat16)
    disc_clip = jnp.concatenate([clip_hist, attended], axis=0)
    disc_grad = lax.psum_scatter(
        lax.dot_general(
            cotangent, disc_clip, (((0,), (0,)), ((), ())), preferred_element_type=jnp.float32
        ),
        "tm",
        scatter_dimension=0,
        tiled=True,
    )
    return (attended, disc_grad)


def cot_kernel(n, tile, lo, off_hbm, cot_hbm, *refs):
    outs, (off, cot, sems) = refs[-3 - n // 2 : -3], refs[-3:]
    own = lax.axis_index("tm")
    chip, side = own // 2, lax.rem(own, 2)
    plane = lax.rem(lax.axis_index("head"), 2)
    clip_rows = n * tile
    all_rows, all_cols = cot.shape
    cols = all_cols // n
    part = all_rows - lo
    low = pl.multiple_of(plane * lo, 16)
    fetch_off = pltpu.make_async_copy(off_hbm, off, sems.at[0])
    fetch_cot = pltpu.make_async_copy(cot_hbm, cot, sems.at[1])
    fetch_off.start()
    fetch_cot.start()
    fetch_off.wait()
    r = lax.broadcasted_iota(jnp.int32, (clip_rows, clip_rows), 0)
    c = lax.broadcasted_iota(jnp.int32, (clip_rows, clip_rows), 1)
    select = jnp.zeros((clip_rows, clip_rows), jnp.float32)
    for j in range(n):
        src = lax.rem(own - off[0, j] + 2 * n, n)
        for t in range(tile):
            select = jnp.where((c == j * tile + t) & (r == src * tile + t), 1.0, select)
    fetch_cot.wait()
    cot[0:clip_rows, :] = jnp.dot(
        select.astype(jnp.bfloat16), cot[0:clip_rows, :], preferred_element_type=jnp.float32
    ).astype(jnp.bfloat16)
    units = cols // HD
    for m, out_ref in enumerate(outs):
        rows, first = (part, low) if m else (all_rows, 0)
        for i, block in enumerate((2 * (chip ^ m) + side, 2 * (chip ^ m) + 1 - side)):
            for u in range(units):
                at = (i * units + u) * rows
                lanes = pl.ds(pl.multiple_of(block * cols + u * HD, HD), HD)
                out_ref[at : at + rows, :] = cot[pl.ds(first, rows), lanes]


def pack_kernel(n, heads, q_hbm, k_hbm, v_hbm, hist_hbm, *refs):
    outs, (q, k, v, hist, sems) = refs[:-5], refs[-5:]
    own = lax.axis_index("tm")
    tok, width = q.shape
    tile = hist.shape[0]
    clip_rows = n * tile
    start = 0 if width == n * HD else pl.multiple_of(((own ^ heads[0]) // 2) * width, width)
    pairs = [(hist_hbm, hist)] + [
        (x.at[:, pl.ds(start, width)], y) for x, y in ((q_hbm, q), (k_hbm, k), (v_hbm, v))
    ]
    copies = [pltpu.make_async_copy(a, b, sems.at[i]) for i, (a, b) in enumerate(pairs)]
    for copy in copies:
        copy.start()
    copies[0].wait()
    for d, out_ref in zip(heads, outs):
        lanes = pl.ds(pl.multiple_of((own ^ d) * HD, HD), HD)
        tiles = hist[:, lanes].astype(jnp.float32)
        row = lax.broadcasted_iota(jnp.int32, (clip_rows, HD), 0)
        placed = jnp.zeros((clip_rows, HD), jnp.float32)
        for t in range(tile):
            placed = jnp.where(row == own * tile + t, tiles[t : t + 1, :], placed)
        out_ref[3 * tok : 3 * tok + clip_rows, :] = placed.astype(jnp.bfloat16)
    for i, x in enumerate((q, k, v)):
        copies[1 + i].wait()
        for d, out_ref in zip(heads, outs):
            lanes = pl.ds(pl.multiple_of((own ^ d) * HD - start, HD), HD)
            out_ref[i * tok : (i + 1) * tok, :] = x[:, lanes]


def attend_kernel(n, tok, order, counts_hbm, *refs):
    parts, (same_ref, cross_ref, x_ref, mixed_ref, counts, sem) = refs[:n], refs[n:]
    copy = pltpu.make_async_copy(counts_hbm, counts, sem)
    copy.start()
    own = lax.axis_index("tm")
    side = lax.rem(own, 2)
    for k, part in zip(order, parts):
        x_ref[own ^ k] = part[...]
    copy.wait()
    rate = math.log2(math.e) / math.sqrt(HD)
    token = lax.broadcasted_iota(jnp.int32, (tok, 1), 0)
    bias = [
        jnp.where(token < counts[s] * TPF, 0.0, -jnp.inf).astype(jnp.float32) for s in range(n)
    ]
    values = [x_ref[s, 2 * tok : 3 * tok, :].T for s in range(n)]
    for block in range(n):
        sources = range(max(0, block - (WINB - 1)), block + 1)
        q = x_ref[block, 0:tok, :]
        scores = [
            lax.dot_general(
                x_ref[s, tok : 2 * tok, :],
                q,
                (((1,), (1,)), ((), ())),
                preferred_element_type=jnp.float32,
            )
            + bias[s]
            for s in sources
        ]
        top = jnp.max(scores[0], axis=0, keepdims=True)
        for s in scores[1:]:
            top = jnp.maximum(top, jnp.max(s, axis=0, keepdims=True))
        weights = [jnp.exp2((s - top) * rate) for s in scores]
        total = jnp.sum(weights[0], axis=0, keepdims=True)
        for w in weights[1:]:
            total = total + jnp.sum(w, axis=0, keepdims=True)
        share = 1.0 / total
        mixed = jnp.zeros((HD, tok), jnp.float32)
        for s, w in zip(sources, weights):
            mixed = mixed + jnp.dot(
                values[s], (w * share).astype(jnp.bfloat16), preferred_element_type=jnp.float32
            )
        mixed_ref[block] = mixed.astype(jnp.bfloat16).T
    rows = n // 2 * tok
    clip_rows = same_ref.shape[0] - rows
    hist = jnp.zeros((clip_rows, HD), jnp.float32)
    for s in range(n):
        hist = hist + x_ref[s, 3 * tok : 3 * tok + clip_rows, :].astype(jnp.float32)
    hist = hist.astype(jnp.bfloat16)
    for flip, out_ref in ((0, same_ref), (1, cross_ref)):
        for i in range(n // 2):
            out_ref[i * tok : (i + 1) * tok, :] = mixed_ref[2 * i + (side ^ flip)]
        out_ref[rows:, :] = hist


def stack_kernel(order, lo, tiles, *refs):
    out_ref = refs[-1]
    plane = lax.rem(lax.axis_index("head"), 2)
    for m, ref in zip(order, refs):
        part = ref.shape[0] // tiles
        for u in range(tiles):
            first = pl.multiple_of(u * part + plane * (part - lo), 16)
            out_ref[m - 1, u * lo : (u + 1) * lo, :] = ref[pl.ds(first, lo), :]


def late_kernel(x_ref, *refs):
    refs[-1][...] = x_ref[...]


def turn_kernel(lo, clip_rows, order, own_in, *refs):
    pieces, (swapped_ref, own_ref, other_ref, whole) = refs[:-4], refs[-4:]
    plane = lax.rem(lax.axis_index("head"), 2)
    chip = lax.axis_index("tm") // 2
    chips, all_rows, width = whole.shape
    part = all_rows - lo
    for u in range(width // HD):
        lanes = slice(u * HD, (u + 1) * HD)
        whole[0, :, lanes] = own_in[u * all_rows : (u + 1) * all_rows, :]
        for m, ref in zip(order, pieces):
            a = ref[u * part : (u + 1) * part, :]
            b = swapped_ref[m - 1, u * lo : (u + 1) * lo, :]
            whole[m, 0:lo, lanes] = jnp.where(plane == 0, a[:lo], b)
            whole[m, lo:part, lanes] = jnp.where(plane == 0, a[lo:], a[: part - lo])
            whole[m, part:all_rows, lanes] = jnp.where(plane == 0, b, a[part - lo :])
    for i, out_ref in enumerate((own_ref, other_ref)):
        lanes = slice(i * width // 2, (i + 1) * width // 2)
        rows = [whole[chip ^ c, clip_rows:all_rows, lanes] for c in range(chips)]
        rows += [whole[chip ^ c, 0:clip_rows, lanes] for c in range(chips)]
        out_ref[...] = jnp.concatenate(rows, axis=0).T


def grad_part(turned_ref, head_refs, rows, copies):
    right = jnp.concatenate([x[0:rows, :] for x in head_refs], axis=1)
    hist = jnp.concatenate([x[rows:, :] for x in head_refs], axis=1)
    clip = copies * hist.shape[0]
    out = jnp.dot(turned_ref[:, 0:rows], right, preferred_element_type=jnp.float32)
    return out + jnp.dot(
        turned_ref[:, rows : rows + clip],
        jnp.concatenate([hist] * copies, axis=0),
        preferred_element_type=jnp.float32,
    )


def grad_kernel(rows, copies, heads, turned_ref, *refs):
    out_ref = refs[-1]
    out_ref[...] = grad_part(turned_ref, refs[:heads], rows, copies).astype(out_ref.dtype)


def store_columns(tok, heads, sums, att_hbm, out_hbm, total, sems):
    own = lax.axis_index("tm")
    at = pl.multiple_of(own // 2 * tok, tok)
    moves = []

    def move(a, b):
        moves.append(pltpu.make_async_copy(a, b, sems.at[len(moves)]))
        moves[-1].start()

    def lanes(k):
        return pl.ds(pl.multiple_of((own ^ k) * HD, HD), HD)

    for k, ref in heads:
        move(ref.at[pl.ds(at, tok), :], att_hbm.at[:, lanes(k)])
    for i, (k, (mine, m), (got, g)) in enumerate(sums):
        columns = got[:, g * HD : (g + 1) * HD].astype(jnp.float32)
        total[i] = mine[:, m * HD : (m + 1) * HD] + columns
        move(total.at[i], out_hbm.at[:, lanes(k)])
    for x in moves:
        x.wait()


def near_kernel(tok, near, own_near, got_near, *refs):
    heads, outs = refs[: len(near)], refs[len(near) :]
    sums = [
        (k, (own_near, i), (got_near, near.index(k ^ 1)))
        for i, k in enumerate(near)
        if k ^ 1 in near
    ]
    store_columns(tok, zip(near, heads), sums, *outs)


def last_kernel(tok, near, far, own_near, got_near, own_far, got_far, *refs):
    heads, outs = refs[: len(far)], refs[len(far) + 2 :]
    sums = [
        (k, (own_near, i), (got_far, far.index(k ^ 1)))
        for i, k in enumerate(near)
        if k ^ 1 in far
    ]
    for i, k in enumerate(far):
        got = (got_far, far.index(k ^ 1)) if k ^ 1 in far else (got_near, near.index(k ^ 1))
        sums.append((k, (own_far, i), got))
    store_columns(tok, zip(far, heads), sums, *outs)


def head_body(query_rows, key_rows, value_rows, frame_counts, history, offsets, cotangent):
    n = lax.axis_size("tm")
    planes = lax.axis_size("head")
    half = n // 2
    tok, width = query_rows.shape
    tile = history.shape[0]
    clip_rows = n * tile
    cot_rows, all_cols = cotangent.shape
    cols = all_cols // n
    units = cols // HD
    lo = cot_rows * 7 // 17 // 16 * 16
    part = cot_rows - lo
    base = 3 * tok + clip_rows
    length = base
    rows = half * tok
    vmem = pl.BlockSpec(memory_space=pltpu.VMEM)
    hbm = pl.BlockSpec(memory_space=pl.ANY)
    bf16 = jnp.bfloat16

    def swap(x, bit):
        return lax.ppermute(x, "tm", [(i, i ^ bit) for i in range(n)])

    def swap_plane(x, bit):
        pairs = [
            (i * planes + p, (i ^ bit) * planes + (p ^ 1)) for i in range(n) for p in range(planes)
        ]
        return lax.ppermute(x, ("tm", "head"), pairs)

    def call(
        kernel, name, outs, specs, flops, scratch=(), exps=0, out_spec=vmem, limit=VMEM_LIMIT, aliases={}
    ):
        shapes = [jax.ShapeDtypeStruct(s, d) for s, d in outs]
        moved = 2 * sum(math.prod(s.shape) * s.dtype.itemsize for s in shapes)
        return pl.pallas_call(
            kernel,
            out_shape=tuple(shapes),
            in_specs=specs,
            out_specs=tuple([out_spec] * len(shapes)),
            scratch_shapes=scratch,
            input_output_aliases=aliases,
            compiler_params=pltpu.CompilerParams(vmem_limit_bytes=limit),
            cost_estimate=pl.CostEstimate(flops=flops, bytes_accessed=moved, transcendentals=exps),
            name=name,
        )

    def pack(heads, lanes, name):
        return call(
            lambda *refs: pack_kernel(n, heads, *refs),
            name,
            [((length, HD), bf16)] * len(heads),
            [hbm] * 4,
            0,
            (
                pltpu.VMEM((tok, lanes), bf16),
                pltpu.VMEM((tok, lanes), bf16),
                pltpu.VMEM((tok, lanes), bf16),
                pltpu.VMEM(history.shape, bf16),
                pltpu.SemaphoreType.DMA((4,)),
            ),
            limit=PACK_LIMIT,
        )(query_rows, key_rows, value_rows, history)

    first, rest = [6, 7], [0, 1, 2, 3, 4, 5]
    packed = dict(zip(first, pack(first, 2 * HD, "pack_first")))
    packed.update(zip(rest, pack(rest, width, "pack_rest")))
    order = [6, 7, 2, 4, 3, 5, 1]
    arrived = {k: swap(packed[k], k) for k in order}
    by_head = [packed[0]] + [arrived[k] for k in order]
    chips = range(half)
    cots = call(
        lambda *refs: cot_kernel(n, tile, lo, *refs),
        "cot",
        [((2 * units * cot_rows, HD), bf16)] + [((2 * units * part, HD), bf16)] * (half - 1),
        [hbm] * 4,
        0,
        (
            pltpu.SMEM(offsets.shape, jnp.int32),
            pltpu.VMEM(cotangent.shape, bf16),
            pltpu.SemaphoreType.DMA((2,)),
        ),
    )(offsets, cotangent, arrived[6], arrived[7])
    moved = {m: swap(cots[m], 2 * m) for m in reversed(chips[1:])}
    cots = [cots[0]] + [moved[m] for m in chips[1:]]
    counts = (
        pltpu.VMEM((n, length, HD), bf16),
        pltpu.VMEM((n, tok, HD), bf16),
        pltpu.SMEM(frame_counts.shape, jnp.int32),
        pltpu.SemaphoreType.DMA,
    )
    pairs = half * tok * WINB * tok
    head_shape = ((rows + clip_rows, HD), bf16)
    same, cross = call(
        lambda *refs: attend_kernel(n, tok, [0] + order, *refs),
        "attend",
        [head_shape, head_shape],
        [hbm] + [vmem] * n,
        8 * pairs * HD,
        counts,
        2 * pairs,
    )(frame_counts, *by_head)
    stack_order = [1, 2, 3]
    (cot_rest,) = call(
        lambda *refs: stack_kernel(stack_order, lo, 2 * units, *refs),
        "stack",
        [((half - 1, 2 * units * lo, HD), bf16)],
        [vmem] * (half - 1) + [hbm],
        0,
    )(*[cots[m] for m in stack_order], same)
    cot_swapped = swap_plane(cot_rest, 0)
    x_same, y_cross = swap(same, 2), swap(cross, 4 ^ 1)
    y_same, x_cross = swap(same, 4), swap(cross, 2 ^ 1)
    far_same, far_cross = swap(x_same, 4), swap(y_cross, 2)
    (late_cross,) = call(late_kernel, "late", [head_shape], [vmem] + [hbm] * 2, 0)(cross, x_cross, y_same)
    c_cross = swap(late_cross, 1)

    turned_own, turned_other = call(
        lambda *refs: turn_kernel(lo, clip_rows, stack_order, *refs),
        "turn",
        [((cols, half * cot_rows), bf16)] * 2,
        [vmem] * (half + 1),
        0,
        (pltpu.VMEM((half, cot_rows, 2 * cols), bf16),),
    )(cots[0], *[cots[m] for m in stack_order], cot_swapped)

    def grad(turned, heads, dtype, name, behind=()):
        (out,) = call(
            lambda *refs: grad_kernel(rows, half, len(heads), *refs),
            name,
            [((cols, len(heads) * HD), dtype)],
            [vmem] * (1 + len(heads)) + [hbm] * len(behind),
            2 * cols * half * cot_rows * len(heads) * HD,
        )(turned, *heads, *behind)
        return out

    near, near_bits = [same, x_cross, y_same, x_same, y_cross], [0, 3, 4, 2, 5]
    far, far_bits = [c_cross, far_same, far_cross], [1, 6, 7]
    whole = [((tok, width), bf16), ((cols, width), jnp.float32)]
    got_near = swap(grad(turned_other, near, bf16, "grad_other_near"), 1)
    own_near = grad(turned_own, near, jnp.float32, "grad_own_near")
    got_far = swap(grad(turned_other, far, bf16, "grad_other_far", (own_near,)), 1)
    own_far = grad(turned_own, far, jnp.float32, "grad_own_far")
    halfway = call(
        lambda *refs: near_kernel(tok, near_bits, *refs),
        "near",
        whole,
        [vmem] * (2 + len(near)),
        0,
        (pltpu.VMEM((4, cols, HD), jnp.float32), pltpu.SemaphoreType.DMA((9,))),
        out_spec=hbm,
    )(own_near, got_near, *near)
    return call(
        lambda *refs: last_kernel(tok, near_bits, far_bits, *refs),
        "last",
        whole,
        [vmem] * (4 + len(far)) + [hbm] * 2,
        0,
        (pltpu.VMEM((4, cols, HD), jnp.float32), pltpu.SemaphoreType.DMA((7,))),
        out_spec=hbm,
        aliases={4 + len(far): 0, 5 + len(far): 1},
    )(own_near, got_near, own_far, got_far, *far, *halfway)


def body(query_rows, key_rows, value_rows, frame_counts, history, offsets, cotangent):
    n = lax.axis_size("tm")
    tok, width = query_rows.shape
    by_heads = (
        n == 8
        and lax.axis_size("head") % 2 == 0
        and width == n * HD
        and offsets.shape[1] == n
        and cotangent.shape[0] == tok + n * history.shape[0]
        and cotangent.shape[1] % (n * HD) == 0
        and tok % 16 == 0
        and (n * history.shape[0]) % 16 == 0
    )
    plan = head_body if by_heads else window_body
    return plan(query_rows, key_rows, value_rows, frame_counts, history, offsets, cotangent)


def solution(mesh):
    in_specs = (
        P("tm", "head"),
        P("tm", "head"),
        P("tm", "head"),
        P(),
        P("tm", "head"),
        P("tm", None),
        P("tm", None),
    )
    out_specs = (P("tm", "head"), P("tm", "head"))
    return jax.shard_map(body, mesh=mesh, in_specs=in_specs, out_specs=out_specs, check_vma=False)
```

```python
import math

import jax
import jax.numpy as jnp
from jax import lax
from jax.experimental import pallas as pl
from jax.experimental.pallas import tpu as pltpu
from jax.sharding import PartitionSpec as P

HD = 128
TPF = 64
WINB = 4
VMEM_LIMIT = 24 * 1024 * 1024
PACK_LIMIT = 58 * 1024 * 1024


def from_behind(x, axis, by):
    devices = lax.axis_size(axis)
    pairs = [(i, i + by) for i in range(devices) if 0 <= i + by < devices]
    return lax.ppermute(x, axis, pairs)


def window_body(query_rows, key_rows, value_rows, frame_counts, history, offsets, cotangent):
    tok_rows, feat_width = query_rows.shape
    local_heads = feat_width // HD
    block_total = lax.axis_size("tm")
    own_block = lax.axis_index("tm")
    score_scale = 1.0 / math.sqrt(HD)
    key_value = jnp.stack([key_rows, value_rows])
    pieces = []
    for distance in range(WINB - 1, 0, -1):
        pieces.append(from_behind(key_value, "tm", distance))
    window = jnp.concatenate(pieces + [key_value], axis=1)
    source_block = own_block - (WINB - 1) + jnp.arange(WINB, dtype=jnp.int32)
    block_match = jnp.arange(block_total, dtype=jnp.int32)[None, :] == source_block[:, None]
    block_count = jnp.sum(jnp.where(block_match, frame_counts[None, :], 0), axis=1)
    frame_index = jnp.arange(tok_rows, dtype=jnp.int32) // TPF
    kept_mask = (
        (source_block[:, None] >= 0) & (frame_index[None, :] < block_count[:, None])
    ).reshape(WINB * tok_rows)
    key_window = window[0].reshape(WINB * tok_rows, local_heads, HD)
    value_window = window[1].reshape(WINB * tok_rows, local_heads, HD)
    query_heads = query_rows.reshape(tok_rows, local_heads, HD)
    scores = (
        jnp.einsum("qhd,khd->hqk", query_heads, key_window, preferred_element_type=jnp.float32)
        * score_scale
    )
    scores = jnp.where(kept_mask[None, None, :], scores, -jnp.inf)
    row_max = jnp.max(scores, axis=-1, keepdims=True)
    weights = jnp.exp(scores - row_max)
    probs = (weights / jnp.sum(weights, axis=-1, keepdims=True)).astype(jnp.bfloat16)
    mixed = jnp.einsum("hqk,khd->qhd", probs, value_window, preferred_element_type=jnp.float32)
    attended = mixed.astype(jnp.bfloat16).reshape(tok_rows, feat_width)
    tile_rows = history.shape[0]
    source_tile = (own_block - offsets[0]) % block_total
    source_row = (
        source_tile[:, None] * tile_rows + jnp.arange(tile_rows, dtype=jnp.int32)[None, :]
    ).reshape(-1)
    incoming = lax.all_gather(history, "tm", axis=0, tiled=True)
    piece_rows = incoming.shape[0]
    selector = (source_row[:, None] == jnp.arange(piece_rows, dtype=jnp.int32)[None, :]).astype(
        jnp.bfloat16
    )
    clip_hist = jnp.dot(selector, incoming, preferred_element_type=jnp.float32).astype(jnp.bfloat16)
    disc_clip = jnp.concatenate([clip_hist, attended], axis=0)
    disc_grad = lax.psum_scatter(
        lax.dot_general(
            cotangent, disc_clip, (((0,), (0,)), ((), ())), preferred_element_type=jnp.float32
        ),
        "tm",
        scatter_dimension=0,
        tiled=True,
    )
    return (attended, disc_grad)


def chip_bits(m, side):
    return m if m in (0, 3) else jnp.where(side == 0, m, 3 - m)


def cot_kernel(n, tile, lo, off_hbm, cot_hbm, *refs):
    outs, (off, cot, sems) = refs[-3 - n // 2 : -3], refs[-3:]
    own = lax.axis_index("tm")
    chip, side = own // 2, lax.rem(own, 2)
    plane = lax.rem(lax.axis_index("head"), 2)
    clip_rows = n * tile
    all_rows, all_cols = cot.shape
    cols = all_cols // n
    part = all_rows - lo
    low = pl.multiple_of(plane * lo, 16)
    fetch_off = pltpu.make_async_copy(off_hbm, off, sems.at[0])
    fetch_cot = pltpu.make_async_copy(cot_hbm, cot, sems.at[1])
    fetch_off.start()
    fetch_cot.start()
    fetch_off.wait()
    r = lax.broadcasted_iota(jnp.int32, (clip_rows, clip_rows), 0)
    c = lax.broadcasted_iota(jnp.int32, (clip_rows, clip_rows), 1)
    select = jnp.zeros((clip_rows, clip_rows), jnp.float32)
    for j in range(n):
        src = lax.rem(own - off[0, j] + 2 * n, n)
        for t in range(tile):
            select = jnp.where((c == j * tile + t) & (r == src * tile + t), 1.0, select)
    fetch_cot.wait()
    cot[0:clip_rows, :] = jnp.dot(
        select.astype(jnp.bfloat16), cot[0:clip_rows, :], preferred_element_type=jnp.float32
    ).astype(jnp.bfloat16)
    units = cols // HD
    for m, out_ref in enumerate(outs):
        rows, first = (part, low) if m else (all_rows, 0)
        there = chip ^ chip_bits(m, side)
        for i, block in enumerate((2 * there + side, 2 * there + 1 - side)):
            for u in range(units):
                at = (i * units + u) * rows
                lanes = pl.ds(pl.multiple_of(block * cols + u * HD, HD), HD)
                out_ref[at : at + rows, :] = cot[pl.ds(first, rows), lanes]


def pack_kernel(n, heads, q_hbm, k_hbm, v_hbm, hist_hbm, *refs):
    outs, (q, k, v, hist, sems) = refs[:-5], refs[-5:]
    own = lax.axis_index("tm")
    tok, width = q.shape
    tile = hist.shape[0]
    clip_rows = n * tile
    start = 0 if width == n * HD else pl.multiple_of(((own ^ heads[0]) // 2) * width, width)
    pairs = [(hist_hbm, hist)] + [
        (x.at[:, pl.ds(start, width)], y) for x, y in ((q_hbm, q), (k_hbm, k), (v_hbm, v))
    ]
    copies = [pltpu.make_async_copy(a, b, sems.at[i]) for i, (a, b) in enumerate(pairs)]
    for copy in copies:
        copy.start()
    copies[0].wait()
    for d, out_ref in zip(heads, outs):
        lanes = pl.ds(pl.multiple_of((own ^ d) * HD, HD), HD)
        tiles = hist[:, lanes].astype(jnp.float32)
        row = lax.broadcasted_iota(jnp.int32, (clip_rows, HD), 0)
        placed = jnp.zeros((clip_rows, HD), jnp.float32)
        for t in range(tile):
            placed = jnp.where(row == own * tile + t, tiles[t : t + 1, :], placed)
        out_ref[3 * tok : 3 * tok + clip_rows, :] = placed.astype(jnp.bfloat16)
    for i, x in enumerate((q, k, v)):
        copies[1 + i].wait()
        for d, out_ref in zip(heads, outs):
            lanes = pl.ds(pl.multiple_of((own ^ d) * HD - start, HD), HD)
            out_ref[i * tok : (i + 1) * tok, :] = x[:, lanes]


def attend_kernel(n, tok, order, counts_hbm, *refs):
    parts, (same_ref, cross_ref, x_ref, mixed_ref, counts, sem) = refs[:n], refs[n:]
    copy = pltpu.make_async_copy(counts_hbm, counts, sem)
    copy.start()
    own = lax.axis_index("tm")
    side = lax.rem(own, 2)
    for k, part in zip(order, parts):
        x_ref[own ^ k] = part[...]
    copy.wait()
    rate = math.log2(math.e) / math.sqrt(HD)
    token = lax.broadcasted_iota(jnp.int32, (tok, 1), 0)
    bias = [
        jnp.where(token < counts[s] * TPF, 0.0, -jnp.inf).astype(jnp.float32) for s in range(n)
    ]
    values = [x_ref[s, 2 * tok : 3 * tok, :].T for s in range(n)]
    for block in range(n):
        sources = range(max(0, block - (WINB - 1)), block + 1)
        q = x_ref[block, 0:tok, :]
        scores = [
            lax.dot_general(
                x_ref[s, tok : 2 * tok, :],
                q,
                (((1,), (1,)), ((), ())),
                preferred_element_type=jnp.float32,
            )
            + bias[s]
            for s in sources
        ]
        top = jnp.max(scores[0], axis=0, keepdims=True)
        for s in scores[1:]:
            top = jnp.maximum(top, jnp.max(s, axis=0, keepdims=True))
        weights = [jnp.exp2((s - top) * rate) for s in scores]
        total = jnp.sum(weights[0], axis=0, keepdims=True)
        for w in weights[1:]:
            total = total + jnp.sum(w, axis=0, keepdims=True)
        share = 1.0 / total
        mixed = jnp.zeros((HD, tok), jnp.float32)
        for s, w in zip(sources, weights):
            mixed = mixed + jnp.dot(
                values[s], (w * share).astype(jnp.bfloat16), preferred_element_type=jnp.float32
            )
        mixed_ref[block] = mixed.astype(jnp.bfloat16).T
    rows = n // 2 * tok
    clip_rows = same_ref.shape[0] - rows
    hist = jnp.zeros((clip_rows, HD), jnp.float32)
    for s in range(n):
        hist = hist + x_ref[s, 3 * tok : 3 * tok + clip_rows, :].astype(jnp.float32)
    hist = hist.astype(jnp.bfloat16)
    for flip, out_ref in ((0, same_ref), (1, cross_ref)):
        for i in range(n // 2):
            out_ref[i * tok : (i + 1) * tok, :] = mixed_ref[2 * i + (side ^ flip)]
        out_ref[rows:, :] = hist


def stack_kernel(order, lo, tiles, *refs):
    out_ref = refs[-1]
    plane = lax.rem(lax.axis_index("head"), 2)
    for m, ref in zip(order, refs):
        part = ref.shape[0] // tiles
        for u in range(tiles):
            first = pl.multiple_of(u * part + plane * (part - lo), 16)
            out_ref[m - 1, u * lo : (u + 1) * lo, :] = ref[pl.ds(first, lo), :]


def late_kernel(x_ref, *refs):
    refs[-1][...] = x_ref[...]


def turn_kernel(lo, clip_rows, order, own_in, *refs):
    pieces, (swapped_ref, own_ref, other_ref, whole) = refs[:-4], refs[-4:]
    plane = lax.rem(lax.axis_index("head"), 2)
    own = lax.axis_index("tm")
    chip, side = own // 2, lax.rem(own, 2)
    chips, all_rows, width = whole.shape
    part = all_rows - lo
    for u in range(width // HD):
        lanes = slice(u * HD, (u + 1) * HD)
        whole[0, :, lanes] = own_in[u * all_rows : (u + 1) * all_rows, :]
        for m, ref in zip(order, pieces):
            at = chip_bits(m, side)
            a = ref[u * part : (u + 1) * part, :]
            b = swapped_ref[m - 1, u * lo : (u + 1) * lo, :]
            whole[at, 0:lo, lanes] = jnp.where(plane == 0, a[:lo], b)
            whole[at, lo:part, lanes] = jnp.where(plane == 0, a[lo:], a[: part - lo])
            whole[at, part:all_rows, lanes] = jnp.where(plane == 0, b, a[part - lo :])
    for i, out_ref in enumerate((own_ref, other_ref)):
        lanes = slice(i * width // 2, (i + 1) * width // 2)
        rows = [whole[chip ^ c, clip_rows:all_rows, lanes] for c in range(chips)]
        rows += [whole[chip ^ c, 0:clip_rows, lanes] for c in range(chips)]
        out_ref[...] = jnp.concatenate(rows, axis=0).T


def grad_part(turned_ref, head_refs, rows, copies):
    right = jnp.concatenate([x[0:rows, :] for x in head_refs], axis=1)
    hist = jnp.concatenate([x[rows:, :] for x in head_refs], axis=1)
    clip = copies * hist.shape[0]
    out = jnp.dot(turned_ref[:, 0:rows], right, preferred_element_type=jnp.float32)
    return out + jnp.dot(
        turned_ref[:, rows : rows + clip],
        jnp.concatenate([hist] * copies, axis=0),
        preferred_element_type=jnp.float32,
    )


def grad_kernel(rows, copies, heads, turned_ref, *refs):
    out_ref = refs[-1]
    out_ref[...] = grad_part(turned_ref, refs[:heads], rows, copies).astype(out_ref.dtype)


NEAR = ((0, 0), (3, 5), (4, 2), (2, 4), (5, 3))
FAR = ((1, 1), (6, 6), (7, 7))
THERE = (5, 2, 1, 4, 3, 0, 7, 6)


def store_columns(tok, heads, sums, att_hbm, out_hbm, total, sems):
    own = lax.axis_index("tm")
    side = lax.rem(own, 2)
    at = pl.multiple_of(own // 2 * tok, tok)
    moves = []

    def move(a, b):
        moves.append(pltpu.make_async_copy(a, b, sems.at[len(moves)]))
        moves[-1].start()

    def lanes(bits):
        return pl.ds(pl.multiple_of((own ^ jnp.where(side == 0, *bits)) * HD, HD), HD)

    for bits, ref in heads:
        move(ref.at[pl.ds(at, tok), :], att_hbm.at[:, lanes(bits)])
    for i, (bits, (mine, m), (got, g)) in enumerate(sums):
        columns = got[:, g * HD : (g + 1) * HD].astype(jnp.float32)
        total[i] = mine[:, m * HD : (m + 1) * HD] + columns
        move(total.at[i], out_hbm.at[:, lanes(bits)])
    for x in moves:
        x.wait()


def near_kernel(tok, own_near, got_near, *refs):
    n = len(NEAR)
    heads, outs = refs[:n], refs[n:]
    sums = [(NEAR[i], (own_near, i), (got_near, THERE[i])) for i in range(n) if THERE[i] < n]
    store_columns(tok, zip(NEAR, heads), sums, *outs)


def last_kernel(tok, own_near, got_near, own_far, got_far, *refs):
    n = len(NEAR)
    heads, outs = refs[: len(FAR)], refs[len(FAR) + 2 :]

    def column(near, far, i):
        return (near, i) if i < n else (far, i - n)

    sums = [
        (bits, column(own_near, own_far, i), column(got_near, got_far, THERE[i]))
        for i, bits in enumerate(NEAR + FAR)
        if i >= n or THERE[i] >= n
    ]
    store_columns(tok, zip(FAR, heads), sums, *outs)


def head_body(query_rows, key_rows, value_rows, frame_counts, history, offsets, cotangent):
    n = lax.axis_size("tm")
    planes = lax.axis_size("head")
    half = n // 2
    tok, width = query_rows.shape
    tile = history.shape[0]
    clip_rows = n * tile
    cot_rows, all_cols = cotangent.shape
    cols = all_cols // n
    units = cols // HD
    lo = cot_rows * 7 // 17 // 16 * 16
    part = cot_rows - lo
    base = 3 * tok + clip_rows
    length = base
    rows = half * tok
    vmem = pl.BlockSpec(memory_space=pltpu.VMEM)
    hbm = pl.BlockSpec(memory_space=pl.ANY)
    bf16 = jnp.bfloat16

    def swap(x, even, odd=None):
        bits = (even, even if odd is None else odd)
        return lax.ppermute(x, "tm", [(i, i ^ bits[i % 2]) for i in range(n)])

    def swap_plane(x, bit):
        pairs = [
            (i * planes + p, (i ^ bit) * planes + (p ^ 1)) for i in range(n) for p in range(planes)
        ]
        return lax.ppermute(x, ("tm", "head"), pairs)

    def call(
        kernel, name, outs, specs, flops, scratch=(), exps=0, out_spec=vmem, limit=VMEM_LIMIT, aliases={}
    ):
        shapes = [jax.ShapeDtypeStruct(s, d) for s, d in outs]
        moved = 2 * sum(math.prod(s.shape) * s.dtype.itemsize for s in shapes)
        return pl.pallas_call(
            kernel,
            out_shape=tuple(shapes),
            in_specs=specs,
            out_specs=tuple([out_spec] * len(shapes)),
            scratch_shapes=scratch,
            input_output_aliases=aliases,
            compiler_params=pltpu.CompilerParams(vmem_limit_bytes=limit),
            cost_estimate=pl.CostEstimate(flops=flops, bytes_accessed=moved, transcendentals=exps),
            name=name,
        )

    def pack(heads, lanes, name):
        return call(
            lambda *refs: pack_kernel(n, heads, *refs),
            name,
            [((length, HD), bf16)] * len(heads),
            [hbm] * 4,
            0,
            (
                pltpu.VMEM((tok, lanes), bf16),
                pltpu.VMEM((tok, lanes), bf16),
                pltpu.VMEM((tok, lanes), bf16),
                pltpu.VMEM(history.shape, bf16),
                pltpu.SemaphoreType.DMA((4,)),
            ),
            limit=PACK_LIMIT,
        )(query_rows, key_rows, value_rows, history)

    first, rest = [6, 7], [0, 1, 2, 3, 4, 5]
    packed = dict(zip(first, pack(first, 2 * HD, "pack_first")))
    packed.update(zip(rest, pack(rest, width, "pack_rest")))
    order = [6, 7, 2, 4, 3, 5, 1]
    arrived = {k: swap(packed[k], k) for k in order}
    by_head = [packed[0]] + [arrived[k] for k in order]
    chips = range(half)
    cots = call(
        lambda *refs: cot_kernel(n, tile, lo, *refs),
        "cot",
        [((2 * units * cot_rows, HD), bf16)] + [((2 * units * part, HD), bf16)] * (half - 1),
        [hbm] * 4,
        0,
        (
            pltpu.SMEM(offsets.shape, jnp.int32),
            pltpu.VMEM(cotangent.shape, bf16),
            pltpu.SemaphoreType.DMA((2,)),
        ),
    )(offsets, cotangent, arrived[6], arrived[7])
    cots = [cots[0], swap(cots[1], 2, 4), swap(cots[2], 4, 2), swap(cots[3], 6)]
    counts = (
        pltpu.VMEM((n, length, HD), bf16),
        pltpu.VMEM((n, tok, HD), bf16),
        pltpu.SMEM(frame_counts.shape, jnp.int32),
        pltpu.SemaphoreType.DMA,
    )
    pairs = half * tok * WINB * tok
    head_shape = ((rows + clip_rows, HD), bf16)
    same, cross = call(
        lambda *refs: attend_kernel(n, tok, [0] + order, *refs),
        "attend",
        [head_shape, head_shape],
        [hbm] + [vmem] * n,
        8 * pairs * HD,
        counts,
        2 * pairs,
    )(frame_counts, *by_head)
    stack_order = [3, 1, 2]
    (cot_rest,) = call(
        lambda *refs: stack_kernel(stack_order, lo, 2 * units, *refs),
        "stack",
        [((half - 1, 2 * units * lo, HD), bf16)],
        [vmem] * (half - 1) + [hbm],
        0,
    )(*[cots[m] for m in stack_order], same)
    cot_swapped = swap_plane(cot_rest, 0)
    first_same, first_cross = swap(same, 2, 4), swap(cross, 3, 5)
    second_same, second_cross = swap(same, 4, 2), swap(cross, 5, 3)
    far_same, far_cross = swap(first_same, 4, 2), swap(first_cross, 2, 4)
    (late_cross,) = call(late_kernel, "late", [head_shape], [vmem] + [hbm] * 2, 0)(
        cross, second_cross, second_same
    )
    c_cross = swap(late_cross, 1)

    turned_own, turned_other = call(
        lambda *refs: turn_kernel(lo, clip_rows, stack_order, *refs),
        "turn",
        [((cols, half * cot_rows), bf16)] * 2,
        [vmem] * (half + 1),
        0,
        (pltpu.VMEM((half, cot_rows, 2 * cols), bf16),),
    )(cots[0], *[cots[m] for m in stack_order], cot_swapped)

    def grad(turned, heads, dtype, name, behind=()):
        (out,) = call(
            lambda *refs: grad_kernel(rows, half, len(heads), *refs),
            name,
            [((cols, len(heads) * HD), dtype)],
            [vmem] * (1 + len(heads)) + [hbm] * len(behind),
            2 * cols * half * cot_rows * len(heads) * HD,
        )(turned, *heads, *behind)
        return out

    near = [same, second_cross, second_same, first_same, first_cross]
    far = [c_cross, far_same, far_cross]
    whole = [((tok, width), bf16), ((cols, width), jnp.float32)]
    got_near = swap(grad(turned_other, near, bf16, "grad_other_near"), 1)
    own_near = grad(turned_own, near, jnp.float32, "grad_own_near")
    got_far = swap(grad(turned_other, far, bf16, "grad_other_far", (own_near,)), 1)
    own_far = grad(turned_own, far, jnp.float32, "grad_own_far")
    halfway = call(
        lambda *refs: near_kernel(tok, *refs),
        "near",
        whole,
        [vmem] * (2 + len(near)),
        0,
        (pltpu.VMEM((4, cols, HD), jnp.float32), pltpu.SemaphoreType.DMA((9,))),
        out_spec=hbm,
    )(own_near, got_near, *near)
    return call(
        lambda *refs: last_kernel(tok, *refs),
        "last",
        whole,
        [vmem] * (4 + len(far)) + [hbm] * 2,
        0,
        (pltpu.VMEM((4, cols, HD), jnp.float32), pltpu.SemaphoreType.DMA((7,))),
        out_spec=hbm,
        aliases={4 + len(far): 0, 5 + len(far): 1},
    )(own_near, got_near, own_far, got_far, *far, *halfway)


def body(query_rows, key_rows, value_rows, frame_counts, history, offsets, cotangent):
    n = lax.axis_size("tm")
    tok, width = query_rows.shape
    by_heads = (
        n == 8
        and lax.axis_size("head") % 2 == 0
        and width == n * HD
        and offsets.shape[1] == n
        and cotangent.shape[0] == tok + n * history.shape[0]
        and cotangent.shape[1] % (n * HD) == 0
        and tok % 16 == 0
        and (n * history.shape[0]) % 16 == 0
    )
    plan = head_body if by_heads else window_body
    return plan(query_rows, key_rows, value_rows, frame_counts, history, offsets, cotangent)


def solution(mesh):
    in_specs = (
        P("tm", "head"),
        P("tm", "head"),
        P("tm", "head"),
        P(),
        P("tm", "head"),
        P("tm", None),
        P("tm", None),
    )
    out_specs = (P("tm", "head"), P("tm", "head"))
    return jax.shard_map(body, mesh=mesh, in_specs=in_specs, out_specs=out_specs, check_vma=False)
```

```python
import math

import jax
import jax.numpy as jnp
from jax import lax
from jax.experimental import pallas as pl
from jax.experimental.pallas import tpu as pltpu
from jax.sharding import PartitionSpec as P

HD = 128
TPF = 64
WINB = 4
VMEM_LIMIT = 24 * 1024 * 1024
PACK_LIMIT = 58 * 1024 * 1024


def from_behind(x, axis, by):
    devices = lax.axis_size(axis)
    pairs = [(i, i + by) for i in range(devices) if 0 <= i + by < devices]
    return lax.ppermute(x, axis, pairs)


def window_body(query_rows, key_rows, value_rows, frame_counts, history, offsets, cotangent):
    tok_rows, feat_width = query_rows.shape
    local_heads = feat_width // HD
    block_total = lax.axis_size("tm")
    own_block = lax.axis_index("tm")
    score_scale = 1.0 / math.sqrt(HD)
    key_value = jnp.stack([key_rows, value_rows])
    pieces = []
    for distance in range(WINB - 1, 0, -1):
        pieces.append(from_behind(key_value, "tm", distance))
    window = jnp.concatenate(pieces + [key_value], axis=1)
    source_block = own_block - (WINB - 1) + jnp.arange(WINB, dtype=jnp.int32)
    block_match = jnp.arange(block_total, dtype=jnp.int32)[None, :] == source_block[:, None]
    block_count = jnp.sum(jnp.where(block_match, frame_counts[None, :], 0), axis=1)
    frame_index = jnp.arange(tok_rows, dtype=jnp.int32) // TPF
    kept_mask = (
        (source_block[:, None] >= 0) & (frame_index[None, :] < block_count[:, None])
    ).reshape(WINB * tok_rows)
    key_window = window[0].reshape(WINB * tok_rows, local_heads, HD)
    value_window = window[1].reshape(WINB * tok_rows, local_heads, HD)
    query_heads = query_rows.reshape(tok_rows, local_heads, HD)
    scores = (
        jnp.einsum("qhd,khd->hqk", query_heads, key_window, preferred_element_type=jnp.float32)
        * score_scale
    )
    scores = jnp.where(kept_mask[None, None, :], scores, -jnp.inf)
    row_max = jnp.max(scores, axis=-1, keepdims=True)
    weights = jnp.exp(scores - row_max)
    probs = (weights / jnp.sum(weights, axis=-1, keepdims=True)).astype(jnp.bfloat16)
    mixed = jnp.einsum("hqk,khd->qhd", probs, value_window, preferred_element_type=jnp.float32)
    attended = mixed.astype(jnp.bfloat16).reshape(tok_rows, feat_width)
    tile_rows = history.shape[0]
    source_tile = (own_block - offsets[0]) % block_total
    source_row = (
        source_tile[:, None] * tile_rows + jnp.arange(tile_rows, dtype=jnp.int32)[None, :]
    ).reshape(-1)
    incoming = lax.all_gather(history, "tm", axis=0, tiled=True)
    piece_rows = incoming.shape[0]
    selector = (source_row[:, None] == jnp.arange(piece_rows, dtype=jnp.int32)[None, :]).astype(
        jnp.bfloat16
    )
    clip_hist = jnp.dot(selector, incoming, preferred_element_type=jnp.float32).astype(jnp.bfloat16)
    disc_clip = jnp.concatenate([clip_hist, attended], axis=0)
    disc_grad = lax.psum_scatter(
        lax.dot_general(
            cotangent, disc_clip, (((0,), (0,)), ((), ())), preferred_element_type=jnp.float32
        ),
        "tm",
        scatter_dimension=0,
        tiled=True,
    )
    return (attended, disc_grad)


def chip_bits(m, side):
    return m if m in (0, 3) else jnp.where(side == 0, m, 3 - m)


def cot_kernel(n, tile, lo, off_hbm, cot_hbm, *refs):
    outs, (off, cot, sems) = refs[-3 - n // 2 : -3], refs[-3:]
    own = lax.axis_index("tm")
    chip, side = own // 2, lax.rem(own, 2)
    plane = lax.rem(lax.axis_index("head"), 2)
    clip_rows = n * tile
    all_rows, all_cols = cot.shape
    cols = all_cols // n
    part = all_rows - lo
    low = pl.multiple_of(plane * lo, 16)
    fetch_off = pltpu.make_async_copy(off_hbm, off, sems.at[0])
    fetch_cot = pltpu.make_async_copy(cot_hbm, cot, sems.at[1])
    fetch_off.start()
    fetch_cot.start()
    fetch_off.wait()
    r = lax.broadcasted_iota(jnp.int32, (clip_rows, clip_rows), 0)
    c = lax.broadcasted_iota(jnp.int32, (clip_rows, clip_rows), 1)
    select = jnp.zeros((clip_rows, clip_rows), jnp.float32)
    for j in range(n):
        src = lax.rem(own - off[0, j] + 2 * n, n)
        for t in range(tile):
            select = jnp.where((c == j * tile + t) & (r == src * tile + t), 1.0, select)
    fetch_cot.wait()
    cot[0:clip_rows, :] = jnp.dot(
        select.astype(jnp.bfloat16), cot[0:clip_rows, :], preferred_element_type=jnp.float32
    ).astype(jnp.bfloat16)
    units = cols // HD
    for m, out_ref in enumerate(outs):
        rows, first = (part, low) if m else (all_rows, 0)
        there = chip ^ chip_bits(m, side)
        for i, block in enumerate((2 * there + side, 2 * there + 1 - side)):
            for u in range(units):
                at = (i * units + u) * rows
                lanes = pl.ds(pl.multiple_of(block * cols + u * HD, HD), HD)
                out_ref[at : at + rows, :] = cot[pl.ds(first, rows), lanes]


def pack_kernel(n, heads, q_hbm, k_hbm, v_hbm, hist_hbm, *refs):
    outs, (q, k, v, hist, sems) = refs[:-5], refs[-5:]
    own = lax.axis_index("tm")
    tok, width = q.shape
    tile = hist.shape[0]
    clip_rows = n * tile
    start = 0 if width == n * HD else pl.multiple_of(((own ^ heads[0]) // 2) * width, width)
    pairs = [(hist_hbm, hist)] + [
        (x.at[:, pl.ds(start, width)], y) for x, y in ((q_hbm, q), (k_hbm, k), (v_hbm, v))
    ]
    copies = [pltpu.make_async_copy(a, b, sems.at[i]) for i, (a, b) in enumerate(pairs)]
    for copy in copies:
        copy.start()
    copies[0].wait()
    for d, out_ref in zip(heads, outs):
        lanes = pl.ds(pl.multiple_of((own ^ d) * HD, HD), HD)
        tiles = hist[:, lanes].astype(jnp.float32)
        row = lax.broadcasted_iota(jnp.int32, (clip_rows, HD), 0)
        placed = jnp.zeros((clip_rows, HD), jnp.float32)
        for t in range(tile):
            placed = jnp.where(row == own * tile + t, tiles[t : t + 1, :], placed)
        out_ref[3 * tok : 3 * tok + clip_rows, :] = placed.astype(jnp.bfloat16)
    for i, x in enumerate((q, k, v)):
        copies[1 + i].wait()
        for d, out_ref in zip(heads, outs):
            lanes = pl.ds(pl.multiple_of((own ^ d) * HD - start, HD), HD)
            out_ref[i * tok : (i + 1) * tok, :] = x[:, lanes]


def attend_kernel(n, tok, order, counts_hbm, *refs):
    parts, (same_ref, cross_ref, x_ref, mixed_ref, counts, sem) = refs[:n], refs[n:]
    copy = pltpu.make_async_copy(counts_hbm, counts, sem)
    copy.start()
    own = lax.axis_index("tm")
    side = lax.rem(own, 2)
    for k, part in zip(order, parts):
        x_ref[own ^ k] = part[...]
    copy.wait()
    rate = math.log2(math.e) / math.sqrt(HD)
    token = lax.broadcasted_iota(jnp.int32, (tok, 1), 0)
    bias = [
        jnp.where(token < counts[s] * TPF, 0.0, -jnp.inf).astype(jnp.float32) for s in range(n)
    ]
    values = [x_ref[s, 2 * tok : 3 * tok, :].T for s in range(n)]
    for block in range(n):
        sources = range(max(0, block - (WINB - 1)), block + 1)
        q = x_ref[block, 0:tok, :]
        scores = [
            lax.dot_general(
                x_ref[s, tok : 2 * tok, :],
                q,
                (((1,), (1,)), ((), ())),
                preferred_element_type=jnp.float32,
            )
            * rate
            + bias[s]
            for s in sources
        ]
        top = jnp.max(scores[0], axis=0, keepdims=True)
        for s in scores[1:]:
            top = jnp.maximum(top, jnp.max(s, axis=0, keepdims=True))
        total = jnp.zeros((1, tok), jnp.float32)
        for s in scores:
            total = total + jnp.sum(jnp.exp2(s - top), axis=0, keepdims=True)
        level = top + jnp.log2(total)
        mixed = jnp.zeros((HD, tok), jnp.float32)
        for i, s in zip(sources, scores):
            mixed = mixed + jnp.dot(
                values[i], jnp.exp2(s - level).astype(jnp.bfloat16), preferred_element_type=jnp.float32
            )
        mixed_ref[block] = mixed.astype(jnp.bfloat16).T
    rows = n // 2 * tok
    clip_rows = same_ref.shape[0] - rows
    hist = jnp.zeros((clip_rows, HD), jnp.float32)
    for s in range(n):
        hist = hist + x_ref[s, 3 * tok : 3 * tok + clip_rows, :].astype(jnp.float32)
    hist = hist.astype(jnp.bfloat16)
    for flip, out_ref in ((0, same_ref), (1, cross_ref)):
        for i in range(n // 2):
            out_ref[i * tok : (i + 1) * tok, :] = mixed_ref[2 * i + (side ^ flip)]
        out_ref[rows:, :] = hist


def stack_kernel(order, lo, tiles, *refs):
    out_ref = refs[-1]
    plane = lax.rem(lax.axis_index("head"), 2)
    for m, ref in zip(order, refs):
        part = ref.shape[0] // tiles
        for u in range(tiles):
            first = pl.multiple_of(u * part + plane * (part - lo), 16)
            out_ref[m - 1, u * lo : (u + 1) * lo, :] = ref[pl.ds(first, lo), :]


def late_kernel(x_ref, *refs):
    refs[-1][...] = x_ref[...]


def turn_kernel(lo, clip_rows, order, own_in, *refs):
    pieces, (swapped_ref, own_ref, other_ref, whole) = refs[:-4], refs[-4:]
    plane = lax.rem(lax.axis_index("head"), 2)
    own = lax.axis_index("tm")
    chip, side = own // 2, lax.rem(own, 2)
    chips, all_rows, width = whole.shape
    part = all_rows - lo
    for u in range(width // HD):
        lanes = slice(u * HD, (u + 1) * HD)
        whole[0, :, lanes] = own_in[u * all_rows : (u + 1) * all_rows, :]
        for m, ref in zip(order, pieces):
            at = chip_bits(m, side)
            a = ref[u * part : (u + 1) * part, :]
            b = swapped_ref[m - 1, u * lo : (u + 1) * lo, :]
            whole[at, 0:lo, lanes] = jnp.where(plane == 0, a[:lo], b)
            whole[at, lo:part, lanes] = jnp.where(plane == 0, a[lo:], a[: part - lo])
            whole[at, part:all_rows, lanes] = jnp.where(plane == 0, b, a[part - lo :])
    for i, out_ref in enumerate((own_ref, other_ref)):
        lanes = slice(i * width // 2, (i + 1) * width // 2)
        rows = [whole[chip ^ c, clip_rows:all_rows, lanes] for c in range(chips)]
        rows += [whole[chip ^ c, 0:clip_rows, lanes] for c in range(chips)]
        out_ref[...] = jnp.concatenate(rows, axis=0).T


def grad_part(turned_ref, head_refs, rows, copies):
    right = jnp.concatenate([x[0:rows, :] for x in head_refs], axis=1)
    hist = jnp.concatenate([x[rows:, :] for x in head_refs], axis=1)
    clip = copies * hist.shape[0]
    out = jnp.dot(turned_ref[:, 0:rows], right, preferred_element_type=jnp.float32)
    return out + jnp.dot(
        turned_ref[:, rows : rows + clip],
        jnp.concatenate([hist] * copies, axis=0),
        preferred_element_type=jnp.float32,
    )


def grad_kernel(rows, copies, heads, turned_ref, *refs):
    out_ref = refs[-1]
    out_ref[...] = grad_part(turned_ref, refs[:heads], rows, copies).astype(out_ref.dtype)


NEAR = ((0, 0), (3, 5), (4, 2), (2, 4), (5, 3))
FAR = ((1, 1), (6, 6), (7, 7))
THERE = (5, 2, 1, 4, 3, 0, 7, 6)


def store_columns(tok, heads, sums, att_hbm, out_hbm, total, sems):
    own = lax.axis_index("tm")
    side = lax.rem(own, 2)
    at = pl.multiple_of(own // 2 * tok, tok)
    moves = []

    def move(a, b):
        moves.append(pltpu.make_async_copy(a, b, sems.at[len(moves)]))
        moves[-1].start()

    def lanes(bits):
        return pl.ds(pl.multiple_of((own ^ jnp.where(side == 0, *bits)) * HD, HD), HD)

    for bits, ref in heads:
        move(ref.at[pl.ds(at, tok), :], att_hbm.at[:, lanes(bits)])
    for i, (bits, (mine, m), (got, g)) in enumerate(sums):
        columns = got[:, g * HD : (g + 1) * HD].astype(jnp.float32)
        total[i] = mine[:, m * HD : (m + 1) * HD] + columns
        move(total.at[i], out_hbm.at[:, lanes(bits)])
    for x in moves:
        x.wait()


def near_kernel(tok, own_near, got_near, *refs):
    n = len(NEAR)
    heads, outs = refs[:n], refs[n:]
    sums = [(NEAR[i], (own_near, i), (got_near, THERE[i])) for i in range(n) if THERE[i] < n]
    store_columns(tok, zip(NEAR, heads), sums, *outs)


def last_kernel(tok, own_near, got_near, own_far, got_far, *refs):
    n = len(NEAR)
    heads, outs = refs[: len(FAR)], refs[len(FAR) + 2 :]

    def column(near, far, i):
        return (near, i) if i < n else (far, i - n)

    sums = [
        (bits, column(own_near, own_far, i), column(got_near, got_far, THERE[i]))
        for i, bits in enumerate(NEAR + FAR)
        if i >= n or THERE[i] >= n
    ]
    store_columns(tok, zip(FAR, heads), sums, *outs)


def head_body(query_rows, key_rows, value_rows, frame_counts, history, offsets, cotangent):
    n = lax.axis_size("tm")
    planes = lax.axis_size("head")
    half = n // 2
    tok, width = query_rows.shape
    tile = history.shape[0]
    clip_rows = n * tile
    cot_rows, all_cols = cotangent.shape
    cols = all_cols // n
    units = cols // HD
    lo = cot_rows * 7 // 17 // 16 * 16
    part = cot_rows - lo
    base = 3 * tok + clip_rows
    length = base
    rows = half * tok
    vmem = pl.BlockSpec(memory_space=pltpu.VMEM)
    hbm = pl.BlockSpec(memory_space=pl.ANY)
    bf16 = jnp.bfloat16

    def swap(x, even, odd=None):
        bits = (even, even if odd is None else odd)
        return lax.ppermute(x, "tm", [(i, i ^ bits[i % 2]) for i in range(n)])

    def swap_plane(x, bit):
        pairs = [
            (i * planes + p, (i ^ bit) * planes + (p ^ 1)) for i in range(n) for p in range(planes)
        ]
        return lax.ppermute(x, ("tm", "head"), pairs)

    def call(
        kernel, name, outs, specs, flops, scratch=(), exps=0, out_spec=vmem, limit=VMEM_LIMIT, aliases={}
    ):
        shapes = [jax.ShapeDtypeStruct(s, d) for s, d in outs]
        moved = 2 * sum(math.prod(s.shape) * s.dtype.itemsize for s in shapes)
        return pl.pallas_call(
            kernel,
            out_shape=tuple(shapes),
            in_specs=specs,
            out_specs=tuple([out_spec] * len(shapes)),
            scratch_shapes=scratch,
            input_output_aliases=aliases,
            compiler_params=pltpu.CompilerParams(vmem_limit_bytes=limit),
            cost_estimate=pl.CostEstimate(flops=flops, bytes_accessed=moved, transcendentals=exps),
            name=name,
        )

    def pack(heads, lanes, name):
        return call(
            lambda *refs: pack_kernel(n, heads, *refs),
            name,
            [((length, HD), bf16)] * len(heads),
            [hbm] * 4,
            0,
            (
                pltpu.VMEM((tok, lanes), bf16),
                pltpu.VMEM((tok, lanes), bf16),
                pltpu.VMEM((tok, lanes), bf16),
                pltpu.VMEM(history.shape, bf16),
                pltpu.SemaphoreType.DMA((4,)),
            ),
            limit=PACK_LIMIT,
        )(query_rows, key_rows, value_rows, history)

    first, rest = [6, 7], [0, 1, 2, 3, 4, 5]
    packed = dict(zip(first, pack(first, 2 * HD, "pack_first")))
    packed.update(zip(rest, pack(rest, width, "pack_rest")))
    order = [6, 7, 2, 4, 3, 5, 1]
    arrived = {k: swap(packed[k], k) for k in order}
    by_head = [packed[0]] + [arrived[k] for k in order]
    chips = range(half)
    cots = call(
        lambda *refs: cot_kernel(n, tile, lo, *refs),
        "cot",
        [((2 * units * cot_rows, HD), bf16)] + [((2 * units * part, HD), bf16)] * (half - 1),
        [hbm] * 4,
        0,
        (
            pltpu.SMEM(offsets.shape, jnp.int32),
            pltpu.VMEM(cotangent.shape, bf16),
            pltpu.SemaphoreType.DMA((2,)),
        ),
    )(offsets, cotangent, arrived[6], arrived[7])
    cots = [cots[0], swap(cots[1], 2, 4), swap(cots[2], 4, 2), swap(cots[3], 6)]
    counts = (
        pltpu.VMEM((n, length, HD), bf16),
        pltpu.VMEM((n, tok, HD), bf16),
        pltpu.SMEM(frame_counts.shape, jnp.int32),
        pltpu.SemaphoreType.DMA,
    )
    pairs = half * tok * WINB * tok
    head_shape = ((rows + clip_rows, HD), bf16)
    same, cross = call(
        lambda *refs: attend_kernel(n, tok, [0] + order, *refs),
        "attend",
        [head_shape, head_shape],
        [hbm] + [vmem] * n,
        8 * pairs * HD,
        counts,
        2 * pairs,
    )(frame_counts, *by_head)
    stack_order = [3, 1, 2]
    (cot_rest,) = call(
        lambda *refs: stack_kernel(stack_order, lo, 2 * units, *refs),
        "stack",
        [((half - 1, 2 * units * lo, HD), bf16)],
        [vmem] * (half - 1) + [hbm],
        0,
    )(*[cots[m] for m in stack_order], same)
    cot_swapped = swap_plane(cot_rest, 0)
    first_same, first_cross = swap(same, 2, 4), swap(cross, 3, 5)
    second_same, second_cross = swap(same, 4, 2), swap(cross, 5, 3)
    far_same, far_cross = swap(first_same, 4, 2), swap(first_cross, 2, 4)
    (late_cross,) = call(late_kernel, "late", [head_shape], [vmem] + [hbm] * 2, 0)(
        cross, second_cross, second_same
    )
    c_cross = swap(late_cross, 1)

    turned_own, turned_other = call(
        lambda *refs: turn_kernel(lo, clip_rows, stack_order, *refs),
        "turn",
        [((cols, half * cot_rows), bf16)] * 2,
        [vmem] * (half + 1),
        0,
        (pltpu.VMEM((half, cot_rows, 2 * cols), bf16),),
    )(cots[0], *[cots[m] for m in stack_order], cot_swapped)

    def grad(turned, heads, dtype, name, behind=()):
        (out,) = call(
            lambda *refs: grad_kernel(rows, half, len(heads), *refs),
            name,
            [((cols, len(heads) * HD), dtype)],
            [vmem] * (1 + len(heads)) + [hbm] * len(behind),
            2 * cols * half * cot_rows * len(heads) * HD,
        )(turned, *heads, *behind)
        return out

    near = [same, second_cross, second_same, first_same, first_cross]
    far = [c_cross, far_same, far_cross]
    whole = [((tok, width), bf16), ((cols, width), jnp.float32)]
    got_near = swap(grad(turned_other, near, bf16, "grad_other_near"), 1)
    own_near = grad(turned_own, near, jnp.float32, "grad_own_near")
    got_far = swap(grad(turned_other, far, bf16, "grad_other_far", (own_near,)), 1)
    own_far = grad(turned_own, far, jnp.float32, "grad_own_far")
    halfway = call(
        lambda *refs: near_kernel(tok, *refs),
        "near",
        whole,
        [vmem] * (2 + len(near)),
        0,
        (pltpu.VMEM((4, cols, HD), jnp.float32), pltpu.SemaphoreType.DMA((9,))),
        out_spec=hbm,
    )(own_near, got_near, *near)
    return call(
        lambda *refs: last_kernel(tok, *refs),
        "last",
        whole,
        [vmem] * (4 + len(far)) + [hbm] * 2,
        0,
        (pltpu.VMEM((4, cols, HD), jnp.float32), pltpu.SemaphoreType.DMA((7,))),
        out_spec=hbm,
        aliases={4 + len(far): 0, 5 + len(far): 1},
    )(own_near, got_near, own_far, got_far, *far, *halfway)


def body(query_rows, key_rows, value_rows, frame_counts, history, offsets, cotangent):
    n = lax.axis_size("tm")
    tok, width = query_rows.shape
    by_heads = (
        n == 8
        and lax.axis_size("head") % 2 == 0
        and width == n * HD
        and offsets.shape[1] == n
        and cotangent.shape[0] == tok + n * history.shape[0]
        and cotangent.shape[1] % (n * HD) == 0
        and tok % 16 == 0
        and (n * history.shape[0]) % 16 == 0
    )
    plan = head_body if by_heads else window_body
    return plan(query_rows, key_rows, value_rows, frame_counts, history, offsets, cotangent)


def solution(mesh):
    in_specs = (
        P("tm", "head"),
        P("tm", "head"),
        P("tm", "head"),
        P(),
        P("tm", "head"),
        P("tm", None),
        P("tm", None),
    )
    out_specs = (P("tm", "head"), P("tm", "head"))
    return jax.shard_map(body, mesh=mesh, in_specs=in_specs, out_specs=out_specs, check_vma=False)
```

```python
import math

import jax
import jax.numpy as jnp
from jax import lax
from jax.experimental import pallas as pl
from jax.experimental.pallas import tpu as pltpu
from jax.sharding import PartitionSpec as P

HD = 128
TPF = 64
WINB = 4
VMEM_LIMIT = 24 * 1024 * 1024
PACK_LIMIT = 58 * 1024 * 1024


def from_behind(x, axis, by):
    devices = lax.axis_size(axis)
    pairs = [(i, i + by) for i in range(devices) if 0 <= i + by < devices]
    return lax.ppermute(x, axis, pairs)


def window_body(query_rows, key_rows, value_rows, frame_counts, history, offsets, cotangent):
    tok_rows, feat_width = query_rows.shape
    local_heads = feat_width // HD
    block_total = lax.axis_size("tm")
    own_block = lax.axis_index("tm")
    score_scale = 1.0 / math.sqrt(HD)
    key_value = jnp.stack([key_rows, value_rows])
    pieces = []
    for distance in range(WINB - 1, 0, -1):
        pieces.append(from_behind(key_value, "tm", distance))
    window = jnp.concatenate(pieces + [key_value], axis=1)
    source_block = own_block - (WINB - 1) + jnp.arange(WINB, dtype=jnp.int32)
    block_match = jnp.arange(block_total, dtype=jnp.int32)[None, :] == source_block[:, None]
    block_count = jnp.sum(jnp.where(block_match, frame_counts[None, :], 0), axis=1)
    frame_index = jnp.arange(tok_rows, dtype=jnp.int32) // TPF
    kept_mask = (
        (source_block[:, None] >= 0) & (frame_index[None, :] < block_count[:, None])
    ).reshape(WINB * tok_rows)
    key_window = window[0].reshape(WINB * tok_rows, local_heads, HD)
    value_window = window[1].reshape(WINB * tok_rows, local_heads, HD)
    query_heads = query_rows.reshape(tok_rows, local_heads, HD)
    scores = (
        jnp.einsum("qhd,khd->hqk", query_heads, key_window, preferred_element_type=jnp.float32)
        * score_scale
    )
    scores = jnp.where(kept_mask[None, None, :], scores, -jnp.inf)
    row_max = jnp.max(scores, axis=-1, keepdims=True)
    weights = jnp.exp(scores - row_max)
    probs = (weights / jnp.sum(weights, axis=-1, keepdims=True)).astype(jnp.bfloat16)
    mixed = jnp.einsum("hqk,khd->qhd", probs, value_window, preferred_element_type=jnp.float32)
    attended = mixed.astype(jnp.bfloat16).reshape(tok_rows, feat_width)
    tile_rows = history.shape[0]
    source_tile = (own_block - offsets[0]) % block_total
    source_row = (
        source_tile[:, None] * tile_rows + jnp.arange(tile_rows, dtype=jnp.int32)[None, :]
    ).reshape(-1)
    incoming = lax.all_gather(history, "tm", axis=0, tiled=True)
    piece_rows = incoming.shape[0]
    selector = (source_row[:, None] == jnp.arange(piece_rows, dtype=jnp.int32)[None, :]).astype(
        jnp.bfloat16
    )
    clip_hist = jnp.dot(selector, incoming, preferred_element_type=jnp.float32).astype(jnp.bfloat16)
    disc_clip = jnp.concatenate([clip_hist, attended], axis=0)
    disc_grad = lax.psum_scatter(
        lax.dot_general(
            cotangent, disc_clip, (((0,), (0,)), ((), ())), preferred_element_type=jnp.float32
        ),
        "tm",
        scatter_dimension=0,
        tiled=True,
    )
    return (attended, disc_grad)


def chip_bits(m, side):
    return m if m in (0, 3) else jnp.where(side == 0, m, 3 - m)


def cot_kernel(n, tile, lo, off_hbm, cot_hbm, *refs):
    outs, (off, cot, sems) = refs[-3 - n // 2 : -3], refs[-3:]
    own = lax.axis_index("tm")
    chip, side = own // 2, lax.rem(own, 2)
    plane = lax.rem(lax.axis_index("head"), 2)
    clip_rows = n * tile
    all_rows, all_cols = cot.shape
    cols = all_cols // n
    part = all_rows - lo
    low = pl.multiple_of(plane * lo, 16)
    fetch_off = pltpu.make_async_copy(off_hbm, off, sems.at[0])
    fetch_cot = pltpu.make_async_copy(cot_hbm, cot, sems.at[1])
    fetch_off.start()
    fetch_cot.start()
    fetch_off.wait()
    r = lax.broadcasted_iota(jnp.int32, (clip_rows, clip_rows), 0)
    c = lax.broadcasted_iota(jnp.int32, (clip_rows, clip_rows), 1)
    select = jnp.zeros((clip_rows, clip_rows), jnp.float32)
    for j in range(n):
        src = lax.rem(own - off[0, j] + 2 * n, n)
        for t in range(tile):
            select = jnp.where((c == j * tile + t) & (r == src * tile + t), 1.0, select)
    fetch_cot.wait()
    cot[0:clip_rows, :] = jnp.dot(
        select.astype(jnp.bfloat16), cot[0:clip_rows, :], preferred_element_type=jnp.float32
    ).astype(jnp.bfloat16)
    units = cols // HD
    for m, out_ref in enumerate(outs):
        rows, first = (part, low) if m else (all_rows, 0)
        there = chip ^ chip_bits(m, side)
        for i, block in enumerate((2 * there + side, 2 * there + 1 - side)):
            for u in range(units):
                at = (i * units + u) * rows
                lanes = pl.ds(pl.multiple_of(block * cols + u * HD, HD), HD)
                out_ref[at : at + rows, :] = cot[pl.ds(first, rows), lanes]


def pack_kernel(n, heads, q_hbm, k_hbm, v_hbm, hist_hbm, *refs):
    outs, (q, k, v, hist, sems) = refs[:-5], refs[-5:]
    own = lax.axis_index("tm")
    tok, width = q.shape
    tile = hist.shape[0]
    clip_rows = n * tile
    start = 0 if width == n * HD else pl.multiple_of(((own ^ heads[0]) // 2) * width, width)
    pairs = [(hist_hbm, hist)] + [
        (x.at[:, pl.ds(start, width)], y) for x, y in ((q_hbm, q), (k_hbm, k), (v_hbm, v))
    ]
    copies = [pltpu.make_async_copy(a, b, sems.at[i]) for i, (a, b) in enumerate(pairs)]
    for copy in copies:
        copy.start()
    copies[0].wait()
    for d, out_ref in zip(heads, outs):
        lanes = pl.ds(pl.multiple_of((own ^ d) * HD, HD), HD)
        tiles = hist[:, lanes].astype(jnp.float32)
        row = lax.broadcasted_iota(jnp.int32, (clip_rows, HD), 0)
        placed = jnp.zeros((clip_rows, HD), jnp.float32)
        for t in range(tile):
            placed = jnp.where(row == own * tile + t, tiles[t : t + 1, :], placed)
        out_ref[3 * tok : 3 * tok + clip_rows, :] = placed.astype(jnp.bfloat16)
    for i, x in enumerate((q, k, v)):
        copies[1 + i].wait()
        for d, out_ref in zip(heads, outs):
            lanes = pl.ds(pl.multiple_of((own ^ d) * HD - start, HD), HD)
            out_ref[i * tok : (i + 1) * tok, :] = x[:, lanes]


def attend_kernel(n, tok, order, counts_hbm, *refs):
    parts, (same_ref, cross_ref, x_ref, mixed_ref, counts, sem) = refs[:n], refs[n:]
    copy = pltpu.make_async_copy(counts_hbm, counts, sem)
    copy.start()
    own = lax.axis_index("tm")
    side = lax.rem(own, 2)
    for k, part in zip(order, parts):
        x_ref[own ^ k] = part[...]
    copy.wait()
    rate = math.log2(math.e) / math.sqrt(HD)
    token = lax.broadcasted_iota(jnp.int32, (tok, 1), 0)
    bias = [
        jnp.where(token < counts[s] * TPF, 0.0, -jnp.inf).astype(jnp.float32) for s in range(n)
    ]
    values = [x_ref[s, 2 * tok : 3 * tok, :].T for s in range(n)]
    def scores_of(block):
        q = x_ref[block, 0:tok, :]
        return {
            s: lax.dot_general(
                x_ref[s, tok : 2 * tok, :],
                q,
                (((1,), (1,)), ((), ())),
                preferred_element_type=jnp.float32,
            )
            + bias[s]
            for s in range(max(0, block - (WINB - 1)), block + 1)
        }

    ahead = scores_of(0)
    for block in range(n):
        scores, ahead = ahead, scores_of(block + 1) if block + 1 < n else None
        top = None
        for x in scores.values():
            high = jnp.max(x, axis=0, keepdims=True)
            top = high if top is None else jnp.maximum(top, high)
        weights = {s: jnp.exp2((x - top) * rate) for s, x in scores.items()}
        total = jnp.zeros((1, tok), jnp.float32)
        for w in weights.values():
            total = total + jnp.sum(w, axis=0, keepdims=True)
        share = 1.0 / total
        mixed = jnp.zeros((HD, tok), jnp.float32)
        for s, w in weights.items():
            mixed = mixed + jnp.dot(
                values[s], (w * share).astype(jnp.bfloat16), preferred_element_type=jnp.float32
            )
        mixed_ref[block] = mixed.astype(jnp.bfloat16).T
    rows = n // 2 * tok
    clip_rows = same_ref.shape[0] - rows
    hist = jnp.zeros((clip_rows, HD), jnp.float32)
    for s in range(n):
        hist = hist + x_ref[s, 3 * tok : 3 * tok + clip_rows, :].astype(jnp.float32)
    hist = hist.astype(jnp.bfloat16)
    for flip, out_ref in ((0, same_ref), (1, cross_ref)):
        for i in range(n // 2):
            out_ref[i * tok : (i + 1) * tok, :] = mixed_ref[2 * i + (side ^ flip)]
        out_ref[rows:, :] = hist


def stack_kernel(order, lo, tiles, *refs):
    out_ref = refs[-1]
    plane = lax.rem(lax.axis_index("head"), 2)
    for m, ref in zip(order, refs):
        part = ref.shape[0] // tiles
        for u in range(tiles):
            first = pl.multiple_of(u * part + plane * (part - lo), 16)
            out_ref[m - 1, u * lo : (u + 1) * lo, :] = ref[pl.ds(first, lo), :]


def late_kernel(x_ref, *refs):
    refs[-1][...] = x_ref[...]


def turn_kernel(lo, clip_rows, order, own_in, *refs):
    pieces, (swapped_ref, own_ref, other_ref, whole) = refs[:-4], refs[-4:]
    plane = lax.rem(lax.axis_index("head"), 2)
    own = lax.axis_index("tm")
    chip, side = own // 2, lax.rem(own, 2)
    chips, all_rows, width = whole.shape
    part = all_rows - lo
    for u in range(width // HD):
        lanes = slice(u * HD, (u + 1) * HD)
        whole[0, :, lanes] = own_in[u * all_rows : (u + 1) * all_rows, :]
        for m, ref in zip(order, pieces):
            at = chip_bits(m, side)
            a = ref[u * part : (u + 1) * part, :]
            b = swapped_ref[m - 1, u * lo : (u + 1) * lo, :]
            whole[at, 0:lo, lanes] = jnp.where(plane == 0, a[:lo], b)
            whole[at, lo:part, lanes] = jnp.where(plane == 0, a[lo:], a[: part - lo])
            whole[at, part:all_rows, lanes] = jnp.where(plane == 0, b, a[part - lo :])
    for i, out_ref in enumerate((own_ref, other_ref)):
        lanes = slice(i * width // 2, (i + 1) * width // 2)
        rows = [whole[chip ^ c, clip_rows:all_rows, lanes] for c in range(chips)]
        rows += [whole[chip ^ c, 0:clip_rows, lanes] for c in range(chips)]
        out_ref[...] = jnp.concatenate(rows, axis=0).T


def grad_part(turned_ref, head_refs, rows, copies):
    right = jnp.concatenate([x[0:rows, :] for x in head_refs], axis=1)
    hist = jnp.concatenate([x[rows:, :] for x in head_refs], axis=1)
    clip = copies * hist.shape[0]
    out = jnp.dot(turned_ref[:, 0:rows], right, preferred_element_type=jnp.float32)
    return out + jnp.dot(
        turned_ref[:, rows : rows + clip],
        jnp.concatenate([hist] * copies, axis=0),
        preferred_element_type=jnp.float32,
    )


def grad_kernel(rows, copies, heads, turned_ref, *refs):
    out_ref = refs[-1]
    out_ref[...] = grad_part(turned_ref, refs[:heads], rows, copies).astype(out_ref.dtype)


NEAR = ((0, 0), (3, 5), (4, 2), (2, 4), (5, 3))
FAR = ((1, 1), (6, 6), (7, 7))
THERE = (5, 2, 1, 4, 3, 0, 7, 6)


def store_columns(tok, heads, sums, att_hbm, out_hbm, total, sems):
    own = lax.axis_index("tm")
    side = lax.rem(own, 2)
    at = pl.multiple_of(own // 2 * tok, tok)
    moves = []

    def move(a, b):
        moves.append(pltpu.make_async_copy(a, b, sems.at[len(moves)]))
        moves[-1].start()

    def lanes(bits):
        return pl.ds(pl.multiple_of((own ^ jnp.where(side == 0, *bits)) * HD, HD), HD)

    for bits, ref in heads:
        move(ref.at[pl.ds(at, tok), :], att_hbm.at[:, lanes(bits)])
    for i, (bits, (mine, m), (got, g)) in enumerate(sums):
        columns = got[:, g * HD : (g + 1) * HD].astype(jnp.float32)
        total[i] = mine[:, m * HD : (m + 1) * HD] + columns
        move(total.at[i], out_hbm.at[:, lanes(bits)])
    for x in moves:
        x.wait()


def near_kernel(tok, own_near, got_near, *refs):
    n = len(NEAR)
    heads, outs = refs[:n], refs[n:]
    sums = [(NEAR[i], (own_near, i), (got_near, THERE[i])) for i in range(n) if THERE[i] < n]
    store_columns(tok, zip(NEAR, heads), sums, *outs)


def last_kernel(tok, own_near, got_near, own_far, got_far, *refs):
    n = len(NEAR)
    heads, outs = refs[: len(FAR)], refs[len(FAR) + 2 :]

    def column(near, far, i):
        return (near, i) if i < n else (far, i - n)

    sums = [
        (bits, column(own_near, own_far, i), column(got_near, got_far, THERE[i]))
        for i, bits in enumerate(NEAR + FAR)
        if i >= n or THERE[i] >= n
    ]
    store_columns(tok, zip(FAR, heads), sums, *outs)


def head_body(query_rows, key_rows, value_rows, frame_counts, history, offsets, cotangent):
    n = lax.axis_size("tm")
    planes = lax.axis_size("head")
    half = n // 2
    tok, width = query_rows.shape
    tile = history.shape[0]
    clip_rows = n * tile
    cot_rows, all_cols = cotangent.shape
    cols = all_cols // n
    units = cols // HD
    lo = cot_rows * 7 // 17 // 16 * 16
    part = cot_rows - lo
    base = 3 * tok + clip_rows
    length = base
    rows = half * tok
    vmem = pl.BlockSpec(memory_space=pltpu.VMEM)
    hbm = pl.BlockSpec(memory_space=pl.ANY)
    bf16 = jnp.bfloat16

    def swap(x, even, odd=None):
        bits = (even, even if odd is None else odd)
        return lax.ppermute(x, "tm", [(i, i ^ bits[i % 2]) for i in range(n)])

    def swap_plane(x, bit):
        pairs = [
            (i * planes + p, (i ^ bit) * planes + (p ^ 1)) for i in range(n) for p in range(planes)
        ]
        return lax.ppermute(x, ("tm", "head"), pairs)

    def call(
        kernel, name, outs, specs, flops, scratch=(), exps=0, out_spec=vmem, limit=VMEM_LIMIT, aliases={}
    ):
        shapes = [jax.ShapeDtypeStruct(s, d) for s, d in outs]
        moved = 2 * sum(math.prod(s.shape) * s.dtype.itemsize for s in shapes)
        return pl.pallas_call(
            kernel,
            out_shape=tuple(shapes),
            in_specs=specs,
            out_specs=tuple([out_spec] * len(shapes)),
            scratch_shapes=scratch,
            input_output_aliases=aliases,
            compiler_params=pltpu.CompilerParams(vmem_limit_bytes=limit),
            cost_estimate=pl.CostEstimate(flops=flops, bytes_accessed=moved, transcendentals=exps),
            name=name,
        )

    def pack(heads, lanes, name):
        return call(
            lambda *refs: pack_kernel(n, heads, *refs),
            name,
            [((length, HD), bf16)] * len(heads),
            [hbm] * 4,
            0,
            (
                pltpu.VMEM((tok, lanes), bf16),
                pltpu.VMEM((tok, lanes), bf16),
                pltpu.VMEM((tok, lanes), bf16),
                pltpu.VMEM(history.shape, bf16),
                pltpu.SemaphoreType.DMA((4,)),
            ),
            limit=PACK_LIMIT,
        )(query_rows, key_rows, value_rows, history)

    first, rest = [6, 7], [0, 1, 2, 3, 4, 5]
    packed = dict(zip(first, pack(first, 2 * HD, "pack_first")))
    packed.update(zip(rest, pack(rest, width, "pack_rest")))
    order = [6, 7, 2, 4, 3, 5, 1]
    arrived = {k: swap(packed[k], k) for k in order}
    by_head = [packed[0]] + [arrived[k] for k in order]
    chips = range(half)
    cots = call(
        lambda *refs: cot_kernel(n, tile, lo, *refs),
        "cot",
        [((2 * units * cot_rows, HD), bf16)] + [((2 * units * part, HD), bf16)] * (half - 1),
        [hbm] * 4,
        0,
        (
            pltpu.SMEM(offsets.shape, jnp.int32),
            pltpu.VMEM(cotangent.shape, bf16),
            pltpu.SemaphoreType.DMA((2,)),
        ),
    )(offsets, cotangent, arrived[6], arrived[7])
    cots = [cots[0], swap(cots[1], 2, 4), swap(cots[2], 4, 2), swap(cots[3], 6)]
    counts = (
        pltpu.VMEM((n, length, HD), bf16),
        pltpu.VMEM((n, tok, HD), bf16),
        pltpu.SMEM(frame_counts.shape, jnp.int32),
        pltpu.SemaphoreType.DMA,
    )
    pairs = half * tok * WINB * tok
    head_shape = ((rows + clip_rows, HD), bf16)
    same, cross = call(
        lambda *refs: attend_kernel(n, tok, [0] + order, *refs),
        "attend",
        [head_shape, head_shape],
        [hbm] + [vmem] * n,
        8 * pairs * HD,
        counts,
        2 * pairs,
    )(frame_counts, *by_head)
    stack_order = [3, 1, 2]
    (cot_rest,) = call(
        lambda *refs: stack_kernel(stack_order, lo, 2 * units, *refs),
        "stack",
        [((half - 1, 2 * units * lo, HD), bf16)],
        [vmem] * (half - 1) + [hbm],
        0,
    )(*[cots[m] for m in stack_order], same)
    cot_swapped = swap_plane(cot_rest, 0)
    first_same, first_cross = swap(same, 2, 4), swap(cross, 3, 5)
    second_same, second_cross = swap(same, 4, 2), swap(cross, 5, 3)
    far_same, far_cross = swap(first_same, 4, 2), swap(first_cross, 2, 4)
    (late_cross,) = call(late_kernel, "late", [head_shape], [vmem] + [hbm] * 2, 0)(
        cross, second_cross, second_same
    )
    c_cross = swap(late_cross, 1)

    turned_own, turned_other = call(
        lambda *refs: turn_kernel(lo, clip_rows, stack_order, *refs),
        "turn",
        [((cols, half * cot_rows), bf16)] * 2,
        [vmem] * (half + 1),
        0,
        (pltpu.VMEM((half, cot_rows, 2 * cols), bf16),),
    )(cots[0], *[cots[m] for m in stack_order], cot_swapped)

    def grad(turned, heads, dtype, name, behind=()):
        (out,) = call(
            lambda *refs: grad_kernel(rows, half, len(heads), *refs),
            name,
            [((cols, len(heads) * HD), dtype)],
            [vmem] * (1 + len(heads)) + [hbm] * len(behind),
            2 * cols * half * cot_rows * len(heads) * HD,
        )(turned, *heads, *behind)
        return out

    near = [same, second_cross, second_same, first_same, first_cross]
    far = [c_cross, far_same, far_cross]
    whole = [((tok, width), bf16), ((cols, width), jnp.float32)]
    got_near = swap(grad(turned_other, near, bf16, "grad_other_near"), 1)
    own_near = grad(turned_own, near, jnp.float32, "grad_own_near")
    got_far = swap(grad(turned_other, far, bf16, "grad_other_far", (own_near,)), 1)
    own_far = grad(turned_own, far, jnp.float32, "grad_own_far")
    halfway = call(
        lambda *refs: near_kernel(tok, *refs),
        "near",
        whole,
        [vmem] * (2 + len(near)),
        0,
        (pltpu.VMEM((4, cols, HD), jnp.float32), pltpu.SemaphoreType.DMA((9,))),
        out_spec=hbm,
    )(own_near, got_near, *near)
    return call(
        lambda *refs: last_kernel(tok, *refs),
        "last",
        whole,
        [vmem] * (4 + len(far)) + [hbm] * 2,
        0,
        (pltpu.VMEM((4, cols, HD), jnp.float32), pltpu.SemaphoreType.DMA((7,))),
        out_spec=hbm,
        aliases={4 + len(far): 0, 5 + len(far): 1},
    )(own_near, got_near, own_far, got_far, *far, *halfway)


def body(query_rows, key_rows, value_rows, frame_counts, history, offsets, cotangent):
    n = lax.axis_size("tm")
    tok, width = query_rows.shape
    by_heads = (
        n == 8
        and lax.axis_size("head") % 2 == 0
        and width == n * HD
        and offsets.shape[1] == n
        and cotangent.shape[0] == tok + n * history.shape[0]
        and cotangent.shape[1] % (n * HD) == 0
        and tok % 16 == 0
        and (n * history.shape[0]) % 16 == 0
    )
    plan = head_body if by_heads else window_body
    return plan(query_rows, key_rows, value_rows, frame_counts, history, offsets, cotangent)


def solution(mesh):
    in_specs = (
        P("tm", "head"),
        P("tm", "head"),
        P("tm", "head"),
        P(),
        P("tm", "head"),
        P("tm", None),
        P("tm", None),
    )
    out_specs = (P("tm", "head"), P("tm", "head"))
    return jax.shard_map(body, mesh=mesh, in_specs=in_specs, out_specs=out_specs, check_vma=False)
```

```python
import math

import jax
import jax.numpy as jnp
from jax import lax
from jax.experimental import pallas as pl
from jax.experimental.pallas import tpu as pltpu
from jax.sharding import PartitionSpec as P

HD = 128
TPF = 64
WINB = 4
VMEM_LIMIT = 24 * 1024 * 1024
PACK_LIMIT = 58 * 1024 * 1024


def from_behind(x, axis, by):
    devices = lax.axis_size(axis)
    pairs = [(i, i + by) for i in range(devices) if 0 <= i + by < devices]
    return lax.ppermute(x, axis, pairs)


def window_body(query_rows, key_rows, value_rows, frame_counts, history, offsets, cotangent):
    tok_rows, feat_width = query_rows.shape
    local_heads = feat_width // HD
    block_total = lax.axis_size("tm")
    own_block = lax.axis_index("tm")
    score_scale = 1.0 / math.sqrt(HD)
    key_value = jnp.stack([key_rows, value_rows])
    pieces = []
    for distance in range(WINB - 1, 0, -1):
        pieces.append(from_behind(key_value, "tm", distance))
    window = jnp.concatenate(pieces + [key_value], axis=1)
    source_block = own_block - (WINB - 1) + jnp.arange(WINB, dtype=jnp.int32)
    block_match = jnp.arange(block_total, dtype=jnp.int32)[None, :] == source_block[:, None]
    block_count = jnp.sum(jnp.where(block_match, frame_counts[None, :], 0), axis=1)
    frame_index = jnp.arange(tok_rows, dtype=jnp.int32) // TPF
    kept_mask = (
        (source_block[:, None] >= 0) & (frame_index[None, :] < block_count[:, None])
    ).reshape(WINB * tok_rows)
    key_window = window[0].reshape(WINB * tok_rows, local_heads, HD)
    value_window = window[1].reshape(WINB * tok_rows, local_heads, HD)
    query_heads = query_rows.reshape(tok_rows, local_heads, HD)
    scores = (
        jnp.einsum("qhd,khd->hqk", query_heads, key_window, preferred_element_type=jnp.float32)
        * score_scale
    )
    scores = jnp.where(kept_mask[None, None, :], scores, -jnp.inf)
    row_max = jnp.max(scores, axis=-1, keepdims=True)
    weights = jnp.exp(scores - row_max)
    probs = (weights / jnp.sum(weights, axis=-1, keepdims=True)).astype(jnp.bfloat16)
    mixed = jnp.einsum("hqk,khd->qhd", probs, value_window, preferred_element_type=jnp.float32)
    attended = mixed.astype(jnp.bfloat16).reshape(tok_rows, feat_width)
    tile_rows = history.shape[0]
    source_tile = (own_block - offsets[0]) % block_total
    source_row = (
        source_tile[:, None] * tile_rows + jnp.arange(tile_rows, dtype=jnp.int32)[None, :]
    ).reshape(-1)
    incoming = lax.all_gather(history, "tm", axis=0, tiled=True)
    piece_rows = incoming.shape[0]
    selector = (source_row[:, None] == jnp.arange(piece_rows, dtype=jnp.int32)[None, :]).astype(
        jnp.bfloat16
    )
    clip_hist = jnp.dot(selector, incoming, preferred_element_type=jnp.float32).astype(jnp.bfloat16)
    disc_clip = jnp.concatenate([clip_hist, attended], axis=0)
    disc_grad = lax.psum_scatter(
        lax.dot_general(
            cotangent, disc_clip, (((0,), (0,)), ((), ())), preferred_element_type=jnp.float32
        ),
        "tm",
        scatter_dimension=0,
        tiled=True,
    )
    return (attended, disc_grad)


def chip_bits(m, side):
    return m if m in (0, 3) else jnp.where(side == 0, m, 3 - m)


def cot_kernel(n, tile, lo, off_hbm, cot_hbm, *refs):
    outs, (off, cot, sems) = refs[-3 - n // 2 : -3], refs[-3:]
    own = lax.axis_index("tm")
    chip, side = own // 2, lax.rem(own, 2)
    plane = lax.rem(lax.axis_index("head"), 2)
    clip_rows = n * tile
    all_rows, all_cols = cot.shape
    cols = all_cols // n
    part = all_rows - lo
    low = pl.multiple_of(plane * lo, 16)
    fetch_off = pltpu.make_async_copy(off_hbm, off, sems.at[0])
    fetch_cot = pltpu.make_async_copy(cot_hbm, cot, sems.at[1])
    fetch_off.start()
    fetch_cot.start()
    fetch_off.wait()
    r = lax.broadcasted_iota(jnp.int32, (clip_rows, clip_rows), 0)
    c = lax.broadcasted_iota(jnp.int32, (clip_rows, clip_rows), 1)
    select = jnp.zeros((clip_rows, clip_rows), jnp.float32)
    for j in range(n):
        src = lax.rem(own - off[0, j] + 2 * n, n)
        for t in range(tile):
            select = jnp.where((c == j * tile + t) & (r == src * tile + t), 1.0, select)
    fetch_cot.wait()
    cot[0:clip_rows, :] = jnp.dot(
        select.astype(jnp.bfloat16), cot[0:clip_rows, :], preferred_element_type=jnp.float32
    ).astype(jnp.bfloat16)
    units = cols // HD
    for m, out_ref in enumerate(outs):
        rows, first = (part, low) if m else (all_rows, 0)
        there = chip ^ chip_bits(m, side)
        for i, block in enumerate((2 * there + side, 2 * there + 1 - side)):
            for u in range(units):
                at = (i * units + u) * rows
                lanes = pl.ds(pl.multiple_of(block * cols + u * HD, HD), HD)
                out_ref[at : at + rows, :] = cot[pl.ds(first, rows), lanes]


def pack_kernel(n, heads, q_hbm, k_hbm, v_hbm, hist_hbm, *refs):
    outs, (q, k, v, hist, sems) = refs[:-5], refs[-5:]
    own = lax.axis_index("tm")
    tok, width = q.shape
    tile = hist.shape[0]
    clip_rows = n * tile
    start = 0 if width == n * HD else pl.multiple_of(((own ^ heads[0]) // 2) * width, width)
    pairs = [(hist_hbm, hist)] + [
        (x.at[:, pl.ds(start, width)], y) for x, y in ((q_hbm, q), (k_hbm, k), (v_hbm, v))
    ]
    copies = [pltpu.make_async_copy(a, b, sems.at[i]) for i, (a, b) in enumerate(pairs)]
    for copy in copies:
        copy.start()
    copies[0].wait()
    for d, out_ref in zip(heads, outs):
        lanes = pl.ds(pl.multiple_of((own ^ d) * HD, HD), HD)
        tiles = hist[:, lanes].astype(jnp.float32)
        row = lax.broadcasted_iota(jnp.int32, (clip_rows, HD), 0)
        placed = jnp.zeros((clip_rows, HD), jnp.float32)
        for t in range(tile):
            placed = jnp.where(row == own * tile + t, tiles[t : t + 1, :], placed)
        out_ref[3 * tok : 3 * tok + clip_rows, :] = placed.astype(jnp.bfloat16)
    for i, x in enumerate((q, k, v)):
        copies[1 + i].wait()
        for d, out_ref in zip(heads, outs):
            lanes = pl.ds(pl.multiple_of((own ^ d) * HD - start, HD), HD)
            out_ref[i * tok : (i + 1) * tok, :] = x[:, lanes]


def attend_kernel(n, tok, order, counts_hbm, *refs):
    parts, (same_ref, cross_ref, x_ref, mixed_ref, counts, sem) = refs[:n], refs[n:]
    copy = pltpu.make_async_copy(counts_hbm, counts, sem)
    copy.start()
    own = lax.axis_index("tm")
    side = lax.rem(own, 2)
    for k, part in zip(order, parts):
        x_ref[own ^ k] = part[...]
    copy.wait()
    rate = math.log2(math.e) / math.sqrt(HD)
    token = lax.broadcasted_iota(jnp.int32, (tok, 1), 0)
    bias = [
        jnp.where(token < counts[s] * TPF, 0.0, -jnp.inf).astype(jnp.float32) for s in range(n)
    ]
    values = [x_ref[s, 2 * tok : 3 * tok, :].T for s in range(n)]
    def scores_of(block):
        q = x_ref[block, 0:tok, :]
        return {
            s: lax.dot_general(
                x_ref[s, tok : 2 * tok, :],
                q,
                (((1,), (1,)), ((), ())),
                preferred_element_type=jnp.float32,
            )
            + bias[s]
            for s in range(max(0, block - (WINB - 1)), block + 1)
        }

    def mix(block, probs):
        mixed = jnp.zeros((HD, tok), jnp.float32)
        for s, p in probs.items():
            mixed = mixed + jnp.dot(values[s], p, preferred_element_type=jnp.float32)
        mixed_ref[block] = mixed.astype(jnp.bfloat16).T

    ahead, behind = scores_of(0), None
    for block in range(n):
        scores, ahead = ahead, scores_of(block + 1) if block + 1 < n else None
        if behind is not None:
            mix(block - 1, behind)
        top = None
        for x in scores.values():
            high = jnp.max(x, axis=0, keepdims=True)
            top = high if top is None else jnp.maximum(top, high)
        weights = {s: jnp.exp2((x - top) * rate) for s, x in scores.items()}
        total = jnp.zeros((1, tok), jnp.float32)
        for w in weights.values():
            total = total + jnp.sum(w, axis=0, keepdims=True)
        share = 1.0 / total
        behind = {s: (w * share).astype(jnp.bfloat16) for s, w in weights.items()}
    mix(n - 1, behind)
    rows = n // 2 * tok
    clip_rows = same_ref.shape[0] - rows
    hist = jnp.zeros((clip_rows, HD), jnp.float32)
    for s in range(n):
        hist = hist + x_ref[s, 3 * tok : 3 * tok + clip_rows, :].astype(jnp.float32)
    hist = hist.astype(jnp.bfloat16)
    for flip, out_ref in ((0, same_ref), (1, cross_ref)):
        for i in range(n // 2):
            out_ref[i * tok : (i + 1) * tok, :] = mixed_ref[2 * i + (side ^ flip)]
        out_ref[rows:, :] = hist


def stack_kernel(order, lo, tiles, *refs):
    out_ref = refs[-1]
    plane = lax.rem(lax.axis_index("head"), 2)
    for m, ref in zip(order, refs):
        part = ref.shape[0] // tiles
        for u in range(tiles):
            first = pl.multiple_of(u * part + plane * (part - lo), 16)
            out_ref[m - 1, u * lo : (u + 1) * lo, :] = ref[pl.ds(first, lo), :]


def late_kernel(x_ref, *refs):
    refs[-1][...] = x_ref[...]


def turn_kernel(lo, clip_rows, order, own_in, *refs):
    pieces, (swapped_ref, own_ref, other_ref, whole) = refs[:-4], refs[-4:]
    plane = lax.rem(lax.axis_index("head"), 2)
    own = lax.axis_index("tm")
    chip, side = own // 2, lax.rem(own, 2)
    chips, all_rows, width = whole.shape
    part = all_rows - lo
    for u in range(width // HD):
        lanes = slice(u * HD, (u + 1) * HD)
        whole[0, :, lanes] = own_in[u * all_rows : (u + 1) * all_rows, :]
        for m, ref in zip(order, pieces):
            at = chip_bits(m, side)
            a = ref[u * part : (u + 1) * part, :]
            b = swapped_ref[m - 1, u * lo : (u + 1) * lo, :]
            whole[at, 0:lo, lanes] = jnp.where(plane == 0, a[:lo], b)
            whole[at, lo:part, lanes] = jnp.where(plane == 0, a[lo:], a[: part - lo])
            whole[at, part:all_rows, lanes] = jnp.where(plane == 0, b, a[part - lo :])
    for i, out_ref in enumerate((own_ref, other_ref)):
        lanes = slice(i * width // 2, (i + 1) * width // 2)
        rows = [whole[chip ^ c, clip_rows:all_rows, lanes] for c in range(chips)]
        rows += [whole[chip ^ c, 0:clip_rows, lanes] for c in range(chips)]
        out_ref[...] = jnp.concatenate(rows, axis=0).T


def grad_part(turned_ref, head_refs, rows, copies):
    right = jnp.concatenate([x[0:rows, :] for x in head_refs], axis=1)
    hist = jnp.concatenate([x[rows:, :] for x in head_refs], axis=1)
    clip = copies * hist.shape[0]
    out = jnp.dot(turned_ref[:, 0:rows], right, preferred_element_type=jnp.float32)
    return out + jnp.dot(
        turned_ref[:, rows : rows + clip],
        jnp.concatenate([hist] * copies, axis=0),
        preferred_element_type=jnp.float32,
    )


def grad_kernel(rows, copies, heads, turned_ref, *refs):
    out_ref = refs[-1]
    out_ref[...] = grad_part(turned_ref, refs[:heads], rows, copies).astype(out_ref.dtype)


NEAR = ((0, 0), (3, 5), (4, 2), (2, 4), (5, 3))
FAR = ((1, 1), (6, 6), (7, 7))
THERE = (5, 2, 1, 4, 3, 0, 7, 6)


def store_columns(tok, heads, sums, att_hbm, out_hbm, total, sems):
    own = lax.axis_index("tm")
    side = lax.rem(own, 2)
    at = pl.multiple_of(own // 2 * tok, tok)
    moves = []

    def move(a, b):
        moves.append(pltpu.make_async_copy(a, b, sems.at[len(moves)]))
        moves[-1].start()

    def lanes(bits):
        return pl.ds(pl.multiple_of((own ^ jnp.where(side == 0, *bits)) * HD, HD), HD)

    for bits, ref in heads:
        move(ref.at[pl.ds(at, tok), :], att_hbm.at[:, lanes(bits)])
    for i, (bits, (mine, m), (got, g)) in enumerate(sums):
        columns = got[:, g * HD : (g + 1) * HD].astype(jnp.float32)
        total[i] = mine[:, m * HD : (m + 1) * HD] + columns
        move(total.at[i], out_hbm.at[:, lanes(bits)])
    for x in moves:
        x.wait()


def near_kernel(tok, own_near, got_near, *refs):
    n = len(NEAR)
    heads, outs = refs[:n], refs[n:]
    sums = [(NEAR[i], (own_near, i), (got_near, THERE[i])) for i in range(n) if THERE[i] < n]
    store_columns(tok, zip(NEAR, heads), sums, *outs)


def last_kernel(tok, own_near, got_near, own_far, got_far, *refs):
    n = len(NEAR)
    heads, outs = refs[: len(FAR)], refs[len(FAR) + 2 :]

    def column(near, far, i):
        return (near, i) if i < n else (far, i - n)

    sums = [
        (bits, column(own_near, own_far, i), column(got_near, got_far, THERE[i]))
        for i, bits in enumerate(NEAR + FAR)
        if i >= n or THERE[i] >= n
    ]
    store_columns(tok, zip(FAR, heads), sums, *outs)


def head_body(query_rows, key_rows, value_rows, frame_counts, history, offsets, cotangent):
    n = lax.axis_size("tm")
    planes = lax.axis_size("head")
    half = n // 2
    tok, width = query_rows.shape
    tile = history.shape[0]
    clip_rows = n * tile
    cot_rows, all_cols = cotangent.shape
    cols = all_cols // n
    units = cols // HD
    lo = cot_rows * 7 // 17 // 16 * 16
    part = cot_rows - lo
    base = 3 * tok + clip_rows
    length = base
    rows = half * tok
    vmem = pl.BlockSpec(memory_space=pltpu.VMEM)
    hbm = pl.BlockSpec(memory_space=pl.ANY)
    bf16 = jnp.bfloat16

    def swap(x, even, odd=None):
        bits = (even, even if odd is None else odd)
        return lax.ppermute(x, "tm", [(i, i ^ bits[i % 2]) for i in range(n)])

    def swap_plane(x, bit):
        pairs = [
            (i * planes + p, (i ^ bit) * planes + (p ^ 1)) for i in range(n) for p in range(planes)
        ]
        return lax.ppermute(x, ("tm", "head"), pairs)

    def call(
        kernel, name, outs, specs, flops, scratch=(), exps=0, out_spec=vmem, limit=VMEM_LIMIT, aliases={}
    ):
        shapes = [jax.ShapeDtypeStruct(s, d) for s, d in outs]
        moved = 2 * sum(math.prod(s.shape) * s.dtype.itemsize for s in shapes)
        return pl.pallas_call(
            kernel,
            out_shape=tuple(shapes),
            in_specs=specs,
            out_specs=tuple([out_spec] * len(shapes)),
            scratch_shapes=scratch,
            input_output_aliases=aliases,
            compiler_params=pltpu.CompilerParams(vmem_limit_bytes=limit),
            cost_estimate=pl.CostEstimate(flops=flops, bytes_accessed=moved, transcendentals=exps),
            name=name,
        )

    def pack(heads, lanes, name):
        return call(
            lambda *refs: pack_kernel(n, heads, *refs),
            name,
            [((length, HD), bf16)] * len(heads),
            [hbm] * 4,
            0,
            (
                pltpu.VMEM((tok, lanes), bf16),
                pltpu.VMEM((tok, lanes), bf16),
                pltpu.VMEM((tok, lanes), bf16),
                pltpu.VMEM(history.shape, bf16),
                pltpu.SemaphoreType.DMA((4,)),
            ),
            limit=PACK_LIMIT,
        )(query_rows, key_rows, value_rows, history)

    first, rest = [6, 7], [0, 1, 2, 3, 4, 5]
    packed = dict(zip(first, pack(first, 2 * HD, "pack_first")))
    packed.update(zip(rest, pack(rest, width, "pack_rest")))
    order = [6, 7, 2, 4, 3, 5, 1]
    arrived = {k: swap(packed[k], k) for k in order}
    by_head = [packed[0]] + [arrived[k] for k in order]
    chips = range(half)
    cots = call(
        lambda *refs: cot_kernel(n, tile, lo, *refs),
        "cot",
        [((2 * units * cot_rows, HD), bf16)] + [((2 * units * part, HD), bf16)] * (half - 1),
        [hbm] * 4,
        0,
        (
            pltpu.SMEM(offsets.shape, jnp.int32),
            pltpu.VMEM(cotangent.shape, bf16),
            pltpu.SemaphoreType.DMA((2,)),
        ),
    )(offsets, cotangent, arrived[6], arrived[7])
    cots = [cots[0], swap(cots[1], 2, 4), swap(cots[2], 4, 2), swap(cots[3], 6)]
    counts = (
        pltpu.VMEM((n, length, HD), bf16),
        pltpu.VMEM((n, tok, HD), bf16),
        pltpu.SMEM(frame_counts.shape, jnp.int32),
        pltpu.SemaphoreType.DMA,
    )
    pairs = half * tok * WINB * tok
    head_shape = ((rows + clip_rows, HD), bf16)
    same, cross = call(
        lambda *refs: attend_kernel(n, tok, [0] + order, *refs),
        "attend",
        [head_shape, head_shape],
        [hbm] + [vmem] * n,
        8 * pairs * HD,
        counts,
        2 * pairs,
    )(frame_counts, *by_head)
    stack_order = [3, 1, 2]
    (cot_rest,) = call(
        lambda *refs: stack_kernel(stack_order, lo, 2 * units, *refs),
        "stack",
        [((half - 1, 2 * units * lo, HD), bf16)],
        [vmem] * (half - 1) + [hbm],
        0,
    )(*[cots[m] for m in stack_order], same)
    cot_swapped = swap_plane(cot_rest, 0)
    first_same, first_cross = swap(same, 2, 4), swap(cross, 3, 5)
    second_same, second_cross = swap(same, 4, 2), swap(cross, 5, 3)
    far_same, far_cross = swap(first_same, 4, 2), swap(first_cross, 2, 4)
    (late_cross,) = call(late_kernel, "late", [head_shape], [vmem] + [hbm] * 2, 0)(
        cross, second_cross, second_same
    )
    c_cross = swap(late_cross, 1)

    turned_own, turned_other = call(
        lambda *refs: turn_kernel(lo, clip_rows, stack_order, *refs),
        "turn",
        [((cols, half * cot_rows), bf16)] * 2,
        [vmem] * (half + 1),
        0,
        (pltpu.VMEM((half, cot_rows, 2 * cols), bf16),),
    )(cots[0], *[cots[m] for m in stack_order], cot_swapped)

    def grad(turned, heads, dtype, name, behind=()):
        (out,) = call(
            lambda *refs: grad_kernel(rows, half, len(heads), *refs),
            name,
            [((cols, len(heads) * HD), dtype)],
            [vmem] * (1 + len(heads)) + [hbm] * len(behind),
            2 * cols * half * cot_rows * len(heads) * HD,
        )(turned, *heads, *behind)
        return out

    near = [same, second_cross, second_same, first_same, first_cross]
    far = [c_cross, far_same, far_cross]
    whole = [((tok, width), bf16), ((cols, width), jnp.float32)]
    got_near = swap(grad(turned_other, near, bf16, "grad_other_near"), 1)
    own_near = grad(turned_own, near, jnp.float32, "grad_own_near")
    got_far = swap(grad(turned_other, far, bf16, "grad_other_far", (own_near,)), 1)
    own_far = grad(turned_own, far, jnp.float32, "grad_own_far")
    halfway = call(
        lambda *refs: near_kernel(tok, *refs),
        "near",
        whole,
        [vmem] * (2 + len(near)),
        0,
        (pltpu.VMEM((4, cols, HD), jnp.float32), pltpu.SemaphoreType.DMA((9,))),
        out_spec=hbm,
    )(own_near, got_near, *near)
    return call(
        lambda *refs: last_kernel(tok, *refs),
        "last",
        whole,
        [vmem] * (4 + len(far)) + [hbm] * 2,
        0,
        (pltpu.VMEM((4, cols, HD), jnp.float32), pltpu.SemaphoreType.DMA((7,))),
        out_spec=hbm,
        aliases={4 + len(far): 0, 5 + len(far): 1},
    )(own_near, got_near, own_far, got_far, *far, *halfway)


def body(query_rows, key_rows, value_rows, frame_counts, history, offsets, cotangent):
    n = lax.axis_size("tm")
    tok, width = query_rows.shape
    by_heads = (
        n == 8
        and lax.axis_size("head") % 2 == 0
        and width == n * HD
        and offsets.shape[1] == n
        and cotangent.shape[0] == tok + n * history.shape[0]
        and cotangent.shape[1] % (n * HD) == 0
        and tok % 16 == 0
        and (n * history.shape[0]) % 16 == 0
    )
    plan = head_body if by_heads else window_body
    return plan(query_rows, key_rows, value_rows, frame_counts, history, offsets, cotangent)


def solution(mesh):
    in_specs = (
        P("tm", "head"),
        P("tm", "head"),
        P("tm", "head"),
        P(),
        P("tm", "head"),
        P("tm", None),
        P("tm", None),
    )
    out_specs = (P("tm", "head"), P("tm", "head"))
    return jax.shard_map(body, mesh=mesh, in_specs=in_specs, out_specs=out_specs, check_vma=False)
```

```python
import math

import jax
import jax.numpy as jnp
from jax import lax
from jax.experimental import pallas as pl
from jax.experimental.pallas import tpu as pltpu
from jax.sharding import PartitionSpec as P

HD = 128
TPF = 64
WINB = 4
VMEM_LIMIT = 24 * 1024 * 1024
PACK_LIMIT = 58 * 1024 * 1024


def from_behind(x, axis, by):
    devices = lax.axis_size(axis)
    pairs = [(i, i + by) for i in range(devices) if 0 <= i + by < devices]
    return lax.ppermute(x, axis, pairs)


def window_body(query_rows, key_rows, value_rows, frame_counts, history, offsets, cotangent):
    tok_rows, feat_width = query_rows.shape
    local_heads = feat_width // HD
    block_total = lax.axis_size("tm")
    own_block = lax.axis_index("tm")
    score_scale = 1.0 / math.sqrt(HD)
    key_value = jnp.stack([key_rows, value_rows])
    pieces = []
    for distance in range(WINB - 1, 0, -1):
        pieces.append(from_behind(key_value, "tm", distance))
    window = jnp.concatenate(pieces + [key_value], axis=1)
    source_block = own_block - (WINB - 1) + jnp.arange(WINB, dtype=jnp.int32)
    block_match = jnp.arange(block_total, dtype=jnp.int32)[None, :] == source_block[:, None]
    block_count = jnp.sum(jnp.where(block_match, frame_counts[None, :], 0), axis=1)
    frame_index = jnp.arange(tok_rows, dtype=jnp.int32) // TPF
    kept_mask = (
        (source_block[:, None] >= 0) & (frame_index[None, :] < block_count[:, None])
    ).reshape(WINB * tok_rows)
    key_window = window[0].reshape(WINB * tok_rows, local_heads, HD)
    value_window = window[1].reshape(WINB * tok_rows, local_heads, HD)
    query_heads = query_rows.reshape(tok_rows, local_heads, HD)
    scores = (
        jnp.einsum("qhd,khd->hqk", query_heads, key_window, preferred_element_type=jnp.float32)
        * score_scale
    )
    scores = jnp.where(kept_mask[None, None, :], scores, -jnp.inf)
    row_max = jnp.max(scores, axis=-1, keepdims=True)
    weights = jnp.exp(scores - row_max)
    probs = (weights / jnp.sum(weights, axis=-1, keepdims=True)).astype(jnp.bfloat16)
    mixed = jnp.einsum("hqk,khd->qhd", probs, value_window, preferred_element_type=jnp.float32)
    attended = mixed.astype(jnp.bfloat16).reshape(tok_rows, feat_width)
    tile_rows = history.shape[0]
    source_tile = (own_block - offsets[0]) % block_total
    source_row = (
        source_tile[:, None] * tile_rows + jnp.arange(tile_rows, dtype=jnp.int32)[None, :]
    ).reshape(-1)
    incoming = lax.all_gather(history, "tm", axis=0, tiled=True)
    piece_rows = incoming.shape[0]
    selector = (source_row[:, None] == jnp.arange(piece_rows, dtype=jnp.int32)[None, :]).astype(
        jnp.bfloat16
    )
    clip_hist = jnp.dot(selector, incoming, preferred_element_type=jnp.float32).astype(jnp.bfloat16)
    disc_clip = jnp.concatenate([clip_hist, attended], axis=0)
    disc_grad = lax.psum_scatter(
        lax.dot_general(
            cotangent, disc_clip, (((0,), (0,)), ((), ())), preferred_element_type=jnp.float32
        ),
        "tm",
        scatter_dimension=0,
        tiled=True,
    )
    return (attended, disc_grad)


def chip_bits(m, side):
    return m if m in (0, 3) else jnp.where(side == 0, m, 3 - m)


def cot_kernel(n, tile, cuts, off_hbm, cot_hbm, *refs):
    outs, (off, cot, sems) = refs[-3 - n // 2 : -3], refs[-3:]
    own = lax.axis_index("tm")
    chip, side = own // 2, lax.rem(own, 2)
    plane = lax.rem(lax.axis_index("head"), 2)
    clip_rows = n * tile
    all_rows, all_cols = cot.shape
    cols = all_cols // n
    fetch_off = pltpu.make_async_copy(off_hbm, off, sems.at[0])
    fetch_cot = pltpu.make_async_copy(cot_hbm, cot, sems.at[1])
    fetch_off.start()
    fetch_cot.start()
    fetch_off.wait()
    r = lax.broadcasted_iota(jnp.int32, (clip_rows, clip_rows), 0)
    c = lax.broadcasted_iota(jnp.int32, (clip_rows, clip_rows), 1)
    select = jnp.zeros((clip_rows, clip_rows), jnp.float32)
    for j in range(n):
        src = lax.rem(own - off[0, j] + 2 * n, n)
        for t in range(tile):
            select = jnp.where((c == j * tile + t) & (r == src * tile + t), 1.0, select)
    fetch_cot.wait()
    cot[0:clip_rows, :] = jnp.dot(
        select.astype(jnp.bfloat16), cot[0:clip_rows, :], preferred_element_type=jnp.float32
    ).astype(jnp.bfloat16)
    units = cols // HD
    for m, out_ref in enumerate(outs):
        rows, first = all_rows - cuts[m], pl.multiple_of(plane * cuts[m], 16)
        there = chip ^ chip_bits(m, side)
        for i, block in enumerate((2 * there + side, 2 * there + 1 - side)):
            for u in range(units):
                at = (i * units + u) * rows
                lanes = pl.ds(pl.multiple_of(block * cols + u * HD, HD), HD)
                out_ref[at : at + rows, :] = cot[pl.ds(first, rows), lanes]


def pack_kernel(n, heads, q_hbm, k_hbm, v_hbm, hist_hbm, *refs):
    outs, (q, k, v, hist, sems) = refs[:-5], refs[-5:]
    own = lax.axis_index("tm")
    tok, width = q.shape
    tile = hist.shape[0]
    clip_rows = n * tile
    start = 0 if width == n * HD else pl.multiple_of(((own ^ heads[0]) // 2) * width, width)
    pairs = [(hist_hbm, hist)] + [
        (x.at[:, pl.ds(start, width)], y) for x, y in ((q_hbm, q), (k_hbm, k), (v_hbm, v))
    ]
    copies = [pltpu.make_async_copy(a, b, sems.at[i]) for i, (a, b) in enumerate(pairs)]
    for copy in copies:
        copy.start()
    copies[0].wait()
    for d, out_ref in zip(heads, outs):
        lanes = pl.ds(pl.multiple_of((own ^ d) * HD, HD), HD)
        tiles = hist[:, lanes].astype(jnp.float32)
        row = lax.broadcasted_iota(jnp.int32, (clip_rows, HD), 0)
        placed = jnp.zeros((clip_rows, HD), jnp.float32)
        for t in range(tile):
            placed = jnp.where(row == own * tile + t, tiles[t : t + 1, :], placed)
        out_ref[3 * tok : 3 * tok + clip_rows, :] = placed.astype(jnp.bfloat16)
    for i, x in enumerate((q, k, v)):
        copies[1 + i].wait()
        for d, out_ref in zip(heads, outs):
            lanes = pl.ds(pl.multiple_of((own ^ d) * HD - start, HD), HD)
            out_ref[i * tok : (i + 1) * tok, :] = x[:, lanes]


def attend_kernel(n, tok, order, counts_hbm, *refs):
    parts, (same_ref, cross_ref, x_ref, mixed_ref, counts, sem) = refs[:n], refs[n:]
    copy = pltpu.make_async_copy(counts_hbm, counts, sem)
    copy.start()
    own = lax.axis_index("tm")
    side = lax.rem(own, 2)
    for k, part in zip(order, parts):
        x_ref[own ^ k] = part[...]
    copy.wait()
    rate = math.log2(math.e) / math.sqrt(HD)
    token = lax.broadcasted_iota(jnp.int32, (tok, 1), 0)
    bias = [
        jnp.where(token < counts[s] * TPF, 0.0, -jnp.inf).astype(jnp.float32) for s in range(n)
    ]
    values = [x_ref[s, 2 * tok : 3 * tok, :].T for s in range(n)]
    def scores_of(block):
        q = x_ref[block, 0:tok, :]
        return {
            s: lax.dot_general(
                x_ref[s, tok : 2 * tok, :],
                q,
                (((1,), (1,)), ((), ())),
                preferred_element_type=jnp.float32,
            )
            + bias[s]
            for s in range(max(0, block - (WINB - 1)), block + 1)
        }

    def mix(block, probs):
        mixed = jnp.zeros((HD, tok), jnp.float32)
        for s, p in probs.items():
            mixed = mixed + jnp.dot(values[s], p, preferred_element_type=jnp.float32)
        mixed_ref[block] = mixed.astype(jnp.bfloat16).T

    ahead, behind = scores_of(0), None
    for block in range(n):
        scores, ahead = ahead, scores_of(block + 1) if block + 1 < n else None
        if behind is not None:
            mix(block - 1, behind)
        top = None
        for x in scores.values():
            high = jnp.max(x, axis=0, keepdims=True)
            top = high if top is None else jnp.maximum(top, high)
        weights = {s: jnp.exp2((x - top) * rate) for s, x in scores.items()}
        total = jnp.zeros((1, tok), jnp.float32)
        for w in weights.values():
            total = total + jnp.sum(w, axis=0, keepdims=True)
        share = 1.0 / total
        behind = {s: (w * share).astype(jnp.bfloat16) for s, w in weights.items()}
    mix(n - 1, behind)
    rows = n // 2 * tok
    clip_rows = same_ref.shape[0] - rows
    hist = jnp.zeros((clip_rows, HD), jnp.float32)
    for s in range(n):
        hist = hist + x_ref[s, 3 * tok : 3 * tok + clip_rows, :].astype(jnp.float32)
    hist = hist.astype(jnp.bfloat16)
    for flip, out_ref in ((0, same_ref), (1, cross_ref)):
        for i in range(n // 2):
            out_ref[i * tok : (i + 1) * tok, :] = mixed_ref[2 * i + (side ^ flip)]
        out_ref[rows:, :] = hist


def stack_kernel(order, cuts, tiles, *refs):
    out_ref = refs[-1]
    plane = lax.rem(lax.axis_index("head"), 2)
    at = 0
    for m, ref in zip(order, refs):
        part = ref.shape[0] // tiles
        for u in range(tiles):
            first = pl.multiple_of(u * part + plane * (part - cuts[m]), 16)
            out_ref[at : at + cuts[m], :] = ref[pl.ds(first, cuts[m]), :]
            at += cuts[m]


def late_kernel(x_ref, *refs):
    refs[-1][...] = x_ref[...]


def turn_kernel(cuts, clip_rows, order, own_in, *refs):
    pieces, (swapped_ref, own_ref, other_ref, whole) = refs[:-4], refs[-4:]
    plane = lax.rem(lax.axis_index("head"), 2)
    own = lax.axis_index("tm")
    chip, side = own // 2, lax.rem(own, 2)
    chips, all_rows, width = whole.shape
    tiles = width // HD
    for u in range(tiles):
        lanes = slice(u * HD, (u + 1) * HD)
        whole[0, :, lanes] = own_in[u * all_rows : (u + 1) * all_rows, :]
        start = 0
        for m, ref in zip(order, pieces):
            at, lo = chip_bits(m, side), cuts[m]
            part = all_rows - lo
            a = ref[u * part : (u + 1) * part, :]
            b = swapped_ref[start + u * lo : start + (u + 1) * lo, :]
            start += tiles * lo
            whole[at, 0:lo, lanes] = jnp.where(plane == 0, a[:lo], b)
            whole[at, lo:part, lanes] = jnp.where(plane == 0, a[lo:], a[: part - lo])
            whole[at, part:all_rows, lanes] = jnp.where(plane == 0, b, a[part - lo :])
    for i, out_ref in enumerate((own_ref, other_ref)):
        lanes = slice(i * width // 2, (i + 1) * width // 2)
        rows = [whole[chip ^ c, clip_rows:all_rows, lanes] for c in range(chips)]
        rows += [whole[chip ^ c, 0:clip_rows, lanes] for c in range(chips)]
        out_ref[...] = jnp.concatenate(rows, axis=0).T


def grad_part(turned_ref, head_refs, rows, copies):
    right = jnp.concatenate([x[0:rows, :] for x in head_refs], axis=1)
    hist = jnp.concatenate([x[rows:, :] for x in head_refs], axis=1)
    clip = copies * hist.shape[0]
    out = jnp.dot(turned_ref[:, 0:rows], right, preferred_element_type=jnp.float32)
    return out + jnp.dot(
        turned_ref[:, rows : rows + clip],
        jnp.concatenate([hist] * copies, axis=0),
        preferred_element_type=jnp.float32,
    )


def grad_kernel(rows, copies, heads, turned_ref, *refs):
    out_ref = refs[-1]
    out_ref[...] = grad_part(turned_ref, refs[:heads], rows, copies).astype(out_ref.dtype)


NEAR = ((0, 0), (3, 5), (4, 2), (2, 4), (5, 3))
FAR = ((1, 1), (6, 6), (7, 7))
THERE = (5, 2, 1, 4, 3, 0, 7, 6)


def store_columns(tok, heads, sums, att_hbm, out_hbm, total, sems):
    own = lax.axis_index("tm")
    side = lax.rem(own, 2)
    at = pl.multiple_of(own // 2 * tok, tok)
    moves = []

    def move(a, b):
        moves.append(pltpu.make_async_copy(a, b, sems.at[len(moves)]))
        moves[-1].start()

    def lanes(bits):
        return pl.ds(pl.multiple_of((own ^ jnp.where(side == 0, *bits)) * HD, HD), HD)

    for bits, ref in heads:
        move(ref.at[pl.ds(at, tok), :], att_hbm.at[:, lanes(bits)])
    for i, (bits, (mine, m), (got, g)) in enumerate(sums):
        columns = got[:, g * HD : (g + 1) * HD].astype(jnp.float32)
        total[i] = mine[:, m * HD : (m + 1) * HD] + columns
        move(total.at[i], out_hbm.at[:, lanes(bits)])
    for x in moves:
        x.wait()


def near_kernel(tok, own_near, got_near, *refs):
    n = len(NEAR)
    heads, outs = refs[:n], refs[n:]
    sums = [(NEAR[i], (own_near, i), (got_near, THERE[i])) for i in range(n) if THERE[i] < n]
    store_columns(tok, zip(NEAR, heads), sums, *outs)


def last_kernel(tok, own_near, got_near, own_far, got_far, *refs):
    n = len(NEAR)
    heads, outs = refs[: len(FAR)], refs[len(FAR) + 2 :]

    def column(near, far, i):
        return (near, i) if i < n else (far, i - n)

    sums = [
        (bits, column(own_near, own_far, i), column(got_near, got_far, THERE[i]))
        for i, bits in enumerate(NEAR + FAR)
        if i >= n or THERE[i] >= n
    ]
    store_columns(tok, zip(FAR, heads), sums, *outs)


def head_body(query_rows, key_rows, value_rows, frame_counts, history, offsets, cotangent):
    n = lax.axis_size("tm")
    planes = lax.axis_size("head")
    half = n // 2
    tok, width = query_rows.shape
    tile = history.shape[0]
    clip_rows = n * tile
    cot_rows, all_cols = cotangent.shape
    cols = all_cols // n
    units = cols // HD
    cuts = [0, cot_rows * 7 // 17 // 16 * 16] + [cot_rows // 32 * 16] * 2
    base = 3 * tok + clip_rows
    length = base
    rows = half * tok
    vmem = pl.BlockSpec(memory_space=pltpu.VMEM)
    hbm = pl.BlockSpec(memory_space=pl.ANY)
    bf16 = jnp.bfloat16

    def swap(x, even, odd=None):
        bits = (even, even if odd is None else odd)
        return lax.ppermute(x, "tm", [(i, i ^ bits[i % 2]) for i in range(n)])

    def swap_plane(x, bit):
        pairs = [
            (i * planes + p, (i ^ bit) * planes + (p ^ 1)) for i in range(n) for p in range(planes)
        ]
        return lax.ppermute(x, ("tm", "head"), pairs)

    def call(
        kernel, name, outs, specs, flops, scratch=(), exps=0, out_spec=vmem, limit=VMEM_LIMIT, aliases={}
    ):
        shapes = [jax.ShapeDtypeStruct(s, d) for s, d in outs]
        moved = 2 * sum(math.prod(s.shape) * s.dtype.itemsize for s in shapes)
        return pl.pallas_call(
            kernel,
            out_shape=tuple(shapes),
            in_specs=specs,
            out_specs=tuple([out_spec] * len(shapes)),
            scratch_shapes=scratch,
            input_output_aliases=aliases,
            compiler_params=pltpu.CompilerParams(vmem_limit_bytes=limit),
            cost_estimate=pl.CostEstimate(flops=flops, bytes_accessed=moved, transcendentals=exps),
            name=name,
        )

    def pack(heads, lanes, name):
        return call(
            lambda *refs: pack_kernel(n, heads, *refs),
            name,
            [((length, HD), bf16)] * len(heads),
            [hbm] * 4,
            0,
            (
                pltpu.VMEM((tok, lanes), bf16),
                pltpu.VMEM((tok, lanes), bf16),
                pltpu.VMEM((tok, lanes), bf16),
                pltpu.VMEM(history.shape, bf16),
                pltpu.SemaphoreType.DMA((4,)),
            ),
            limit=PACK_LIMIT,
        )(query_rows, key_rows, value_rows, history)

    first, rest = [6, 7], [0, 1, 2, 3, 4, 5]
    packed = dict(zip(first, pack(first, 2 * HD, "pack_first")))
    packed.update(zip(rest, pack(rest, width, "pack_rest")))
    order = [6, 7, 2, 4, 3, 5, 1]
    arrived = {k: swap(packed[k], k) for k in order}
    by_head = [packed[0]] + [arrived[k] for k in order]
    chips = range(half)
    cots = call(
        lambda *refs: cot_kernel(n, tile, cuts, *refs),
        "cot",
        [((2 * units * (cot_rows - cut), HD), bf16) for cut in cuts],
        [hbm] * 4,
        0,
        (
            pltpu.SMEM(offsets.shape, jnp.int32),
            pltpu.VMEM(cotangent.shape, bf16),
            pltpu.SemaphoreType.DMA((2,)),
        ),
    )(offsets, cotangent, arrived[6], arrived[7])
    cots = [cots[0], swap(cots[1], 2, 4), swap(cots[2], 4, 2), swap(cots[3], 6)]
    counts = (
        pltpu.VMEM((n, length, HD), bf16),
        pltpu.VMEM((n, tok, HD), bf16),
        pltpu.SMEM(frame_counts.shape, jnp.int32),
        pltpu.SemaphoreType.DMA,
    )
    pairs = half * tok * WINB * tok
    head_shape = ((rows + clip_rows, HD), bf16)
    same, cross = call(
        lambda *refs: attend_kernel(n, tok, [0] + order, *refs),
        "attend",
        [head_shape, head_shape],
        [hbm] + [vmem] * n,
        8 * pairs * HD,
        counts,
        2 * pairs,
    )(frame_counts, *by_head)
    stack_order = [3, 1, 2]
    (cot_rest,) = call(
        lambda *refs: stack_kernel(stack_order, cuts, 2 * units, *refs),
        "stack",
        [((2 * units * sum(cuts), HD), bf16)],
        [vmem] * (half - 1) + [hbm],
        0,
    )(*[cots[m] for m in stack_order], same)
    cot_swapped = swap_plane(cot_rest, 0)
    first_same, first_cross = swap(same, 2, 4), swap(cross, 3, 5)
    second_same, second_cross = swap(same, 4, 2), swap(cross, 5, 3)
    far_same, far_cross = swap(first_same, 4, 2), swap(first_cross, 2, 4)
    (late_cross,) = call(late_kernel, "late", [head_shape], [vmem] + [hbm] * 2, 0)(
        cross, second_cross, second_same
    )
    c_cross = swap(late_cross, 1)

    turned_own, turned_other = call(
        lambda *refs: turn_kernel(cuts, clip_rows, stack_order, *refs),
        "turn",
        [((cols, half * cot_rows), bf16)] * 2,
        [vmem] * (half + 1),
        0,
        (pltpu.VMEM((half, cot_rows, 2 * cols), bf16),),
    )(cots[0], *[cots[m] for m in stack_order], cot_swapped)

    def grad(turned, heads, dtype, name, behind=()):
        (out,) = call(
            lambda *refs: grad_kernel(rows, half, len(heads), *refs),
            name,
            [((cols, len(heads) * HD), dtype)],
            [vmem] * (1 + len(heads)) + [hbm] * len(behind),
            2 * cols * half * cot_rows * len(heads) * HD,
        )(turned, *heads, *behind)
        return out

    near = [same, second_cross, second_same, first_same, first_cross]
    far = [c_cross, far_same, far_cross]
    whole = [((tok, width), bf16), ((cols, width), jnp.float32)]
    got_near = swap(grad(turned_other, near, bf16, "grad_other_near"), 1)
    own_near = grad(turned_own, near, jnp.float32, "grad_own_near")
    got_far = swap(grad(turned_other, far, bf16, "grad_other_far", (own_near,)), 1)
    own_far = grad(turned_own, far, jnp.float32, "grad_own_far")
    halfway = call(
        lambda *refs: near_kernel(tok, *refs),
        "near",
        whole,
        [vmem] * (2 + len(near)),
        0,
        (pltpu.VMEM((4, cols, HD), jnp.float32), pltpu.SemaphoreType.DMA((9,))),
        out_spec=hbm,
    )(own_near, got_near, *near)
    return call(
        lambda *refs: last_kernel(tok, *refs),
        "last",
        whole,
        [vmem] * (4 + len(far)) + [hbm] * 2,
        0,
        (pltpu.VMEM((4, cols, HD), jnp.float32), pltpu.SemaphoreType.DMA((7,))),
        out_spec=hbm,
        aliases={4 + len(far): 0, 5 + len(far): 1},
    )(own_near, got_near, own_far, got_far, *far, *halfway)


def body(query_rows, key_rows, value_rows, frame_counts, history, offsets, cotangent):
    n = lax.axis_size("tm")
    tok, width = query_rows.shape
    by_heads = (
        n == 8
        and lax.axis_size("head") % 2 == 0
        and width == n * HD
        and offsets.shape[1] == n
        and cotangent.shape[0] == tok + n * history.shape[0]
        and cotangent.shape[1] % (n * HD) == 0
        and tok % 16 == 0
        and (n * history.shape[0]) % 16 == 0
    )
    plan = head_body if by_heads else window_body
    return plan(query_rows, key_rows, value_rows, frame_counts, history, offsets, cotangent)


def solution(mesh):
    in_specs = (
        P("tm", "head"),
        P("tm", "head"),
        P("tm", "head"),
        P(),
        P("tm", "head"),
        P("tm", None),
        P("tm", None),
    )
    out_specs = (P("tm", "head"), P("tm", "head"))
    return jax.shard_map(body, mesh=mesh, in_specs=in_specs, out_specs=out_specs, check_vma=False)
```

```python
import math

import jax
import jax.numpy as jnp
from jax import lax
from jax.experimental import pallas as pl
from jax.experimental.pallas import tpu as pltpu
from jax.sharding import PartitionSpec as P

HD = 128
TPF = 64
WINB = 4
VMEM_LIMIT = 24 * 1024 * 1024
PACK_LIMIT = 58 * 1024 * 1024


def from_behind(x, axis, by):
    devices = lax.axis_size(axis)
    pairs = [(i, i + by) for i in range(devices) if 0 <= i + by < devices]
    return lax.ppermute(x, axis, pairs)


def window_body(query_rows, key_rows, value_rows, frame_counts, history, offsets, cotangent):
    tok_rows, feat_width = query_rows.shape
    local_heads = feat_width // HD
    block_total = lax.axis_size("tm")
    own_block = lax.axis_index("tm")
    score_scale = 1.0 / math.sqrt(HD)
    key_value = jnp.stack([key_rows, value_rows])
    pieces = []
    for distance in range(WINB - 1, 0, -1):
        pieces.append(from_behind(key_value, "tm", distance))
    window = jnp.concatenate(pieces + [key_value], axis=1)
    source_block = own_block - (WINB - 1) + jnp.arange(WINB, dtype=jnp.int32)
    block_match = jnp.arange(block_total, dtype=jnp.int32)[None, :] == source_block[:, None]
    block_count = jnp.sum(jnp.where(block_match, frame_counts[None, :], 0), axis=1)
    frame_index = jnp.arange(tok_rows, dtype=jnp.int32) // TPF
    kept_mask = (
        (source_block[:, None] >= 0) & (frame_index[None, :] < block_count[:, None])
    ).reshape(WINB * tok_rows)
    key_window = window[0].reshape(WINB * tok_rows, local_heads, HD)
    value_window = window[1].reshape(WINB * tok_rows, local_heads, HD)
    query_heads = query_rows.reshape(tok_rows, local_heads, HD)
    scores = (
        jnp.einsum("qhd,khd->hqk", query_heads, key_window, preferred_element_type=jnp.float32)
        * score_scale
    )
    scores = jnp.where(kept_mask[None, None, :], scores, -jnp.inf)
    row_max = jnp.max(scores, axis=-1, keepdims=True)
    weights = jnp.exp(scores - row_max)
    probs = (weights / jnp.sum(weights, axis=-1, keepdims=True)).astype(jnp.bfloat16)
    mixed = jnp.einsum("hqk,khd->qhd", probs, value_window, preferred_element_type=jnp.float32)
    attended = mixed.astype(jnp.bfloat16).reshape(tok_rows, feat_width)
    tile_rows = history.shape[0]
    source_tile = (own_block - offsets[0]) % block_total
    source_row = (
        source_tile[:, None] * tile_rows + jnp.arange(tile_rows, dtype=jnp.int32)[None, :]
    ).reshape(-1)
    incoming = lax.all_gather(history, "tm", axis=0, tiled=True)
    piece_rows = incoming.shape[0]
    selector = (source_row[:, None] == jnp.arange(piece_rows, dtype=jnp.int32)[None, :]).astype(
        jnp.bfloat16
    )
    clip_hist = jnp.dot(selector, incoming, preferred_element_type=jnp.float32).astype(jnp.bfloat16)
    disc_clip = jnp.concatenate([clip_hist, attended], axis=0)
    disc_grad = lax.psum_scatter(
        lax.dot_general(
            cotangent, disc_clip, (((0,), (0,)), ((), ())), preferred_element_type=jnp.float32
        ),
        "tm",
        scatter_dimension=0,
        tiled=True,
    )
    return (attended, disc_grad)


def chip_bits(m, side):
    return m if m in (0, 3) else jnp.where(side == 0, m, 3 - m)


def cot_kernel(n, tile, cuts, off_hbm, cot_hbm, *refs):
    outs, (off, cot, sems) = refs[-3 - n // 2 : -3], refs[-3:]
    own = lax.axis_index("tm")
    chip, side = own // 2, lax.rem(own, 2)
    plane = lax.rem(lax.axis_index("head"), 2)
    clip_rows = n * tile
    all_rows, all_cols = cot.shape
    cols = all_cols // n
    fetch_off = pltpu.make_async_copy(off_hbm, off, sems.at[0])
    fetch_cot = pltpu.make_async_copy(cot_hbm, cot, sems.at[1])
    fetch_off.start()
    fetch_cot.start()
    fetch_off.wait()
    r = lax.broadcasted_iota(jnp.int32, (clip_rows, clip_rows), 0)
    c = lax.broadcasted_iota(jnp.int32, (clip_rows, clip_rows), 1)
    select = jnp.zeros((clip_rows, clip_rows), jnp.float32)
    for j in range(n):
        src = lax.rem(own - off[0, j] + 2 * n, n)
        for t in range(tile):
            select = jnp.where((c == j * tile + t) & (r == src * tile + t), 1.0, select)
    fetch_cot.wait()
    cot[0:clip_rows, :] = jnp.dot(
        select.astype(jnp.bfloat16), cot[0:clip_rows, :], preferred_element_type=jnp.float32
    ).astype(jnp.bfloat16)
    units = cols // HD
    for m, out_ref in enumerate(outs):
        rows, first = all_rows - cuts[m], pl.multiple_of(plane * cuts[m], 16)
        there = chip ^ chip_bits(m, side)
        for i, block in enumerate((2 * there + side, 2 * there + 1 - side)):
            for u in range(units):
                at = (i * units + u) * rows
                lanes = pl.ds(pl.multiple_of(block * cols + u * HD, HD), HD)
                out_ref[at : at + rows, :] = cot[pl.ds(first, rows), lanes]


def pack_kernel(n, heads, q_hbm, k_hbm, v_hbm, hist_hbm, *refs):
    outs, (q, k, v, hist, sems) = refs[:-5], refs[-5:]
    own = lax.axis_index("tm")
    tok, width = q.shape
    tile = hist.shape[0]
    clip_rows = n * tile
    start = 0 if width == n * HD else pl.multiple_of(((own ^ heads[0]) // 2) * width, width)
    pairs = [(hist_hbm, hist)] + [
        (x.at[:, pl.ds(start, width)], y) for x, y in ((q_hbm, q), (k_hbm, k), (v_hbm, v))
    ]
    copies = [pltpu.make_async_copy(a, b, sems.at[i]) for i, (a, b) in enumerate(pairs)]
    for copy in copies:
        copy.start()
    copies[0].wait()
    for d, out_ref in zip(heads, outs):
        lanes = pl.ds(pl.multiple_of((own ^ d) * HD, HD), HD)
        tiles = hist[:, lanes].astype(jnp.float32)
        row = lax.broadcasted_iota(jnp.int32, (clip_rows, HD), 0)
        placed = jnp.zeros((clip_rows, HD), jnp.float32)
        for t in range(tile):
            placed = jnp.where(row == own * tile + t, tiles[t : t + 1, :], placed)
        out_ref[3 * tok : 3 * tok + clip_rows, :] = placed.astype(jnp.bfloat16)
    for i, x in enumerate((q, k, v)):
        copies[1 + i].wait()
        for d, out_ref in zip(heads, outs):
            lanes = pl.ds(pl.multiple_of((own ^ d) * HD - start, HD), HD)
            out_ref[i * tok : (i + 1) * tok, :] = x[:, lanes]


def attend_kernel(n, tok, order, counts_hbm, *refs):
    parts, (same_ref, cross_ref, x_ref, mixed_ref, counts, sem) = refs[:n], refs[n:]
    copy = pltpu.make_async_copy(counts_hbm, counts, sem)
    copy.start()
    own = lax.axis_index("tm")
    side = lax.rem(own, 2)
    for k, part in zip(order, parts):
        x_ref[own ^ k] = part[...]
    copy.wait()
    rate = math.log2(math.e) / math.sqrt(HD)
    token = lax.broadcasted_iota(jnp.int32, (tok, 1), 0)
    bias = [
        jnp.where(token < counts[s] * TPF, 0.0, -jnp.inf).astype(jnp.float32) for s in range(n)
    ]
    values = [x_ref[s, 2 * tok : 3 * tok, :].T for s in range(n)]
    def scores_of(block):
        q = x_ref[block, 0:tok, :]
        return {
            s: lax.dot_general(
                x_ref[s, tok : 2 * tok, :],
                q,
                (((1,), (1,)), ((), ())),
                preferred_element_type=jnp.float32,
            )
            + bias[s]
            for s in range(max(0, block - (WINB - 1)), block + 1)
        }

    def mix(block, probs):
        mixed = jnp.zeros((HD, tok), jnp.float32)
        for s, p in probs.items():
            mixed = mixed + jnp.dot(values[s], p, preferred_element_type=jnp.float32)
        mixed_ref[block] = mixed.astype(jnp.bfloat16).T

    ahead, behind = scores_of(0), None
    for block in range(n):
        scores, ahead = ahead, scores_of(block + 1) if block + 1 < n else None
        if behind is not None:
            mix(block - 1, behind)
        top = None
        for x in scores.values():
            high = jnp.max(x, axis=0, keepdims=True)
            top = high if top is None else jnp.maximum(top, high)
        weights = {s: jnp.exp2((x - top) * rate) for s, x in scores.items()}
        total = jnp.zeros((1, tok), jnp.float32)
        for w in weights.values():
            total = total + jnp.sum(w, axis=0, keepdims=True)
        share = 1.0 / total
        behind = {s: (w * share).astype(jnp.bfloat16) for s, w in weights.items()}
    mix(n - 1, behind)
    rows = n // 2 * tok
    clip_rows = same_ref.shape[0] - rows
    hist = jnp.zeros((clip_rows, HD), jnp.float32)
    for s in range(n):
        hist = hist + x_ref[s, 3 * tok : 3 * tok + clip_rows, :].astype(jnp.float32)
    hist = hist.astype(jnp.bfloat16)
    for flip, out_ref in ((0, same_ref), (1, cross_ref)):
        for i in range(n // 2):
            out_ref[i * tok : (i + 1) * tok, :] = mixed_ref[2 * i + (side ^ flip)]
        out_ref[rows:, :] = hist


def stack_kernel(order, cuts, tiles, *refs):
    out_ref = refs[-1]
    plane = lax.rem(lax.axis_index("head"), 2)
    at = 0
    for m, ref in zip(order, refs):
        part = ref.shape[0] // tiles
        for u in range(tiles):
            first = pl.multiple_of(u * part + plane * (part - cuts[m]), 16)
            out_ref[at : at + cuts[m], :] = ref[pl.ds(first, cuts[m]), :]
            at += cuts[m]


def late_kernel(x_ref, *refs):
    refs[-1][...] = x_ref[...]


def turn_kernel(cuts, clip_rows, order, own_in, *refs):
    pieces, (swapped_ref, own_ref, other_ref, whole) = refs[:-4], refs[-4:]
    plane = lax.rem(lax.axis_index("head"), 2)
    own = lax.axis_index("tm")
    chip, side = own // 2, lax.rem(own, 2)
    chips, all_rows, width = whole.shape
    tiles = width // HD
    for u in range(tiles):
        lanes = slice(u * HD, (u + 1) * HD)
        whole[0, :, lanes] = own_in[u * all_rows : (u + 1) * all_rows, :]
        start = 0
        for m, ref in zip(order, pieces):
            at, lo = chip_bits(m, side), cuts[m]
            part = all_rows - lo
            a = ref[u * part : (u + 1) * part, :]
            b = swapped_ref[start + u * lo : start + (u + 1) * lo, :]
            start += tiles * lo
            whole[at, 0:lo, lanes] = jnp.where(plane == 0, a[:lo], b)
            whole[at, lo:part, lanes] = jnp.where(plane == 0, a[lo:], a[: part - lo])
            whole[at, part:all_rows, lanes] = jnp.where(plane == 0, b, a[part - lo :])
    for i, out_ref in enumerate((own_ref, other_ref)):
        lanes = slice(i * width // 2, (i + 1) * width // 2)
        rows = [whole[chip ^ c, clip_rows:all_rows, lanes] for c in range(chips)]
        rows += [whole[chip ^ c, 0:clip_rows, lanes] for c in range(chips)]
        out_ref[...] = jnp.concatenate(rows, axis=0).T


def grad_part(turned_ref, head_refs, rows, copies):
    right = jnp.concatenate([x[0:rows, :] for x in head_refs], axis=1)
    hist = jnp.concatenate([x[rows:, :] for x in head_refs], axis=1)
    clip = copies * hist.shape[0]
    out = jnp.dot(turned_ref[:, 0:rows], right, preferred_element_type=jnp.float32)
    return out + jnp.dot(
        turned_ref[:, rows : rows + clip],
        jnp.concatenate([hist] * copies, axis=0),
        preferred_element_type=jnp.float32,
    )


def grad_kernel(rows, copies, heads, turned_ref, *refs):
    out_ref = refs[-1]
    out_ref[...] = grad_part(turned_ref, refs[:heads], rows, copies).astype(out_ref.dtype)


NEAR = ((0, 0), (3, 5), (4, 2), (2, 4), (5, 3))
FAR = ((1, 1), (6, 6), (7, 7))
THERE = (5, 2, 1, 4, 3, 0, 7, 6)


def store_columns(tok, heads, sums, att_hbm, out_hbm, total, sems):
    own = lax.axis_index("tm")
    side = lax.rem(own, 2)
    at = pl.multiple_of(own // 2 * tok, tok)
    moves = []

    def move(a, b):
        moves.append(pltpu.make_async_copy(a, b, sems.at[len(moves)]))
        moves[-1].start()

    def lanes(bits):
        return pl.ds(pl.multiple_of((own ^ jnp.where(side == 0, *bits)) * HD, HD), HD)

    for bits, ref in heads:
        move(ref.at[pl.ds(at, tok), :], att_hbm.at[:, lanes(bits)])
    for i, (bits, (mine, m), (got, g)) in enumerate(sums):
        columns = got[:, g * HD : (g + 1) * HD].astype(jnp.float32)
        total[i] = mine[:, m * HD : (m + 1) * HD] + columns
        move(total.at[i], out_hbm.at[:, lanes(bits)])
    for x in moves:
        x.wait()


def own_near_kernel(rows, copies, tok, turned_ref, *refs):
    n = len(NEAR)
    heads, (out_ref, att_hbm, sems) = refs[:n], refs[n:]
    own = lax.axis_index("tm")
    side = lax.rem(own, 2)
    at = pl.multiple_of(own // 2 * tok, tok)
    moves = []
    for i, (bits, ref) in enumerate(zip(NEAR, heads)):
        lanes = pl.ds(pl.multiple_of((own ^ jnp.where(side == 0, *bits)) * HD, HD), HD)
        moves.append(
            pltpu.make_async_copy(ref.at[pl.ds(at, tok), :], att_hbm.at[:, lanes], sems.at[i])
        )
        moves[-1].start()
    out_ref[...] = grad_part(turned_ref, heads, rows, copies)
    for x in moves:
        x.wait()


def near_kernel(tok, own_near, got_near, *refs):
    n = len(NEAR)
    sums = [(NEAR[i], (own_near, i), (got_near, THERE[i])) for i in range(n) if THERE[i] < n]
    store_columns(tok, [], sums, None, *refs)


def last_kernel(tok, own_near, got_near, own_far, got_far, *refs):
    n = len(NEAR)
    heads, outs = refs[: len(FAR)], refs[len(FAR) + 2 :]

    def column(near, far, i):
        return (near, i) if i < n else (far, i - n)

    sums = [
        (bits, column(own_near, own_far, i), column(got_near, got_far, THERE[i]))
        for i, bits in enumerate(NEAR + FAR)
        if i >= n or THERE[i] >= n
    ]
    store_columns(tok, zip(FAR, heads), sums, *outs)


def head_body(query_rows, key_rows, value_rows, frame_counts, history, offsets, cotangent):
    n = lax.axis_size("tm")
    planes = lax.axis_size("head")
    half = n // 2
    tok, width = query_rows.shape
    tile = history.shape[0]
    clip_rows = n * tile
    cot_rows, all_cols = cotangent.shape
    cols = all_cols // n
    units = cols // HD
    cuts = [0, cot_rows * 7 // 17 // 16 * 16] + [cot_rows // 32 * 16] * 2
    base = 3 * tok + clip_rows
    length = base
    rows = half * tok
    vmem = pl.BlockSpec(memory_space=pltpu.VMEM)
    hbm = pl.BlockSpec(memory_space=pl.ANY)
    bf16 = jnp.bfloat16

    def swap(x, even, odd=None):
        bits = (even, even if odd is None else odd)
        return lax.ppermute(x, "tm", [(i, i ^ bits[i % 2]) for i in range(n)])

    def swap_plane(x, bit):
        pairs = [
            (i * planes + p, (i ^ bit) * planes + (p ^ 1)) for i in range(n) for p in range(planes)
        ]
        return lax.ppermute(x, ("tm", "head"), pairs)

    def call(
        kernel, name, outs, specs, flops, scratch=(), exps=0, out_spec=vmem, limit=VMEM_LIMIT, aliases={}
    ):
        shapes = [jax.ShapeDtypeStruct(s, d) for s, d in outs]
        moved = 2 * sum(math.prod(s.shape) * s.dtype.itemsize for s in shapes)
        return pl.pallas_call(
            kernel,
            out_shape=tuple(shapes),
            in_specs=specs,
            out_specs=out_spec if isinstance(out_spec, tuple) else (out_spec,) * len(shapes),
            scratch_shapes=scratch,
            input_output_aliases=aliases,
            compiler_params=pltpu.CompilerParams(vmem_limit_bytes=limit),
            cost_estimate=pl.CostEstimate(flops=flops, bytes_accessed=moved, transcendentals=exps),
            name=name,
        )

    def pack(heads, lanes, name):
        return call(
            lambda *refs: pack_kernel(n, heads, *refs),
            name,
            [((length, HD), bf16)] * len(heads),
            [hbm] * 4,
            0,
            (
                pltpu.VMEM((tok, lanes), bf16),
                pltpu.VMEM((tok, lanes), bf16),
                pltpu.VMEM((tok, lanes), bf16),
                pltpu.VMEM(history.shape, bf16),
                pltpu.SemaphoreType.DMA((4,)),
            ),
            limit=PACK_LIMIT,
        )(query_rows, key_rows, value_rows, history)

    first, rest = [6, 7], [0, 1, 2, 3, 4, 5]
    packed = dict(zip(first, pack(first, 2 * HD, "pack_first")))
    packed.update(zip(rest, pack(rest, width, "pack_rest")))
    order = [6, 7, 2, 4, 3, 5, 1]
    arrived = {k: swap(packed[k], k) for k in order}
    by_head = [packed[0]] + [arrived[k] for k in order]
    chips = range(half)
    cots = call(
        lambda *refs: cot_kernel(n, tile, cuts, *refs),
        "cot",
        [((2 * units * (cot_rows - cut), HD), bf16) for cut in cuts],
        [hbm] * 4,
        0,
        (
            pltpu.SMEM(offsets.shape, jnp.int32),
            pltpu.VMEM(cotangent.shape, bf16),
            pltpu.SemaphoreType.DMA((2,)),
        ),
    )(offsets, cotangent, arrived[6], arrived[7])
    cots = [cots[0], swap(cots[1], 2, 4), swap(cots[2], 4, 2), swap(cots[3], 6)]
    counts = (
        pltpu.VMEM((n, length, HD), bf16),
        pltpu.VMEM((n, tok, HD), bf16),
        pltpu.SMEM(frame_counts.shape, jnp.int32),
        pltpu.SemaphoreType.DMA,
    )
    pairs = half * tok * WINB * tok
    head_shape = ((rows + clip_rows, HD), bf16)
    same, cross = call(
        lambda *refs: attend_kernel(n, tok, [0] + order, *refs),
        "attend",
        [head_shape, head_shape],
        [hbm] + [vmem] * n,
        8 * pairs * HD,
        counts,
        2 * pairs,
    )(frame_counts, *by_head)
    stack_order = [3, 1, 2]
    (cot_rest,) = call(
        lambda *refs: stack_kernel(stack_order, cuts, 2 * units, *refs),
        "stack",
        [((2 * units * sum(cuts), HD), bf16)],
        [vmem] * (half - 1) + [hbm],
        0,
    )(*[cots[m] for m in stack_order], same)
    cot_swapped = swap_plane(cot_rest, 0)
    first_same, first_cross = swap(same, 2, 4), swap(cross, 3, 5)
    second_same, second_cross = swap(same, 4, 2), swap(cross, 5, 3)
    far_same, far_cross = swap(first_same, 4, 2), swap(first_cross, 2, 4)
    (late_cross,) = call(late_kernel, "late", [head_shape], [vmem] + [hbm] * 2, 0)(
        cross, second_cross, second_same
    )
    c_cross = swap(late_cross, 1)

    turned_own, turned_other = call(
        lambda *refs: turn_kernel(cuts, clip_rows, stack_order, *refs),
        "turn",
        [((cols, half * cot_rows), bf16)] * 2,
        [vmem] * (half + 1),
        0,
        (pltpu.VMEM((half, cot_rows, 2 * cols), bf16),),
    )(cots[0], *[cots[m] for m in stack_order], cot_swapped)

    def grad(turned, heads, dtype, name, behind=()):
        (out,) = call(
            lambda *refs: grad_kernel(rows, half, len(heads), *refs),
            name,
            [((cols, len(heads) * HD), dtype)],
            [vmem] * (1 + len(heads)) + [hbm] * len(behind),
            2 * cols * half * cot_rows * len(heads) * HD,
        )(turned, *heads, *behind)
        return out

    near = [same, second_cross, second_same, first_same, first_cross]
    far = [c_cross, far_same, far_cross]
    whole = [((tok, width), bf16), ((cols, width), jnp.float32)]
    got_near = swap(grad(turned_other, near, bf16, "grad_other_near"), 1)
    own_near, attended = call(
        lambda *refs: own_near_kernel(rows, half, tok, *refs),
        "grad_own_near",
        [((cols, len(near) * HD), jnp.float32), whole[0]],
        [vmem] * (1 + len(near)),
        2 * cols * half * cot_rows * len(near) * HD,
        (pltpu.SemaphoreType.DMA((len(near),)),),
        out_spec=(vmem, hbm),
    )(turned_own, *near)
    got_far = swap(grad(turned_other, far, bf16, "grad_other_far", (own_near,)), 1)
    own_far = grad(turned_own, far, jnp.float32, "grad_own_far")
    (grads,) = call(
        lambda *refs: near_kernel(tok, *refs),
        "near",
        whole[1:],
        [vmem] * 2,
        0,
        (pltpu.VMEM((4, cols, HD), jnp.float32), pltpu.SemaphoreType.DMA((4,))),
        out_spec=hbm,
    )(own_near, got_near)
    return call(
        lambda *refs: last_kernel(tok, *refs),
        "last",
        whole,
        [vmem] * (4 + len(far)) + [hbm] * 2,
        0,
        (pltpu.VMEM((4, cols, HD), jnp.float32), pltpu.SemaphoreType.DMA((7,))),
        out_spec=hbm,
        aliases={4 + len(far): 0, 5 + len(far): 1},
    )(own_near, got_near, own_far, got_far, *far, attended, grads)


def body(query_rows, key_rows, value_rows, frame_counts, history, offsets, cotangent):
    n = lax.axis_size("tm")
    tok, width = query_rows.shape
    by_heads = (
        n == 8
        and lax.axis_size("head") % 2 == 0
        and width == n * HD
        and offsets.shape[1] == n
        and cotangent.shape[0] == tok + n * history.shape[0]
        and cotangent.shape[1] % (n * HD) == 0
        and tok % 16 == 0
        and (n * history.shape[0]) % 16 == 0
    )
    plan = head_body if by_heads else window_body
    return plan(query_rows, key_rows, value_rows, frame_counts, history, offsets, cotangent)


def solution(mesh):
    in_specs = (
        P("tm", "head"),
        P("tm", "head"),
        P("tm", "head"),
        P(),
        P("tm", "head"),
        P("tm", None),
        P("tm", None),
    )
    out_specs = (P("tm", "head"), P("tm", "head"))
    return jax.shard_map(body, mesh=mesh, in_specs=in_specs, out_specs=out_specs, check_vma=False)
```

```python
import math

import jax
import jax.numpy as jnp
from jax import lax
from jax.experimental import pallas as pl
from jax.experimental.pallas import tpu as pltpu
from jax.sharding import PartitionSpec as P

HD = 128
TPF = 64
WINB = 4
VMEM_LIMIT = 24 * 1024 * 1024
PACK_LIMIT = 58 * 1024 * 1024


def from_behind(x, axis, by):
    devices = lax.axis_size(axis)
    pairs = [(i, i + by) for i in range(devices) if 0 <= i + by < devices]
    return lax.ppermute(x, axis, pairs)


def window_body(query_rows, key_rows, value_rows, frame_counts, history, offsets, cotangent):
    tok_rows, feat_width = query_rows.shape
    local_heads = feat_width // HD
    block_total = lax.axis_size("tm")
    own_block = lax.axis_index("tm")
    score_scale = 1.0 / math.sqrt(HD)
    key_value = jnp.stack([key_rows, value_rows])
    pieces = []
    for distance in range(WINB - 1, 0, -1):
        pieces.append(from_behind(key_value, "tm", distance))
    window = jnp.concatenate(pieces + [key_value], axis=1)
    source_block = own_block - (WINB - 1) + jnp.arange(WINB, dtype=jnp.int32)
    block_match = jnp.arange(block_total, dtype=jnp.int32)[None, :] == source_block[:, None]
    block_count = jnp.sum(jnp.where(block_match, frame_counts[None, :], 0), axis=1)
    frame_index = jnp.arange(tok_rows, dtype=jnp.int32) // TPF
    kept_mask = (
        (source_block[:, None] >= 0) & (frame_index[None, :] < block_count[:, None])
    ).reshape(WINB * tok_rows)
    key_window = window[0].reshape(WINB * tok_rows, local_heads, HD)
    value_window = window[1].reshape(WINB * tok_rows, local_heads, HD)
    query_heads = query_rows.reshape(tok_rows, local_heads, HD)
    scores = (
        jnp.einsum("qhd,khd->hqk", query_heads, key_window, preferred_element_type=jnp.float32)
        * score_scale
    )
    scores = jnp.where(kept_mask[None, None, :], scores, -jnp.inf)
    row_max = jnp.max(scores, axis=-1, keepdims=True)
    weights = jnp.exp(scores - row_max)
    probs = (weights / jnp.sum(weights, axis=-1, keepdims=True)).astype(jnp.bfloat16)
    mixed = jnp.einsum("hqk,khd->qhd", probs, value_window, preferred_element_type=jnp.float32)
    attended = mixed.astype(jnp.bfloat16).reshape(tok_rows, feat_width)
    tile_rows = history.shape[0]
    source_tile = (own_block - offsets[0]) % block_total
    source_row = (
        source_tile[:, None] * tile_rows + jnp.arange(tile_rows, dtype=jnp.int32)[None, :]
    ).reshape(-1)
    incoming = lax.all_gather(history, "tm", axis=0, tiled=True)
    piece_rows = incoming.shape[0]
    selector = (source_row[:, None] == jnp.arange(piece_rows, dtype=jnp.int32)[None, :]).astype(
        jnp.bfloat16
    )
    clip_hist = jnp.dot(selector, incoming, preferred_element_type=jnp.float32).astype(jnp.bfloat16)
    disc_clip = jnp.concatenate([clip_hist, attended], axis=0)
    disc_grad = lax.psum_scatter(
        lax.dot_general(
            cotangent, disc_clip, (((0,), (0,)), ((), ())), preferred_element_type=jnp.float32
        ),
        "tm",
        scatter_dimension=0,
        tiled=True,
    )
    return (attended, disc_grad)


def chip_bits(m, side):
    return m if m in (0, 3) else jnp.where(side == 0, m, 3 - m)


def cot_kernel(n, tile, cuts, off_hbm, cot_hbm, *refs):
    outs, (off, cot, sems) = refs[-3 - n // 2 : -3], refs[-3:]
    own = lax.axis_index("tm")
    chip, side = own // 2, lax.rem(own, 2)
    plane = lax.rem(lax.axis_index("head"), 2)
    clip_rows = n * tile
    all_rows, all_cols = cot.shape
    cols = all_cols // n
    fetch_off = pltpu.make_async_copy(off_hbm, off, sems.at[0])
    fetch_cot = pltpu.make_async_copy(cot_hbm, cot, sems.at[1])
    fetch_off.start()
    fetch_cot.start()
    fetch_off.wait()
    r = lax.broadcasted_iota(jnp.int32, (clip_rows, clip_rows), 0)
    c = lax.broadcasted_iota(jnp.int32, (clip_rows, clip_rows), 1)
    select = jnp.zeros((clip_rows, clip_rows), jnp.float32)
    for j in range(n):
        src = lax.rem(own - off[0, j] + 2 * n, n)
        for t in range(tile):
            select = jnp.where((c == j * tile + t) & (r == src * tile + t), 1.0, select)
    fetch_cot.wait()
    cot[0:clip_rows, :] = jnp.dot(
        select.astype(jnp.bfloat16), cot[0:clip_rows, :], preferred_element_type=jnp.float32
    ).astype(jnp.bfloat16)
    units = cols // HD
    for m, out_ref in enumerate(outs):
        rows, first = all_rows - cuts[m], pl.multiple_of(plane * cuts[m], 16)
        there = chip ^ chip_bits(m, side)
        for i, block in enumerate((2 * there + side, 2 * there + 1 - side)):
            for u in range(units):
                at = (i * units + u) * rows
                lanes = pl.ds(pl.multiple_of(block * cols + u * HD, HD), HD)
                out_ref[at : at + rows, :] = cot[pl.ds(first, rows), lanes]


def pack_kernel(n, heads, q_hbm, k_hbm, v_hbm, hist_hbm, *refs):
    outs, (q, k, v, hist, sems) = refs[:-5], refs[-5:]
    own = lax.axis_index("tm")
    tok, width = q.shape
    tile = hist.shape[0]
    clip_rows = n * tile
    start = 0 if width == n * HD else pl.multiple_of(((own ^ heads[0]) // 2) * width, width)
    pairs = [(hist_hbm, hist)] + [
        (x.at[:, pl.ds(start, width)], y) for x, y in ((q_hbm, q), (k_hbm, k), (v_hbm, v))
    ]
    copies = [pltpu.make_async_copy(a, b, sems.at[i]) for i, (a, b) in enumerate(pairs)]
    for copy in copies:
        copy.start()
    copies[0].wait()
    for d, out_ref in zip(heads, outs):
        lanes = pl.ds(pl.multiple_of((own ^ d) * HD, HD), HD)
        tiles = hist[:, lanes].astype(jnp.float32)
        row = lax.broadcasted_iota(jnp.int32, (clip_rows, HD), 0)
        placed = jnp.zeros((clip_rows, HD), jnp.float32)
        for t in range(tile):
            placed = jnp.where(row == own * tile + t, tiles[t : t + 1, :], placed)
        out_ref[3 * tok : 3 * tok + clip_rows, :] = placed.astype(jnp.bfloat16)
    for i, x in enumerate((q, k, v)):
        copies[1 + i].wait()
        for d, out_ref in zip(heads, outs):
            lanes = pl.ds(pl.multiple_of((own ^ d) * HD - start, HD), HD)
            out_ref[i * tok : (i + 1) * tok, :] = x[:, lanes]


def attend_kernel(n, tok, order, counts_hbm, *refs):
    parts, (same_ref, cross_ref, x_ref, mixed_ref, counts, sem) = refs[:n], refs[n:]
    copy = pltpu.make_async_copy(counts_hbm, counts, sem)
    copy.start()
    own = lax.axis_index("tm")
    side = lax.rem(own, 2)
    for k, part in zip(order, parts):
        x_ref[own ^ k] = part[...]
    copy.wait()
    rate = math.log2(math.e) / math.sqrt(HD)
    token = lax.broadcasted_iota(jnp.int32, (tok, 1), 0)
    bias = [
        jnp.where(token < counts[s] * TPF, 0.0, -jnp.inf).astype(jnp.float32) for s in range(n)
    ]
    values = []
    def scores_of(block):
        q = x_ref[block, 0:tok, :]
        return {
            s: lax.dot_general(
                x_ref[s, tok : 2 * tok, :],
                q,
                (((1,), (1,)), ((), ())),
                preferred_element_type=jnp.float32,
            )
            + bias[s]
            for s in range(max(0, block - (WINB - 1)), block + 1)
        }

    def mix(block, probs):
        mixed = jnp.zeros((HD, tok), jnp.float32)
        for s, p in probs.items():
            mixed = mixed + jnp.dot(values[s], p, preferred_element_type=jnp.float32)
        mixed_ref[block] = mixed.astype(jnp.bfloat16).T

    ahead, behind = scores_of(0), None
    for block in range(n):
        scores, ahead = ahead, scores_of(block + 1) if block + 1 < n else None
        if behind is not None:
            mix(block - 1, behind)
        values.append(x_ref[block, 2 * tok : 3 * tok, :].T)
        top = None
        for x in scores.values():
            high = jnp.max(x, axis=0, keepdims=True)
            top = high if top is None else jnp.maximum(top, high)
        weights = {s: jnp.exp2((x - top) * rate) for s, x in scores.items()}
        total = jnp.zeros((1, tok), jnp.float32)
        for w in weights.values():
            total = total + jnp.sum(w, axis=0, keepdims=True)
        share = 1.0 / total
        behind = {s: (w * share).astype(jnp.bfloat16) for s, w in weights.items()}
    mix(n - 1, behind)
    rows = n // 2 * tok
    clip_rows = same_ref.shape[0] - rows
    hist = jnp.zeros((clip_rows, HD), jnp.float32)
    for s in range(n):
        hist = hist + x_ref[s, 3 * tok : 3 * tok + clip_rows, :].astype(jnp.float32)
    hist = hist.astype(jnp.bfloat16)
    for flip, out_ref in ((0, same_ref), (1, cross_ref)):
        for i in range(n // 2):
            out_ref[i * tok : (i + 1) * tok, :] = mixed_ref[2 * i + (side ^ flip)]
        out_ref[rows:, :] = hist


def stack_kernel(order, cuts, tiles, *refs):
    out_ref = refs[-1]
    plane = lax.rem(lax.axis_index("head"), 2)
    at = 0
    for m, ref in zip(order, refs):
        part = ref.shape[0] // tiles
        for u in range(tiles):
            first = pl.multiple_of(u * part + plane * (part - cuts[m]), 16)
            out_ref[at : at + cuts[m], :] = ref[pl.ds(first, cuts[m]), :]
            at += cuts[m]


def late_kernel(x_ref, *refs):
    refs[-1][...] = x_ref[...]


def turn_kernel(cuts, clip_rows, order, own_in, *refs):
    pieces, (swapped_ref, own_ref, other_ref, whole) = refs[:-4], refs[-4:]
    plane = lax.rem(lax.axis_index("head"), 2)
    own = lax.axis_index("tm")
    chip, side = own // 2, lax.rem(own, 2)
    chips, all_rows, width = whole.shape
    tiles = width // HD
    for u in range(tiles):
        lanes = slice(u * HD, (u + 1) * HD)
        whole[0, :, lanes] = own_in[u * all_rows : (u + 1) * all_rows, :]
        start = 0
        for m, ref in zip(order, pieces):
            at, lo = chip_bits(m, side), cuts[m]
            part = all_rows - lo
            a = ref[u * part : (u + 1) * part, :]
            b = swapped_ref[start + u * lo : start + (u + 1) * lo, :]
            start += tiles * lo
            whole[at, 0:lo, lanes] = jnp.where(plane == 0, a[:lo], b)
            whole[at, lo:part, lanes] = jnp.where(plane == 0, a[lo:], a[: part - lo])
            whole[at, part:all_rows, lanes] = jnp.where(plane == 0, b, a[part - lo :])
    for i, out_ref in enumerate((own_ref, other_ref)):
        lanes = slice(i * width // 2, (i + 1) * width // 2)
        rows = [whole[chip ^ c, clip_rows:all_rows, lanes] for c in range(chips)]
        rows += [whole[chip ^ c, 0:clip_rows, lanes] for c in range(chips)]
        out_ref[...] = jnp.concatenate(rows, axis=0).T


def grad_part(turned_ref, head_refs, rows, copies):
    right = jnp.concatenate([x[0:rows, :] for x in head_refs], axis=1)
    hist = jnp.concatenate([x[rows:, :] for x in head_refs], axis=1)
    clip = copies * hist.shape[0]
    out = jnp.dot(turned_ref[:, 0:rows], right, preferred_element_type=jnp.float32)
    return out + jnp.dot(
        turned_ref[:, rows : rows + clip],
        jnp.concatenate([hist] * copies, axis=0),
        preferred_element_type=jnp.float32,
    )


def grad_kernel(rows, copies, heads, turned_ref, *refs):
    out_ref = refs[-1]
    out_ref[...] = grad_part(turned_ref, refs[:heads], rows, copies).astype(out_ref.dtype)


NEAR = ((0, 0), (3, 5), (4, 2), (2, 4), (5, 3))
FAR = ((1, 1), (6, 6), (7, 7))
THERE = (5, 2, 1, 4, 3, 0, 7, 6)


def store_columns(tok, heads, sums, att_hbm, out_hbm, total, sems):
    own = lax.axis_index("tm")
    side = lax.rem(own, 2)
    at = pl.multiple_of(own // 2 * tok, tok)
    moves = []

    def move(a, b):
        moves.append(pltpu.make_async_copy(a, b, sems.at[len(moves)]))
        moves[-1].start()

    def lanes(bits):
        return pl.ds(pl.multiple_of((own ^ jnp.where(side == 0, *bits)) * HD, HD), HD)

    for bits, ref in heads:
        move(ref.at[pl.ds(at, tok), :], att_hbm.at[:, lanes(bits)])
    for i, (bits, (mine, m), (got, g)) in enumerate(sums):
        columns = got[:, g * HD : (g + 1) * HD].astype(jnp.float32)
        total[i] = mine[:, m * HD : (m + 1) * HD] + columns
        move(total.at[i], out_hbm.at[:, lanes(bits)])
    for x in moves:
        x.wait()


def own_near_kernel(rows, copies, tok, turned_ref, *refs):
    n = len(NEAR)
    heads, (out_ref, att_hbm, sems) = refs[:n], refs[n:]
    own = lax.axis_index("tm")
    side = lax.rem(own, 2)
    at = pl.multiple_of(own // 2 * tok, tok)
    moves = []
    for i, (bits, ref) in enumerate(zip(NEAR, heads)):
        lanes = pl.ds(pl.multiple_of((own ^ jnp.where(side == 0, *bits)) * HD, HD), HD)
        moves.append(
            pltpu.make_async_copy(ref.at[pl.ds(at, tok), :], att_hbm.at[:, lanes], sems.at[i])
        )
        moves[-1].start()
    out_ref[...] = grad_part(turned_ref, heads, rows, copies)
    for x in moves:
        x.wait()


def near_kernel(tok, own_near, got_near, *refs):
    n = len(NEAR)
    sums = [(NEAR[i], (own_near, i), (got_near, THERE[i])) for i in range(n) if THERE[i] < n]
    store_columns(tok, [], sums, None, *refs)


def last_kernel(tok, own_near, got_near, own_far, got_far, *refs):
    n = len(NEAR)
    heads, outs = refs[: len(FAR)], refs[len(FAR) + 2 :]

    def column(near, far, i):
        return (near, i) if i < n else (far, i - n)

    sums = [
        (bits, column(own_near, own_far, i), column(got_near, got_far, THERE[i]))
        for i, bits in enumerate(NEAR + FAR)
        if i >= n or THERE[i] >= n
    ]
    store_columns(tok, zip(FAR, heads), sums, *outs)


def head_body(query_rows, key_rows, value_rows, frame_counts, history, offsets, cotangent):
    n = lax.axis_size("tm")
    planes = lax.axis_size("head")
    half = n // 2
    tok, width = query_rows.shape
    tile = history.shape[0]
    clip_rows = n * tile
    cot_rows, all_cols = cotangent.shape
    cols = all_cols // n
    units = cols // HD
    cuts = [0, cot_rows * 7 // 17 // 16 * 16] + [cot_rows // 32 * 16] * 2
    base = 3 * tok + clip_rows
    length = base
    rows = half * tok
    vmem = pl.BlockSpec(memory_space=pltpu.VMEM)
    hbm = pl.BlockSpec(memory_space=pl.ANY)
    bf16 = jnp.bfloat16

    def swap(x, even, odd=None):
        bits = (even, even if odd is None else odd)
        return lax.ppermute(x, "tm", [(i, i ^ bits[i % 2]) for i in range(n)])

    def swap_plane(x, bit):
        pairs = [
            (i * planes + p, (i ^ bit) * planes + (p ^ 1)) for i in range(n) for p in range(planes)
        ]
        return lax.ppermute(x, ("tm", "head"), pairs)

    def call(
        kernel, name, outs, specs, flops, scratch=(), exps=0, out_spec=vmem, limit=VMEM_LIMIT, aliases={}
    ):
        shapes = [jax.ShapeDtypeStruct(s, d) for s, d in outs]
        moved = 2 * sum(math.prod(s.shape) * s.dtype.itemsize for s in shapes)
        return pl.pallas_call(
            kernel,
            out_shape=tuple(shapes),
            in_specs=specs,
            out_specs=out_spec if isinstance(out_spec, tuple) else (out_spec,) * len(shapes),
            scratch_shapes=scratch,
            input_output_aliases=aliases,
            compiler_params=pltpu.CompilerParams(vmem_limit_bytes=limit),
            cost_estimate=pl.CostEstimate(flops=flops, bytes_accessed=moved, transcendentals=exps),
            name=name,
        )

    def pack(heads, lanes, name):
        return call(
            lambda *refs: pack_kernel(n, heads, *refs),
            name,
            [((length, HD), bf16)] * len(heads),
            [hbm] * 4,
            0,
            (
                pltpu.VMEM((tok, lanes), bf16),
                pltpu.VMEM((tok, lanes), bf16),
                pltpu.VMEM((tok, lanes), bf16),
                pltpu.VMEM(history.shape, bf16),
                pltpu.SemaphoreType.DMA((4,)),
            ),
            limit=PACK_LIMIT,
        )(query_rows, key_rows, value_rows, history)

    first, rest = [6, 7], [0, 1, 2, 3, 4, 5]
    packed = dict(zip(first, pack(first, 2 * HD, "pack_first")))
    packed.update(zip(rest, pack(rest, width, "pack_rest")))
    order = [6, 7, 2, 4, 3, 5, 1]
    arrived = {k: swap(packed[k], k) for k in order}
    by_head = [packed[0]] + [arrived[k] for k in order]
    chips = range(half)
    cots = call(
        lambda *refs: cot_kernel(n, tile, cuts, *refs),
        "cot",
        [((2 * units * (cot_rows - cut), HD), bf16) for cut in cuts],
        [hbm] * 4,
        0,
        (
            pltpu.SMEM(offsets.shape, jnp.int32),
            pltpu.VMEM(cotangent.shape, bf16),
            pltpu.SemaphoreType.DMA((2,)),
        ),
    )(offsets, cotangent, arrived[6], arrived[7])
    cots = [cots[0], swap(cots[1], 2, 4), swap(cots[2], 4, 2), swap(cots[3], 6)]
    counts = (
        pltpu.VMEM((n, length, HD), bf16),
        pltpu.VMEM((n, tok, HD), bf16),
        pltpu.SMEM(frame_counts.shape, jnp.int32),
        pltpu.SemaphoreType.DMA,
    )
    pairs = half * tok * WINB * tok
    head_shape = ((rows + clip_rows, HD), bf16)
    same, cross = call(
        lambda *refs: attend_kernel(n, tok, [0] + order, *refs),
        "attend",
        [head_shape, head_shape],
        [hbm] + [vmem] * n,
        8 * pairs * HD,
        counts,
        2 * pairs,
    )(frame_counts, *by_head)
    stack_order = [3, 1, 2]
    (cot_rest,) = call(
        lambda *refs: stack_kernel(stack_order, cuts, 2 * units, *refs),
        "stack",
        [((2 * units * sum(cuts), HD), bf16)],
        [vmem] * (half - 1) + [hbm],
        0,
    )(*[cots[m] for m in stack_order], same)
    cot_swapped = swap_plane(cot_rest, 0)
    first_same, first_cross = swap(same, 2, 4), swap(cross, 3, 5)
    second_same, second_cross = swap(same, 4, 2), swap(cross, 5, 3)
    far_same, far_cross = swap(first_same, 4, 2), swap(first_cross, 2, 4)
    (late_cross,) = call(late_kernel, "late", [head_shape], [vmem] + [hbm] * 2, 0)(
        cross, second_cross, second_same
    )
    c_cross = swap(late_cross, 1)

    turned_own, turned_other = call(
        lambda *refs: turn_kernel(cuts, clip_rows, stack_order, *refs),
        "turn",
        [((cols, half * cot_rows), bf16)] * 2,
        [vmem] * (half + 1),
        0,
        (pltpu.VMEM((half, cot_rows, 2 * cols), bf16),),
    )(cots[0], *[cots[m] for m in stack_order], cot_swapped)

    def grad(turned, heads, dtype, name, behind=()):
        (out,) = call(
            lambda *refs: grad_kernel(rows, half, len(heads), *refs),
            name,
            [((cols, len(heads) * HD), dtype)],
            [vmem] * (1 + len(heads)) + [hbm] * len(behind),
            2 * cols * half * cot_rows * len(heads) * HD,
        )(turned, *heads, *behind)
        return out

    near = [same, second_cross, second_same, first_same, first_cross]
    far = [c_cross, far_same, far_cross]
    whole = [((tok, width), bf16), ((cols, width), jnp.float32)]
    got_near = swap(grad(turned_other, near, bf16, "grad_other_near"), 1)
    own_near, attended = call(
        lambda *refs: own_near_kernel(rows, half, tok, *refs),
        "grad_own_near",
        [((cols, len(near) * HD), jnp.float32), whole[0]],
        [vmem] * (1 + len(near)),
        2 * cols * half * cot_rows * len(near) * HD,
        (pltpu.SemaphoreType.DMA((len(near),)),),
        out_spec=(vmem, hbm),
    )(turned_own, *near)
    got_far = swap(grad(turned_other, far, bf16, "grad_other_far", (own_near,)), 1)
    own_far = grad(turned_own, far, jnp.float32, "grad_own_far")
    (grads,) = call(
        lambda *refs: near_kernel(tok, *refs),
        "near",
        whole[1:],
        [vmem] * 2,
        0,
        (pltpu.VMEM((4, cols, HD), jnp.float32), pltpu.SemaphoreType.DMA((4,))),
        out_spec=hbm,
    )(own_near, got_near)
    return call(
        lambda *refs: last_kernel(tok, *refs),
        "last",
        whole,
        [vmem] * (4 + len(far)) + [hbm] * 2,
        0,
        (pltpu.VMEM((4, cols, HD), jnp.float32), pltpu.SemaphoreType.DMA((7,))),
        out_spec=hbm,
        aliases={4 + len(far): 0, 5 + len(far): 1},
    )(own_near, got_near, own_far, got_far, *far, attended, grads)


def body(query_rows, key_rows, value_rows, frame_counts, history, offsets, cotangent):
    n = lax.axis_size("tm")
    tok, width = query_rows.shape
    by_heads = (
        n == 8
        and lax.axis_size("head") % 2 == 0
        and width == n * HD
        and offsets.shape[1] == n
        and cotangent.shape[0] == tok + n * history.shape[0]
        and cotangent.shape[1] % (n * HD) == 0
        and tok % 16 == 0
        and (n * history.shape[0]) % 16 == 0
    )
    plan = head_body if by_heads else window_body
    return plan(query_rows, key_rows, value_rows, frame_counts, history, offsets, cotangent)


def solution(mesh):
    in_specs = (
        P("tm", "head"),
        P("tm", "head"),
        P("tm", "head"),
        P(),
        P("tm", "head"),
        P("tm", None),
        P("tm", None),
    )
    out_specs = (P("tm", "head"), P("tm", "head"))
    return jax.shard_map(body, mesh=mesh, in_specs=in_specs, out_specs=out_specs, check_vma=False)
```

```python
import math

import jax
import jax.numpy as jnp
from jax import lax
from jax.experimental import pallas as pl
from jax.experimental.pallas import tpu as pltpu
from jax.sharding import PartitionSpec as P

HD = 128
TPF = 64
WINB = 4
VMEM_LIMIT = 24 * 1024 * 1024
PACK_LIMIT = 58 * 1024 * 1024


def from_behind(x, axis, by):
    devices = lax.axis_size(axis)
    pairs = [(i, i + by) for i in range(devices) if 0 <= i + by < devices]
    return lax.ppermute(x, axis, pairs)


def window_body(query_rows, key_rows, value_rows, frame_counts, history, offsets, cotangent):
    tok_rows, feat_width = query_rows.shape
    local_heads = feat_width // HD
    block_total = lax.axis_size("tm")
    own_block = lax.axis_index("tm")
    score_scale = 1.0 / math.sqrt(HD)
    key_value = jnp.stack([key_rows, value_rows])
    pieces = []
    for distance in range(WINB - 1, 0, -1):
        pieces.append(from_behind(key_value, "tm", distance))
    window = jnp.concatenate(pieces + [key_value], axis=1)
    source_block = own_block - (WINB - 1) + jnp.arange(WINB, dtype=jnp.int32)
    block_match = jnp.arange(block_total, dtype=jnp.int32)[None, :] == source_block[:, None]
    block_count = jnp.sum(jnp.where(block_match, frame_counts[None, :], 0), axis=1)
    frame_index = jnp.arange(tok_rows, dtype=jnp.int32) // TPF
    kept_mask = (
        (source_block[:, None] >= 0) & (frame_index[None, :] < block_count[:, None])
    ).reshape(WINB * tok_rows)
    key_window = window[0].reshape(WINB * tok_rows, local_heads, HD)
    value_window = window[1].reshape(WINB * tok_rows, local_heads, HD)
    query_heads = query_rows.reshape(tok_rows, local_heads, HD)
    scores = (
        jnp.einsum("qhd,khd->hqk", query_heads, key_window, preferred_element_type=jnp.float32)
        * score_scale
    )
    scores = jnp.where(kept_mask[None, None, :], scores, -jnp.inf)
    row_max = jnp.max(scores, axis=-1, keepdims=True)
    weights = jnp.exp(scores - row_max)
    probs = (weights / jnp.sum(weights, axis=-1, keepdims=True)).astype(jnp.bfloat16)
    mixed = jnp.einsum("hqk,khd->qhd", probs, value_window, preferred_element_type=jnp.float32)
    attended = mixed.astype(jnp.bfloat16).reshape(tok_rows, feat_width)
    tile_rows = history.shape[0]
    source_tile = (own_block - offsets[0]) % block_total
    source_row = (
        source_tile[:, None] * tile_rows + jnp.arange(tile_rows, dtype=jnp.int32)[None, :]
    ).reshape(-1)
    incoming = lax.all_gather(history, "tm", axis=0, tiled=True)
    piece_rows = incoming.shape[0]
    selector = (source_row[:, None] == jnp.arange(piece_rows, dtype=jnp.int32)[None, :]).astype(
        jnp.bfloat16
    )
    clip_hist = jnp.dot(selector, incoming, preferred_element_type=jnp.float32).astype(jnp.bfloat16)
    disc_clip = jnp.concatenate([clip_hist, attended], axis=0)
    disc_grad = lax.psum_scatter(
        lax.dot_general(
            cotangent, disc_clip, (((0,), (0,)), ((), ())), preferred_element_type=jnp.float32
        ),
        "tm",
        scatter_dimension=0,
        tiled=True,
    )
    return (attended, disc_grad)


def chip_bits(m, side):
    return m if m in (0, 3) else jnp.where(side == 0, m, 3 - m)


def cot_kernel(n, tile, cuts, off_hbm, cot_hbm, *refs):
    outs, (off, cot, sems) = refs[-3 - n // 2 : -3], refs[-3:]
    own = lax.axis_index("tm")
    chip, side = own // 2, lax.rem(own, 2)
    plane = lax.rem(lax.axis_index("head"), 2)
    clip_rows = n * tile
    all_rows, all_cols = cot.shape
    cols = all_cols // n
    fetch_off = pltpu.make_async_copy(off_hbm, off, sems.at[0])
    fetch_cot = pltpu.make_async_copy(cot_hbm, cot, sems.at[1])
    fetch_off.start()
    fetch_cot.start()
    fetch_off.wait()
    r = lax.broadcasted_iota(jnp.int32, (clip_rows, clip_rows), 0)
    c = lax.broadcasted_iota(jnp.int32, (clip_rows, clip_rows), 1)
    select = jnp.zeros((clip_rows, clip_rows), jnp.float32)
    for j in range(n):
        src = lax.rem(own - off[0, j] + 2 * n, n)
        for t in range(tile):
            select = jnp.where((c == j * tile + t) & (r == src * tile + t), 1.0, select)
    fetch_cot.wait()
    cot[0:clip_rows, :] = jnp.dot(
        select.astype(jnp.bfloat16), cot[0:clip_rows, :], preferred_element_type=jnp.float32
    ).astype(jnp.bfloat16)
    units = cols // HD
    for m, out_ref in enumerate(outs):
        rows, first = all_rows - cuts[m], pl.multiple_of(plane * cuts[m], 16)
        there = chip ^ chip_bits(m, side)
        for i, block in enumerate((2 * there + side, 2 * there + 1 - side)):
            for u in range(units):
                at = (i * units + u) * rows
                lanes = pl.ds(pl.multiple_of(block * cols + u * HD, HD), HD)
                out_ref[at : at + rows, :] = cot[pl.ds(first, rows), lanes]


def pack_kernel(n, heads, q_hbm, k_hbm, v_hbm, hist_hbm, *refs):
    outs, (q, k, v, hist, sems) = refs[:-5], refs[-5:]
    own = lax.axis_index("tm")
    tok, width = q.shape
    tile = hist.shape[0]
    clip_rows = n * tile
    start = 0 if width == n * HD else pl.multiple_of(((own ^ heads[0]) // 2) * width, width)
    pairs = [(hist_hbm, hist)] + [
        (x.at[:, pl.ds(start, width)], y) for x, y in ((q_hbm, q), (k_hbm, k), (v_hbm, v))
    ]
    copies = [pltpu.make_async_copy(a, b, sems.at[i]) for i, (a, b) in enumerate(pairs)]
    for copy in copies:
        copy.start()
    copies[0].wait()
    for d, out_ref in zip(heads, outs):
        lanes = pl.ds(pl.multiple_of((own ^ d) * HD, HD), HD)
        tiles = hist[:, lanes].astype(jnp.float32)
        row = lax.broadcasted_iota(jnp.int32, (clip_rows, HD), 0)
        placed = jnp.zeros((clip_rows, HD), jnp.float32)
        for t in range(tile):
            placed = jnp.where(row == own * tile + t, tiles[t : t + 1, :], placed)
        out_ref[3 * tok : 3 * tok + clip_rows, :] = placed.astype(jnp.bfloat16)
    for i, x in enumerate((q, k, v)):
        copies[1 + i].wait()
        for d, out_ref in zip(heads, outs):
            lanes = pl.ds(pl.multiple_of((own ^ d) * HD - start, HD), HD)
            out_ref[i * tok : (i + 1) * tok, :] = x[:, lanes]


def attend_kernel(n, tok, order, counts_hbm, *refs):
    parts, (same_ref, cross_ref, x_ref, mixed_ref, counts, sem) = refs[:n], refs[n:]
    copy = pltpu.make_async_copy(counts_hbm, counts, sem)
    copy.start()
    own = lax.axis_index("tm")
    side = lax.rem(own, 2)
    for k, part in zip(order, parts):
        x_ref[own ^ k] = part[...]
    copy.wait()
    rate = math.log2(math.e) / math.sqrt(HD)
    token = lax.broadcasted_iota(jnp.int32, (tok, 1), 0)
    bias = [
        jnp.where(token < counts[s] * TPF, 0.0, -jnp.inf).astype(jnp.float32) for s in range(n)
    ]
    values = [x_ref[s, 2 * tok : 3 * tok, :].T for s in range(n)]
    def scores_of(block):
        q = x_ref[block, 0:tok, :]
        return {
            s: lax.dot_general(
                x_ref[s, tok : 2 * tok, :],
                q,
                (((1,), (1,)), ((), ())),
                preferred_element_type=jnp.float32,
            )
            + bias[s]
            for s in range(max(0, block - (WINB - 1)), block + 1)
        }

    def mix(block, probs):
        mixed = jnp.zeros((HD, tok), jnp.float32)
        for s, p in probs.items():
            mixed = mixed + jnp.dot(values[s], p, preferred_element_type=jnp.float32)
        mixed_ref[block] = mixed.astype(jnp.bfloat16).T

    ahead, behind = scores_of(0), None
    for block in range(n):
        scores, ahead = ahead, scores_of(block + 1) if block + 1 < n else None
        if behind is not None:
            mix(block - 1, behind)
        top = None
        for x in scores.values():
            high = jnp.max(x, axis=0, keepdims=True)
            top = high if top is None else jnp.maximum(top, high)
        weights = {s: jnp.exp2((x - top) * rate) for s, x in scores.items()}
        total = jnp.zeros((1, tok), jnp.float32)
        for w in weights.values():
            total = total + jnp.sum(w, axis=0, keepdims=True)
        share = 1.0 / total
        behind = {s: (w * share).astype(jnp.bfloat16) for s, w in weights.items()}
    mix(n - 1, behind)
    rows = n // 2 * tok
    clip_rows = same_ref.shape[0] - rows
    hist = jnp.zeros((clip_rows, HD), jnp.float32)
    for s in range(n):
        hist = hist + x_ref[s, 3 * tok : 3 * tok + clip_rows, :].astype(jnp.float32)
    hist = hist.astype(jnp.bfloat16)
    for flip, out_ref in ((0, same_ref), (1, cross_ref)):
        for i in range(n // 2):
            out_ref[i * tok : (i + 1) * tok, :] = mixed_ref[2 * i + (side ^ flip)]
        out_ref[rows:, :] = hist


def stack_kernel(order, cuts, tiles, *refs):
    out_ref = refs[-1]
    plane = lax.rem(lax.axis_index("head"), 2)
    at = 0
    for m, ref in zip(order, refs):
        part = ref.shape[0] // tiles
        for u in range(tiles):
            first = pl.multiple_of(u * part + plane * (part - cuts[m]), 16)
            out_ref[at : at + cuts[m], :] = ref[pl.ds(first, cuts[m]), :]
            at += cuts[m]


def late_kernel(x_ref, *refs):
    refs[-1][...] = x_ref[...]


def turn_kernel(cuts, clip_rows, order, own_in, *refs):
    pieces, (swapped_ref, own_ref, other_ref, whole) = refs[:-4], refs[-4:]
    plane = lax.rem(lax.axis_index("head"), 2)
    own = lax.axis_index("tm")
    chip, side = own // 2, lax.rem(own, 2)
    chips, all_rows, width = whole.shape
    tiles = width // HD
    for u in range(tiles):
        lanes = slice(u * HD, (u + 1) * HD)
        whole[0, :, lanes] = own_in[u * all_rows : (u + 1) * all_rows, :]
        start = 0
        for m, ref in zip(order, pieces):
            at, lo = chip_bits(m, side), cuts[m]
            part = all_rows - lo
            a = ref[u * part : (u + 1) * part, :]
            b = swapped_ref[start + u * lo : start + (u + 1) * lo, :]
            start += tiles * lo
            whole[at, 0:lo, lanes] = jnp.where(plane == 0, a[:lo], b)
            whole[at, lo:part, lanes] = jnp.where(plane == 0, a[lo:], a[: part - lo])
            whole[at, part:all_rows, lanes] = jnp.where(plane == 0, b, a[part - lo :])
    for i, out_ref in enumerate((own_ref, other_ref)):
        lanes = slice(i * width // 2, (i + 1) * width // 2)
        rows = [whole[chip ^ c, clip_rows:all_rows, lanes] for c in range(chips)]
        rows += [whole[chip ^ c, 0:clip_rows, lanes] for c in range(chips)]
        out_ref[...] = jnp.concatenate(rows, axis=0).T


def grad_part(turned_ref, head_refs, rows, copies):
    right = jnp.concatenate([x[0:rows, :] for x in head_refs], axis=1)
    hist = jnp.concatenate([x[rows:, :] for x in head_refs], axis=1)
    clip = copies * hist.shape[0]
    out = jnp.dot(turned_ref[:, 0:rows], right, preferred_element_type=jnp.float32)
    return out + jnp.dot(
        turned_ref[:, rows : rows + clip],
        jnp.concatenate([hist] * copies, axis=0),
        preferred_element_type=jnp.float32,
    )


def grad_kernel(rows, copies, heads, turned_ref, *refs):
    out_ref = refs[-1]
    out_ref[...] = grad_part(turned_ref, refs[:heads], rows, copies).astype(out_ref.dtype)


NEAR = ((0, 0), (3, 5), (4, 2), (2, 4), (5, 3))
FAR = ((1, 1), (6, 6), (7, 7))
THERE = (5, 2, 1, 4, 3, 0, 7, 6)


def store_columns(tok, heads, sums, att_hbm, out_hbm, total, sems):
    own = lax.axis_index("tm")
    side = lax.rem(own, 2)
    at = pl.multiple_of(own // 2 * tok, tok)
    moves = []

    def move(a, b):
        moves.append(pltpu.make_async_copy(a, b, sems.at[len(moves)]))
        moves[-1].start()

    def lanes(bits):
        return pl.ds(pl.multiple_of((own ^ jnp.where(side == 0, *bits)) * HD, HD), HD)

    for bits, ref in heads:
        move(ref.at[pl.ds(at, tok), :], att_hbm.at[:, lanes(bits)])
    for i, (bits, (mine, m), (got, g)) in enumerate(sums):
        columns = got[:, g * HD : (g + 1) * HD].astype(jnp.float32)
        total[i] = mine[:, m * HD : (m + 1) * HD] + columns
        move(total.at[i], out_hbm.at[:, lanes(bits)])
    for x in moves:
        x.wait()


def own_near_kernel(rows, copies, tok, turned_ref, *refs):
    n = len(NEAR)
    heads, (out_ref, att_hbm, sems) = refs[:n], refs[n:]
    own = lax.axis_index("tm")
    side = lax.rem(own, 2)
    at = pl.multiple_of(own // 2 * tok, tok)
    moves = []
    for i, (bits, ref) in enumerate(zip(NEAR, heads)):
        lanes = pl.ds(pl.multiple_of((own ^ jnp.where(side == 0, *bits)) * HD, HD), HD)
        moves.append(
            pltpu.make_async_copy(ref.at[pl.ds(at, tok), :], att_hbm.at[:, lanes], sems.at[i])
        )
        moves[-1].start()
    out_ref[...] = grad_part(turned_ref, heads, rows, copies)
    for x in moves:
        x.wait()


def near_kernel(tok, own_near, got_near, *refs):
    n = len(NEAR)
    sums = [(NEAR[i], (own_near, i), (got_near, THERE[i])) for i in range(n) if THERE[i] < n]
    store_columns(tok, [], sums, None, *refs)


def last_kernel(tok, own_near, got_near, own_far, got_far, *refs):
    n = len(NEAR)
    heads, outs = refs[: len(FAR)], refs[len(FAR) + 2 :]

    def column(near, far, i):
        return (near, i) if i < n else (far, i - n)

    sums = [
        (bits, column(own_near, own_far, i), column(got_near, got_far, THERE[i]))
        for i, bits in enumerate(NEAR + FAR)
        if i >= n or THERE[i] >= n
    ]
    store_columns(tok, zip(FAR, heads), sums, *outs)


def head_body(query_rows, key_rows, value_rows, frame_counts, history, offsets, cotangent):
    n = lax.axis_size("tm")
    planes = lax.axis_size("head")
    half = n // 2
    tok, width = query_rows.shape
    tile = history.shape[0]
    clip_rows = n * tile
    cot_rows, all_cols = cotangent.shape
    cols = all_cols // n
    units = cols // HD
    cuts = [0, cot_rows * 7 // 17 // 16 * 16] + [cot_rows // 32 * 16] * 2
    base = 3 * tok + clip_rows
    length = base
    rows = half * tok
    vmem = pl.BlockSpec(memory_space=pltpu.VMEM)
    hbm = pl.BlockSpec(memory_space=pl.ANY)
    bf16 = jnp.bfloat16

    def swap(x, even, odd=None):
        bits = (even, even if odd is None else odd)
        return lax.ppermute(x, "tm", [(i, i ^ bits[i % 2]) for i in range(n)])

    def swap_plane(x, bit):
        pairs = [
            (i * planes + p, (i ^ bit) * planes + (p ^ 1)) for i in range(n) for p in range(planes)
        ]
        return lax.ppermute(x, ("tm", "head"), pairs)

    def call(
        kernel, name, outs, specs, flops, scratch=(), exps=0, out_spec=vmem, limit=VMEM_LIMIT, aliases={}
    ):
        shapes = [jax.ShapeDtypeStruct(s, d) for s, d in outs]
        moved = 2 * sum(math.prod(s.shape) * s.dtype.itemsize for s in shapes)
        return pl.pallas_call(
            kernel,
            out_shape=tuple(shapes),
            in_specs=specs,
            out_specs=out_spec if isinstance(out_spec, tuple) else (out_spec,) * len(shapes),
            scratch_shapes=scratch,
            input_output_aliases=aliases,
            compiler_params=pltpu.CompilerParams(vmem_limit_bytes=limit),
            cost_estimate=pl.CostEstimate(flops=flops, bytes_accessed=moved, transcendentals=exps),
            name=name,
        )

    def pack(heads, lanes, name):
        return call(
            lambda *refs: pack_kernel(n, heads, *refs),
            name,
            [((length, HD), bf16)] * len(heads),
            [hbm] * 4,
            0,
            (
                pltpu.VMEM((tok, lanes), bf16),
                pltpu.VMEM((tok, lanes), bf16),
                pltpu.VMEM((tok, lanes), bf16),
                pltpu.VMEM(history.shape, bf16),
                pltpu.SemaphoreType.DMA((4,)),
            ),
            limit=PACK_LIMIT,
        )(query_rows, key_rows, value_rows, history)

    first, rest = [6, 7], [0, 1, 2, 3, 4, 5]
    packed = dict(zip(first, pack(first, 2 * HD, "pack_first")))
    packed.update(zip(rest, pack(rest, width, "pack_rest")))
    order = [6, 7, 2, 4, 3, 5, 1]
    arrived = {k: swap(packed[k], k) for k in order}
    by_head = [packed[0]] + [arrived[k] for k in order]
    chips = range(half)
    cots = call(
        lambda *refs: cot_kernel(n, tile, cuts, *refs),
        "cot",
        [((2 * units * (cot_rows - cut), HD), bf16) for cut in cuts],
        [hbm] * 4,
        0,
        (
            pltpu.SMEM(offsets.shape, jnp.int32),
            pltpu.VMEM(cotangent.shape, bf16),
            pltpu.SemaphoreType.DMA((2,)),
        ),
    )(offsets, cotangent, arrived[6], arrived[7])
    cots = [cots[0], swap(cots[1], 2, 4), swap(cots[2], 4, 2), swap(cots[3], 6)]
    counts = (
        pltpu.VMEM((n, length, HD), bf16),
        pltpu.VMEM((n, tok, HD), bf16),
        pltpu.SMEM(frame_counts.shape, jnp.int32),
        pltpu.SemaphoreType.DMA,
    )
    pairs = half * tok * WINB * tok
    head_shape = ((rows + clip_rows, HD), bf16)
    same, cross = call(
        lambda *refs: attend_kernel(n, tok, [0] + order, *refs),
        "attend",
        [head_shape, head_shape],
        [hbm] + [vmem] * n,
        8 * pairs * HD,
        counts,
        2 * pairs,
    )(frame_counts, *by_head)
    stack_order = [3, 1, 2]
    (cot_rest,) = call(
        lambda *refs: stack_kernel(stack_order, cuts, 2 * units, *refs),
        "stack",
        [((2 * units * sum(cuts), HD), bf16)],
        [vmem] * (half - 1) + [hbm],
        0,
    )(*[cots[m] for m in stack_order], same)
    cot_swapped = swap_plane(cot_rest, 0)
    first_same, first_cross = swap(same, 2, 4), swap(cross, 3, 5)
    second_same, second_cross = swap(same, 4, 2), swap(cross, 5, 3)
    far_same, far_cross = swap(first_same, 4, 2), swap(first_cross, 2, 4)
    (late_cross,) = call(late_kernel, "late", [head_shape], [vmem, hbm], 0)(
        cross, second_same
    )
    c_cross = swap(late_cross, 1)

    turned_own, turned_other = call(
        lambda *refs: turn_kernel(cuts, clip_rows, stack_order, *refs),
        "turn",
        [((cols, half * cot_rows), bf16)] * 2,
        [vmem] * (half + 1),
        0,
        (pltpu.VMEM((half, cot_rows, 2 * cols), bf16),),
    )(cots[0], *[cots[m] for m in stack_order], cot_swapped)

    def grad(turned, heads, dtype, name, behind=()):
        (out,) = call(
            lambda *refs: grad_kernel(rows, half, len(heads), *refs),
            name,
            [((cols, len(heads) * HD), dtype)],
            [vmem] * (1 + len(heads)) + [hbm] * len(behind),
            2 * cols * half * cot_rows * len(heads) * HD,
        )(turned, *heads, *behind)
        return out

    near = [same, second_cross, second_same, first_same, first_cross]
    far = [c_cross, far_same, far_cross]
    whole = [((tok, width), bf16), ((cols, width), jnp.float32)]
    got_near = swap(grad(turned_other, near, bf16, "grad_other_near"), 1)
    own_near, attended = call(
        lambda *refs: own_near_kernel(rows, half, tok, *refs),
        "grad_own_near",
        [((cols, len(near) * HD), jnp.float32), whole[0]],
        [vmem] * (1 + len(near)),
        2 * cols * half * cot_rows * len(near) * HD,
        (pltpu.SemaphoreType.DMA((len(near),)),),
        out_spec=(vmem, hbm),
    )(turned_own, *near)
    got_far = swap(grad(turned_other, far, bf16, "grad_other_far", (own_near,)), 1)
    own_far = grad(turned_own, far, jnp.float32, "grad_own_far")
    (grads,) = call(
        lambda *refs: near_kernel(tok, *refs),
        "near",
        whole[1:],
        [vmem] * 2,
        0,
        (pltpu.VMEM((4, cols, HD), jnp.float32), pltpu.SemaphoreType.DMA((4,))),
        out_spec=hbm,
    )(own_near, got_near)
    return call(
        lambda *refs: last_kernel(tok, *refs),
        "last",
        whole,
        [vmem] * (4 + len(far)) + [hbm] * 2,
        0,
        (pltpu.VMEM((4, cols, HD), jnp.float32), pltpu.SemaphoreType.DMA((7,))),
        out_spec=hbm,
        aliases={4 + len(far): 0, 5 + len(far): 1},
    )(own_near, got_near, own_far, got_far, *far, attended, grads)


def body(query_rows, key_rows, value_rows, frame_counts, history, offsets, cotangent):
    n = lax.axis_size("tm")
    tok, width = query_rows.shape
    by_heads = (
        n == 8
        and lax.axis_size("head") % 2 == 0
        and width == n * HD
        and offsets.shape[1] == n
        and cotangent.shape[0] == tok + n * history.shape[0]
        and cotangent.shape[1] % (n * HD) == 0
        and tok % 16 == 0
        and (n * history.shape[0]) % 16 == 0
    )
    plan = head_body if by_heads else window_body
    return plan(query_rows, key_rows, value_rows, frame_counts, history, offsets, cotangent)


def solution(mesh):
    in_specs = (
        P("tm", "head"),
        P("tm", "head"),
        P("tm", "head"),
        P(),
        P("tm", "head"),
        P("tm", None),
        P("tm", None),
    )
    out_specs = (P("tm", "head"), P("tm", "head"))
    return jax.shard_map(body, mesh=mesh, in_specs=in_specs, out_specs=out_specs, check_vma=False)
```
